32 devices in a mesh: patch: 16 (over z, x, core), head: 2 (over y).
Axes of the slice: x: 2, y: 2, z: 4, core: 2. Of those that a mesh axis runs over, the one named last changes fastest.
Arguments:
- queries: bfloat16 [768, 3072], P('patch', 'head'), as said below
- stale_kv: bfloat16 [2, 768, 3072], P(None, None, 'head'), may hold values from -6 to 6, as said below
- codes: int32 [2, 768, 3072], P(None, 'patch', 'head'), may hold values from -127 to 127
- exponents: int32 [2, 768, 24], P(None, 'patch', 'head'), may hold values from -9 to -6
- text_kv: bfloat16 [2, 512, 3072], P(None, None, 'head'), may hold values from -6 to 6, as said below
- out_weight: bfloat16 [3072, 3072], P('head', 'patch'), may hold values from -0.109375 to 0.109375
- out_bias: float32 [3072], P('head'), may hold values from -0.6 to 0.6
- out_gate: float32 [3072], P('head'), may hold values from 2 to 8
Outputs:
- gated_out: bfloat16 [768, 3072], P('patch', 'head')
The draws below stay inside these ranges and needn't reach their ends.
Inputs may be any that keep to these rules, and one draw needn't show every extreme that they name: queries are real-valued. `stale_kv`: last step's keys and values are real-valued. `text_kv`: text keys and values are real-valued.
All inputs are finite; a program needn't handle non-finite values.
Results may differ from the reference program's by a relative error of at most 0.0075.
Values may be sent and summed in bfloat16 or wider, within the bound.
No kernel may reach another device: no remote copies, remote signals or barrier semaphores. Data moves between devices by JAX's collectives and lax.ppermute only.
A program may use at most 64 MiB of HBM per device.

```python
import math
import jax
import jax.numpy as jnp
from jax import lax

D = 3072
HEADS = 24
HD = 128
TEXT = 512
TOKENS = 768


def draw_queries(key, part):
    key = jax.random.fold_in(key, 12)
    return (2.0 * jnp.clip(jax.random.normal(key, (TOKENS, HEADS * HD), jnp.float32), -4.0, 4.0)).astype(jnp.bfloat16)


def draw_stale_kv(key, part):
    key = jax.random.fold_in(key, 13)
    return jnp.clip(jax.random.normal(key, (2, TOKENS, HEADS * HD), jnp.float32), -6.0, 6.0).astype(jnp.bfloat16)


def draw_text_kv(key, part):
    key = jax.random.fold_in(key, 11)
    return jnp.clip(jax.random.normal(key, (2, TEXT, HEADS * HD), jnp.float32), -6.0, 6.0).astype(jnp.bfloat16)


def plant(values, own_key, smallest, largest):
    spot = [jax.random.randint(jax.random.fold_in(own_key, axis), (), 0, length) for axis, length in enumerate(values.shape)]
    longest = values.shape.index(max(values.shape))
    beside = spot[:longest] + [(spot[longest] + 1) % values.shape[longest]] + spot[longest + 1:]
    return values.at[tuple(spot)].set(smallest).at[tuple(beside)].set(largest)


def level_of(rng, shape, pieces, low, high):
    gain, own = 1.0, jax.random.fold_in(rng, 6)
    for dim, shards_of in pieces:
        steps = jnp.exp(jax.random.uniform(jax.random.fold_in(own, dim), (shards_of,), jnp.float32, low / len(pieces), high / len(pieces)))
        gain = gain * jnp.repeat(steps, shape[dim] // shards_of).reshape([-1 if axis == dim else 1 for axis in range(len(shape))])
    return gain


def centred(own_key, dims, width, reach, cuts=(), kind=jnp.bfloat16):
    gain = level_of(own_key, dims, cuts, -0.22, 0.18) if cuts else 1.0
    values = jax.random.normal(own_key, dims, jnp.float32) * width * gain
    return jnp.minimum(jnp.maximum(values, -reach), reach).astype(kind)


def setup_inputs(seed: int = 0) -> dict:
    streams_of = jax.random.split(jax.random.key(seed), 9)
    queries = draw_queries(jax.random.fold_in(streams_of[8], 71), 0)
    stale_kv = draw_stale_kv(jax.random.fold_in(streams_of[8], 71), 0)
    codes = plant(jax.random.randint(streams_of[2], (2, TOKENS, HEADS * HD), -127, 128), jax.random.fold_in(streams_of[2], 1), -127, 127).astype(jnp.int32)
    exponents = plant(jax.random.randint(streams_of[3], (2, TOKENS, HEADS), -9, -5), jax.random.fold_in(streams_of[3], 1), -9, (-5) - 1).astype(jnp.int32)
    text_kv = draw_text_kv(jax.random.fold_in(streams_of[8], 71), 0)
    out_weight = centred(streams_of[5], (HEADS * HD, D), (HEADS * HD) ** -0.5, 0.109375, ((0, 2), (1, 16)))
    out_bias = centred(streams_of[6], (D,), 0.1, 0.6, ((0, 2),), jnp.float32)
    out_gate = jnp.clip(jnp.exp(math.log(8.0) - 1.3862944 * jax.random.uniform(streams_of[7], (D,), jnp.float32) ** level_of(streams_of[7], (D,), ((0, 2),), -0.2, 0.2)), 2.0, 8.0)
    return {"queries": queries, "stale_kv": stale_kv, "codes": codes, "exponents": exponents, "text_kv": text_kv, "out_weight": out_weight, "out_bias": out_bias, "out_gate": out_gate}


def one_head(inputs):
    query, text_key, text_value, image_key, image_value = inputs
    text_scores = jnp.dot(query, text_key.T, preferred_element_type=jnp.float32)
    image_scores = jnp.dot(query.astype(jnp.float32), image_key.T, precision=lax.Precision.HIGHEST)
    scores = jnp.concatenate([text_scores, image_scores], axis=1) * (HD ** -0.5)
    row_peak = jnp.max(scores, axis=1, keepdims=True)
    weights = jnp.exp(scores - row_peak).astype(jnp.bfloat16)
    row_total = jnp.sum(weights.astype(jnp.float32), axis=1, keepdims=True)
    text_part = jnp.dot(weights[:, :TEXT], text_value, preferred_element_type=jnp.float32)
    image_part = jnp.dot(weights[:, TEXT:].astype(jnp.float32), image_value, precision=lax.Precision.HIGHEST)
    return ((text_part + image_part) / row_total).astype(jnp.bfloat16)


def reference(queries, stale_kv, codes, exponents, text_kv, out_weight, out_bias, out_gate):
    blocks = jnp.exp2(exponents.astype(jnp.float32))
    decoded = (codes.astype(jnp.float32).reshape(2, TOKENS, HEADS, HD) * blocks[..., None]).astype(jnp.bfloat16)
    rebuilt = stale_kv.astype(jnp.float32).reshape(2, TOKENS, HEADS, HD) + decoded.astype(jnp.float32)
    rebuilt = rebuilt.transpose(0, 2, 1, 3)
    query_heads = queries.reshape(TOKENS, HEADS, HD).transpose(1, 0, 2)
    text_heads = text_kv.reshape(2, TEXT, HEADS, HD).transpose(0, 2, 1, 3)
    attended = lax.map(one_head, (query_heads, text_heads[0], text_heads[1], rebuilt[0], rebuilt[1]))
    attended = attended.transpose(1, 0, 2).reshape(TOKENS, HEADS * HD)
    projected = jnp.dot(attended, out_weight, preferred_element_type=jnp.float32)
    return (out_gate * (projected + out_bias)).astype(jnp.bfloat16)
```

```python
import functools

import jax
import jax.numpy as jnp
from jax import lax
from jax.experimental import pallas as pl
from jax.experimental.pallas import tpu as pltpu
from jax.sharding import PartitionSpec as P

HD = 128
SPREAD = 4
VMEM = pl.BlockSpec(memory_space=pltpu.VMEM)
ANY = pl.BlockSpec(memory_space=pl.ANY)
NT = (((1,), (1,)), ((), ()))


def plain_body(queries, stale_kv, codes, exponents, text_kv, out_weight, out_bias, out_gate):
    tok_rows = queries.shape[0]
    row_width = queries.shape[1]
    head_count = row_width // HD
    text_count = text_kv.shape[1]
    scale_factor = HD ** (-0.5)
    blocks = jnp.exp2(exponents.astype(jnp.float32))
    decoded = codes.astype(jnp.float32).reshape(2, tok_rows, head_count, HD) * blocks[..., None]
    decoded = decoded.astype(jnp.bfloat16).reshape(2, tok_rows, row_width)
    arrived = lax.all_gather(decoded, "patch", axis=1, tiled=True)
    all_rows = arrived.shape[1]
    query_heads = queries.reshape(tok_rows, head_count, HD)
    text_heads = text_kv.reshape(2, text_count, head_count, HD)
    stale_heads = stale_kv.reshape(2, all_rows, head_count, HD)
    arrived_heads = arrived.reshape(2, all_rows, head_count, HD)
    text_scores = jnp.einsum("thd,khd->htk", query_heads, text_heads[0], preferred_element_type=jnp.float32)
    rebuilt = stale_heads.astype(jnp.float32) + arrived_heads.astype(jnp.float32)
    image_scores = jnp.einsum(
        "thd,khd->htk", query_heads.astype(jnp.float32), rebuilt[0], precision=lax.Precision.HIGHEST
    )
    scores = jnp.concatenate([text_scores, image_scores], axis=2) * scale_factor
    row_peak = jnp.max(scores, axis=2, keepdims=True)
    weights = jnp.exp(scores - row_peak).astype(jnp.bfloat16)
    row_total = jnp.sum(weights.astype(jnp.float32), axis=2)
    text_part = jnp.einsum(
        "htk,khd->thd", weights[:, :, :text_count], text_heads[1], preferred_element_type=jnp.float32
    )
    image_part = jnp.einsum(
        "htk,khd->thd",
        weights[:, :, text_count:].astype(jnp.float32),
        rebuilt[1],
        precision=lax.Precision.HIGHEST,
    )
    attended = ((text_part + image_part) / row_total.T[:, :, None]).astype(jnp.bfloat16).reshape(tok_rows, row_width)
    partial_terms = jnp.dot(
        attended, lax.all_gather(out_weight, "patch", axis=1, tiled=True), preferred_element_type=jnp.float32
    )
    column_share = lax.psum_scatter(partial_terms, "head", scatter_dimension=1, tiled=True)
    return (out_gate * (column_share + out_bias)).astype(jnp.bfloat16)


def aligned(value, step):
    return pl.multiple_of(value * step, step)


def place(groups):
    me = lax.axis_index("patch")
    return me // SPREAD, lax.rem(me, SPREAD)


def pack_kernel(groups, queries, codes, exponents, *rest):
    outs, (held,) = rest[: 2 * groups], rest[2 * groups :]
    group, _ = place(groups)
    heads = queries.shape[1] // HD
    per = heads // groups
    for kind in range(2):
        scales = jnp.left_shift(1, exponents[kind] + 16).astype(jnp.float32) * (2.0**-16)
        for head in range(heads):
            slot = lax.rem(head // per - group + groups, groups)
            inside = slice((head % per) * HD, (head % per + 1) * HD)
            whole = slice(head * HD, (head + 1) * HD)
            decoded = codes[kind, :, whole].astype(jnp.float32) * scales[:, head : head + 1]
            held[slot, kind, :, inside] = decoded.astype(jnp.bfloat16)
    for target in range(groups):
        slot = lax.rem(target - group + groups, groups)
        held[slot, 2] = queries[:, target * per * HD : (target + 1) * per * HD]
    for slot in range(groups):
        outs[2 * slot][...] = held[slot, 0:2]
        outs[2 * slot + 1][...] = held[slot, 2]


def pack(groups, queries, codes, exponents):
    rows, width = queries.shape
    share = width // groups
    shapes = []
    for _ in range(groups):
        shapes += [
            jax.ShapeDtypeStruct((2, rows, share), jnp.bfloat16),
            jax.ShapeDtypeStruct((rows, share), jnp.bfloat16),
        ]
    outs = pl.pallas_call(
        functools.partial(pack_kernel, groups),
        out_shape=shapes,
        in_specs=[VMEM] * 3,
        out_specs=[VMEM] * len(shapes),
        scratch_shapes=[pltpu.VMEM((groups, 3, rows, share), jnp.bfloat16)],
        compiler_params=pltpu.CompilerParams(vmem_limit_bytes=16 << 20),
        cost_estimate=pl.CostEstimate(flops=2 * codes.size, bytes_accessed=6 * codes.size, transcendentals=0),
    )(queries, codes, exponents)
    return outs[0::2], outs[1::2]


def attend_kernel(groups, *refs):
    parts, refs = refs[: groups * SPREAD], refs[groups * SPREAD :]
    query_parts, refs = refs[:groups], refs[groups:]
    text_hbm, stale_hbm, out, query, residual, text, stale, sems = refs
    group, spot = place(groups)
    rows, width = query_parts[0].shape
    columns = pl.ds(aligned(group, width), width)
    text_copy = pltpu.make_async_copy(text_hbm.at[:, :, columns], text, sems.at[0])
    stale_copy = pltpu.make_async_copy(stale_hbm.at[:, :, columns], stale, sems.at[1])
    text_copy.start()
    stale_copy.start()
    for slot in range(groups):
        origin = lax.rem(group - slot + groups, groups)
        query[pl.ds(aligned(origin, rows), rows), :] = query_parts[slot][...]
        for twist in range(SPREAD):
            token = origin * SPREAD + jnp.bitwise_xor(spot, twist)
            residual[:, pl.ds(aligned(token, rows), rows), :] = parts[slot * SPREAD + twist][...]
    text_copy.wait()
    stale_copy.wait()
    for head in range(width // HD):
        cols = slice(head * HD, (head + 1) * HD)
        asked = query[:, cols]
        text_scores = lax.dot_general(asked, text[0, :, cols], NT, preferred_element_type=jnp.float32)
        image_scores = lax.dot_general(asked, stale[0, :, cols], NT, preferred_element_type=jnp.float32)
        image_scores += lax.dot_general(asked, residual[0, :, cols], NT, preferred_element_type=jnp.float32)
        text_scores *= HD**-0.5
        image_scores *= HD**-0.5
        peak = jnp.maximum(
            jnp.max(text_scores, axis=1, keepdims=True), jnp.max(image_scores, axis=1, keepdims=True)
        )
        text_weights = jnp.exp(text_scores - peak).astype(jnp.bfloat16)
        image_weights = jnp.exp(image_scores - peak).astype(jnp.bfloat16)
        total = jnp.sum(text_weights.astype(jnp.float32), axis=1, keepdims=True)
        total += jnp.sum(image_weights.astype(jnp.float32), axis=1, keepdims=True)
        mixed = jnp.dot(text_weights, text[1, :, cols], preferred_element_type=jnp.float32)
        mixed += jnp.dot(image_weights, stale[1, :, cols], preferred_element_type=jnp.float32)
        mixed += jnp.dot(image_weights, residual[1, :, cols], preferred_element_type=jnp.float32)
        out[:, cols] = (mixed / total).astype(jnp.bfloat16)


def attend(groups, parts, query_parts, text_kv, stale_kv):
    rows, width = query_parts[0].shape
    keys = stale_kv.shape[1]
    texts = text_kv.shape[1]
    bf16 = jnp.bfloat16
    return pl.pallas_call(
        functools.partial(attend_kernel, groups),
        out_shape=jax.ShapeDtypeStruct((groups * rows, width), bf16),
        in_specs=[VMEM] * (len(parts) + len(query_parts)) + [ANY] * 2,
        out_specs=VMEM,
        scratch_shapes=[
            pltpu.VMEM((groups * rows, width), bf16),
            pltpu.VMEM((2, keys, width), bf16),
            pltpu.VMEM((2, texts, width), bf16),
            pltpu.VMEM((2, keys, width), bf16),
            pltpu.SemaphoreType.DMA((2,)),
        ],
        compiler_params=pltpu.CompilerParams(vmem_limit_bytes=40 << 20),
        cost_estimate=pl.CostEstimate(
            flops=4 * groups * rows * width * (texts + 2 * keys),
            bytes_accessed=4 * width * (texts + 2 * keys),
            transcendentals=groups * rows * (texts + keys) * (width // HD),
        ),
    )(*parts, *query_parts, text_kv, stale_kv)


def order_kernel(groups, *refs):
    parts, out = refs[:SPREAD], refs[SPREAD]
    _, spot = place(groups)
    rows = parts[0].shape[0]
    for twist in range(SPREAD):
        out[pl.ds(aligned(jnp.bitwise_xor(spot, twist), rows), rows), :] = parts[twist][...]


def order(groups, parts):
    rows, width = parts[0].shape
    return pl.pallas_call(
        functools.partial(order_kernel, groups),
        out_shape=jax.ShapeDtypeStruct((SPREAD * rows, width), jnp.bfloat16),
        in_specs=[VMEM] * SPREAD,
        out_specs=VMEM,
        compiler_params=pltpu.CompilerParams(vmem_limit_bytes=16 << 20),
        cost_estimate=pl.CostEstimate(flops=0, bytes_accessed=4 * SPREAD * rows * width, transcendentals=0),
    )(*parts)


def project_kernel(groups, halves, *refs):
    parts, weight, refs = refs[:groups], refs[groups], refs[groups + 1 :]
    outs, (total,) = refs[:groups], refs[groups:]
    group, _ = place(groups)
    half = lax.axis_index("head")
    width = parts[0].shape[1]
    rows = outs[0].shape[0]
    for slot in range(groups):
        origin = lax.rem(group - slot + groups, groups)
        term = lax.dot_general(
            parts[slot][...],
            weight[:, pl.ds(aligned(origin, width), width)],
            NT,
            preferred_element_type=jnp.float32,
        )
        if slot == 0:
            total[...] = term
        else:
            total[...] += term
    first = lax.rem(group, groups // halves) * halves + half
    for turn in range(groups):
        target = lax.rem(first + turn, groups)
        outs[turn][...] = total[pl.ds(aligned(target, rows), rows), :].astype(jnp.bfloat16)


def project(groups, halves, parts, weight):
    tokens, width = parts[0].shape
    columns = weight.shape[0]
    shape = jax.ShapeDtypeStruct((tokens // groups, columns), jnp.bfloat16)
    return pl.pallas_call(
        functools.partial(project_kernel, groups, halves),
        out_shape=[shape] * groups,
        in_specs=[VMEM] * (groups + 1),
        out_specs=[VMEM] * groups,
        scratch_shapes=[pltpu.VMEM((tokens, columns), jnp.float32)],
        compiler_params=pltpu.CompilerParams(vmem_limit_bytes=24 << 20),
        cost_estimate=pl.CostEstimate(
            flops=2 * tokens * columns * width * groups,
            bytes_accessed=2 * columns * width * groups,
            transcendentals=0,
        ),
    )(*parts, weight)


def finish_kernel(groups, halves, *refs):
    parts, (bias, gate, out, held) = refs[:groups], refs[groups:]
    group, _ = place(groups)
    columns = parts[0].shape[1]
    for turn in range(groups):
        held[lax.rem(group - turn + groups, groups)] = parts[turn][...]
    for block in range(groups // halves):
        cols = slice(block * columns, (block + 1) * columns)
        total = bias[:, cols]
        for half in range(halves):
            total = total + held[block * halves + half].astype(jnp.float32)
        out[:, cols] = (gate[:, cols] * total).astype(jnp.bfloat16)


def finish(groups, halves, parts, bias, gate):
    rows, columns = parts[0].shape
    width = columns * groups // halves
    return pl.pallas_call(
        functools.partial(finish_kernel, groups, halves),
        out_shape=jax.ShapeDtypeStruct((rows, width), jnp.bfloat16),
        in_specs=[VMEM] * (groups + 2),
        out_specs=VMEM,
        scratch_shapes=[pltpu.VMEM((groups, rows, columns), jnp.bfloat16)],
        compiler_params=pltpu.CompilerParams(vmem_limit_bytes=16 << 20),
        cost_estimate=pl.CostEstimate(flops=3 * rows * width, bytes_accessed=4 * rows * width, transcendentals=0),
    )(*parts, bias.reshape(1, width), gate.reshape(1, width))


def grouped_body(groups, halves, queries, stale_kv, codes, exponents, text_kv, out_weight, out_bias, out_gate):
    size = groups * SPREAD

    def to_group(value, turn):
        pairs = [(p, (p // SPREAD + turn) % groups * SPREAD + p % SPREAD) for p in range(size)]
        return lax.ppermute(value, "patch", pairs)

    def swap(value, twist):
        return lax.ppermute(value, "patch", [(p, p ^ twist) for p in range(size)])

    def spread(value):
        far = swap(value, 2)
        return [value, swap(value, 1), far, swap(far, 1)]

    residuals, query_parts = pack(groups, queries, codes, exponents)
    parts = []
    for turn in range(groups):
        parts += spread(residuals[turn] if turn == 0 else to_group(residuals[turn], turn))
    query_parts = [q if turn == 0 else to_group(q, turn) for turn, q in enumerate(query_parts)]
    weight = order(groups, spread(out_weight.T))
    attended = attend(groups, parts, query_parts, text_kv, stale_kv)
    attended_parts = [attended] + [to_group(attended, turn) for turn in range(1, groups)]
    terms = project(groups, halves, attended_parts, weight)
    per = groups // halves
    arrived = []
    for turn, term in enumerate(terms):
        pairs = []
        for p in range(size):
            for half in range(halves):
                group, spot = divmod(p, SPREAD)
                target = (group % per * halves + half + turn) % groups
                pairs.append((p * halves + half, (target * SPREAD + spot) * halves + group // per))
        arrived.append(lax.ppermute(term, ("patch", "head"), pairs))
    return finish(groups, halves, arrived, out_bias, out_gate)


def solution(mesh):
    patches, halves = mesh.shape["patch"], mesh.shape["head"]
    placed = (
        P("patch", "head"),
        P(None, None, "head"),
        P(None, "patch", "head"),
        P(None, "patch", "head"),
        P(None, None, "head"),
        P("head", "patch"),
        P("head"),
        P("head"),
    )

    def body(*args):
        heads = args[0].shape[1] // HD
        groups = patches // SPREAD
        if patches % SPREAD or heads % groups or groups % halves:
            return plain_body(*args)
        return grouped_body(groups, halves, *args)

    return jax.shard_map(body, mesh=mesh, in_specs=placed, out_specs=P("patch", "head"), check_vma=False)
```

```python
import jax
import jax.numpy as jnp
from jax import lax
from jax.experimental import pallas as pl
from jax.experimental.pallas import tpu as pltpu
from jax.sharding import PartitionSpec as P

HD = 128
SPREAD = 4
VMEM = pl.BlockSpec(memory_space=pltpu.VMEM)
HBM = pl.BlockSpec(memory_space=pltpu.HBM)
NT = (((1,), (1,)), ((), ()))


def plain_body(queries, stale_kv, codes, exponents, text_kv, out_weight, out_bias, out_gate):
    tok_rows = queries.shape[0]
    row_width = queries.shape[1]
    head_count = row_width // HD
    text_count = text_kv.shape[1]
    scale_factor = HD ** (-0.5)
    blocks = jnp.exp2(exponents.astype(jnp.float32))
    decoded = codes.astype(jnp.float32).reshape(2, tok_rows, head_count, HD) * blocks[..., None]
    decoded = decoded.astype(jnp.bfloat16).reshape(2, tok_rows, row_width)
    arrived = lax.all_gather(decoded, "patch", axis=1, tiled=True)
    all_rows = arrived.shape[1]
    query_heads = queries.reshape(tok_rows, head_count, HD)
    text_heads = text_kv.reshape(2, text_count, head_count, HD)
    stale_heads = stale_kv.reshape(2, all_rows, head_count, HD)
    arrived_heads = arrived.reshape(2, all_rows, head_count, HD)
    text_scores = jnp.einsum("thd,khd->htk", query_heads, text_heads[0], preferred_element_type=jnp.float32)
    rebuilt = stale_heads.astype(jnp.float32) + arrived_heads.astype(jnp.float32)
    image_scores = jnp.einsum(
        "thd,khd->htk", query_heads.astype(jnp.float32), rebuilt[0], precision=lax.Precision.HIGHEST
    )
    scores = jnp.concatenate([text_scores, image_scores], axis=2) * scale_factor
    row_peak = jnp.max(scores, axis=2, keepdims=True)
    weights = jnp.exp(scores - row_peak).astype(jnp.bfloat16)
    row_total = jnp.sum(weights.astype(jnp.float32), axis=2)
    text_part = jnp.einsum(
        "htk,khd->thd", weights[:, :, :text_count], text_heads[1], preferred_element_type=jnp.float32
    )
    image_part = jnp.einsum(
        "htk,khd->thd",
        weights[:, :, text_count:].astype(jnp.float32),
        rebuilt[1],
        precision=lax.Precision.HIGHEST,
    )
    attended = ((text_part + image_part) / row_total.T[:, :, None]).astype(jnp.bfloat16).reshape(tok_rows, row_width)
    partial_terms = jnp.dot(
        attended, lax.all_gather(out_weight, "patch", axis=1, tiled=True), preferred_element_type=jnp.float32
    )
    column_share = lax.psum_scatter(partial_terms, "head", scatter_dimension=1, tiled=True)
    return (out_gate * (column_share + out_bias)).astype(jnp.bfloat16)


def aligned(value, step):
    return pl.multiple_of(value * step, step)


def place():
    me = lax.axis_index("patch")
    return me // SPREAD, lax.rem(me, SPREAD)


def pack_kernel(queries_hbm, codes_hbm, exponents, residual, query, codes, queries, sems):
    groups, rows, width = query.shape
    codes_copy = pltpu.make_async_copy(codes_hbm, codes, sems.at[0])
    queries_copy = pltpu.make_async_copy(queries_hbm, queries, sems.at[1])
    codes_copy.start()
    queries_copy.start()
    codes_copy.wait()
    per = width // HD
    for kind in range(2):
        scales = jnp.left_shift(1, exponents[kind] + 16).astype(jnp.float32) * (2.0**-16)
        for head in range(groups * per):
            inside = slice((head % per) * HD, (head % per + 1) * HD)
            whole = slice(head * HD, (head + 1) * HD)
            decoded = codes[kind, :, whole].astype(jnp.float32) * scales[:, head : head + 1]
            residual[head // per, kind, :, inside] = decoded.astype(jnp.bfloat16)
    queries_copy.wait()
    for group in range(groups):
        query[group] = queries[:, group * width : (group + 1) * width]


def pack(groups, queries, codes, exponents):
    rows, width = queries.shape
    share = width // groups
    bf16 = jnp.bfloat16
    return pl.pallas_call(
        pack_kernel,
        out_shape=[
            jax.ShapeDtypeStruct((groups, 2, rows, share), bf16),
            jax.ShapeDtypeStruct((groups, rows, share), bf16),
        ],
        in_specs=[HBM, HBM, VMEM],
        out_specs=[VMEM] * 2,
        scratch_shapes=[
            pltpu.VMEM(codes.shape, jnp.int32),
            pltpu.VMEM(queries.shape, bf16),
            pltpu.SemaphoreType.DMA((2,)),
        ],
        compiler_params=pltpu.CompilerParams(vmem_limit_bytes=56 << 20),
        cost_estimate=pl.CostEstimate(flops=2 * codes.size, bytes_accessed=6 * codes.size, transcendentals=0),
    )(queries, codes, exponents)


def attend_kernel(*refs):
    parts, (asked, text_hbm, stale_hbm, out, query, residual, text, stale, sems) = refs[:SPREAD], refs[SPREAD:]
    group, spot = place()
    groups, rows, width = asked.shape
    columns = pl.ds(aligned(group, width), width)
    text_copy = pltpu.make_async_copy(text_hbm.at[:, :, columns], text, sems.at[0])
    stale_copy = pltpu.make_async_copy(stale_hbm.at[:, :, columns], stale, sems.at[1])
    text_copy.start()
    stale_copy.start()
    for origin in range(groups):
        query[origin * rows : (origin + 1) * rows, :] = asked[origin]
        for twist in range(SPREAD):
            token = origin * SPREAD + jnp.bitwise_xor(spot, twist)
            residual[:, pl.ds(aligned(token, rows), rows), :] = parts[twist][origin]
    text_copy.wait()
    stale_copy.wait()
    for head in range(width // HD):
        cols = slice(head * HD, (head + 1) * HD)
        heads_query = query[:, cols]
        text_scores = lax.dot_general(heads_query, text[0, :, cols], NT, preferred_element_type=jnp.float32)
        image_scores = lax.dot_general(heads_query, stale[0, :, cols], NT, preferred_element_type=jnp.float32)
        image_scores += lax.dot_general(heads_query, residual[0, :, cols], NT, preferred_element_type=jnp.float32)
        text_scores *= HD**-0.5
        image_scores *= HD**-0.5
        peak = jnp.maximum(
            jnp.max(text_scores, axis=1, keepdims=True), jnp.max(image_scores, axis=1, keepdims=True)
        )
        text_weights = jnp.exp(text_scores - peak).astype(jnp.bfloat16)
        image_weights = jnp.exp(image_scores - peak).astype(jnp.bfloat16)
        total = jnp.sum(text_weights.astype(jnp.float32), axis=1, keepdims=True)
        total += jnp.sum(image_weights.astype(jnp.float32), axis=1, keepdims=True)
        mixed = jnp.dot(text_weights, text[1, :, cols], preferred_element_type=jnp.float32)
        mixed += jnp.dot(image_weights, stale[1, :, cols], preferred_element_type=jnp.float32)
        mixed += jnp.dot(image_weights, residual[1, :, cols], preferred_element_type=jnp.float32)
        out[:, cols] = (mixed / total).astype(jnp.bfloat16)


def attend(parts, query, text_kv, stale_kv):
    groups, rows, width = query.shape
    keys = stale_kv.shape[1]
    texts = text_kv.shape[1]
    bf16 = jnp.bfloat16
    return pl.pallas_call(
        attend_kernel,
        out_shape=jax.ShapeDtypeStruct((groups * rows, width), bf16),
        in_specs=[VMEM] * (SPREAD + 1) + [HBM] * 2,
        out_specs=VMEM,
        scratch_shapes=[
            pltpu.VMEM((groups * rows, width), bf16),
            pltpu.VMEM((2, keys, width), bf16),
            pltpu.VMEM((2, texts, width), bf16),
            pltpu.VMEM((2, keys, width), bf16),
            pltpu.SemaphoreType.DMA((2,)),
        ],
        compiler_params=pltpu.CompilerParams(vmem_limit_bytes=50 << 20),
        cost_estimate=pl.CostEstimate(
            flops=4 * groups * rows * width * (texts + 2 * keys),
            bytes_accessed=4 * width * (texts + 2 * keys),
            transcendentals=groups * rows * (texts + keys) * (width // HD),
        ),
    )(*parts, query, text_kv, stale_kv)


def project_kernel(parts, weights, out, weight):
    group, spot = place()
    width = parts[0].shape[1]
    rows = weight.shape[0] // SPREAD
    for twist in range(SPREAD):
        start = jnp.bitwise_xor(spot, twist) * rows
        for piece in weights[twist]:
            height = piece.shape[0]
            weight[pl.ds(pl.multiple_of(start, height), height), :] = piece[...]
            start += height
    total = None
    for twist, part in enumerate(parts):
        origin = jnp.bitwise_xor(group, twist)
        term = lax.dot_general(
            part[...], weight[:, pl.ds(aligned(origin, width), width)], NT, preferred_element_type=jnp.float32
        )
        total = term if total is None else total + term
    out[...] = total.astype(jnp.bfloat16).reshape(out.shape)


def project(parts, weights):
    groups = len(parts)
    tokens, width = parts[0].shape
    rows, depth = weights[0][0].shape
    flat, tree = jax.tree.flatten(weights)

    def kernel(*refs):
        project_kernel(refs[:groups], jax.tree.unflatten(tree, refs[groups:-2]), *refs[-2:])

    return pl.pallas_call(
        kernel,
        out_shape=jax.ShapeDtypeStruct((groups, tokens // groups, SPREAD * rows), jnp.bfloat16),
        in_specs=[VMEM] * (groups + len(flat)),
        out_specs=VMEM,
        scratch_shapes=[pltpu.VMEM((SPREAD * rows, depth), jnp.bfloat16)],
        compiler_params=pltpu.CompilerParams(vmem_limit_bytes=24 << 20),
        cost_estimate=pl.CostEstimate(
            flops=2 * tokens * SPREAD * rows * depth,
            bytes_accessed=2 * SPREAD * rows * depth,
            transcendentals=0,
        ),
    )(*parts, *flat)


def finish_kernel(terms, bias, gate, out):
    halves, blocks, _, columns = terms.shape
    for block in range(blocks):
        cols = slice(block * columns, (block + 1) * columns)
        total = terms[0, block].astype(jnp.float32)
        for half in range(1, halves):
            total = total + terms[half, block].astype(jnp.float32)
        out[:, cols] = (gate[:, cols] * (total + bias[:, cols])).astype(jnp.bfloat16)


def finish(terms, bias, gate):
    _, blocks, rows, columns = terms.shape
    width = blocks * columns
    return pl.pallas_call(
        finish_kernel,
        out_shape=jax.ShapeDtypeStruct((rows, width), jnp.bfloat16),
        in_specs=[VMEM] * 3,
        out_specs=VMEM,
        compiler_params=pltpu.CompilerParams(vmem_limit_bytes=16 << 20),
        cost_estimate=pl.CostEstimate(flops=3 * rows * width, bytes_accessed=4 * rows * width, transcendentals=0),
    )(terms, bias.reshape(1, width), gate.reshape(1, width))


def grouped_body(groups, halves, queries, stale_kv, codes, exponents, text_kv, out_weight, out_bias, out_gate):
    size = groups * SPREAD
    columns = [[group * SPREAD + spot for group in range(groups)] for spot in range(SPREAD)]

    def exchange(value):
        return lax.all_to_all(value, "patch", 0, 0, axis_index_groups=columns, tiled=True)

    def swap(value, twist):
        return lax.ppermute(value, "patch", [(p, p ^ twist) for p in range(size)])

    def after(value, *others):
        return lax.optimization_barrier((value, *others))[0]

    residual, query = pack(groups, queries, codes, exponents)
    weight = out_weight.T
    half = weight.shape[0] // 2
    early = swap(weight[:half], 2)
    own = exchange(residual)
    far = swap(own, 2)
    near = swap(own, 1)
    query = exchange(after(query, own))
    corner = swap(after(far, query), 1)
    late = swap(after(weight[half:], corner), 2)
    beside = swap(after(weight, near), 1)
    attended = attend([own, near, far, corner], after(query, beside), text_kv, stale_kv)
    across = swap(attended, 2 * SPREAD)
    next_to = swap(attended, SPREAD)
    last = swap(across, SPREAD)
    early, late = after(early, across), after(late, across)
    weights = [(weight,), (beside,), (early, late), (swap(early, 1), swap(late, 1))]
    attended_parts = [attended, next_to, across, last]
    terms = exchange(project(attended_parts, weights))
    terms = lax.all_to_all(terms, "head", 0, 0, tiled=True)
    return finish(terms.reshape(halves, groups // halves, *terms.shape[1:]), out_bias, out_gate)


def solution(mesh):
    patches, halves = mesh.shape["patch"], mesh.shape["head"]
    placed = (
        P("patch", "head"),
        P(None, None, "head"),
        P(None, "patch", "head"),
        P(None, "patch", "head"),
        P(None, None, "head"),
        P("head", "patch"),
        P("head"),
        P("head"),
    )

    def body(*args):
        heads = args[0].shape[1] // HD
        groups = patches // SPREAD
        if patches != 4 * SPREAD or heads % groups or groups % halves:
            return plain_body(*args)
        return grouped_body(groups, halves, *args)

    return jax.shard_map(body, mesh=mesh, in_specs=placed, out_specs=P("patch", "head"), check_vma=False)
```

```python
import functools

import jax
import jax.numpy as jnp
from jax import lax
from jax.experimental import pallas as pl
from jax.experimental.pallas import tpu as pltpu
from jax.sharding import PartitionSpec as P

HD = 128
SPREAD = 4
PACK_LIMIT = 56 << 20
PICK_LIMIT = 50 << 20
VMEM = pl.BlockSpec(memory_space=pltpu.VMEM)
HBM = pl.BlockSpec(memory_space=pltpu.HBM)
NT = (((1,), (1,)), ((), ()))


def plain_body(queries, stale_kv, codes, exponents, text_kv, out_weight, out_bias, out_gate):
    tok_rows = queries.shape[0]
    row_width = queries.shape[1]
    head_count = row_width // HD
    text_count = text_kv.shape[1]
    scale_factor = HD ** (-0.5)
    blocks = jnp.exp2(exponents.astype(jnp.float32))
    decoded = codes.astype(jnp.float32).reshape(2, tok_rows, head_count, HD) * blocks[..., None]
    decoded = decoded.astype(jnp.bfloat16).reshape(2, tok_rows, row_width)
    arrived = lax.all_gather(decoded, "patch", axis=1, tiled=True)
    all_rows = arrived.shape[1]
    query_heads = queries.reshape(tok_rows, head_count, HD)
    text_heads = text_kv.reshape(2, text_count, head_count, HD)
    stale_heads = stale_kv.reshape(2, all_rows, head_count, HD)
    arrived_heads = arrived.reshape(2, all_rows, head_count, HD)
    text_scores = jnp.einsum("thd,khd->htk", query_heads, text_heads[0], preferred_element_type=jnp.float32)
    rebuilt = stale_heads.astype(jnp.float32) + arrived_heads.astype(jnp.float32)
    image_scores = jnp.einsum(
        "thd,khd->htk", query_heads.astype(jnp.float32), rebuilt[0], precision=lax.Precision.HIGHEST
    )
    scores = jnp.concatenate([text_scores, image_scores], axis=2) * scale_factor
    row_peak = jnp.max(scores, axis=2, keepdims=True)
    weights = jnp.exp(scores - row_peak).astype(jnp.bfloat16)
    row_total = jnp.sum(weights.astype(jnp.float32), axis=2)
    text_part = jnp.einsum(
        "htk,khd->thd", weights[:, :, :text_count], text_heads[1], preferred_element_type=jnp.float32
    )
    image_part = jnp.einsum(
        "htk,khd->thd",
        weights[:, :, text_count:].astype(jnp.float32),
        rebuilt[1],
        precision=lax.Precision.HIGHEST,
    )
    attended = ((text_part + image_part) / row_total.T[:, :, None]).astype(jnp.bfloat16).reshape(tok_rows, row_width)
    partial_terms = jnp.dot(
        attended, lax.all_gather(out_weight, "patch", axis=1, tiled=True), preferred_element_type=jnp.float32
    )
    column_share = lax.psum_scatter(partial_terms, "head", scatter_dimension=1, tiled=True)
    return (out_gate * (column_share + out_bias)).astype(jnp.bfloat16)


def aligned(value, step):
    return pl.multiple_of(value * step, step)


def place():
    me = lax.axis_index("patch")
    return me // SPREAD, lax.rem(me, SPREAD)


def pack_kernel(queries_hbm, codes_hbm, exponents_hbm, *rest):
    outs, (codes, queries, exponents, held, sems) = rest[:-5], rest[-5:]
    groups, kinds, rows, width = held.shape
    group, _ = place()
    per = width // HD
    copies = [
        pltpu.make_async_copy(exponents_hbm, exponents, sems.at[0]),
        pltpu.make_async_copy(codes_hbm, codes, sems.at[1]),
        pltpu.make_async_copy(queries_hbm, queries, sems.at[2]),
    ]
    for copy in copies:
        copy.start()
    copies[0].wait()
    copies[1].wait()
    eye = lax.broadcasted_iota(jnp.int32, (rows, rows), 0) == lax.broadcasted_iota(jnp.int32, (rows, rows), 1)
    eye = eye.astype(jnp.float32).astype(jnp.bfloat16)
    for kind in range(kinds - 1):
        scales = jnp.left_shift(1, exponents[:, kind, :] + 16).astype(jnp.float32) * (2.0**-16)
        scales = lax.dot_general(eye, scales.astype(jnp.bfloat16), NT, preferred_element_type=jnp.float32)
        for head in range(groups * per):
            inside = slice((head % per) * HD, (head % per + 1) * HD)
            whole = slice(head * HD, (head + 1) * HD)
            decoded = codes[kind, :, whole].astype(jnp.float32) * scales[:, head : head + 1]
            held[head // per, kind, :, inside] = decoded.astype(jnp.bfloat16)
    copies[2].wait()
    for target in range(groups):
        held[target, kinds - 1] = queries[:, target * width : (target + 1) * width]
    for turn in range(groups):
        target = jnp.bitwise_xor(group, turn)
        outs[turn][...] = held[target, 0 : kinds - 1]
        outs[groups + turn][...] = held[target, kinds - 1]


def pack(groups, queries, codes, exponents):
    rows, width = queries.shape
    kinds = codes.shape[0]
    share = width // groups
    bf16 = jnp.bfloat16
    exponents = exponents.transpose(2, 0, 1)
    outs = pl.pallas_call(
        pack_kernel,
        out_shape=[jax.ShapeDtypeStruct((kinds, rows, share), bf16)] * groups
        + [jax.ShapeDtypeStruct((rows, share), bf16)] * groups,
        in_specs=[HBM] * 3,
        out_specs=[VMEM] * (2 * groups),
        scratch_shapes=[
            pltpu.VMEM(codes.shape, jnp.int32),
            pltpu.VMEM(queries.shape, bf16),
            pltpu.VMEM(exponents.shape, jnp.int32),
            pltpu.VMEM((groups, kinds + 1, rows, share), bf16),
            pltpu.SemaphoreType.DMA((3,)),
        ],
        compiler_params=pltpu.CompilerParams(vmem_limit_bytes=PACK_LIMIT),
        cost_estimate=pl.CostEstimate(flops=2 * codes.size, bytes_accessed=6 * codes.size, transcendentals=0),
    )(queries, codes, exponents)
    return outs[:groups], outs[groups:]


def pick_kernel(text_hbm, stale_hbm, text, stale, sems):
    group, _ = place()
    width = text.shape[2]
    columns = pl.ds(aligned(group, width), width)
    text_copy = pltpu.make_async_copy(text_hbm.at[:, :, columns], text, sems.at[0])
    stale_copy = pltpu.make_async_copy(stale_hbm.at[:, :, columns], stale, sems.at[1])
    text_copy.start()
    stale_copy.start()
    text_copy.wait()
    stale_copy.wait()


def pick(groups, text_kv, stale_kv):
    shapes = [(2, value.shape[1], value.shape[2] // groups) for value in (text_kv, stale_kv)]
    return pl.pallas_call(
        pick_kernel,
        out_shape=[jax.ShapeDtypeStruct(shape, jnp.bfloat16) for shape in shapes],
        in_specs=[HBM] * 2,
        out_specs=[VMEM] * 2,
        scratch_shapes=[pltpu.SemaphoreType.DMA((2,))],
        compiler_params=pltpu.CompilerParams(vmem_limit_bytes=PICK_LIMIT),
        cost_estimate=pl.CostEstimate(flops=0, bytes_accessed=8 << 20, transcendentals=0),
    )(text_kv, stale_kv)


def merge_kernel(*refs):
    for index, ref in enumerate(refs[:-1]):
        refs[-1][index] = ref[...]


def merge(parts):
    return pl.pallas_call(
        merge_kernel,
        out_shape=jax.ShapeDtypeStruct((len(parts), *parts[0].shape), parts[0].dtype),
        in_specs=[VMEM] * len(parts),
        out_specs=VMEM,
        cost_estimate=pl.CostEstimate(flops=0, bytes_accessed=4 * len(parts) * parts[0].size, transcendentals=0),
    )(*parts)


def attend_kernel(groups, *refs):
    owns, merged, asked, refs = refs[:SPREAD], refs[SPREAD : 2 * SPREAD], refs[2 * SPREAD : 2 * SPREAD + groups], refs[2 * SPREAD + groups :]
    text, stale, out, query, residual = refs
    group, spot = place()
    rows, width = asked[0].shape
    for turn in range(groups):
        origin = jnp.bitwise_xor(group, turn)
        query[pl.ds(aligned(origin, rows), rows), :] = asked[turn][...]
        for twist in range(SPREAD):
            token = origin * SPREAD + jnp.bitwise_xor(spot, twist)
            part = owns[twist][...] if turn == 0 else merged[twist][turn - 1]
            residual[:, pl.ds(aligned(token, rows), rows), :] = part
    for head in range(width // HD):
        cols = slice(head * HD, (head + 1) * HD)
        heads_query = query[:, cols]
        text_scores = lax.dot_general(heads_query, text[0, :, cols], NT, preferred_element_type=jnp.float32)
        image_scores = lax.dot_general(heads_query, stale[0, :, cols], NT, preferred_element_type=jnp.float32)
        image_scores += lax.dot_general(heads_query, residual[0, :, cols], NT, preferred_element_type=jnp.float32)
        text_scores *= HD**-0.5
        image_scores *= HD**-0.5
        peak = jnp.maximum(
            jnp.max(text_scores, axis=1, keepdims=True), jnp.max(image_scores, axis=1, keepdims=True)
        )
        text_weights = jnp.exp(text_scores - peak).astype(jnp.bfloat16)
        image_weights = jnp.exp(image_scores - peak).astype(jnp.bfloat16)
        total = jnp.sum(text_weights.astype(jnp.float32), axis=1, keepdims=True)
        total += jnp.sum(image_weights.astype(jnp.float32), axis=1, keepdims=True)
        mixed = jnp.dot(text_weights, text[1, :, cols], preferred_element_type=jnp.float32)
        mixed += jnp.dot(image_weights, stale[1, :, cols], preferred_element_type=jnp.float32)
        mixed += jnp.dot(image_weights, residual[1, :, cols], preferred_element_type=jnp.float32)
        out[:, cols] = (mixed / total).astype(jnp.bfloat16)


def attend(owns, merged, query_parts, text, stale):
    groups = len(query_parts)
    rows, width = query_parts[0].shape
    keys = stale.shape[1]
    texts = text.shape[1]
    bf16 = jnp.bfloat16
    return pl.pallas_call(
        functools.partial(attend_kernel, groups),
        out_shape=jax.ShapeDtypeStruct((groups * rows, width), bf16),
        in_specs=[VMEM] * (2 * SPREAD + groups + 2),
        out_specs=VMEM,
        scratch_shapes=[pltpu.VMEM((groups * rows, width), bf16), pltpu.VMEM((2, keys, width), bf16)],
        compiler_params=pltpu.CompilerParams(vmem_limit_bytes=24 << 20),
        cost_estimate=pl.CostEstimate(
            flops=4 * groups * rows * width * (texts + 2 * keys),
            bytes_accessed=4 * width * (texts + 2 * keys),
            transcendentals=groups * rows * (texts + keys) * (width // HD),
        ),
    )(*owns, *merged, *query_parts, text, stale)


def project_kernel(parts, weights, outs, weight, total):
    group, spot = place()
    width = parts[0].shape[1]
    span = weight.shape[0] // SPREAD
    rows = outs[0].shape[0]
    for twist in range(SPREAD):
        start = jnp.bitwise_xor(spot, twist) * span
        for piece in weights[twist]:
            height = piece.shape[0]
            weight[pl.ds(pl.multiple_of(start, height), height), :] = piece[...]
            start += height
    added = None
    for turn, part in enumerate(parts):
        origin = jnp.bitwise_xor(group, turn)
        term = lax.dot_general(
            part[...], weight[:, pl.ds(aligned(origin, width), width)], NT, preferred_element_type=jnp.float32
        )
        added = term if added is None else added + term
    total[...] = added.astype(jnp.bfloat16)
    for turn, out in enumerate(outs):
        out[...] = total[pl.ds(aligned(jnp.bitwise_xor(group, turn), rows), rows), :]


def project(parts, weights):
    groups = len(parts)
    tokens, width = parts[0].shape
    depth = weights[0][0].shape[1]
    columns = SPREAD * sum(piece.shape[0] for piece in weights[0])
    flat, tree = jax.tree.flatten(weights)

    def kernel(*refs):
        ins, outs, scratch = refs[: groups + len(flat)], refs[groups + len(flat) : -2], refs[-2:]
        project_kernel(ins[:groups], jax.tree.unflatten(tree, ins[groups:]), outs, *scratch)

    return pl.pallas_call(
        kernel,
        out_shape=[jax.ShapeDtypeStruct((tokens // groups, columns), jnp.bfloat16)] * groups,
        in_specs=[VMEM] * (groups + len(flat)),
        out_specs=[VMEM] * groups,
        scratch_shapes=[pltpu.VMEM((columns, depth), jnp.bfloat16), pltpu.VMEM((tokens, columns), jnp.bfloat16)],
        compiler_params=pltpu.CompilerParams(vmem_limit_bytes=24 << 20),
        cost_estimate=pl.CostEstimate(
            flops=2 * tokens * columns * depth, bytes_accessed=2 * columns * depth, transcendentals=0
        ),
    )(*parts, *flat)


def divide_kernel(*refs):
    parts, (keep, send, held) = refs[:-3], refs[-3:]
    group, _ = place()
    half = lax.axis_index("head")
    blocks = keep.shape[0]
    for turn, part in enumerate(parts):
        held[jnp.bitwise_xor(group, turn)] = part[...]
    for block in range(blocks):
        keep[block] = held[half * blocks + block]
        send[block] = held[(1 - half) * blocks + block]


def divide(parts):
    groups = len(parts)
    shape = jax.ShapeDtypeStruct((groups // 2, *parts[0].shape), jnp.bfloat16)
    return pl.pallas_call(
        divide_kernel,
        out_shape=[shape] * 2,
        in_specs=[VMEM] * groups,
        out_specs=[VMEM] * 2,
        scratch_shapes=[pltpu.VMEM((groups, *parts[0].shape), jnp.bfloat16)],
        cost_estimate=pl.CostEstimate(flops=0, bytes_accessed=4 * groups * parts[0].size, transcendentals=0),
    )(*parts)


def finish_kernel(kept, arrived, bias, gate, out):
    blocks, _, columns = kept.shape
    for block in range(blocks):
        cols = slice(block * columns, (block + 1) * columns)
        total = kept[block].astype(jnp.float32) + arrived[block].astype(jnp.float32)
        out[:, cols] = (gate[:, cols] * (total + bias[:, cols])).astype(jnp.bfloat16)


def finish(kept, arrived, bias, gate):
    blocks, rows, columns = kept.shape
    width = blocks * columns
    return pl.pallas_call(
        finish_kernel,
        out_shape=jax.ShapeDtypeStruct((rows, width), jnp.bfloat16),
        in_specs=[VMEM] * 4,
        out_specs=VMEM,
        cost_estimate=pl.CostEstimate(flops=3 * rows * width, bytes_accessed=4 * rows * width, transcendentals=0),
    )(kept, arrived, bias.reshape(1, width), gate.reshape(1, width))


def after(value, *others):
    return lax.optimization_barrier((value, *others))[0]


def grouped_body(queries, stale_kv, codes, exponents, text_kv, out_weight, out_bias, out_gate):
    groups = lax.axis_size("patch") // SPREAD
    size = groups * SPREAD

    def swap(value, twist):
        return lax.ppermute(value, "patch", [(p, p ^ twist) for p in range(size)])

    def along(values):
        return [swap(values[turn], turn * SPREAD) for turn in range(1, groups)]

    residuals, queries = pack(groups, queries, codes, exponents)
    weight = out_weight.T
    half = weight.shape[0] // 2
    text, stale = pick(groups, text_kv, stale_kv)

    own = residuals[0]
    arrived = along(residuals)
    own_far, own_near = swap(own, 2), swap(own, 1)
    early = swap(weight[:half], 2)

    merged = merge(arrived)
    merged = after(merged, own_far, own_near, text, stale)
    queries = lax.optimization_barrier((*queries, merged))[:groups]
    merged_far, merged_near = swap(merged, 2), swap(merged, 1)
    own_corner = swap(after(own_far, merged), 1)
    asked = [queries[0], *along(queries)]

    merged_corner = swap(after(merged_far, merged_near, own_corner, *asked), 1)
    owns = [own, own_near, own_far, own_corner]
    attended = attend(owns, [merged, merged_near, merged_far, merged_corner], asked, text, stale)

    weight, late, early = lax.optimization_barrier((weight, weight[half:], early, merged_corner))[:3]
    across, beside = swap(attended, 2 * SPREAD), swap(attended, SPREAD)
    late = swap(late, 2)
    early_near = swap(early, 1)
    weight_near = swap(weight, 1)

    across, late = lax.optimization_barrier((across, late, beside, weight_near, early_near))[:2]
    last = swap(across, SPREAD)
    late_near = swap(late, 1)
    weights = [(weight,), (weight_near,), (early, late), (early_near, late_near)]
    terms = project([attended, beside, across, last], weights)

    kept, sent = divide([terms[0], *along(terms)])
    received = lax.ppermute(sent, "head", [(0, 1), (1, 0)])
    return finish(kept, received, out_bias, out_gate)


def solution(mesh):
    patches, halves = mesh.shape["patch"], mesh.shape["head"]
    placed = (
        P("patch", "head"),
        P(None, None, "head"),
        P(None, "patch", "head"),
        P(None, "patch", "head"),
        P(None, None, "head"),
        P("head", "patch"),
        P("head"),
        P("head"),
    )

    def body(*args):
        heads = args[0].shape[1] // HD
        groups = patches // SPREAD
        if groups != 4 or patches % SPREAD or heads % groups or halves != 2:
            return plain_body(*args)
        return grouped_body(*args)

    return jax.shard_map(body, mesh=mesh, in_specs=placed, out_specs=P("patch", "head"), check_vma=False)
```

```python
import functools

import jax
import jax.numpy as jnp
from jax import lax
from jax.experimental import pallas as pl
from jax.experimental.pallas import tpu as pltpu
from jax.sharding import PartitionSpec as P

HD = 128
SPREAD = 4
PACK_LIMIT = 56 << 20
SMALL = 16 << 20
PICK_LIMIT = 50 << 20
VMEM = pl.BlockSpec(memory_space=pltpu.VMEM)
HBM = pl.BlockSpec(memory_space=pltpu.HBM)
NT = (((1,), (1,)), ((), ()))


def plain_body(queries, stale_kv, codes, exponents, text_kv, out_weight, out_bias, out_gate):
    tok_rows = queries.shape[0]
    row_width = queries.shape[1]
    head_count = row_width // HD
    text_count = text_kv.shape[1]
    scale_factor = HD ** (-0.5)
    blocks = jnp.exp2(exponents.astype(jnp.float32))
    decoded = codes.astype(jnp.float32).reshape(2, tok_rows, head_count, HD) * blocks[..., None]
    decoded = decoded.astype(jnp.bfloat16).reshape(2, tok_rows, row_width)
    arrived = lax.all_gather(decoded, "patch", axis=1, tiled=True)
    all_rows = arrived.shape[1]
    query_heads = queries.reshape(tok_rows, head_count, HD)
    text_heads = text_kv.reshape(2, text_count, head_count, HD)
    stale_heads = stale_kv.reshape(2, all_rows, head_count, HD)
    arrived_heads = arrived.reshape(2, all_rows, head_count, HD)
    text_scores = jnp.einsum("thd,khd->htk", query_heads, text_heads[0], preferred_element_type=jnp.float32)
    rebuilt = stale_heads.astype(jnp.float32) + arrived_heads.astype(jnp.float32)
    image_scores = jnp.einsum(
        "thd,khd->htk", query_heads.astype(jnp.float32), rebuilt[0], precision=lax.Precision.HIGHEST
    )
    scores = jnp.concatenate([text_scores, image_scores], axis=2) * scale_factor
    row_peak = jnp.max(scores, axis=2, keepdims=True)
    weights = jnp.exp(scores - row_peak).astype(jnp.bfloat16)
    row_total = jnp.sum(weights.astype(jnp.float32), axis=2)
    text_part = jnp.einsum(
        "htk,khd->thd", weights[:, :, :text_count], text_heads[1], preferred_element_type=jnp.float32
    )
    image_part = jnp.einsum(
        "htk,khd->thd",
        weights[:, :, text_count:].astype(jnp.float32),
        rebuilt[1],
        precision=lax.Precision.HIGHEST,
    )
    attended = ((text_part + image_part) / row_total.T[:, :, None]).astype(jnp.bfloat16).reshape(tok_rows, row_width)
    partial_terms = jnp.dot(
        attended, lax.all_gather(out_weight, "patch", axis=1, tiled=True), preferred_element_type=jnp.float32
    )
    column_share = lax.psum_scatter(partial_terms, "head", scatter_dimension=1, tiled=True)
    return (out_gate * (column_share + out_bias)).astype(jnp.bfloat16)


def aligned(value, step):
    return pl.multiple_of(value * step, step)


def place():
    me = lax.axis_index("patch")
    return me // SPREAD, lax.rem(me, SPREAD)


def pack_kernel(queries_hbm, codes_hbm, exponents_hbm, *rest):
    outs, (codes, queries, exponents, held, sems) = rest[:-5], rest[-5:]
    groups, kinds, rows, width = held.shape
    group, _ = place()
    per = width // HD
    copies = [
        pltpu.make_async_copy(exponents_hbm, exponents, sems.at[0]),
        pltpu.make_async_copy(codes_hbm, codes, sems.at[1]),
        pltpu.make_async_copy(queries_hbm, queries, sems.at[2]),
    ]
    for copy in copies:
        copy.start()
    copies[0].wait()
    copies[1].wait()
    eye = lax.broadcasted_iota(jnp.int32, (rows, rows), 0) == lax.broadcasted_iota(jnp.int32, (rows, rows), 1)
    eye = eye.astype(jnp.float32).astype(jnp.bfloat16)
    for kind in range(kinds - 1):
        scales = jnp.left_shift(1, exponents[:, kind, :] + 16).astype(jnp.float32) * (2.0**-16)
        scales = lax.dot_general(eye, scales.astype(jnp.bfloat16), NT, preferred_element_type=jnp.float32)
        for head in range(groups * per):
            inside = slice((head % per) * HD, (head % per + 1) * HD)
            whole = slice(head * HD, (head + 1) * HD)
            decoded = codes[kind, :, whole].astype(jnp.float32) * scales[:, head : head + 1]
            held[head // per, kind, :, inside] = decoded.astype(jnp.bfloat16)
    copies[2].wait()
    for target in range(groups):
        held[target, kinds - 1] = queries[:, target * width : (target + 1) * width]
    for turn in range(groups):
        target = jnp.bitwise_xor(group, turn)
        outs[turn][...] = held[target, 0 : kinds - 1]
        outs[groups + turn][...] = held[target, kinds - 1]


def pack(groups, queries, codes, exponents):
    rows, width = queries.shape
    kinds = codes.shape[0]
    share = width // groups
    bf16 = jnp.bfloat16
    exponents = exponents.transpose(2, 0, 1)
    outs = pl.pallas_call(
        pack_kernel,
        out_shape=[jax.ShapeDtypeStruct((kinds, rows, share), bf16)] * groups
        + [jax.ShapeDtypeStruct((rows, share), bf16)] * groups,
        in_specs=[HBM] * 3,
        out_specs=[VMEM] * (2 * groups),
        scratch_shapes=[
            pltpu.VMEM(codes.shape, jnp.int32),
            pltpu.VMEM(queries.shape, bf16),
            pltpu.VMEM(exponents.shape, jnp.int32),
            pltpu.VMEM((groups, kinds + 1, rows, share), bf16),
            pltpu.SemaphoreType.DMA((3,)),
        ],
        compiler_params=pltpu.CompilerParams(vmem_limit_bytes=PACK_LIMIT),
        cost_estimate=pl.CostEstimate(flops=2 * codes.size, bytes_accessed=6 * codes.size, transcendentals=0),
    )(queries, codes, exponents)
    return outs[:groups], outs[groups:]


def pick_kernel(text_hbm, stale_hbm, text, stale, sems):
    group, _ = place()
    width = text.shape[2]
    columns = pl.ds(aligned(group, width), width)
    text_copy = pltpu.make_async_copy(text_hbm.at[:, :, columns], text, sems.at[0])
    stale_copy = pltpu.make_async_copy(stale_hbm.at[:, :, columns], stale, sems.at[1])
    text_copy.start()
    stale_copy.start()
    text_copy.wait()
    stale_copy.wait()


def pick(groups, text_kv, stale_kv):
    shapes = [(2, value.shape[1], value.shape[2] // groups) for value in (text_kv, stale_kv)]
    return pl.pallas_call(
        pick_kernel,
        out_shape=[jax.ShapeDtypeStruct(shape, jnp.bfloat16) for shape in shapes],
        in_specs=[HBM] * 2,
        out_specs=[VMEM] * 2,
        scratch_shapes=[pltpu.SemaphoreType.DMA((2,))],
        compiler_params=pltpu.CompilerParams(vmem_limit_bytes=PICK_LIMIT),
        cost_estimate=pl.CostEstimate(flops=0, bytes_accessed=8 << 20, transcendentals=0),
    )(text_kv, stale_kv)


def merge_kernel(*refs):
    parts, (some, every) = refs[:-2], refs[-2:]
    for index, part in enumerate(parts):
        every[index] = part[...]
        if index:
            some[index - 1] = part[...]


def merge(parts):
    shapes = [(count, *parts[0].shape) for count in (len(parts) - 1, len(parts))]
    return pl.pallas_call(
        merge_kernel,
        out_shape=[jax.ShapeDtypeStruct(shape, parts[0].dtype) for shape in shapes],
        in_specs=[VMEM] * len(parts),
        out_specs=[VMEM] * 2,
        compiler_params=pltpu.CompilerParams(vmem_limit_bytes=SMALL),
        cost_estimate=pl.CostEstimate(flops=0, bytes_accessed=4 * len(parts) * parts[0].size, transcendentals=0),
    )(*parts)


def attend_kernel(groups, *refs):
    (every, near, own_far, some_far, own_corner, some_corner), refs = refs[:6], refs[6:]
    asked, (text, stale, out, query, residual) = refs[:groups], refs[groups:]
    group, spot = place()
    rows, width = asked[0].shape
    for turn in range(groups):
        origin = jnp.bitwise_xor(group, turn)
        query[pl.ds(aligned(origin, rows), rows), :] = asked[turn][...]
        for twist in range(SPREAD):
            token = origin * SPREAD + jnp.bitwise_xor(spot, twist)
            if twist < 2:
                part = (every, near)[twist][turn]
            elif turn == 0:
                part = (own_far, own_corner)[twist - 2][...]
            else:
                part = (some_far, some_corner)[twist - 2][turn - 1]
            residual[:, pl.ds(aligned(token, rows), rows), :] = part
    for head in range(width // HD):
        cols = slice(head * HD, (head + 1) * HD)
        heads_query = query[:, cols]
        text_scores = lax.dot_general(heads_query, text[0, :, cols], NT, preferred_element_type=jnp.float32)
        image_scores = lax.dot_general(heads_query, stale[0, :, cols], NT, preferred_element_type=jnp.float32)
        image_scores += lax.dot_general(heads_query, residual[0, :, cols], NT, preferred_element_type=jnp.float32)
        text_scores *= HD**-0.5
        image_scores *= HD**-0.5
        peak = jnp.maximum(
            jnp.max(text_scores, axis=1, keepdims=True), jnp.max(image_scores, axis=1, keepdims=True)
        )
        text_weights = jnp.exp(text_scores - peak).astype(jnp.bfloat16)
        image_weights = jnp.exp(image_scores - peak).astype(jnp.bfloat16)
        total = jnp.sum(text_weights.astype(jnp.float32), axis=1, keepdims=True)
        total += jnp.sum(image_weights.astype(jnp.float32), axis=1, keepdims=True)
        mixed = jnp.dot(text_weights, text[1, :, cols], preferred_element_type=jnp.float32)
        mixed += jnp.dot(image_weights, stale[1, :, cols], preferred_element_type=jnp.float32)
        mixed += jnp.dot(image_weights, residual[1, :, cols], preferred_element_type=jnp.float32)
        out[:, cols] = (mixed / total).astype(jnp.bfloat16)


def attend(pieces, query_parts, text, stale):
    groups = len(query_parts)
    rows, width = query_parts[0].shape
    keys = stale.shape[1]
    texts = text.shape[1]
    bf16 = jnp.bfloat16
    return pl.pallas_call(
        functools.partial(attend_kernel, groups),
        out_shape=jax.ShapeDtypeStruct((groups * rows, width), bf16),
        in_specs=[VMEM] * (len(pieces) + groups + 2),
        out_specs=VMEM,
        scratch_shapes=[pltpu.VMEM((groups * rows, width), bf16), pltpu.VMEM((2, keys, width), bf16)],
        compiler_params=pltpu.CompilerParams(vmem_limit_bytes=24 << 20),
        cost_estimate=pl.CostEstimate(
            flops=4 * groups * rows * width * (texts + 2 * keys),
            bytes_accessed=4 * width * (texts + 2 * keys),
            transcendentals=groups * rows * (texts + keys) * (width // HD),
        ),
    )(*pieces, *query_parts, text, stale)


def project_kernel(parts, weights, outs, weight, total):
    group, spot = place()
    width = parts[0].shape[1]
    span = weight.shape[0] // SPREAD
    rows = outs[0].shape[0]
    for twist in range(SPREAD):
        start = jnp.bitwise_xor(spot, twist) * span
        for piece in weights[twist]:
            height = piece.shape[0]
            weight[pl.ds(pl.multiple_of(start, 16), height), :] = piece[...]
            start += height
    added = None
    for turn, part in enumerate(parts):
        origin = jnp.bitwise_xor(group, turn)
        term = lax.dot_general(
            part[...], weight[:, pl.ds(aligned(origin, width), width)], NT, preferred_element_type=jnp.float32
        )
        added = term if added is None else added + term
    total[...] = added.astype(jnp.bfloat16)
    for turn, out in enumerate(outs):
        out[...] = total[pl.ds(aligned(jnp.bitwise_xor(group, turn), rows), rows), :]


def project(parts, weights):
    groups = len(parts)
    tokens, width = parts[0].shape
    depth = weights[0][0].shape[1]
    columns = SPREAD * sum(piece.shape[0] for piece in weights[0])
    flat, tree = jax.tree.flatten(weights)

    def kernel(*refs):
        ins, outs, scratch = refs[: groups + len(flat)], refs[groups + len(flat) : -2], refs[-2:]
        project_kernel(ins[:groups], jax.tree.unflatten(tree, ins[groups:]), outs, *scratch)

    return pl.pallas_call(
        kernel,
        out_shape=[jax.ShapeDtypeStruct((tokens // groups, columns), jnp.bfloat16)] * groups,
        in_specs=[VMEM] * (groups + len(flat)),
        out_specs=[VMEM] * groups,
        scratch_shapes=[pltpu.VMEM((columns, depth), jnp.bfloat16), pltpu.VMEM((tokens, columns), jnp.bfloat16)],
        compiler_params=pltpu.CompilerParams(vmem_limit_bytes=24 << 20),
        cost_estimate=pl.CostEstimate(
            flops=2 * tokens * columns * depth, bytes_accessed=2 * columns * depth, transcendentals=0
        ),
    )(*parts, *flat)


def divide_kernel(*refs):
    parts, (keep, send, held) = refs[:-3], refs[-3:]
    group, _ = place()
    half = lax.axis_index("head")
    blocks = keep.shape[0]
    for turn, part in enumerate(parts):
        held[jnp.bitwise_xor(group, turn)] = part[...]
    for block in range(blocks):
        keep[block] = held[half * blocks + block]
        send[block] = held[(1 - half) * blocks + block]


def divide(parts):
    groups = len(parts)
    shape = jax.ShapeDtypeStruct((groups // 2, *parts[0].shape), jnp.bfloat16)
    return pl.pallas_call(
        divide_kernel,
        out_shape=[shape] * 2,
        in_specs=[VMEM] * groups,
        out_specs=[VMEM] * 2,
        scratch_shapes=[pltpu.VMEM((groups, *parts[0].shape), jnp.bfloat16)],
        compiler_params=pltpu.CompilerParams(vmem_limit_bytes=SMALL),
        cost_estimate=pl.CostEstimate(flops=0, bytes_accessed=4 * groups * parts[0].size, transcendentals=0),
    )(*parts)


def finish_kernel(kept, arrived, bias, gate, out):
    blocks, _, columns = kept.shape
    for block in range(blocks):
        cols = slice(block * columns, (block + 1) * columns)
        total = kept[block].astype(jnp.float32) + arrived[block].astype(jnp.float32)
        out[:, cols] = (gate[:, cols] * (total + bias[:, cols])).astype(jnp.bfloat16)


def finish(kept, arrived, bias, gate):
    blocks, rows, columns = kept.shape
    width = blocks * columns
    return pl.pallas_call(
        finish_kernel,
        out_shape=jax.ShapeDtypeStruct((rows, width), jnp.bfloat16),
        in_specs=[VMEM] * 4,
        out_specs=VMEM,
        compiler_params=pltpu.CompilerParams(vmem_limit_bytes=SMALL),
        cost_estimate=pl.CostEstimate(flops=3 * rows * width, bytes_accessed=4 * rows * width, transcendentals=0),
    )(kept, arrived, bias.reshape(1, width), gate.reshape(1, width))


def after(value, *others):
    return lax.optimization_barrier((value, *others))[0]


def grouped_body(queries, stale_kv, codes, exponents, text_kv, out_weight, out_bias, out_gate):
    groups = lax.axis_size("patch") // SPREAD
    size = groups * SPREAD

    def swap(value, twist):
        return lax.ppermute(value, "patch", [(p, p ^ twist) for p in range(size)])

    def along(values):
        moved = {turn: swap(values[turn], turn * SPREAD) for turn in (2, 1, 3)}
        return [moved[turn] for turn in range(1, groups)]

    residuals, queries = pack(groups, queries, codes, exponents)
    weight = out_weight.T
    cut = weight.shape[0] // SPREAD
    early, late = weight[:cut], weight[cut:]
    text, stale = pick(groups, text_kv, stale_kv)

    own = residuals[0]
    arrived = along(residuals)
    own_far = swap(own, 2)
    early = swap(early, 2)

    some, every = merge([own, *arrived])
    some, every = lax.optimization_barrier((some, every, own_far, early, text, stale))[:2]
    queries = lax.optimization_barrier((*queries, some))[:groups]
    some_far, near = swap(some, 2), swap(every, 1)
    asked = [queries[0], *along(queries)]

    own_far, some_far = lax.optimization_barrier((own_far, some_far, near, *asked))[:2]
    own_corner, some_corner = swap(own_far, 1), swap(some_far, 1)
    attended = attend([every, near, own_far, some_far, own_corner, some_corner], asked, text, stale)

    late = swap(after(late, some_far), 2)
    weight, early = lax.optimization_barrier((weight, early, own_corner, some_corner))[:2]
    across, beside = swap(attended, 2 * SPREAD), swap(attended, SPREAD)
    early_near = swap(early, 1)
    weight_near = swap(weight, 1)

    across, late = lax.optimization_barrier((across, late, beside, weight_near, early_near))[:2]
    last = swap(across, SPREAD)
    late_near = swap(late, 1)
    weights = [(weight,), (weight_near,), (early, late), (early_near, late_near)]
    terms = project([attended, beside, across, last], weights)
    kept, sent = divide([terms[0], *along(terms)])
    received = lax.ppermute(sent, "head", [(0, 1), (1, 0)])
    return finish(kept, received, out_bias, out_gate)


def solution(mesh):
    patches, halves = mesh.shape["patch"], mesh.shape["head"]
    placed = (
        P("patch", "head"),
        P(None, None, "head"),
        P(None, "patch", "head"),
        P(None, "patch", "head"),
        P(None, None, "head"),
        P("head", "patch"),
        P("head"),
        P("head"),
    )

    def body(*args):
        heads = args[0].shape[1] // HD
        groups = patches // SPREAD
        if groups != 4 or patches % SPREAD or heads % groups or halves != 2:
            return plain_body(*args)
        return grouped_body(*args)

    return jax.shard_map(body, mesh=mesh, in_specs=placed, out_specs=P("patch", "head"), check_vma=False)
```

```python
import functools

import jax
import jax.numpy as jnp
from jax import lax
from jax.experimental import pallas as pl
from jax.experimental.pallas import tpu as pltpu
from jax.sharding import PartitionSpec as P

HD = 128
SPREAD = 4
PACK_LIMIT = 56 << 20
SMALL = 16 << 20
PICK_LIMIT = 50 << 20
VMEM = pl.BlockSpec(memory_space=pltpu.VMEM)
HBM = pl.BlockSpec(memory_space=pltpu.HBM)
NT = (((1,), (1,)), ((), ()))


def plain_body(queries, stale_kv, codes, exponents, text_kv, out_weight, out_bias, out_gate):
    tok_rows = queries.shape[0]
    row_width = queries.shape[1]
    head_count = row_width // HD
    text_count = text_kv.shape[1]
    scale_factor = HD ** (-0.5)
    blocks = jnp.exp2(exponents.astype(jnp.float32))
    decoded = codes.astype(jnp.float32).reshape(2, tok_rows, head_count, HD) * blocks[..., None]
    decoded = decoded.astype(jnp.bfloat16).reshape(2, tok_rows, row_width)
    arrived = lax.all_gather(decoded, "patch", axis=1, tiled=True)
    all_rows = arrived.shape[1]
    query_heads = queries.reshape(tok_rows, head_count, HD)
    text_heads = text_kv.reshape(2, text_count, head_count, HD)
    stale_heads = stale_kv.reshape(2, all_rows, head_count, HD)
    arrived_heads = arrived.reshape(2, all_rows, head_count, HD)
    text_scores = jnp.einsum("thd,khd->htk", query_heads, text_heads[0], preferred_element_type=jnp.float32)
    rebuilt = stale_heads.astype(jnp.float32) + arrived_heads.astype(jnp.float32)
    image_scores = jnp.einsum(
        "thd,khd->htk", query_heads.astype(jnp.float32), rebuilt[0], precision=lax.Precision.HIGHEST
    )
    scores = jnp.concatenate([text_scores, image_scores], axis=2) * scale_factor
    row_peak = jnp.max(scores, axis=2, keepdims=True)
    weights = jnp.exp(scores - row_peak).astype(jnp.bfloat16)
    row_total = jnp.sum(weights.astype(jnp.float32), axis=2)
    text_part = jnp.einsum(
        "htk,khd->thd", weights[:, :, :text_count], text_heads[1], preferred_element_type=jnp.float32
    )
    image_part = jnp.einsum(
        "htk,khd->thd",
        weights[:, :, text_count:].astype(jnp.float32),
        rebuilt[1],
        precision=lax.Precision.HIGHEST,
    )
    attended = ((text_part + image_part) / row_total.T[:, :, None]).astype(jnp.bfloat16).reshape(tok_rows, row_width)
    partial_terms = jnp.dot(
        attended, lax.all_gather(out_weight, "patch", axis=1, tiled=True), preferred_element_type=jnp.float32
    )
    column_share = lax.psum_scatter(partial_terms, "head", scatter_dimension=1, tiled=True)
    return (out_gate * (column_share + out_bias)).astype(jnp.bfloat16)


def aligned(value, step):
    return pl.multiple_of(value * step, step)


def place():
    me = lax.axis_index("patch")
    return me // SPREAD, lax.rem(me, SPREAD)


def pack_kernel(queries_hbm, codes_hbm, exponents_hbm, weight_hbm, *rest):
    outs, early, (codes, queries, exponents, held, sems) = rest[:-6], rest[-6], rest[-5:]
    groups, kinds, rows, width = held.shape
    group, _ = place()
    per = width // HD
    copies = [
        pltpu.make_async_copy(exponents_hbm, exponents, sems.at[0]),
        pltpu.make_async_copy(codes_hbm, codes, sems.at[1]),
        pltpu.make_async_copy(queries_hbm, queries, sems.at[2]),
        pltpu.make_async_copy(weight_hbm.at[0 : early.shape[0]], early, sems.at[3]),
    ]
    for copy in copies:
        copy.start()
    copies[0].wait()
    copies[1].wait()
    eye = lax.broadcasted_iota(jnp.int32, (rows, rows), 0) == lax.broadcasted_iota(jnp.int32, (rows, rows), 1)
    eye = eye.astype(jnp.float32).astype(jnp.bfloat16)
    for kind in range(kinds - 1):
        scales = jnp.left_shift(1, exponents[:, kind, :] + 16).astype(jnp.float32) * (2.0**-16)
        scales = lax.dot_general(eye, scales.astype(jnp.bfloat16), NT, preferred_element_type=jnp.float32)
        for head in range(groups * per):
            inside = slice((head % per) * HD, (head % per + 1) * HD)
            whole = slice(head * HD, (head + 1) * HD)
            decoded = codes[kind, :, whole].astype(jnp.float32) * scales[:, head : head + 1]
            held[head // per, kind, :, inside] = decoded.astype(jnp.bfloat16)
    copies[2].wait()
    for target in range(groups):
        held[target, kinds - 1] = queries[:, target * width : (target + 1) * width]
    for turn in range(groups):
        target = jnp.bitwise_xor(group, turn)
        outs[turn][...] = held[target, 0 : kinds - 1]
        outs[groups + turn][...] = held[target, kinds - 1]
    copies[3].wait()


def pack(groups, queries, codes, exponents, weight):
    rows, width = queries.shape
    kinds = codes.shape[0]
    share = width // groups
    bf16 = jnp.bfloat16
    exponents = exponents.transpose(2, 0, 1)
    outs = pl.pallas_call(
        pack_kernel,
        out_shape=[jax.ShapeDtypeStruct((kinds, rows, share), bf16)] * groups
        + [jax.ShapeDtypeStruct((rows, share), bf16)] * groups
        + [jax.ShapeDtypeStruct((weight.shape[0] // 2, weight.shape[1]), bf16)],
        in_specs=[HBM] * 4,
        out_specs=[VMEM] * (2 * groups) + [HBM],
        scratch_shapes=[
            pltpu.VMEM(codes.shape, jnp.int32),
            pltpu.VMEM(queries.shape, bf16),
            pltpu.VMEM(exponents.shape, jnp.int32),
            pltpu.VMEM((groups, kinds + 1, rows, share), bf16),
            pltpu.SemaphoreType.DMA((4,)),
        ],
        compiler_params=pltpu.CompilerParams(vmem_limit_bytes=PACK_LIMIT),
        cost_estimate=pl.CostEstimate(flops=2 * codes.size, bytes_accessed=6 * codes.size, transcendentals=0),
    )(queries, codes, exponents, weight)
    return outs[:groups], outs[groups : 2 * groups], outs[-1]


def pick_kernel(text_hbm, stale_hbm, text, stale, sems):
    group, _ = place()
    width = text.shape[2]
    columns = pl.ds(aligned(group, width), width)
    text_copy = pltpu.make_async_copy(text_hbm.at[:, :, columns], text, sems.at[0])
    stale_copy = pltpu.make_async_copy(stale_hbm.at[:, :, columns], stale, sems.at[1])
    text_copy.start()
    stale_copy.start()
    text_copy.wait()
    stale_copy.wait()


def pick(groups, text_kv, stale_kv):
    shapes = [(2, value.shape[1], value.shape[2] // groups) for value in (text_kv, stale_kv)]
    return pl.pallas_call(
        pick_kernel,
        out_shape=[jax.ShapeDtypeStruct(shape, jnp.bfloat16) for shape in shapes],
        in_specs=[HBM] * 2,
        out_specs=[VMEM] * 2,
        scratch_shapes=[pltpu.SemaphoreType.DMA((2,))],
        compiler_params=pltpu.CompilerParams(vmem_limit_bytes=PICK_LIMIT),
        cost_estimate=pl.CostEstimate(flops=0, bytes_accessed=8 << 20, transcendentals=0),
    )(text_kv, stale_kv)


def merge_kernel(*refs):
    parts, (some, every) = refs[:-2], refs[-2:]
    for index, part in enumerate(parts):
        every[index] = part[...]
        if index:
            some[index - 1] = part[...]


def merge(parts):
    shapes = [(count, *parts[0].shape) for count in (len(parts) - 1, len(parts))]
    return pl.pallas_call(
        merge_kernel,
        out_shape=[jax.ShapeDtypeStruct(shape, parts[0].dtype) for shape in shapes],
        in_specs=[VMEM] * len(parts),
        out_specs=[VMEM] * 2,
        compiler_params=pltpu.CompilerParams(vmem_limit_bytes=SMALL),
        cost_estimate=pl.CostEstimate(flops=0, bytes_accessed=4 * len(parts) * parts[0].size, transcendentals=0),
    )(*parts)


def head_output(query, text, stale, residual, cols):
    text_scores = lax.dot_general(query, text[0, :, cols], NT, preferred_element_type=jnp.float32)
    image_scores = lax.dot_general(query, stale[0, :, cols], NT, preferred_element_type=jnp.float32)
    image_scores += lax.dot_general(query, residual[0, :, cols], NT, preferred_element_type=jnp.float32)
    text_scores *= HD**-0.5
    image_scores *= HD**-0.5
    peak = jnp.maximum(jnp.max(text_scores, axis=1, keepdims=True), jnp.max(image_scores, axis=1, keepdims=True))
    text_weights = jnp.exp(text_scores - peak).astype(jnp.bfloat16)
    image_weights = jnp.exp(image_scores - peak).astype(jnp.bfloat16)
    total = jnp.sum(text_weights.astype(jnp.float32), axis=1, keepdims=True)
    total += jnp.sum(image_weights.astype(jnp.float32), axis=1, keepdims=True)
    mixed = jnp.dot(text_weights, text[1, :, cols], preferred_element_type=jnp.float32)
    mixed += jnp.dot(image_weights, stale[1, :, cols], preferred_element_type=jnp.float32)
    mixed += jnp.dot(image_weights, residual[1, :, cols], preferred_element_type=jnp.float32)
    return (mixed / total).astype(jnp.bfloat16)


def attend_kernel(groups, *refs):
    (every, near, own_far, some_far, own_corner, some_corner), refs = refs[:6], refs[6:]
    asked, (text, stale, out, query, residual) = refs[:groups], refs[groups:]
    group, spot = place()
    rows, width = asked[0].shape
    for turn in range(groups):
        origin = jnp.bitwise_xor(group, turn)
        query[pl.ds(aligned(origin, rows), rows), :] = asked[turn][...]
        for twist in range(SPREAD):
            token = origin * SPREAD + jnp.bitwise_xor(spot, twist)
            if twist < 2:
                part = (every, near)[twist][turn]
            elif turn == 0:
                part = (own_far, own_corner)[twist - 2][...]
            else:
                part = (some_far, some_corner)[twist - 2][turn - 1]
            residual[:, pl.ds(aligned(token, rows), rows), :] = part
    for head in range(width // HD):
        cols = slice(head * HD, (head + 1) * HD)
        out[:, cols] = head_output(query[:, cols], text, stale, residual, cols)


def attend_cost(heads, tokens, texts, keys):
    return pl.CostEstimate(
        flops=4 * heads * tokens * HD * (texts + 2 * keys),
        bytes_accessed=4 * heads * HD * (texts + 2 * keys),
        transcendentals=heads * tokens * (texts + keys),
    )


def attend(pieces, query_parts, text, stale):
    groups = len(query_parts)
    rows, width = query_parts[0].shape
    tokens = groups * rows
    keys = stale.shape[1]
    texts = text.shape[1]
    heads = width // HD

    return pl.pallas_call(
        functools.partial(attend_kernel, groups),
        out_shape=jax.ShapeDtypeStruct((tokens, width), jnp.bfloat16),
        in_specs=[VMEM] * (len(pieces) + groups + 2),
        out_specs=VMEM,
        scratch_shapes=[pltpu.VMEM((tokens, width), jnp.bfloat16), pltpu.VMEM((2, keys, width), jnp.bfloat16)],
        compiler_params=pltpu.CompilerParams(vmem_limit_bytes=SMALL),
        cost_estimate=attend_cost(heads, tokens, texts, keys),
    )(*pieces, *query_parts, text, stale)


def order_kernel(*refs):
    wholes, halves, out = refs[:2], refs[2:-1], refs[-1]
    _, spot = place()
    span = out.shape[0] // SPREAD
    for twist, whole in enumerate(wholes):
        start = jnp.bitwise_xor(spot, twist) * span
        out[pl.ds(pl.multiple_of(start, 16), span), :] = whole[...]
    for index, piece in enumerate(halves):
        start = jnp.bitwise_xor(spot, 2 + index // 2) * span + index % 2 * (span // 2)
        out[pl.ds(pl.multiple_of(start, 16), span // 2), :] = piece[...]


def order(weight, near, halves):
    pieces = [weight, near, *halves]
    span, depth = weight.shape
    shape = (SPREAD * span, depth)
    return pl.pallas_call(
        order_kernel,
        out_shape=jax.ShapeDtypeStruct(shape, jnp.bfloat16),
        in_specs=[VMEM] * len(pieces),
        out_specs=VMEM,
        compiler_params=pltpu.CompilerParams(vmem_limit_bytes=SMALL),
        cost_estimate=pl.CostEstimate(flops=0, bytes_accessed=4 * shape[0] * depth, transcendentals=0),
    )(*pieces)


def term_of(part, weight, turn):
    group, _ = place()
    width = part.shape[1]
    columns = pl.ds(aligned(jnp.bitwise_xor(group, turn), width), width)
    return lax.dot_general(part[...], weight[:, columns], NT, preferred_element_type=jnp.float32)


def begin_kernel(*refs):
    parts, (weight, out) = refs[:-2], refs[-2:]
    total = term_of(parts[0], weight, 0)
    for turn in range(1, len(parts)):
        total += term_of(parts[turn], weight, turn)
    out[...] = total


def begin(parts, weight):
    tokens, width = parts[0].shape
    columns = weight.shape[0]
    return pl.pallas_call(
        begin_kernel,
        out_shape=jax.ShapeDtypeStruct((tokens, columns), jnp.float32),
        in_specs=[VMEM] * (len(parts) + 1),
        out_specs=VMEM,
        compiler_params=pltpu.CompilerParams(vmem_limit_bytes=SMALL),
        cost_estimate=pl.CostEstimate(
            flops=2 * tokens * columns * width * len(parts), bytes_accessed=4 * tokens * columns, transcendentals=0
        ),
    )(*parts, weight)


def close_kernel(partial, part, weight, *rest):
    outs, total = rest[:-1], rest[-1]
    group, _ = place()
    rows = outs[0].shape[0]
    total[...] = (partial[...] + term_of(part, weight, len(outs) - 1)).astype(jnp.bfloat16)
    for turn, out in enumerate(outs):
        out[...] = total[pl.ds(aligned(jnp.bitwise_xor(group, turn), rows), rows), :]


def close(groups, partial, part, weight):
    tokens, columns = partial.shape
    return pl.pallas_call(
        close_kernel,
        out_shape=[jax.ShapeDtypeStruct((tokens // groups, columns), jnp.bfloat16)] * groups,
        in_specs=[VMEM] * 3,
        out_specs=[VMEM] * groups,
        scratch_shapes=[pltpu.VMEM((tokens, columns), jnp.bfloat16)],
        compiler_params=pltpu.CompilerParams(vmem_limit_bytes=SMALL),
        cost_estimate=pl.CostEstimate(
            flops=2 * tokens * columns * part.shape[1], bytes_accessed=8 * tokens * columns, transcendentals=0
        ),
    )(partial, part, weight)


def finish_kernel(groups, *refs):
    mine, other, (bias, gate, out, held) = refs[:groups], refs[groups : 2 * groups], refs[2 * groups :]
    group, _ = place()
    columns = mine[0].shape[1]
    blocks = groups // 2
    first = lax.axis_index("head") * blocks
    for turn in range(groups):
        origin = jnp.bitwise_xor(group, turn)
        held[origin] = mine[turn][...].astype(jnp.float32) + other[turn][...].astype(jnp.float32)
    for block in range(blocks):
        cols = slice(block * columns, (block + 1) * columns)
        out[:, cols] = (gate[:, cols] * (held[first + block] + bias[:, cols])).astype(jnp.bfloat16)


def finish(mine, other, bias, gate):
    groups = len(mine)
    rows, columns = mine[0].shape
    width = columns * groups // 2
    return pl.pallas_call(
        functools.partial(finish_kernel, groups),
        out_shape=jax.ShapeDtypeStruct((rows, width), jnp.bfloat16),
        in_specs=[VMEM] * (2 * groups + 2),
        out_specs=VMEM,
        scratch_shapes=[pltpu.VMEM((groups, rows, columns), jnp.float32)],
        compiler_params=pltpu.CompilerParams(vmem_limit_bytes=SMALL),
        cost_estimate=pl.CostEstimate(flops=3 * rows * width, bytes_accessed=4 * rows * width, transcendentals=0),
    )(*mine, *other, bias.reshape(1, width), gate.reshape(1, width))


def after(value, *others):
    return lax.optimization_barrier((value, *others))[0]


def grouped_body(queries, stale_kv, codes, exponents, text_kv, out_weight, out_bias, out_gate):
    groups = lax.axis_size("patch") // SPREAD
    size = groups * SPREAD

    def swap(value, twist):
        return lax.ppermute(value, "patch", [(p, p ^ twist) for p in range(size)])

    def along(values):
        moved = {turn: swap(values[turn], turn * SPREAD) for turn in (2, 1, 3)}
        return [moved[turn] for turn in range(1, groups)]

    weight = out_weight.T
    half = weight.shape[0] // 2
    residuals, queries, early = pack(groups, queries, codes, exponents, weight)
    text, stale = pick(groups, text_kv, stale_kv)

    own = residuals[0]
    arrived = along(residuals)
    own_far, early = swap(own, 2), swap(early, 2)

    some, every = merge([own, *arrived])
    some, every = lax.optimization_barrier((some, every, own_far, early, text, stale))[:2]
    queries = lax.optimization_barrier((*queries, some))[:groups]
    some_far, near = swap(some, 2), swap(every, 1)
    asked = [queries[0], *along(queries)]

    own_far, some_far = lax.optimization_barrier((own_far, some_far, near, *asked[2:]))[:2]
    own_corner, some_corner = swap(own_far, 1), swap(some_far, 1)
    weight, early = lax.optimization_barrier((weight, early, own_corner, some_corner))[:2]
    weight_near, early_near, late = swap(weight, 1), swap(early, 1), swap(weight[half:], 2)
    attended = attend([every, near, own_far, some_far, own_corner, some_corner], asked, text, stale)

    across, beside = swap(attended, 2 * SPREAD), swap(attended, SPREAD)
    across, beside, late = lax.optimization_barrier((across, beside, late, weight_near, early_near))[:3]
    last = swap(across, SPREAD)
    weight = order(weight, weight_near, [early, late, early_near, swap(late, 1)])
    terms = close(groups, begin([attended, beside, across], weight), last, weight)

    terms = [terms[0], *along(terms)]
    received = [lax.ppermute(term, "head", [(0, 1), (1, 0)]) for term in terms]
    return finish(terms, received, out_bias, out_gate)


def solution(mesh):
    patches, halves = mesh.shape["patch"], mesh.shape["head"]
    placed = (
        P("patch", "head"),
        P(None, None, "head"),
        P(None, "patch", "head"),
        P(None, "patch", "head"),
        P(None, None, "head"),
        P("head", "patch"),
        P("head"),
        P("head"),
    )

    def body(*args):
        heads = args[0].shape[1] // HD
        groups = patches // SPREAD
        if groups != 4 or patches % SPREAD or heads % groups or halves != 2:
            return plain_body(*args)
        return grouped_body(*args)

    return jax.shard_map(body, mesh=mesh, in_specs=placed, out_specs=P("patch", "head"), check_vma=False)
```

```python
import functools

import jax
import jax.numpy as jnp
from jax import lax
from jax.experimental import pallas as pl
from jax.experimental.pallas import tpu as pltpu
from jax.sharding import PartitionSpec as P

HD = 128
SPREAD = 4
PACK_LIMIT = 56 << 20
SMALL = 16 << 20
PICK_LIMIT = 50 << 20
VMEM = pl.BlockSpec(memory_space=pltpu.VMEM)
HBM = pl.BlockSpec(memory_space=pltpu.HBM)
NT = (((1,), (1,)), ((), ()))


def plain_body(queries, stale_kv, codes, exponents, text_kv, out_weight, out_bias, out_gate):
    tok_rows = queries.shape[0]
    row_width = queries.shape[1]
    head_count = row_width // HD
    text_count = text_kv.shape[1]
    scale_factor = HD ** (-0.5)
    blocks = jnp.exp2(exponents.astype(jnp.float32))
    decoded = codes.astype(jnp.float32).reshape(2, tok_rows, head_count, HD) * blocks[..., None]
    decoded = decoded.astype(jnp.bfloat16).reshape(2, tok_rows, row_width)
    arrived = lax.all_gather(decoded, "patch", axis=1, tiled=True)
    all_rows = arrived.shape[1]
    query_heads = queries.reshape(tok_rows, head_count, HD)
    text_heads = text_kv.reshape(2, text_count, head_count, HD)
    stale_heads = stale_kv.reshape(2, all_rows, head_count, HD)
    arrived_heads = arrived.reshape(2, all_rows, head_count, HD)
    text_scores = jnp.einsum("thd,khd->htk", query_heads, text_heads[0], preferred_element_type=jnp.float32)
    rebuilt = stale_heads.astype(jnp.float32) + arrived_heads.astype(jnp.float32)
    image_scores = jnp.einsum(
        "thd,khd->htk", query_heads.astype(jnp.float32), rebuilt[0], precision=lax.Precision.HIGHEST
    )
    scores = jnp.concatenate([text_scores, image_scores], axis=2) * scale_factor
    row_peak = jnp.max(scores, axis=2, keepdims=True)
    weights = jnp.exp(scores - row_peak).astype(jnp.bfloat16)
    row_total = jnp.sum(weights.astype(jnp.float32), axis=2)
    text_part = jnp.einsum(
        "htk,khd->thd", weights[:, :, :text_count], text_heads[1], preferred_element_type=jnp.float32
    )
    image_part = jnp.einsum(
        "htk,khd->thd",
        weights[:, :, text_count:].astype(jnp.float32),
        rebuilt[1],
        precision=lax.Precision.HIGHEST,
    )
    attended = ((text_part + image_part) / row_total.T[:, :, None]).astype(jnp.bfloat16).reshape(tok_rows, row_width)
    partial_terms = jnp.dot(
        attended, lax.all_gather(out_weight, "patch", axis=1, tiled=True), preferred_element_type=jnp.float32
    )
    column_share = lax.psum_scatter(partial_terms, "head", scatter_dimension=1, tiled=True)
    return (out_gate * (column_share + out_bias)).astype(jnp.bfloat16)


def aligned(value, step):
    return pl.multiple_of(value * step, step)


def place():
    me = lax.axis_index("patch")
    return me // SPREAD, lax.rem(me, SPREAD)


def pack_kernel(queries_hbm, codes_hbm, exponents_hbm, *rest):
    outs, (codes, queries, exponents, held, sems) = rest[:-5], rest[-5:]
    groups, kinds, rows, width = held.shape
    group, _ = place()
    per = width // HD
    copies = [
        pltpu.make_async_copy(exponents_hbm, exponents, sems.at[0]),
        pltpu.make_async_copy(codes_hbm, codes, sems.at[1]),
        pltpu.make_async_copy(queries_hbm, queries, sems.at[2]),
    ]
    for copy in copies:
        copy.start()
    copies[0].wait()
    copies[1].wait()
    eye = lax.broadcasted_iota(jnp.int32, (rows, rows), 0) == lax.broadcasted_iota(jnp.int32, (rows, rows), 1)
    eye = eye.astype(jnp.float32).astype(jnp.bfloat16)
    for kind in range(kinds - 1):
        scales = jnp.left_shift(1, exponents[:, kind, :] + 16).astype(jnp.float32) * (2.0**-16)
        scales = lax.dot_general(eye, scales.astype(jnp.bfloat16), NT, preferred_element_type=jnp.float32)
        for head in range(groups * per):
            inside = slice((head % per) * HD, (head % per + 1) * HD)
            whole = slice(head * HD, (head + 1) * HD)
            decoded = codes[kind, :, whole].astype(jnp.float32) * scales[:, head : head + 1]
            held[head // per, kind, :, inside] = decoded.astype(jnp.bfloat16)
    copies[2].wait()
    for target in range(groups):
        held[target, kinds - 1] = queries[:, target * width : (target + 1) * width]
    for turn in range(groups):
        target = jnp.bitwise_xor(group, turn)
        outs[turn][...] = held[target, 0 : kinds - 1]
        outs[groups + turn][...] = held[target, kinds - 1]


def pack(groups, queries, codes, exponents):
    rows, width = queries.shape
    kinds = codes.shape[0]
    share = width // groups
    bf16 = jnp.bfloat16
    exponents = exponents.transpose(2, 0, 1)
    outs = pl.pallas_call(
        pack_kernel,
        out_shape=[jax.ShapeDtypeStruct((kinds, rows, share), bf16)] * groups
        + [jax.ShapeDtypeStruct((rows, share), bf16)] * groups,
        in_specs=[HBM] * 3,
        out_specs=[VMEM] * (2 * groups),
        scratch_shapes=[
            pltpu.VMEM(codes.shape, jnp.int32),
            pltpu.VMEM(queries.shape, bf16),
            pltpu.VMEM(exponents.shape, jnp.int32),
            pltpu.VMEM((groups, kinds + 1, rows, share), bf16),
            pltpu.SemaphoreType.DMA((3,)),
        ],
        compiler_params=pltpu.CompilerParams(vmem_limit_bytes=PACK_LIMIT),
        cost_estimate=pl.CostEstimate(flops=2 * codes.size, bytes_accessed=6 * codes.size, transcendentals=0),
    )(queries, codes, exponents)
    return outs[:groups], outs[groups:]


def pick_kernel(text_hbm, stale_hbm, text, stale, sems):
    group, _ = place()
    width = text.shape[2]
    columns = pl.ds(aligned(group, width), width)
    text_copy = pltpu.make_async_copy(text_hbm.at[:, :, columns], text, sems.at[0])
    stale_copy = pltpu.make_async_copy(stale_hbm.at[:, :, columns], stale, sems.at[1])
    text_copy.start()
    stale_copy.start()
    text_copy.wait()
    stale_copy.wait()


def pick(groups, text_kv, stale_kv):
    shapes = [(2, value.shape[1], value.shape[2] // groups) for value in (text_kv, stale_kv)]
    return pl.pallas_call(
        pick_kernel,
        out_shape=[jax.ShapeDtypeStruct(shape, jnp.bfloat16) for shape in shapes],
        in_specs=[HBM] * 2,
        out_specs=[VMEM] * 2,
        scratch_shapes=[pltpu.SemaphoreType.DMA((2,))],
        compiler_params=pltpu.CompilerParams(vmem_limit_bytes=PICK_LIMIT),
        cost_estimate=pl.CostEstimate(flops=0, bytes_accessed=8 << 20, transcendentals=0),
    )(text_kv, stale_kv)


def merge_kernel(*refs):
    parts, (some, every) = refs[:-2], refs[-2:]
    for index, part in enumerate(parts):
        every[index] = part[...]
        if index:
            some[index - 1] = part[...]


def merge(parts):
    shapes = [(count, *parts[0].shape) for count in (len(parts) - 1, len(parts))]
    return pl.pallas_call(
        merge_kernel,
        out_shape=[jax.ShapeDtypeStruct(shape, parts[0].dtype) for shape in shapes],
        in_specs=[VMEM] * len(parts),
        out_specs=[VMEM] * 2,
        compiler_params=pltpu.CompilerParams(vmem_limit_bytes=SMALL),
        cost_estimate=pl.CostEstimate(flops=0, bytes_accessed=4 * len(parts) * parts[0].size, transcendentals=0),
    )(*parts)


def head_output(query, text, stale, residual, cols):
    text_scores = lax.dot_general(query, text[0, :, cols], NT, preferred_element_type=jnp.float32)
    image_scores = lax.dot_general(query, stale[0, :, cols], NT, preferred_element_type=jnp.float32)
    image_scores += lax.dot_general(query, residual[0, :, cols], NT, preferred_element_type=jnp.float32)
    text_scores *= HD**-0.5
    image_scores *= HD**-0.5
    peak = jnp.maximum(jnp.max(text_scores, axis=1, keepdims=True), jnp.max(image_scores, axis=1, keepdims=True))
    text_weights = jnp.exp(text_scores - peak).astype(jnp.bfloat16)
    image_weights = jnp.exp(image_scores - peak).astype(jnp.bfloat16)
    total = jnp.sum(text_weights.astype(jnp.float32), axis=1, keepdims=True)
    total += jnp.sum(image_weights.astype(jnp.float32), axis=1, keepdims=True)
    mixed = jnp.dot(text_weights, text[1, :, cols], preferred_element_type=jnp.float32)
    mixed += jnp.dot(image_weights, stale[1, :, cols], preferred_element_type=jnp.float32)
    mixed += jnp.dot(image_weights, residual[1, :, cols], preferred_element_type=jnp.float32)
    return (mixed / total).astype(jnp.bfloat16)


def attend_kernel(groups, *refs):
    (every, near, own_far, some_far, own_corner, some_corner), refs = refs[:6], refs[6:]
    asked, (text, stale, out, most, last, query, residual) = refs[:groups], refs[groups:]
    group, spot = place()
    rows, width = asked[0].shape
    for turn in range(groups):
        origin = jnp.bitwise_xor(group, turn)
        query[pl.ds(aligned(origin, rows), rows), :] = asked[turn][...]
        for twist in range(SPREAD):
            token = origin * SPREAD + jnp.bitwise_xor(spot, twist)
            if twist < 2:
                part = (every, near)[twist][turn]
            elif turn == 0:
                part = (own_far, own_corner)[twist - 2][...]
            else:
                part = (some_far, some_corner)[twist - 2][turn - 1]
            residual[:, pl.ds(aligned(token, rows), rows), :] = part
    for head in range(width // HD):
        cols = slice(head * HD, (head + 1) * HD)
        value = head_output(query[:, cols], text, stale, residual, cols)
        out[:, cols] = value
        if head < width // HD - 1:
            most[:, cols] = value
        else:
            last[...] = value


def attend_cost(heads, tokens, texts, keys):
    return pl.CostEstimate(
        flops=4 * heads * tokens * HD * (texts + 2 * keys),
        bytes_accessed=4 * heads * HD * (texts + 2 * keys),
        transcendentals=heads * tokens * (texts + keys),
    )


def attend(pieces, query_parts, text, stale):
    groups = len(query_parts)
    rows, width = query_parts[0].shape
    tokens = groups * rows
    keys = stale.shape[1]
    texts = text.shape[1]
    heads = width // HD

    return pl.pallas_call(
        functools.partial(attend_kernel, groups),
        out_shape=[jax.ShapeDtypeStruct((tokens, size), jnp.bfloat16) for size in (width, width - HD, HD)],
        in_specs=[VMEM] * (len(pieces) + groups + 2),
        out_specs=[VMEM] * 3,
        scratch_shapes=[pltpu.VMEM((tokens, width), jnp.bfloat16), pltpu.VMEM((2, keys, width), jnp.bfloat16)],
        compiler_params=pltpu.CompilerParams(vmem_limit_bytes=SMALL),
        cost_estimate=attend_cost(heads, tokens, texts, keys),
    )(*pieces, *query_parts, text, stale)


def order_kernel(*refs):
    pieces, out = refs[:-1], refs[-1]
    _, spot = place()
    span = out.shape[0] // SPREAD
    for twist, piece in enumerate(pieces):
        out[pl.ds(aligned(jnp.bitwise_xor(spot, twist), span), span), :] = piece[...]


def order(pieces):
    span, depth = pieces[0].shape
    shape = (SPREAD * span, depth)
    return pl.pallas_call(
        order_kernel,
        out_shape=jax.ShapeDtypeStruct(shape, jnp.bfloat16),
        in_specs=[VMEM] * len(pieces),
        out_specs=VMEM,
        compiler_params=pltpu.CompilerParams(vmem_limit_bytes=SMALL),
        cost_estimate=pl.CostEstimate(flops=0, bytes_accessed=4 * shape[0] * depth, transcendentals=0),
    )(*pieces)


def term_of(part, weight, turn, skip, width):
    group, _ = place()
    start = jnp.bitwise_xor(group, turn) * width + skip
    columns = pl.ds(pl.multiple_of(start, HD), part.shape[1])
    return lax.dot_general(part[...], weight[:, columns], NT, preferred_element_type=jnp.float32)


def begin_kernel(full, beside, across_most, across_last, weight, out):
    width = full.shape[1]
    total = term_of(full, weight, 0, 0, width) + term_of(beside, weight, 1, 0, width)
    total += term_of(across_most, weight, 2, 0, width)
    out[...] = total + term_of(across_last, weight, 2, width - HD, width)


def begin(parts, weight):
    tokens = parts[0].shape[0]
    columns, depth = weight.shape
    return pl.pallas_call(
        begin_kernel,
        out_shape=jax.ShapeDtypeStruct((tokens, columns), jnp.float32),
        in_specs=[VMEM] * (len(parts) + 1),
        out_specs=VMEM,
        compiler_params=pltpu.CompilerParams(vmem_limit_bytes=SMALL),
        cost_estimate=pl.CostEstimate(
            flops=2 * tokens * columns * depth, bytes_accessed=4 * tokens * columns, transcendentals=0
        ),
    )(*parts, weight)


def close_kernel(partial, most, last, weight, *rest):
    outs, total = rest[:-1], rest[-1]
    group, _ = place()
    rows = outs[0].shape[0]
    width = most.shape[1] + last.shape[1]
    added = partial[...] + term_of(most, weight, 3, 0, width) + term_of(last, weight, 3, width - HD, width)
    total[...] = added.astype(jnp.bfloat16)
    for turn, out in enumerate(outs):
        out[...] = total[pl.ds(aligned(jnp.bitwise_xor(group, turn), rows), rows), :]


def close(groups, partial, parts, weight):
    tokens, columns = partial.shape
    return pl.pallas_call(
        close_kernel,
        out_shape=[jax.ShapeDtypeStruct((tokens // groups, columns), jnp.bfloat16)] * groups,
        in_specs=[VMEM] * 4,
        out_specs=[VMEM] * groups,
        scratch_shapes=[pltpu.VMEM((tokens, columns), jnp.bfloat16)],
        compiler_params=pltpu.CompilerParams(vmem_limit_bytes=SMALL),
        cost_estimate=pl.CostEstimate(
            flops=tokens * weight.size, bytes_accessed=8 * tokens * columns, transcendentals=0
        ),
    )(partial, *parts, weight)


def divide_kernel(*refs):
    parts, (keep, send, held) = refs[:-3], refs[-3:]
    group, _ = place()
    half = lax.axis_index("head")
    blocks = keep.shape[0]
    for turn, part in enumerate(parts):
        held[jnp.bitwise_xor(group, turn)] = part[...]
    for block in range(blocks):
        keep[block] = held[half * blocks + block]
        send[block] = held[(1 - half) * blocks + block]


def divide(parts):
    groups = len(parts)
    shape = jax.ShapeDtypeStruct((groups // 2, *parts[0].shape), jnp.bfloat16)
    return pl.pallas_call(
        divide_kernel,
        out_shape=[shape] * 2,
        in_specs=[VMEM] * groups,
        out_specs=[VMEM] * 2,
        scratch_shapes=[pltpu.VMEM((groups, *parts[0].shape), jnp.bfloat16)],
        compiler_params=pltpu.CompilerParams(vmem_limit_bytes=SMALL),
        cost_estimate=pl.CostEstimate(flops=0, bytes_accessed=4 * groups * parts[0].size, transcendentals=0),
    )(*parts)


def finish_kernel(kept, arrived, bias, gate, out):
    blocks, _, columns = kept.shape
    for block in range(blocks):
        cols = slice(block * columns, (block + 1) * columns)
        total = kept[block].astype(jnp.float32) + arrived[block].astype(jnp.float32)
        out[:, cols] = (gate[:, cols] * (total + bias[:, cols])).astype(jnp.bfloat16)


def finish(kept, arrived, bias, gate):
    blocks, rows, columns = kept.shape
    width = blocks * columns
    return pl.pallas_call(
        finish_kernel,
        out_shape=jax.ShapeDtypeStruct((rows, width), jnp.bfloat16),
        in_specs=[VMEM] * 4,
        out_specs=VMEM,
        compiler_params=pltpu.CompilerParams(vmem_limit_bytes=SMALL),
        cost_estimate=pl.CostEstimate(flops=3 * rows * width, bytes_accessed=4 * rows * width, transcendentals=0),
    )(kept, arrived, bias.reshape(1, width), gate.reshape(1, width))


def after(value, *others):
    return lax.optimization_barrier((value, *others))[0]


def grouped_body(queries, stale_kv, codes, exponents, text_kv, out_weight, out_bias, out_gate):
    groups = lax.axis_size("patch") // SPREAD
    size = groups * SPREAD

    def swap(value, twist):
        return lax.ppermute(value, "patch", [(p, p ^ twist) for p in range(size)])

    def along(values):
        moved = {turn: swap(values[turn], turn * SPREAD) for turn in (3, 2, 1)}
        return [moved[turn] for turn in range(1, groups)]

    weight = out_weight.T
    weight_far = swap(weight, 2)
    residuals, queries = pack(groups, queries, codes, exponents)
    text, stale = pick(groups, text_kv, stale_kv)

    own = residuals[0]
    arrived = along(residuals)
    own_far = swap(own, 2)

    some, every = merge([own, *arrived])
    some, every = lax.optimization_barrier((some, every, own_far, weight_far, text, stale))[:2]
    queries = lax.optimization_barrier((*queries, some))[:groups]
    some_far, near = swap(some, 2), swap(every, 1)
    asked = [queries[0], *along(queries)]

    own_far, some_far = lax.optimization_barrier((own_far, some_far, near, *asked))[:2]
    own_corner, some_corner = swap(own_far, 1), swap(some_far, 1)
    weight, weight_far = lax.optimization_barrier((weight, weight_far, own_corner, some_corner))[:2]
    weight_near, weight_corner = swap(weight, 1), swap(weight_far, 1)
    full, most, last = attend([every, near, own_far, some_far, own_corner, some_corner], asked, text, stale)

    across_most, across_last = swap(most, 2 * SPREAD), swap(last, 2 * SPREAD)
    beside = swap(full, SPREAD)
    final_most = swap(across_most, SPREAD)
    final_last = swap(after(across_last, beside, weight_near, weight_corner), SPREAD)
    weight = order([weight, weight_near, weight_far, weight_corner])
    partial = begin([full, beside, across_most, across_last], weight)
    terms = close(groups, partial, [final_most, final_last], weight)

    kept, sent = divide([terms[0], *along(terms)])
    received = lax.ppermute(sent, "head", [(0, 1), (1, 0)])
    return finish(kept, received, out_bias, out_gate)


def solution(mesh):
    patches, halves = mesh.shape["patch"], mesh.shape["head"]
    placed = (
        P("patch", "head"),
        P(None, None, "head"),
        P(None, "patch", "head"),
        P(None, "patch", "head"),
        P(None, None, "head"),
        P("head", "patch"),
        P("head"),
        P("head"),
    )

    def body(*args):
        heads = args[0].shape[1] // HD
        groups = patches // SPREAD
        if groups != 4 or patches % SPREAD or heads % groups or halves != 2:
            return plain_body(*args)
        return grouped_body(*args)

    return jax.shard_map(body, mesh=mesh, in_specs=placed, out_specs=P("patch", "head"), check_vma=False)
```

```python
import functools

import jax
import jax.numpy as jnp
from jax import lax
from jax.experimental import pallas as pl
from jax.experimental.pallas import tpu as pltpu
from jax.sharding import PartitionSpec as P

HD = 128
SPREAD = 4
PACK_LIMIT = 56 << 20
SMALL = 16 << 20
PICK_LIMIT = 50 << 20
VMEM = pl.BlockSpec(memory_space=pltpu.VMEM)
HBM = pl.BlockSpec(memory_space=pltpu.HBM)
NT = (((1,), (1,)), ((), ()))


def plain_body(queries, stale_kv, codes, exponents, text_kv, out_weight, out_bias, out_gate):
    tok_rows = queries.shape[0]
    row_width = queries.shape[1]
    head_count = row_width // HD
    text_count = text_kv.shape[1]
    scale_factor = HD ** (-0.5)
    blocks = jnp.exp2(exponents.astype(jnp.float32))
    decoded = codes.astype(jnp.float32).reshape(2, tok_rows, head_count, HD) * blocks[..., None]
    decoded = decoded.astype(jnp.bfloat16).reshape(2, tok_rows, row_width)
    arrived = lax.all_gather(decoded, "patch", axis=1, tiled=True)
    all_rows = arrived.shape[1]
    query_heads = queries.reshape(tok_rows, head_count, HD)
    text_heads = text_kv.reshape(2, text_count, head_count, HD)
    stale_heads = stale_kv.reshape(2, all_rows, head_count, HD)
    arrived_heads = arrived.reshape(2, all_rows, head_count, HD)
    text_scores = jnp.einsum("thd,khd->htk", query_heads, text_heads[0], preferred_element_type=jnp.float32)
    rebuilt = stale_heads.astype(jnp.float32) + arrived_heads.astype(jnp.float32)
    image_scores = jnp.einsum(
        "thd,khd->htk", query_heads.astype(jnp.float32), rebuilt[0], precision=lax.Precision.HIGHEST
    )
    scores = jnp.concatenate([text_scores, image_scores], axis=2) * scale_factor
    row_peak = jnp.max(scores, axis=2, keepdims=True)
    weights = jnp.exp(scores - row_peak).astype(jnp.bfloat16)
    row_total = jnp.sum(weights.astype(jnp.float32), axis=2)
    text_part = jnp.einsum(
        "htk,khd->thd", weights[:, :, :text_count], text_heads[1], preferred_element_type=jnp.float32
    )
    image_part = jnp.einsum(
        "htk,khd->thd",
        weights[:, :, text_count:].astype(jnp.float32),
        rebuilt[1],
        precision=lax.Precision.HIGHEST,
    )
    attended = ((text_part + image_part) / row_total.T[:, :, None]).astype(jnp.bfloat16).reshape(tok_rows, row_width)
    partial_terms = jnp.dot(
        attended, lax.all_gather(out_weight, "patch", axis=1, tiled=True), preferred_element_type=jnp.float32
    )
    column_share = lax.psum_scatter(partial_terms, "head", scatter_dimension=1, tiled=True)
    return (out_gate * (column_share + out_bias)).astype(jnp.bfloat16)


def aligned(value, step):
    return pl.multiple_of(value * step, step)


def place():
    me = lax.axis_index("patch")
    return me // SPREAD, lax.rem(me, SPREAD)


def pack_kernel(queries_hbm, codes_hbm, exponents_hbm, weight_hbm, *rest):
    outs, early, (codes, queries, exponents, held, sems) = rest[:-6], rest[-6], rest[-5:]
    groups, kinds, rows, width = held.shape
    group, _ = place()
    per = width // HD
    copies = [
        pltpu.make_async_copy(exponents_hbm, exponents, sems.at[0]),
        pltpu.make_async_copy(codes_hbm, codes, sems.at[1]),
        pltpu.make_async_copy(queries_hbm, queries, sems.at[2]),
        pltpu.make_async_copy(weight_hbm.at[0 : early.shape[0]], early, sems.at[3]),
    ]
    for copy in copies:
        copy.start()
    copies[0].wait()
    copies[1].wait()
    eye = lax.broadcasted_iota(jnp.int32, (rows, rows), 0) == lax.broadcasted_iota(jnp.int32, (rows, rows), 1)
    eye = eye.astype(jnp.float32).astype(jnp.bfloat16)
    for kind in range(kinds - 1):
        scales = jnp.left_shift(1, exponents[:, kind, :] + 16).astype(jnp.float32) * (2.0**-16)
        scales = lax.dot_general(eye, scales.astype(jnp.bfloat16), NT, preferred_element_type=jnp.float32)
        for head in range(groups * per):
            inside = slice((head % per) * HD, (head % per + 1) * HD)
            whole = slice(head * HD, (head + 1) * HD)
            decoded = codes[kind, :, whole].astype(jnp.float32) * scales[:, head : head + 1]
            held[head // per, kind, :, inside] = decoded.astype(jnp.bfloat16)
    copies[2].wait()
    for target in range(groups):
        held[target, kinds - 1] = queries[:, target * width : (target + 1) * width]
    for turn in range(groups):
        target = jnp.bitwise_xor(group, turn)
        outs[turn][...] = held[target, 0 : kinds - 1]
        outs[groups + turn][...] = held[target, kinds - 1]
    copies[3].wait()


def pack(groups, queries, codes, exponents, weight, cut):
    rows, width = queries.shape
    kinds = codes.shape[0]
    share = width // groups
    bf16 = jnp.bfloat16
    exponents = exponents.transpose(2, 0, 1)
    outs = pl.pallas_call(
        pack_kernel,
        out_shape=[jax.ShapeDtypeStruct((kinds, rows, share), bf16)] * groups
        + [jax.ShapeDtypeStruct((rows, share), bf16)] * groups
        + [jax.ShapeDtypeStruct((cut, weight.shape[1]), bf16)],
        in_specs=[HBM] * 4,
        out_specs=[VMEM] * (2 * groups + 1),
        scratch_shapes=[
            pltpu.VMEM(codes.shape, jnp.int32),
            pltpu.VMEM(queries.shape, bf16),
            pltpu.VMEM(exponents.shape, jnp.int32),
            pltpu.VMEM((groups, kinds + 1, rows, share), bf16),
            pltpu.SemaphoreType.DMA((4,)),
        ],
        compiler_params=pltpu.CompilerParams(vmem_limit_bytes=PACK_LIMIT),
        cost_estimate=pl.CostEstimate(flops=2 * codes.size, bytes_accessed=6 * codes.size, transcendentals=0),
    )(queries, codes, exponents, weight)
    return outs[:groups], outs[groups : 2 * groups], outs[-1]


def pick_kernel(text_hbm, stale_hbm, text, stale, sems):
    group, _ = place()
    width = text.shape[2]
    columns = pl.ds(aligned(group, width), width)
    text_copy = pltpu.make_async_copy(text_hbm.at[:, :, columns], text, sems.at[0])
    stale_copy = pltpu.make_async_copy(stale_hbm.at[:, :, columns], stale, sems.at[1])
    text_copy.start()
    stale_copy.start()
    text_copy.wait()
    stale_copy.wait()


def pick(groups, text_kv, stale_kv):
    shapes = [(2, value.shape[1], value.shape[2] // groups) for value in (text_kv, stale_kv)]
    return pl.pallas_call(
        pick_kernel,
        out_shape=[jax.ShapeDtypeStruct(shape, jnp.bfloat16) for shape in shapes],
        in_specs=[HBM] * 2,
        out_specs=[VMEM] * 2,
        scratch_shapes=[pltpu.SemaphoreType.DMA((2,))],
        compiler_params=pltpu.CompilerParams(vmem_limit_bytes=PICK_LIMIT),
        cost_estimate=pl.CostEstimate(flops=0, bytes_accessed=8 << 20, transcendentals=0),
    )(text_kv, stale_kv)


def merge_kernel(*refs):
    for index, ref in enumerate(refs[:-1]):
        refs[-1][index] = ref[...]


def merge(parts):
    return pl.pallas_call(
        merge_kernel,
        out_shape=jax.ShapeDtypeStruct((len(parts), *parts[0].shape), parts[0].dtype),
        in_specs=[VMEM] * len(parts),
        out_specs=VMEM,
        compiler_params=pltpu.CompilerParams(vmem_limit_bytes=SMALL),
        cost_estimate=pl.CostEstimate(flops=0, bytes_accessed=4 * len(parts) * parts[0].size, transcendentals=0),
    )(*parts)


def head_output(query, text, stale, residual, cols):
    text_scores = lax.dot_general(query, text[0, :, cols], NT, preferred_element_type=jnp.float32)
    image_scores = lax.dot_general(query, stale[0, :, cols], NT, preferred_element_type=jnp.float32)
    image_scores += lax.dot_general(query, residual[0, :, cols], NT, preferred_element_type=jnp.float32)
    text_scores *= HD**-0.5
    image_scores *= HD**-0.5
    peak = jnp.maximum(jnp.max(text_scores, axis=1, keepdims=True), jnp.max(image_scores, axis=1, keepdims=True))
    text_weights = jnp.exp(text_scores - peak).astype(jnp.bfloat16)
    image_weights = jnp.exp(image_scores - peak).astype(jnp.bfloat16)
    total = jnp.sum(text_weights.astype(jnp.float32), axis=1, keepdims=True)
    total += jnp.sum(image_weights.astype(jnp.float32), axis=1, keepdims=True)
    mixed = jnp.dot(text_weights, text[1, :, cols], preferred_element_type=jnp.float32)
    mixed += jnp.dot(image_weights, stale[1, :, cols], preferred_element_type=jnp.float32)
    mixed += jnp.dot(image_weights, residual[1, :, cols], preferred_element_type=jnp.float32)
    return (mixed / total).astype(jnp.bfloat16)


def attend_kernel(groups, *refs):
    pieces, refs = refs[:SPREAD], refs[SPREAD:]
    asked, (text, stale, out, most, last, query, residual) = refs[:groups], refs[groups:]
    group, spot = place()
    rows, width = asked[0].shape
    for turn in range(groups):
        origin = jnp.bitwise_xor(group, turn)
        position = (groups - turn) % groups
        query[pl.ds(aligned(origin, rows), rows), :] = asked[position][...]
        for twist in range(SPREAD):
            token = origin * SPREAD + jnp.bitwise_xor(spot, twist)
            residual[:, pl.ds(aligned(token, rows), rows), :] = pieces[twist][position]
    for head in range(width // HD):
        cols = slice(head * HD, (head + 1) * HD)
        value = head_output(query[:, cols], text, stale, residual, cols)
        out[:, cols] = value
        if head < width // HD - 1:
            most[:, cols] = value
        else:
            last[...] = value


def attend_cost(heads, tokens, texts, keys):
    return pl.CostEstimate(
        flops=4 * heads * tokens * HD * (texts + 2 * keys),
        bytes_accessed=4 * heads * HD * (texts + 2 * keys),
        transcendentals=heads * tokens * (texts + keys),
    )


def attend(pieces, query_parts, text, stale):
    groups = len(query_parts)
    rows, width = query_parts[0].shape
    tokens = groups * rows
    keys = stale.shape[1]
    texts = text.shape[1]
    heads = width // HD

    return pl.pallas_call(
        functools.partial(attend_kernel, groups),
        out_shape=[jax.ShapeDtypeStruct((tokens, size), jnp.bfloat16) for size in (width, width - HD, HD)],
        in_specs=[VMEM] * (len(pieces) + groups + 2),
        out_specs=[VMEM] * 3,
        scratch_shapes=[pltpu.VMEM((tokens, width), jnp.bfloat16), pltpu.VMEM((2, keys, width), jnp.bfloat16)],
        compiler_params=pltpu.CompilerParams(vmem_limit_bytes=SMALL),
        cost_estimate=attend_cost(heads, tokens, texts, keys),
    )(*pieces, *query_parts, text, stale)


def order_kernel(weight, near, early, late, early_corner, late_corner, out):
    _, spot = place()
    span, cut = weight.shape[0], early.shape[0]
    pieces = [(0, 0, weight), (1, 0, near), (2, 0, early), (2, cut, late), (3, 0, early_corner), (3, cut, late_corner)]
    for twist, skip, piece in pieces:
        start = jnp.bitwise_xor(spot, twist) * span + skip
        out[pl.ds(pl.multiple_of(start, 16), piece.shape[0]), :] = piece[...]


def order(*pieces):
    span, depth = pieces[0].shape
    shape = (SPREAD * span, depth)
    return pl.pallas_call(
        order_kernel,
        out_shape=jax.ShapeDtypeStruct(shape, jnp.bfloat16),
        in_specs=[VMEM] * len(pieces),
        out_specs=VMEM,
        compiler_params=pltpu.CompilerParams(vmem_limit_bytes=SMALL),
        cost_estimate=pl.CostEstimate(flops=0, bytes_accessed=4 * shape[0] * depth, transcendentals=0),
    )(*pieces)


def term_of(part, weight, turn, skip, width):
    group, _ = place()
    start = jnp.bitwise_xor(group, turn) * width + skip
    columns = pl.ds(pl.multiple_of(start, HD), part.shape[1])
    return lax.dot_general(part[...], weight[:, columns], NT, preferred_element_type=jnp.float32)


def begin_kernel(full, beside, across_most, across_last, weight, out):
    width = full.shape[1]
    total = term_of(full, weight, 0, 0, width) + term_of(beside, weight, 1, 0, width)
    total += term_of(across_most, weight, 2, 0, width)
    out[...] = total + term_of(across_last, weight, 2, width - HD, width)


def begin(parts, weight):
    tokens = parts[0].shape[0]
    columns, depth = weight.shape
    return pl.pallas_call(
        begin_kernel,
        out_shape=jax.ShapeDtypeStruct((tokens, columns), jnp.float32),
        in_specs=[VMEM] * (len(parts) + 1),
        out_specs=VMEM,
        compiler_params=pltpu.CompilerParams(vmem_limit_bytes=SMALL),
        cost_estimate=pl.CostEstimate(
            flops=2 * tokens * columns * depth, bytes_accessed=4 * tokens * columns, transcendentals=0
        ),
    )(*parts, weight)


def close_kernel(partial, most, last, weight, *rest):
    outs, total = rest[:-1], rest[-1]
    group, _ = place()
    rows = outs[0].shape[0]
    width = most.shape[1] + last.shape[1]
    added = partial[...] + term_of(most, weight, 3, 0, width) + term_of(last, weight, 3, width - HD, width)
    total[...] = added.astype(jnp.bfloat16)
    for turn, out in enumerate(outs):
        out[...] = total[pl.ds(aligned(jnp.bitwise_xor(group, turn), rows), rows), :]


def close(groups, partial, parts, weight):
    tokens, columns = partial.shape
    return pl.pallas_call(
        close_kernel,
        out_shape=[jax.ShapeDtypeStruct((tokens // groups, columns), jnp.bfloat16)] * groups,
        in_specs=[VMEM] * 4,
        out_specs=[VMEM] * groups,
        scratch_shapes=[pltpu.VMEM((tokens, columns), jnp.bfloat16)],
        compiler_params=pltpu.CompilerParams(vmem_limit_bytes=SMALL),
        cost_estimate=pl.CostEstimate(
            flops=tokens * weight.size, bytes_accessed=8 * tokens * columns, transcendentals=0
        ),
    )(partial, *parts, weight)


def divide_kernel(*refs):
    parts, (keep, send, held) = refs[:-3], refs[-3:]
    group, _ = place()
    half = lax.axis_index("head")
    blocks = keep.shape[0]
    for position, part in enumerate(parts):
        held[jnp.bitwise_xor(group, (len(parts) - position) % len(parts))] = part[...]
    for block in range(blocks):
        keep[block] = held[half * blocks + block]
        send[block] = held[(1 - half) * blocks + block]


def divide(parts):
    groups = len(parts)
    shape = jax.ShapeDtypeStruct((groups // 2, *parts[0].shape), jnp.bfloat16)
    return pl.pallas_call(
        divide_kernel,
        out_shape=[shape] * 2,
        in_specs=[VMEM] * groups,
        out_specs=[VMEM] * 2,
        scratch_shapes=[pltpu.VMEM((groups, *parts[0].shape), jnp.bfloat16)],
        compiler_params=pltpu.CompilerParams(vmem_limit_bytes=SMALL),
        cost_estimate=pl.CostEstimate(flops=0, bytes_accessed=4 * groups * parts[0].size, transcendentals=0),
    )(*parts)


def finish_kernel(kept, arrived, bias, gate, out):
    blocks, _, columns = kept.shape
    for block in range(blocks):
        cols = slice(block * columns, (block + 1) * columns)
        total = kept[block].astype(jnp.float32) + arrived[block].astype(jnp.float32)
        out[:, cols] = (gate[:, cols] * (total + bias[:, cols])).astype(jnp.bfloat16)


def finish(kept, arrived, bias, gate):
    blocks, rows, columns = kept.shape
    width = blocks * columns
    return pl.pallas_call(
        finish_kernel,
        out_shape=jax.ShapeDtypeStruct((rows, width), jnp.bfloat16),
        in_specs=[VMEM] * 4,
        out_specs=VMEM,
        compiler_params=pltpu.CompilerParams(vmem_limit_bytes=SMALL),
        cost_estimate=pl.CostEstimate(flops=3 * rows * width, bytes_accessed=4 * rows * width, transcendentals=0),
    )(kept, arrived, bias.reshape(1, width), gate.reshape(1, width))


def after(value, *others):
    return lax.optimization_barrier((value, *others))[0]


def grouped_body(queries, stale_kv, codes, exponents, text_kv, out_weight, out_bias, out_gate):
    groups = lax.axis_size("patch") // SPREAD
    size = groups * SPREAD

    def swap(value, twist):
        return lax.ppermute(value, "patch", [(p, p ^ twist) for p in range(size)])

    def along(values):
        return [swap(values[turn], turn * SPREAD) for turn in reversed(range(1, groups))]

    weight = out_weight.T
    cut = weight.shape[0] // 48 * 32
    residuals, queries, early = pack(groups, queries, codes, exponents, weight, cut)
    text, stale = pick(groups, text_kv, stale_kv)

    own = merge([residuals[0], *along(residuals)])
    early = swap(early, 2)

    own = after(own, text, stale, early)
    queries = lax.optimization_barrier((*queries, own))[:groups]
    far, near = swap(own, 2), swap(own, 1)
    asked = [queries[0], *along(queries)]

    far, early = lax.optimization_barrier((far, early, near, *asked))[:2]
    corner, early_corner = swap(far, 1), swap(early, 1)
    weight = after(weight, corner, early_corner)
    weight_near, late, late_corner = swap(weight, 1), swap(weight[cut:], 2), swap(weight[cut:], 3)
    full, most, last = attend([own, near, far, corner], asked, text, stale)

    across_most, across_last = swap(most, 2 * SPREAD), swap(after(last, weight_near), 2 * SPREAD)
    beside = swap(full, SPREAD)
    final_most = swap(across_most, SPREAD)
    final_last = swap(after(across_last, beside, late, late_corner), SPREAD)
    weight = order(weight, weight_near, early, late, early_corner, late_corner)
    partial = begin([full, beside, across_most, across_last], weight)
    terms = close(groups, partial, [final_most, final_last], weight)

    kept, sent = divide([terms[0], *along(terms)])
    received = lax.ppermute(sent, "head", [(0, 1), (1, 0)])
    return finish(kept, received, out_bias, out_gate)


def solution(mesh):
    patches, halves = mesh.shape["patch"], mesh.shape["head"]
    placed = (
        P("patch", "head"),
        P(None, None, "head"),
        P(None, "patch", "head"),
        P(None, "patch", "head"),
        P(None, None, "head"),
        P("head", "patch"),
        P("head"),
        P("head"),
    )

    def body(*args):
        heads = args[0].shape[1] // HD
        groups = patches // SPREAD
        if groups != 4 or patches % SPREAD or heads % groups or halves != 2:
            return plain_body(*args)
        return grouped_body(*args)

    return jax.shard_map(body, mesh=mesh, in_specs=placed, out_specs=P("patch", "head"), check_vma=False)
```

```python
import functools

import jax
import jax.numpy as jnp
from jax import lax
from jax.experimental import pallas as pl
from jax.experimental.pallas import tpu as pltpu
from jax.sharding import PartitionSpec as P

HD = 128
SPREAD = 4
PACK_LIMIT = 56 << 20
SMALL = 16 << 20
PICK_LIMIT = 50 << 20
VMEM = pl.BlockSpec(memory_space=pltpu.VMEM)
HBM = pl.BlockSpec(memory_space=pltpu.HBM)
NT = (((1,), (1,)), ((), ()))


def plain_body(queries, stale_kv, codes, exponents, text_kv, out_weight, out_bias, out_gate):
    tok_rows = queries.shape[0]
    row_width = queries.shape[1]
    head_count = row_width // HD
    text_count = text_kv.shape[1]
    scale_factor = HD ** (-0.5)
    blocks = jnp.exp2(exponents.astype(jnp.float32))
    decoded = codes.astype(jnp.float32).reshape(2, tok_rows, head_count, HD) * blocks[..., None]
    decoded = decoded.astype(jnp.bfloat16).reshape(2, tok_rows, row_width)
    arrived = lax.all_gather(decoded, "patch", axis=1, tiled=True)
    all_rows = arrived.shape[1]
    query_heads = queries.reshape(tok_rows, head_count, HD)
    text_heads = text_kv.reshape(2, text_count, head_count, HD)
    stale_heads = stale_kv.reshape(2, all_rows, head_count, HD)
    arrived_heads = arrived.reshape(2, all_rows, head_count, HD)
    text_scores = jnp.einsum("thd,khd->htk", query_heads, text_heads[0], preferred_element_type=jnp.float32)
    rebuilt = stale_heads.astype(jnp.float32) + arrived_heads.astype(jnp.float32)
    image_scores = jnp.einsum(
        "thd,khd->htk", query_heads.astype(jnp.float32), rebuilt[0], precision=lax.Precision.HIGHEST
    )
    scores = jnp.concatenate([text_scores, image_scores], axis=2) * scale_factor
    row_peak = jnp.max(scores, axis=2, keepdims=True)
    weights = jnp.exp(scores - row_peak).astype(jnp.bfloat16)
    row_total = jnp.sum(weights.astype(jnp.float32), axis=2)
    text_part = jnp.einsum(
        "htk,khd->thd", weights[:, :, :text_count], text_heads[1], preferred_element_type=jnp.float32
    )
    image_part = jnp.einsum(
        "htk,khd->thd",
        weights[:, :, text_count:].astype(jnp.float32),
        rebuilt[1],
        precision=lax.Precision.HIGHEST,
    )
    attended = ((text_part + image_part) / row_total.T[:, :, None]).astype(jnp.bfloat16).reshape(tok_rows, row_width)
    partial_terms = jnp.dot(
        attended, lax.all_gather(out_weight, "patch", axis=1, tiled=True), preferred_element_type=jnp.float32
    )
    column_share = lax.psum_scatter(partial_terms, "head", scatter_dimension=1, tiled=True)
    return (out_gate * (column_share + out_bias)).astype(jnp.bfloat16)


def aligned(value, step):
    return pl.multiple_of(value * step, step)


def place():
    me = lax.axis_index("patch")
    return me // SPREAD, lax.rem(me, SPREAD)


def pack_kernel(queries_hbm, codes_hbm, exponents_hbm, weight_hbm, *rest):
    outs, early, (codes, queries, exponents, held, sems) = rest[:-6], rest[-6], rest[-5:]
    groups, kinds, rows, width = held.shape
    group, _ = place()
    per = width // HD
    copies = [
        pltpu.make_async_copy(exponents_hbm, exponents, sems.at[0]),
        pltpu.make_async_copy(codes_hbm, codes, sems.at[1]),
        pltpu.make_async_copy(queries_hbm, queries, sems.at[2]),
        pltpu.make_async_copy(weight_hbm.at[0 : early.shape[0]], early, sems.at[3]),
    ]
    for copy in copies:
        copy.start()
    copies[0].wait()
    copies[1].wait()
    eye = lax.broadcasted_iota(jnp.int32, (rows, rows), 0) == lax.broadcasted_iota(jnp.int32, (rows, rows), 1)
    eye = eye.astype(jnp.float32).astype(jnp.bfloat16)
    for kind in range(kinds - 1):
        scales = jnp.left_shift(1, exponents[:, kind, :] + 16).astype(jnp.float32) * (2.0**-16)
        scales = lax.dot_general(eye, scales.astype(jnp.bfloat16), NT, preferred_element_type=jnp.float32)
        for head in range(groups * per):
            inside = slice((head % per) * HD, (head % per + 1) * HD)
            whole = slice(head * HD, (head + 1) * HD)
            decoded = codes[kind, :, whole].astype(jnp.float32) * scales[:, head : head + 1]
            held[head // per, kind, :, inside] = decoded.astype(jnp.bfloat16)
    copies[2].wait()
    for target in range(groups):
        held[target, kinds - 1] = queries[:, target * width : (target + 1) * width]
    for turn in range(groups):
        target = jnp.bitwise_xor(group, turn)
        if turn == 1:
            outs[turn][...] = held[target]
        else:
            outs[turn][...] = held[target, 0 : kinds - 1]
            outs[groups + max(turn - 1, 0)][...] = held[target, kinds - 1]
    copies[3].wait()


def pack(groups, queries, codes, exponents, weight, cut):
    rows, width = queries.shape
    kinds = codes.shape[0]
    share = width // groups
    bf16 = jnp.bfloat16
    exponents = exponents.transpose(2, 0, 1)
    residual, query = (kinds, rows, share), (rows, share)
    shapes = [residual, (kinds + 1, rows, share)] + [residual] * (groups - 2) + [query] * (groups - 1) + [(cut, weight.shape[1])]
    outs = pl.pallas_call(
        pack_kernel,
        out_shape=[jax.ShapeDtypeStruct(shape, bf16) for shape in shapes],
        in_specs=[HBM] * 4,
        out_specs=[VMEM] * len(shapes),
        scratch_shapes=[
            pltpu.VMEM(codes.shape, jnp.int32),
            pltpu.VMEM(queries.shape, bf16),
            pltpu.VMEM(exponents.shape, jnp.int32),
            pltpu.VMEM((groups, kinds + 1, rows, share), bf16),
            pltpu.SemaphoreType.DMA((4,)),
        ],
        compiler_params=pltpu.CompilerParams(vmem_limit_bytes=PACK_LIMIT),
        cost_estimate=pl.CostEstimate(flops=2 * codes.size, bytes_accessed=6 * codes.size, transcendentals=0),
    )(queries, codes, exponents, weight)
    return outs[:groups], outs[groups:-1], outs[-1]


def pick_kernel(text_hbm, stale_hbm, text, stale, sems):
    group, _ = place()
    width = text.shape[2]
    columns = pl.ds(aligned(group, width), width)
    text_copy = pltpu.make_async_copy(text_hbm.at[:, :, columns], text, sems.at[0])
    stale_copy = pltpu.make_async_copy(stale_hbm.at[:, :, columns], stale, sems.at[1])
    text_copy.start()
    stale_copy.start()
    text_copy.wait()
    stale_copy.wait()


def pick(groups, text_kv, stale_kv):
    shapes = [(2, value.shape[1], value.shape[2] // groups) for value in (text_kv, stale_kv)]
    return pl.pallas_call(
        pick_kernel,
        out_shape=[jax.ShapeDtypeStruct(shape, jnp.bfloat16) for shape in shapes],
        in_specs=[HBM] * 2,
        out_specs=[VMEM] * 2,
        scratch_shapes=[pltpu.SemaphoreType.DMA((2,))],
        compiler_params=pltpu.CompilerParams(vmem_limit_bytes=PICK_LIMIT),
        cost_estimate=pl.CostEstimate(flops=0, bytes_accessed=8 << 20, transcendentals=0),
    )(text_kv, stale_kv)


def merge_kernel(*refs):
    parts, (out, query) = refs[:-2], refs[-2:]
    kinds = out.shape[1]
    for index, part in enumerate(parts):
        out[index] = part[0:kinds]
    query[...] = parts[-1][kinds]


def merge(parts):
    kinds, *block = parts[0].shape
    return pl.pallas_call(
        merge_kernel,
        out_shape=[
            jax.ShapeDtypeStruct((len(parts), kinds, *block), parts[0].dtype),
            jax.ShapeDtypeStruct(tuple(block), parts[0].dtype),
        ],
        in_specs=[VMEM] * len(parts),
        out_specs=[VMEM] * 2,
        compiler_params=pltpu.CompilerParams(vmem_limit_bytes=SMALL),
        cost_estimate=pl.CostEstimate(flops=0, bytes_accessed=4 * len(parts) * parts[0].size, transcendentals=0),
    )(*parts)


def head_output(query, text, stale, residual, cols):
    text_scores = lax.dot_general(query, text[0, :, cols], NT, preferred_element_type=jnp.float32)
    image_scores = lax.dot_general(query, stale[0, :, cols], NT, preferred_element_type=jnp.float32)
    image_scores += lax.dot_general(query, residual[0, :, cols], NT, preferred_element_type=jnp.float32)
    text_scores *= HD**-0.5
    image_scores *= HD**-0.5
    peak = jnp.maximum(jnp.max(text_scores, axis=1, keepdims=True), jnp.max(image_scores, axis=1, keepdims=True))
    text_weights = jnp.exp(text_scores - peak).astype(jnp.bfloat16)
    image_weights = jnp.exp(image_scores - peak).astype(jnp.bfloat16)
    total = jnp.sum(text_weights.astype(jnp.float32), axis=1, keepdims=True)
    total += jnp.sum(image_weights.astype(jnp.float32), axis=1, keepdims=True)
    mixed = jnp.dot(text_weights, text[1, :, cols], preferred_element_type=jnp.float32)
    mixed += jnp.dot(image_weights, stale[1, :, cols], preferred_element_type=jnp.float32)
    mixed += jnp.dot(image_weights, residual[1, :, cols], preferred_element_type=jnp.float32)
    return (mixed / total).astype(jnp.bfloat16)


def attend_kernel(groups, *refs):
    pieces, refs = refs[:SPREAD], refs[SPREAD:]
    asked, (text, stale, out, most, last, query, residual) = refs[:groups], refs[groups:]
    group, spot = place()
    rows, width = asked[0].shape
    for turn in range(groups):
        origin = jnp.bitwise_xor(group, turn)
        position = (groups - turn) % groups
        query[pl.ds(aligned(origin, rows), rows), :] = asked[position][...]
        for twist in range(SPREAD):
            token = origin * SPREAD + jnp.bitwise_xor(spot, twist)
            residual[:, pl.ds(aligned(token, rows), rows), :] = pieces[twist][position]
    for head in range(width // HD):
        cols = slice(head * HD, (head + 1) * HD)
        value = head_output(query[:, cols], text, stale, residual, cols)
        out[:, cols] = value
        if head < width // HD - 1:
            most[:, cols] = value
        else:
            last[...] = value


def attend_cost(heads, tokens, texts, keys):
    return pl.CostEstimate(
        flops=4 * heads * tokens * HD * (texts + 2 * keys),
        bytes_accessed=4 * heads * HD * (texts + 2 * keys),
        transcendentals=heads * tokens * (texts + keys),
    )


def attend(pieces, query_parts, text, stale):
    groups = len(query_parts)
    rows, width = query_parts[0].shape
    tokens = groups * rows
    keys = stale.shape[1]
    texts = text.shape[1]
    heads = width // HD

    return pl.pallas_call(
        functools.partial(attend_kernel, groups),
        out_shape=[jax.ShapeDtypeStruct((tokens, size), jnp.bfloat16) for size in (width, width - HD, HD)],
        in_specs=[VMEM] * (len(pieces) + groups + 2),
        out_specs=[VMEM] * 3,
        scratch_shapes=[pltpu.VMEM((tokens, width), jnp.bfloat16), pltpu.VMEM((2, keys, width), jnp.bfloat16)],
        compiler_params=pltpu.CompilerParams(vmem_limit_bytes=SMALL),
        cost_estimate=attend_cost(heads, tokens, texts, keys),
    )(*pieces, *query_parts, text, stale)


def order_kernel(weight, near, early, late, early_corner, late_corner, out):
    _, spot = place()
    span, cut = weight.shape[0], early.shape[0]
    pieces = [(0, 0, weight), (1, 0, near), (2, 0, early), (2, cut, late), (3, 0, early_corner), (3, cut, late_corner)]
    for twist, skip, piece in pieces:
        start = jnp.bitwise_xor(spot, twist) * span + skip
        out[pl.ds(pl.multiple_of(start, 16), piece.shape[0]), :] = piece[...]


def order(*pieces):
    span, depth = pieces[0].shape
    shape = (SPREAD * span, depth)
    return pl.pallas_call(
        order_kernel,
        out_shape=jax.ShapeDtypeStruct(shape, jnp.bfloat16),
        in_specs=[VMEM] * len(pieces),
        out_specs=VMEM,
        compiler_params=pltpu.CompilerParams(vmem_limit_bytes=SMALL),
        cost_estimate=pl.CostEstimate(flops=0, bytes_accessed=4 * shape[0] * depth, transcendentals=0),
    )(*pieces)


def term_of(part, weight, turn, skip, width):
    group, _ = place()
    start = jnp.bitwise_xor(group, turn) * width + skip
    columns = pl.ds(pl.multiple_of(start, HD), part.shape[1])
    return lax.dot_general(part[...], weight[:, columns], NT, preferred_element_type=jnp.float32)


def begin_kernel(full, beside, across_most, across_last, weight, out):
    width = full.shape[1]
    total = term_of(full, weight, 0, 0, width) + term_of(beside, weight, 1, 0, width)
    total += term_of(across_most, weight, 2, 0, width)
    out[...] = total + term_of(across_last, weight, 2, width - HD, width)


def begin(parts, weight):
    tokens = parts[0].shape[0]
    columns, depth = weight.shape
    return pl.pallas_call(
        begin_kernel,
        out_shape=jax.ShapeDtypeStruct((tokens, columns), jnp.float32),
        in_specs=[VMEM] * (len(parts) + 1),
        out_specs=VMEM,
        compiler_params=pltpu.CompilerParams(vmem_limit_bytes=SMALL),
        cost_estimate=pl.CostEstimate(
            flops=2 * tokens * columns * depth, bytes_accessed=4 * tokens * columns, transcendentals=0
        ),
    )(*parts, weight)


def close_kernel(partial, most, last, weight, *rest):
    outs, total = rest[:-1], rest[-1]
    group, _ = place()
    rows = outs[0].shape[0]
    width = most.shape[1] + last.shape[1]
    added = partial[...] + term_of(most, weight, 3, 0, width) + term_of(last, weight, 3, width - HD, width)
    total[...] = added.astype(jnp.bfloat16)
    for turn, out in enumerate(outs):
        out[...] = total[pl.ds(aligned(jnp.bitwise_xor(group, turn), rows), rows), :]


def close(groups, partial, parts, weight):
    tokens, columns = partial.shape
    return pl.pallas_call(
        close_kernel,
        out_shape=[jax.ShapeDtypeStruct((tokens // groups, columns), jnp.bfloat16)] * groups,
        in_specs=[VMEM] * 4,
        out_specs=[VMEM] * groups,
        scratch_shapes=[pltpu.VMEM((tokens, columns), jnp.bfloat16)],
        compiler_params=pltpu.CompilerParams(vmem_limit_bytes=SMALL),
        cost_estimate=pl.CostEstimate(
            flops=tokens * weight.size, bytes_accessed=8 * tokens * columns, transcendentals=0
        ),
    )(partial, *parts, weight)


def divide_kernel(*refs):
    parts, (keep, send, held) = refs[:-3], refs[-3:]
    group, _ = place()
    half = lax.axis_index("head")
    blocks = keep.shape[0]
    for position, part in enumerate(parts):
        held[jnp.bitwise_xor(group, (len(parts) - position) % len(parts))] = part[...]
    for block in range(blocks):
        keep[block] = held[half * blocks + block]
        send[block] = held[(1 - half) * blocks + block]


def divide(parts):
    groups = len(parts)
    shape = jax.ShapeDtypeStruct((groups // 2, *parts[0].shape), jnp.bfloat16)
    return pl.pallas_call(
        divide_kernel,
        out_shape=[shape] * 2,
        in_specs=[VMEM] * groups,
        out_specs=[VMEM] * 2,
        scratch_shapes=[pltpu.VMEM((groups, *parts[0].shape), jnp.bfloat16)],
        compiler_params=pltpu.CompilerParams(vmem_limit_bytes=SMALL),
        cost_estimate=pl.CostEstimate(flops=0, bytes_accessed=4 * groups * parts[0].size, transcendentals=0),
    )(*parts)


def finish_kernel(kept, arrived, bias, gate, out):
    blocks, _, columns = kept.shape
    for block in range(blocks):
        cols = slice(block * columns, (block + 1) * columns)
        total = kept[block].astype(jnp.float32) + arrived[block].astype(jnp.float32)
        out[:, cols] = (gate[:, cols] * (total + bias[:, cols])).astype(jnp.bfloat16)


def finish(kept, arrived, bias, gate):
    blocks, rows, columns = kept.shape
    width = blocks * columns
    return pl.pallas_call(
        finish_kernel,
        out_shape=jax.ShapeDtypeStruct((rows, width), jnp.bfloat16),
        in_specs=[VMEM] * 4,
        out_specs=VMEM,
        compiler_params=pltpu.CompilerParams(vmem_limit_bytes=SMALL),
        cost_estimate=pl.CostEstimate(flops=3 * rows * width, bytes_accessed=4 * rows * width, transcendentals=0),
    )(kept, arrived, bias.reshape(1, width), gate.reshape(1, width))


def after(value, *others):
    return lax.optimization_barrier((value, *others))[0]


def grouped_body(queries, stale_kv, codes, exponents, text_kv, out_weight, out_bias, out_gate):
    groups = lax.axis_size("patch") // SPREAD
    size = groups * SPREAD

    def swap(value, twist):
        return lax.ppermute(value, "patch", [(p, p ^ twist) for p in range(size)])

    def along(values):
        return [swap(values[turn], turn * SPREAD) for turn in reversed(range(1, groups))]

    weight = out_weight.T
    cut = weight.shape[0] // 2
    residuals, (asked_own, *asked_far), early = pack(groups, queries, codes, exponents, weight, cut)
    text, stale = pick(groups, text_kv, stale_kv)
    weight = after(weight, residuals[0])

    own, asked_near = merge([residuals[0], *along(residuals)])
    early, weight_near = swap(early, 2), swap(weight, 1)

    own, early = lax.optimization_barrier((own, early, weight_near, text, stale))[:2]
    asked_far = lax.optimization_barrier((*asked_far, own))[:-1]
    far, near, early_corner = swap(own, 2), swap(own, 1), swap(early, 1)
    asked_far = [swap(value, turn * SPREAD) for turn, value in reversed(list(enumerate(asked_far, 2)))]

    far, weight = lax.optimization_barrier((far, weight, near, early_corner, *asked_far))[:2]
    corner, late, late_corner = swap(far, 1), swap(weight[cut:], 2), swap(weight[cut:], 3)
    asked = [asked_own, *asked_far, asked_near]
    full, most, last = attend([own, near, far, corner], asked, text, stale)

    across_most, across_last = swap(most, 2 * SPREAD), swap(last, 2 * SPREAD)
    beside = swap(full, SPREAD)
    final_most = swap(across_most, SPREAD)
    final_last = swap(after(across_last, beside, late, late_corner), SPREAD)
    weight = order(weight, weight_near, early, late, early_corner, late_corner)
    partial = begin([full, beside, across_most, across_last], weight)
    terms = close(groups, partial, [final_most, final_last], weight)

    kept, sent = divide([terms[0], *along(terms)])
    received = lax.ppermute(sent, "head", [(0, 1), (1, 0)])
    return finish(kept, received, out_bias, out_gate)


def solution(mesh):
    patches, halves = mesh.shape["patch"], mesh.shape["head"]
    placed = (
        P("patch", "head"),
        P(None, None, "head"),
        P(None, "patch", "head"),
        P(None, "patch", "head"),
        P(None, None, "head"),
        P("head", "patch"),
        P("head"),
        P("head"),
    )

    def body(*args):
        heads = args[0].shape[1] // HD
        groups = patches // SPREAD
        if groups != 4 or patches % SPREAD or heads % groups or halves != 2:
            return plain_body(*args)
        return grouped_body(*args)

    return jax.shard_map(body, mesh=mesh, in_specs=placed, out_specs=P("patch", "head"), check_vma=False)
```

```python
import functools

import jax
import jax.numpy as jnp
from jax import lax
from jax.experimental import pallas as pl
from jax.experimental.pallas import tpu as pltpu
from jax.sharding import PartitionSpec as P

HD = 128
SPREAD = 4
PACK_LIMIT = 56 << 20
SMALL = 16 << 20
PICK_LIMIT = 50 << 20
VMEM = pl.BlockSpec(memory_space=pltpu.VMEM)
HBM = pl.BlockSpec(memory_space=pltpu.HBM)
NT = (((1,), (1,)), ((), ()))


def plain_body(queries, stale_kv, codes, exponents, text_kv, out_weight, out_bias, out_gate):
    tok_rows = queries.shape[0]
    row_width = queries.shape[1]
    head_count = row_width // HD
    text_count = text_kv.shape[1]
    scale_factor = HD ** (-0.5)
    blocks = jnp.exp2(exponents.astype(jnp.float32))
    decoded = codes.astype(jnp.float32).reshape(2, tok_rows, head_count, HD) * blocks[..., None]
    decoded = decoded.astype(jnp.bfloat16).reshape(2, tok_rows, row_width)
    arrived = lax.all_gather(decoded, "patch", axis=1, tiled=True)
    all_rows = arrived.shape[1]
    query_heads = queries.reshape(tok_rows, head_count, HD)
    text_heads = text_kv.reshape(2, text_count, head_count, HD)
    stale_heads = stale_kv.reshape(2, all_rows, head_count, HD)
    arrived_heads = arrived.reshape(2, all_rows, head_count, HD)
    text_scores = jnp.einsum("thd,khd->htk", query_heads, text_heads[0], preferred_element_type=jnp.float32)
    rebuilt = stale_heads.astype(jnp.float32) + arrived_heads.astype(jnp.float32)
    image_scores = jnp.einsum(
        "thd,khd->htk", query_heads.astype(jnp.float32), rebuilt[0], precision=lax.Precision.HIGHEST
    )
    scores = jnp.concatenate([text_scores, image_scores], axis=2) * scale_factor
    row_peak = jnp.max(scores, axis=2, keepdims=True)
    weights = jnp.exp(scores - row_peak).astype(jnp.bfloat16)
    row_total = jnp.sum(weights.astype(jnp.float32), axis=2)
    text_part = jnp.einsum(
        "htk,khd->thd", weights[:, :, :text_count], text_heads[1], preferred_element_type=jnp.float32
    )
    image_part = jnp.einsum(
        "htk,khd->thd",
        weights[:, :, text_count:].astype(jnp.float32),
        rebuilt[1],
        precision=lax.Precision.HIGHEST,
    )
    attended = ((text_part + image_part) / row_total.T[:, :, None]).astype(jnp.bfloat16).reshape(tok_rows, row_width)
    partial_terms = jnp.dot(
        attended, lax.all_gather(out_weight, "patch", axis=1, tiled=True), preferred_element_type=jnp.float32
    )
    column_share = lax.psum_scatter(partial_terms, "head", scatter_dimension=1, tiled=True)
    return (out_gate * (column_share + out_bias)).astype(jnp.bfloat16)


def aligned(value, step):
    return pl.multiple_of(value * step, step)


def place():
    me = lax.axis_index("patch")
    return me // SPREAD, lax.rem(me, SPREAD)


def pack_kernel(queries_hbm, codes_hbm, exponents_hbm, weight_hbm, *rest):
    outs, early, (codes, queries, exponents, held, sems) = rest[:-6], rest[-6], rest[-5:]
    groups, kinds, rows, width = held.shape
    group, _ = place()
    per = width // HD
    copies = [
        pltpu.make_async_copy(exponents_hbm, exponents, sems.at[0]),
        pltpu.make_async_copy(codes_hbm, codes, sems.at[1]),
        pltpu.make_async_copy(queries_hbm, queries, sems.at[2]),
        pltpu.make_async_copy(weight_hbm.at[0 : early.shape[0]], early, sems.at[3]),
    ]
    for copy in copies:
        copy.start()
    copies[0].wait()
    copies[1].wait()
    eye = lax.broadcasted_iota(jnp.int32, (rows, rows), 0) == lax.broadcasted_iota(jnp.int32, (rows, rows), 1)
    eye = eye.astype(jnp.float32).astype(jnp.bfloat16)
    for kind in range(kinds - 1):
        scales = jnp.left_shift(1, exponents[:, kind, :] + 16).astype(jnp.float32) * (2.0**-16)
        scales = lax.dot_general(eye, scales.astype(jnp.bfloat16), NT, preferred_element_type=jnp.float32)
        for head in range(groups * per):
            inside = slice((head % per) * HD, (head % per + 1) * HD)
            whole = slice(head * HD, (head + 1) * HD)
            decoded = codes[kind, :, whole].astype(jnp.float32) * scales[:, head : head + 1]
            held[head // per, kind, :, inside] = decoded.astype(jnp.bfloat16)
    copies[2].wait()
    for target in range(groups):
        held[target, kinds - 1] = queries[:, target * width : (target + 1) * width]
    for turn in range(groups):
        outs[turn][...] = held[jnp.bitwise_xor(group, turn)]
    outs[groups][...] = held[group, 0 : kinds - 1]
    copies[3].wait()


def pack(groups, queries, codes, exponents, weight, cut):
    rows, width = queries.shape
    kinds = codes.shape[0]
    share = width // groups
    bf16 = jnp.bfloat16
    exponents = exponents.transpose(2, 0, 1)
    shapes = [(kinds + 1, rows, share)] * groups + [(kinds, rows, share), (cut, weight.shape[1])]
    outs = pl.pallas_call(
        pack_kernel,
        out_shape=[jax.ShapeDtypeStruct(shape, bf16) for shape in shapes],
        in_specs=[HBM] * 4,
        out_specs=[VMEM] * len(shapes),
        scratch_shapes=[
            pltpu.VMEM(codes.shape, jnp.int32),
            pltpu.VMEM(queries.shape, bf16),
            pltpu.VMEM(exponents.shape, jnp.int32),
            pltpu.VMEM((groups, kinds + 1, rows, share), bf16),
            pltpu.SemaphoreType.DMA((4,)),
        ],
        compiler_params=pltpu.CompilerParams(vmem_limit_bytes=PACK_LIMIT),
        cost_estimate=pl.CostEstimate(flops=2 * codes.size, bytes_accessed=6 * codes.size, transcendentals=0),
    )(queries, codes, exponents, weight)
    return outs


def pick_kernel(text_hbm, stale_hbm, text, stale, sems):
    group, spot = place()
    width = text.shape[2]
    groups = text_hbm.shape[2] // width
    rows = stale.shape[2] // groups
    columns = pl.ds(aligned(group, width), width)
    copies = [pltpu.make_async_copy(text_hbm.at[:, :, columns], text, sems.at[0])]
    for twist in range(SPREAD):
        for position in range(groups):
            origin = jnp.bitwise_xor(group, (groups - position) % groups)
            token = origin * SPREAD + jnp.bitwise_xor(spot, twist)
            copies.append(
                pltpu.make_async_copy(
                    stale_hbm.at[:, pl.ds(aligned(token, rows), rows), columns],
                    stale.at[twist, :, pl.ds(position * rows, rows), :],
                    sems.at[len(copies)],
                )
            )
    for copy in copies:
        copy.start()
    for copy in copies:
        copy.wait()


def pick(groups, text_kv, stale_kv):
    kinds, texts, heads_width = text_kv.shape
    width = heads_width // groups
    return pl.pallas_call(
        pick_kernel,
        out_shape=[
            jax.ShapeDtypeStruct((kinds, texts, width), jnp.bfloat16),
            jax.ShapeDtypeStruct((SPREAD, kinds, stale_kv.shape[1] // SPREAD, width), jnp.bfloat16),
        ],
        in_specs=[HBM] * 2,
        out_specs=[VMEM] * 2,
        scratch_shapes=[pltpu.SemaphoreType.DMA((1 + SPREAD * groups,))],
        compiler_params=pltpu.CompilerParams(vmem_limit_bytes=PICK_LIMIT),
        cost_estimate=pl.CostEstimate(flops=0, bytes_accessed=8 << 20, transcendentals=0),
    )(text_kv, stale_kv)


def merge_kernel(*refs):
    parts, (every, some, query) = refs[:-3], refs[-3:]
    groups, kinds, rows, _ = every.shape
    group, _ = place()
    for position, part in enumerate(parts):
        every[position] = part[0:kinds]
        if position:
            some[position - 1] = part[0:kinds]
        origin = jnp.bitwise_xor(group, (groups - position) % groups)
        query[pl.ds(aligned(origin, rows), rows), :] = part[kinds]


def merge(parts):
    kinds, rows, width = parts[0].shape
    shapes = [(len(parts), kinds - 1, rows, width), (len(parts) - 1, kinds - 1, rows, width), (len(parts) * rows, width)]
    return pl.pallas_call(
        merge_kernel,
        out_shape=[jax.ShapeDtypeStruct(shape, jnp.bfloat16) for shape in shapes],
        in_specs=[VMEM] * len(parts),
        out_specs=[VMEM] * 3,
        compiler_params=pltpu.CompilerParams(vmem_limit_bytes=SMALL),
        cost_estimate=pl.CostEstimate(flops=0, bytes_accessed=4 * len(parts) * parts[0].size, transcendentals=0),
    )(*parts)


def absorb(query, segments, state):
    scores = []
    for keys, _ in segments:
        score = sum(lax.dot_general(query, key, NT, preferred_element_type=jnp.float32) for key in keys)
        scores.append(score * HD**-0.5)
    peaks = [jnp.max(score, axis=1, keepdims=True) for score in scores]
    if state is not None:
        peaks.append(state[0])
    peak = functools.reduce(jnp.maximum, peaks)
    total = mixed = 0.0
    if state is not None:
        fade = jnp.exp(state[0] - peak)
        total, mixed = state[1] * fade, state[2] * fade
    for score, (_, values) in zip(scores, segments):
        weights = jnp.exp(score - peak).astype(jnp.bfloat16)
        total += jnp.sum(weights.astype(jnp.float32), axis=1, keepdims=True)
        for value in values:
            mixed += jnp.dot(weights, value, preferred_element_type=jnp.float32)
    return peak, total, mixed


def image_segment(stale, twist, residual, cols):
    both = [(stale[twist, kind, :, cols], residual(kind)) for kind in range(2)]
    return both[0], both[1]


def whole_part(part, cols):
    return lambda kind: part[:, kind, :, cols].reshape(-1, HD)


def split_part(own, some, cols):
    return lambda kind: jnp.concatenate([own[kind, :, cols], some[:, kind, :, cols].reshape(-1, HD)], axis=0)


def near_kernel(query, every, text, stale, peak, total, mixed):
    for head in range(mixed.shape[0]):
        cols = slice(head * HD, (head + 1) * HD)
        segments = [
            ((text[0, :, cols],), (text[1, :, cols],)),
            image_segment(stale, 0, whole_part(every, cols), cols),
        ]
        peak[head], total[head], mixed[head] = absorb(query[:, cols], segments, None)


def middle_kernel(query, near, own_far, some_far, stale, peak_in, total_in, mixed_in, peak, total, mixed):
    for head in range(mixed.shape[0]):
        cols = slice(head * HD, (head + 1) * HD)
        segments = [
            image_segment(stale, 1, whole_part(near, cols), cols),
            image_segment(stale, 2, split_part(own_far, some_far, cols), cols),
        ]
        state = peak_in[head], total_in[head], mixed_in[head]
        peak[head], total[head], mixed[head] = absorb(query[:, cols], segments, state)


def last_kernel(query, own_corner, some_corner, stale, peak, total, mixed, full, most, last):
    heads = mixed.shape[0]
    for head in range(heads):
        cols = slice(head * HD, (head + 1) * HD)
        segments = [image_segment(stale, 3, split_part(own_corner, some_corner, cols), cols)]
        state = peak[head], total[head], mixed[head]
        _, sums, mix = absorb(query[:, cols], segments, state)
        value = (mix / sums).astype(jnp.bfloat16)
        full[:, cols] = value
        if head < heads - 1:
            most[:, cols] = value
        else:
            last[...] = value


def attend_call(kernel, operands, shapes, keys):
    tokens, width = operands[0].shape
    return pl.pallas_call(
        kernel,
        out_shape=shapes,
        in_specs=[VMEM] * len(operands),
        out_specs=[VMEM] * len(shapes),
        compiler_params=pltpu.CompilerParams(vmem_limit_bytes=SMALL),
        cost_estimate=pl.CostEstimate(
            flops=8 * tokens * width * keys, bytes_accessed=8 * width * keys, transcendentals=tokens * keys * width // HD
        ),
    )(*operands)


def state_shapes(query):
    tokens, width = query.shape
    heads = width // HD
    return [jax.ShapeDtypeStruct((heads, tokens, size), jnp.float32) for size in (1, 1, HD)]


def result_shapes(query):
    tokens, width = query.shape
    return [jax.ShapeDtypeStruct((tokens, size), jnp.bfloat16) for size in (width, width - HD, HD)]


def order_kernel(weight, near, early, late, early_corner, late_corner, out):
    _, spot = place()
    span, cut = weight.shape[0], early.shape[0]
    pieces = [(0, 0, weight), (1, 0, near), (2, 0, early), (2, cut, late), (3, 0, early_corner), (3, cut, late_corner)]
    for twist, skip, piece in pieces:
        start = jnp.bitwise_xor(spot, twist) * span + skip
        out[pl.ds(pl.multiple_of(start, 16), piece.shape[0]), :] = piece[...]


def order(*pieces):
    span, depth = pieces[0].shape
    shape = (SPREAD * span, depth)
    return pl.pallas_call(
        order_kernel,
        out_shape=jax.ShapeDtypeStruct(shape, jnp.bfloat16),
        in_specs=[VMEM] * len(pieces),
        out_specs=VMEM,
        compiler_params=pltpu.CompilerParams(vmem_limit_bytes=SMALL),
        cost_estimate=pl.CostEstimate(flops=0, bytes_accessed=4 * shape[0] * depth, transcendentals=0),
    )(*pieces)


def term_of(part, weight, turn, skip, width):
    group, _ = place()
    start = jnp.bitwise_xor(group, turn) * width + skip
    columns = pl.ds(pl.multiple_of(start, HD), part.shape[1])
    return lax.dot_general(part[...], weight[:, columns], NT, preferred_element_type=jnp.float32)


def begin_kernel(full, beside, across_most, across_last, weight, out):
    width = full.shape[1]
    total = term_of(full, weight, 0, 0, width) + term_of(beside, weight, 1, 0, width)
    total += term_of(across_most, weight, 2, 0, width)
    out[...] = total + term_of(across_last, weight, 2, width - HD, width)


def begin(parts, weight):
    tokens = parts[0].shape[0]
    columns, depth = weight.shape
    return pl.pallas_call(
        begin_kernel,
        out_shape=jax.ShapeDtypeStruct((tokens, columns), jnp.float32),
        in_specs=[VMEM] * (len(parts) + 1),
        out_specs=VMEM,
        compiler_params=pltpu.CompilerParams(vmem_limit_bytes=SMALL),
        cost_estimate=pl.CostEstimate(
            flops=2 * tokens * columns * depth, bytes_accessed=4 * tokens * columns, transcendentals=0
        ),
    )(*parts, weight)


def close_kernel(partial, most, last, weight, *rest):
    outs, total = rest[:-1], rest[-1]
    group, _ = place()
    rows = outs[0].shape[0]
    width = most.shape[1] + last.shape[1]
    added = partial[...] + term_of(most, weight, 3, 0, width) + term_of(last, weight, 3, width - HD, width)
    total[...] = added.astype(jnp.bfloat16)
    for turn, out in enumerate(outs):
        out[...] = total[pl.ds(aligned(jnp.bitwise_xor(group, turn), rows), rows), :]


def close(groups, partial, parts, weight):
    tokens, columns = partial.shape
    return pl.pallas_call(
        close_kernel,
        out_shape=[jax.ShapeDtypeStruct((tokens // groups, columns), jnp.bfloat16)] * groups,
        in_specs=[VMEM] * 4,
        out_specs=[VMEM] * groups,
        scratch_shapes=[pltpu.VMEM((tokens, columns), jnp.bfloat16)],
        compiler_params=pltpu.CompilerParams(vmem_limit_bytes=SMALL),
        cost_estimate=pl.CostEstimate(
            flops=tokens * weight.size, bytes_accessed=8 * tokens * columns, transcendentals=0
        ),
    )(partial, *parts, weight)


def divide_kernel(*refs):
    parts, (keep, send, held) = refs[:-3], refs[-3:]
    group, _ = place()
    half = lax.axis_index("head")
    blocks = keep.shape[0]
    for position, part in enumerate(parts):
        held[jnp.bitwise_xor(group, (len(parts) - position) % len(parts))] = part[...]
    for block in range(blocks):
        keep[block] = held[half * blocks + block]
        send[block] = held[(1 - half) * blocks + block]


def divide(parts):
    groups = len(parts)
    shape = jax.ShapeDtypeStruct((groups // 2, *parts[0].shape), jnp.bfloat16)
    return pl.pallas_call(
        divide_kernel,
        out_shape=[shape] * 2,
        in_specs=[VMEM] * groups,
        out_specs=[VMEM] * 2,
        scratch_shapes=[pltpu.VMEM((groups, *parts[0].shape), jnp.bfloat16)],
        compiler_params=pltpu.CompilerParams(vmem_limit_bytes=SMALL),
        cost_estimate=pl.CostEstimate(flops=0, bytes_accessed=4 * groups * parts[0].size, transcendentals=0),
    )(*parts)


def finish_kernel(kept, arrived, bias, gate, out):
    blocks, _, columns = kept.shape
    for block in range(blocks):
        cols = slice(block * columns, (block + 1) * columns)
        total = kept[block].astype(jnp.float32) + arrived[block].astype(jnp.float32)
        out[:, cols] = (gate[:, cols] * (total + bias[:, cols])).astype(jnp.bfloat16)


def finish(kept, arrived, bias, gate):
    blocks, rows, columns = kept.shape
    width = blocks * columns
    return pl.pallas_call(
        finish_kernel,
        out_shape=jax.ShapeDtypeStruct((rows, width), jnp.bfloat16),
        in_specs=[VMEM] * 4,
        out_specs=VMEM,
        compiler_params=pltpu.CompilerParams(vmem_limit_bytes=SMALL),
        cost_estimate=pl.CostEstimate(flops=3 * rows * width, bytes_accessed=4 * rows * width, transcendentals=0),
    )(kept, arrived, bias.reshape(1, width), gate.reshape(1, width))


def after(value, *others):
    return lax.optimization_barrier((value, *others))[0]


def grouped_body(queries, stale_kv, codes, exponents, text_kv, out_weight, out_bias, out_gate):
    groups = lax.axis_size("patch") // SPREAD
    size = groups * SPREAD

    def swap(value, twist):
        return lax.ppermute(value, "patch", [(p, p ^ twist) for p in range(size)])

    def along(values):
        return [swap(values[turn], turn * SPREAD) for turn in reversed(range(1, groups))]

    weight = out_weight.T
    cut = weight.shape[0] // 48 * 32
    *packed, own, early = pack(groups, queries, codes, exponents, weight, cut)
    text, stale = pick(groups, text_kv, stale_kv)

    every, some, query = merge([packed[0], *along(packed)])
    own_far, early = swap(own, 2), swap(early, 2)

    every, some, early, query = lax.optimization_barrier((every, some, early, query, own_far, text, stale))[:4]
    some_far, near = swap(some, 2), swap(every, 1)
    weight, early = lax.optimization_barrier((weight, early, near))[:2]
    early_corner, weight_near = swap(early, 1), swap(weight, 1)
    share = stale.shape[2]
    state = attend_call(near_kernel, [query, every, text, stale], state_shapes(query), share + text.shape[1])

    ready = (own_far, some_far, weight, near, early_corner, weight_near, *state)
    own_far, some_far, weight, near = lax.optimization_barrier(ready)[:4]
    own_corner, some_corner = swap(own_far, 1), swap(some_far, 1)
    late, late_corner = swap(weight[cut:], 2), swap(weight[cut:], 3)
    state = attend_call(middle_kernel, [query, near, own_far, some_far, stale, *state], state_shapes(query), 2 * share)
    operands = [query, own_corner, some_corner, stale, *state]
    full, most, last = attend_call(last_kernel, operands, result_shapes(query), share)

    across_most, across_last = swap(most, 2 * SPREAD), swap(last, 2 * SPREAD)
    beside = swap(full, SPREAD)
    final_most = swap(across_most, SPREAD)
    final_last = swap(after(across_last, beside, late, late_corner), SPREAD)
    weight = order(weight, weight_near, early, late, early_corner, late_corner)
    partial = begin([full, beside, across_most, across_last], weight)
    terms = close(groups, partial, [final_most, final_last], weight)

    kept, sent = divide([terms[0], *along(terms)])
    received = lax.ppermute(sent, "head", [(0, 1), (1, 0)])
    return finish(kept, received, out_bias, out_gate)


def solution(mesh):
    patches, halves = mesh.shape["patch"], mesh.shape["head"]
    placed = (
        P("patch", "head"),
        P(None, None, "head"),
        P(None, "patch", "head"),
        P(None, "patch", "head"),
        P(None, None, "head"),
        P("head", "patch"),
        P("head"),
        P("head"),
    )

    def body(*args):
        heads = args[0].shape[1] // HD
        groups = patches // SPREAD
        if groups != 4 or patches % SPREAD or heads % groups or halves != 2:
            return plain_body(*args)
        return grouped_body(*args)

    return jax.shard_map(body, mesh=mesh, in_specs=placed, out_specs=P("patch", "head"), check_vma=False)
```

```python
import functools

import jax
import jax.numpy as jnp
from jax import lax
from jax.experimental import pallas as pl
from jax.experimental.pallas import tpu as pltpu
from jax.sharding import PartitionSpec as P

HD = 128
SPREAD = 4
PACK_LIMIT = 56 << 20
SMALL = 16 << 20
PICK_LIMIT = 50 << 20
VMEM = pl.BlockSpec(memory_space=pltpu.VMEM)
HBM = pl.BlockSpec(memory_space=pltpu.HBM)
NT = (((1,), (1,)), ((), ()))


def plain_body(queries, stale_kv, codes, exponents, text_kv, out_weight, out_bias, out_gate):
    tok_rows = queries.shape[0]
    row_width = queries.shape[1]
    head_count = row_width // HD
    text_count = text_kv.shape[1]
    scale_factor = HD ** (-0.5)
    blocks = jnp.exp2(exponents.astype(jnp.float32))
    decoded = codes.astype(jnp.float32).reshape(2, tok_rows, head_count, HD) * blocks[..., None]
    decoded = decoded.astype(jnp.bfloat16).reshape(2, tok_rows, row_width)
    arrived = lax.all_gather(decoded, "patch", axis=1, tiled=True)
    all_rows = arrived.shape[1]
    query_heads = queries.reshape(tok_rows, head_count, HD)
    text_heads = text_kv.reshape(2, text_count, head_count, HD)
    stale_heads = stale_kv.reshape(2, all_rows, head_count, HD)
    arrived_heads = arrived.reshape(2, all_rows, head_count, HD)
    text_scores = jnp.einsum("thd,khd->htk", query_heads, text_heads[0], preferred_element_type=jnp.float32)
    rebuilt = stale_heads.astype(jnp.float32) + arrived_heads.astype(jnp.float32)
    image_scores = jnp.einsum(
        "thd,khd->htk", query_heads.astype(jnp.float32), rebuilt[0], precision=lax.Precision.HIGHEST
    )
    scores = jnp.concatenate([text_scores, image_scores], axis=2) * scale_factor
    row_peak = jnp.max(scores, axis=2, keepdims=True)
    weights = jnp.exp(scores - row_peak).astype(jnp.bfloat16)
    row_total = jnp.sum(weights.astype(jnp.float32), axis=2)
    text_part = jnp.einsum(
        "htk,khd->thd", weights[:, :, :text_count], text_heads[1], preferred_element_type=jnp.float32
    )
    image_part = jnp.einsum(
        "htk,khd->thd",
        weights[:, :, text_count:].astype(jnp.float32),
        rebuilt[1],
        precision=lax.Precision.HIGHEST,
    )
    attended = ((text_part + image_part) / row_total.T[:, :, None]).astype(jnp.bfloat16).reshape(tok_rows, row_width)
    partial_terms = jnp.dot(
        attended, lax.all_gather(out_weight, "patch", axis=1, tiled=True), preferred_element_type=jnp.float32
    )
    column_share = lax.psum_scatter(partial_terms, "head", scatter_dimension=1, tiled=True)
    return (out_gate * (column_share + out_bias)).astype(jnp.bfloat16)


def aligned(value, step):
    return pl.multiple_of(value * step, step)


def place():
    me = lax.axis_index("patch")
    return me // SPREAD, lax.rem(me, SPREAD)


def pack_kernel(queries_hbm, codes_hbm, exponents_hbm, *rest):
    outs, (codes, queries, exponents, held, sems) = rest[:-5], rest[-5:]
    groups, kinds, rows, width = held.shape
    group, _ = place()
    per = width // HD
    copies = [
        pltpu.make_async_copy(exponents_hbm, exponents, sems.at[0]),
        pltpu.make_async_copy(codes_hbm, codes, sems.at[1]),
        pltpu.make_async_copy(queries_hbm, queries, sems.at[2]),
    ]
    for copy in copies:
        copy.start()
    copies[0].wait()
    copies[1].wait()
    eye = lax.broadcasted_iota(jnp.int32, (rows, rows), 0) == lax.broadcasted_iota(jnp.int32, (rows, rows), 1)
    eye = eye.astype(jnp.float32).astype(jnp.bfloat16)
    for kind in range(kinds - 1):
        scales = jnp.left_shift(1, exponents[:, kind, :] + 16).astype(jnp.float32) * (2.0**-16)
        scales = lax.dot_general(eye, scales.astype(jnp.bfloat16), NT, preferred_element_type=jnp.float32)
        for head in range(groups * per):
            inside = slice((head % per) * HD, (head % per + 1) * HD)
            whole = slice(head * HD, (head + 1) * HD)
            decoded = codes[kind, :, whole].astype(jnp.float32) * scales[:, head : head + 1]
            held[head // per, kind, :, inside] = decoded.astype(jnp.bfloat16)
    copies[2].wait()
    for target in range(groups):
        held[target, kinds - 1] = queries[:, target * width : (target + 1) * width]
    for turn in range(groups):
        outs[turn][...] = held[jnp.bitwise_xor(group, turn)]
    outs[groups][...] = held[group, 0 : kinds - 1]


def pack(groups, queries, codes, exponents):
    rows, width = queries.shape
    kinds = codes.shape[0]
    share = width // groups
    bf16 = jnp.bfloat16
    exponents = exponents.transpose(2, 0, 1)
    shapes = [(kinds + 1, rows, share)] * groups + [(kinds, rows, share)]
    outs = pl.pallas_call(
        pack_kernel,
        out_shape=[jax.ShapeDtypeStruct(shape, bf16) for shape in shapes],
        in_specs=[HBM] * 3,
        out_specs=[VMEM] * len(shapes),
        scratch_shapes=[
            pltpu.VMEM(codes.shape, jnp.int32),
            pltpu.VMEM(queries.shape, bf16),
            pltpu.VMEM(exponents.shape, jnp.int32),
            pltpu.VMEM((groups, kinds + 1, rows, share), bf16),
            pltpu.SemaphoreType.DMA((3,)),
        ],
        compiler_params=pltpu.CompilerParams(vmem_limit_bytes=PACK_LIMIT),
        cost_estimate=pl.CostEstimate(flops=2 * codes.size, bytes_accessed=6 * codes.size, transcendentals=0),
    )(queries, codes, exponents)
    return outs


def pick_kernel(text_hbm, stale_hbm, text, stale, sems):
    group, spot = place()
    width = text.shape[2]
    groups = text_hbm.shape[2] // width
    rows = stale.shape[2] // groups
    columns = pl.ds(aligned(group, width), width)
    copies = [pltpu.make_async_copy(text_hbm.at[:, :, columns], text, sems.at[0])]
    for twist in range(SPREAD):
        for position in range(groups):
            origin = jnp.bitwise_xor(group, (groups - position) % groups)
            token = origin * SPREAD + jnp.bitwise_xor(spot, twist)
            copies.append(
                pltpu.make_async_copy(
                    stale_hbm.at[:, pl.ds(aligned(token, rows), rows), columns],
                    stale.at[twist, :, pl.ds(position * rows, rows), :],
                    sems.at[len(copies)],
                )
            )
    for copy in copies:
        copy.start()
    for copy in copies:
        copy.wait()


def pick(groups, text_kv, stale_kv):
    kinds, texts, heads_width = text_kv.shape
    width = heads_width // groups
    return pl.pallas_call(
        pick_kernel,
        out_shape=[
            jax.ShapeDtypeStruct((kinds, texts, width), jnp.bfloat16),
            jax.ShapeDtypeStruct((SPREAD, kinds, stale_kv.shape[1] // SPREAD, width), jnp.bfloat16),
        ],
        in_specs=[HBM] * 2,
        out_specs=[VMEM] * 2,
        scratch_shapes=[pltpu.SemaphoreType.DMA((1 + SPREAD * groups,))],
        compiler_params=pltpu.CompilerParams(vmem_limit_bytes=PICK_LIMIT),
        cost_estimate=pl.CostEstimate(flops=0, bytes_accessed=8 << 20, transcendentals=0),
    )(text_kv, stale_kv)


def merge_kernel(*refs):
    parts, (every, some, query) = refs[:-3], refs[-3:]
    groups, kinds, rows, _ = every.shape
    group, _ = place()
    for position, part in enumerate(parts):
        every[position] = part[0:kinds]
        if position:
            some[position - 1] = part[0:kinds]
        origin = jnp.bitwise_xor(group, (groups - position) % groups)
        query[pl.ds(aligned(origin, rows), rows), :] = part[kinds]


def merge(parts):
    kinds, rows, width = parts[0].shape
    shapes = [(len(parts), kinds - 1, rows, width), (len(parts) - 1, kinds - 1, rows, width), (len(parts) * rows, width)]
    return pl.pallas_call(
        merge_kernel,
        out_shape=[jax.ShapeDtypeStruct(shape, jnp.bfloat16) for shape in shapes],
        in_specs=[VMEM] * len(parts),
        out_specs=[VMEM] * 3,
        compiler_params=pltpu.CompilerParams(vmem_limit_bytes=SMALL),
        cost_estimate=pl.CostEstimate(flops=0, bytes_accessed=4 * len(parts) * parts[0].size, transcendentals=0),
    )(*parts)


def absorb(queries, segments, states):
    scores = [
        [
            sum(lax.dot_general(query, key, NT, preferred_element_type=jnp.float32) for key in keys) * HD**-0.5
            for keys, _ in parts
        ]
        for query, parts in zip(queries, segments)
    ]
    peaks = [[jnp.max(score, axis=1, keepdims=True) for score in row] for row in scores]
    if states is not None:
        peaks = [row + [state[0]] for row, state in zip(peaks, states)]
    peaks = [functools.reduce(jnp.maximum, row) for row in peaks]
    weights = [
        [jnp.exp(score - peak).astype(jnp.bfloat16) for score in row] for row, peak in zip(scores, peaks)
    ]
    totals = [sum(jnp.sum(w.astype(jnp.float32), axis=1, keepdims=True) for w in row) for row in weights]
    mixes = [
        sum(
            jnp.dot(w, value, preferred_element_type=jnp.float32)
            for w, (_, values) in zip(row, parts)
            for value in values
        )
        for row, parts in zip(weights, segments)
    ]
    if states is not None:
        fades = [jnp.exp(state[0] - peak) for state, peak in zip(states, peaks)]
        totals = [total + state[1] * fade for total, state, fade in zip(totals, states, fades)]
        mixes = [mix + state[2] * fade for mix, state, fade in zip(mixes, states, fades)]
    return list(zip(peaks, totals, mixes))


def columns_of(width):
    return [slice(start, start + HD) for start in range(0, width, HD)]


def image_segment(stale, twist, residual):
    def of(cols):
        both = [(stale[twist, kind, :, cols], residual(kind, cols)) for kind in range(2)]
        return both[0], both[1]

    return of


def whole_part(part):
    return lambda kind, cols: part[:, kind, :, cols].reshape(-1, HD)


def split_part(own, some):
    return lambda kind, cols: jnp.concatenate([own[kind, :, cols], some[:, kind, :, cols].reshape(-1, HD)], axis=0)


def near_kernel(query, every, text, stale, peak, total, mixed):
    heads = columns_of(query.shape[1])
    image = image_segment(stale, 0, whole_part(every))
    segments = [[((text[0, :, cols],), (text[1, :, cols],)), image(cols)] for cols in heads]
    states = absorb([query[:, cols] for cols in heads], segments, None)
    for head, state in enumerate(states):
        peak[head], total[head], mixed[head] = state


def middle_kernel(query, near, own_far, some_far, stale, peak_in, total_in, mixed_in, peak, total, mixed):
    heads = columns_of(query.shape[1])
    images = [
        image_segment(stale, 1, whole_part(near)),
        image_segment(stale, 2, split_part(own_far, some_far)),
    ]
    segments = [[image(cols) for image in images] for cols in heads]
    states = [(peak_in[head], total_in[head], mixed_in[head]) for head in range(len(heads))]
    states = absorb([query[:, cols] for cols in heads], segments, states)
    for head, state in enumerate(states):
        peak[head], total[head], mixed[head] = state


def last_kernel(query, own_corner, some_corner, stale, peak, total, mixed, full, most, last):
    heads = columns_of(query.shape[1])
    image = image_segment(stale, 3, split_part(own_corner, some_corner))
    states = [(peak[head], total[head], mixed[head]) for head in range(len(heads))]
    states = absorb([query[:, cols] for cols in heads], [[image(cols)] for cols in heads], states)
    for cols, (_, sums, mix) in zip(heads, states):
        value = (mix / sums).astype(jnp.bfloat16)
        full[:, cols] = value
        if cols is not heads[-1]:
            most[:, cols] = value
        else:
            last[...] = value


def attend_call(kernel, operands, shapes, keys):
    tokens, width = operands[0].shape
    return pl.pallas_call(
        kernel,
        out_shape=shapes,
        in_specs=[VMEM] * len(operands),
        out_specs=[VMEM] * len(shapes),
        compiler_params=pltpu.CompilerParams(vmem_limit_bytes=SMALL),
        cost_estimate=pl.CostEstimate(
            flops=8 * tokens * width * keys, bytes_accessed=8 * width * keys, transcendentals=tokens * keys * width // HD
        ),
    )(*operands)


def state_shapes(query):
    tokens, width = query.shape
    heads = width // HD
    return [jax.ShapeDtypeStruct((heads, tokens, size), jnp.float32) for size in (1, 1, HD)]


def result_shapes(query):
    tokens, width = query.shape
    return [jax.ShapeDtypeStruct((tokens, size), jnp.bfloat16) for size in (width, width - HD, HD)]


def order_kernel(*refs):
    pieces, out = refs[:-1], refs[-1]
    _, spot = place()
    span = out.shape[0] // SPREAD
    for twist, piece in enumerate(pieces):
        out[pl.ds(aligned(jnp.bitwise_xor(spot, twist), span), span), :] = piece[...]


def order(pieces):
    span, depth = pieces[0].shape
    shape = (SPREAD * span, depth)
    return pl.pallas_call(
        order_kernel,
        out_shape=jax.ShapeDtypeStruct(shape, jnp.bfloat16),
        in_specs=[VMEM] * len(pieces),
        out_specs=VMEM,
        compiler_params=pltpu.CompilerParams(vmem_limit_bytes=SMALL),
        cost_estimate=pl.CostEstimate(flops=0, bytes_accessed=4 * shape[0] * depth, transcendentals=0),
    )(*pieces)


def term_of(part, weight, turn, skip, width):
    group, _ = place()
    start = jnp.bitwise_xor(group, turn) * width + skip
    columns = pl.ds(pl.multiple_of(start, HD), part.shape[1])
    return lax.dot_general(part[...], weight[:, columns], NT, preferred_element_type=jnp.float32)


def begin_kernel(full, beside, across_most, across_last, weight, out):
    width = full.shape[1]
    total = term_of(full, weight, 0, 0, width) + term_of(beside, weight, 1, 0, width)
    total += term_of(across_most, weight, 2, 0, width)
    out[...] = total + term_of(across_last, weight, 2, width - HD, width)


def begin(parts, weight):
    tokens = parts[0].shape[0]
    columns, depth = weight.shape
    return pl.pallas_call(
        begin_kernel,
        out_shape=jax.ShapeDtypeStruct((tokens, columns), jnp.float32),
        in_specs=[VMEM] * (len(parts) + 1),
        out_specs=VMEM,
        compiler_params=pltpu.CompilerParams(vmem_limit_bytes=SMALL),
        cost_estimate=pl.CostEstimate(
            flops=2 * tokens * columns * depth, bytes_accessed=4 * tokens * columns, transcendentals=0
        ),
    )(*parts, weight)


def close_kernel(partial, most, last, weight, *rest):
    outs, total = rest[:-1], rest[-1]
    group, _ = place()
    rows = outs[0].shape[0]
    width = most.shape[1] + last.shape[1]
    added = partial[...] + term_of(most, weight, 3, 0, width) + term_of(last, weight, 3, width - HD, width)
    total[...] = added.astype(jnp.bfloat16)
    for turn, out in enumerate(outs):
        out[...] = total[pl.ds(aligned(jnp.bitwise_xor(group, turn), rows), rows), :]


def close(groups, partial, parts, weight):
    tokens, columns = partial.shape
    return pl.pallas_call(
        close_kernel,
        out_shape=[jax.ShapeDtypeStruct((tokens // groups, columns), jnp.bfloat16)] * groups,
        in_specs=[VMEM] * 4,
        out_specs=[VMEM] * groups,
        scratch_shapes=[pltpu.VMEM((tokens, columns), jnp.bfloat16)],
        compiler_params=pltpu.CompilerParams(vmem_limit_bytes=SMALL),
        cost_estimate=pl.CostEstimate(
            flops=tokens * weight.size, bytes_accessed=8 * tokens * columns, transcendentals=0
        ),
    )(partial, *parts, weight)


def divide_kernel(*refs):
    parts, (keep, send, held) = refs[:-3], refs[-3:]
    group, _ = place()
    half = lax.axis_index("head")
    blocks = keep.shape[0]
    for position, part in enumerate(parts):
        held[jnp.bitwise_xor(group, (len(parts) - position) % len(parts))] = part[...]
    for block in range(blocks):
        keep[block] = held[half * blocks + block]
        send[block] = held[(1 - half) * blocks + block]


def divide(parts):
    groups = len(parts)
    shape = jax.ShapeDtypeStruct((groups // 2, *parts[0].shape), jnp.bfloat16)
    return pl.pallas_call(
        divide_kernel,
        out_shape=[shape] * 2,
        in_specs=[VMEM] * groups,
        out_specs=[VMEM] * 2,
        scratch_shapes=[pltpu.VMEM((groups, *parts[0].shape), jnp.bfloat16)],
        compiler_params=pltpu.CompilerParams(vmem_limit_bytes=SMALL),
        cost_estimate=pl.CostEstimate(flops=0, bytes_accessed=4 * groups * parts[0].size, transcendentals=0),
    )(*parts)


def finish_kernel(kept, arrived, bias, gate, out):
    blocks, _, columns = kept.shape
    for block in range(blocks):
        cols = slice(block * columns, (block + 1) * columns)
        total = kept[block].astype(jnp.float32) + arrived[block].astype(jnp.float32)
        out[:, cols] = (gate[:, cols] * (total + bias[:, cols])).astype(jnp.bfloat16)


def finish(kept, arrived, bias, gate):
    blocks, rows, columns = kept.shape
    width = blocks * columns
    return pl.pallas_call(
        finish_kernel,
        out_shape=jax.ShapeDtypeStruct((rows, width), jnp.bfloat16),
        in_specs=[VMEM] * 4,
        out_specs=VMEM,
        compiler_params=pltpu.CompilerParams(vmem_limit_bytes=SMALL),
        cost_estimate=pl.CostEstimate(flops=3 * rows * width, bytes_accessed=4 * rows * width, transcendentals=0),
    )(kept, arrived, bias.reshape(1, width), gate.reshape(1, width))


def after(value, *others):
    return lax.optimization_barrier((value, *others))[0]


def grouped_body(queries, stale_kv, codes, exponents, text_kv, out_weight, out_bias, out_gate):
    groups = lax.axis_size("patch") // SPREAD
    size = groups * SPREAD

    def swap(value, twist):
        return lax.ppermute(value, "patch", [(p, p ^ twist) for p in range(size)])

    def along(values):
        return [swap(values[turn], turn * SPREAD) for turn in reversed(range(1, groups))]

    weight = out_weight.T
    weight_far = swap(weight, 2)
    *packed, own = pack(groups, queries, codes, exponents)
    text, stale = pick(groups, text_kv, stale_kv)

    every, some, query = merge([packed[0], *along(packed)])
    own_far = swap(own, 2)

    ready = (every, some, query, weight, weight_far, own_far, text, stale)
    every, some, query, weight, weight_far = lax.optimization_barrier(ready)[:5]
    near, some_far = swap(every, 1), swap(some, 2)
    share = stale.shape[2]
    state = attend_call(near_kernel, [query, every, text, stale], state_shapes(query), share + text.shape[1])

    near, some_far, own_far = lax.optimization_barrier((near, some_far, own_far, *state))[:3]
    own_corner, some_corner = swap(own_far, 1), swap(some_far, 1)
    state = attend_call(middle_kernel, [query, near, own_far, some_far, stale, *state], state_shapes(query), 2 * share)
    weight, weight_far = lax.optimization_barrier((weight, weight_far, *state))[:2]
    weight_near, weight_corner = swap(weight, 1), swap(weight_far, 1)
    operands = [query, own_corner, some_corner, stale, *state]
    full, most, last = attend_call(last_kernel, operands, result_shapes(query), share)

    across_most, across_last = swap(most, 2 * SPREAD), swap(last, 2 * SPREAD)
    beside = swap(full, SPREAD)
    final_most = swap(across_most, SPREAD)
    final_last = swap(after(across_last, beside, weight_near, weight_corner), SPREAD)
    weight = order([weight, weight_near, weight_far, weight_corner])
    partial = begin([full, beside, across_most, across_last], weight)
    terms = close(groups, partial, [final_most, final_last], weight)

    kept, sent = divide([terms[0], *along(terms)])
    received = lax.ppermute(sent, "head", [(0, 1), (1, 0)])
    return finish(kept, received, out_bias, out_gate)


def solution(mesh):
    patches, halves = mesh.shape["patch"], mesh.shape["head"]
    placed = (
        P("patch", "head"),
        P(None, None, "head"),
        P(None, "patch", "head"),
        P(None, "patch", "head"),
        P(None, None, "head"),
        P("head", "patch"),
        P("head"),
        P("head"),
    )

    def body(*args):
        heads = args[0].shape[1] // HD
        groups = patches // SPREAD
        if groups != 4 or patches % SPREAD or heads % groups or halves != 2:
            return plain_body(*args)
        return grouped_body(*args)

    return jax.shard_map(body, mesh=mesh, in_specs=placed, out_specs=P("patch", "head"), check_vma=False)
```

```python
import functools

import jax
import jax.numpy as jnp
from jax import lax
from jax.experimental import pallas as pl
from jax.experimental.pallas import tpu as pltpu
from jax.sharding import PartitionSpec as P

HD = 128
SPREAD = 4
PACK_LIMIT = 56 << 20
SMALL = 16 << 20
PICK_LIMIT = 50 << 20
VMEM = pl.BlockSpec(memory_space=pltpu.VMEM)
HBM = pl.BlockSpec(memory_space=pltpu.HBM)
NT = (((1,), (1,)), ((), ()))


def plain_body(queries, stale_kv, codes, exponents, text_kv, out_weight, out_bias, out_gate):
    tok_rows = queries.shape[0]
    row_width = queries.shape[1]
    head_count = row_width // HD
    text_count = text_kv.shape[1]
    scale_factor = HD ** (-0.5)
    blocks = jnp.exp2(exponents.astype(jnp.float32))
    decoded = codes.astype(jnp.float32).reshape(2, tok_rows, head_count, HD) * blocks[..., None]
    decoded = decoded.astype(jnp.bfloat16).reshape(2, tok_rows, row_width)
    arrived = lax.all_gather(decoded, "patch", axis=1, tiled=True)
    all_rows = arrived.shape[1]
    query_heads = queries.reshape(tok_rows, head_count, HD)
    text_heads = text_kv.reshape(2, text_count, head_count, HD)
    stale_heads = stale_kv.reshape(2, all_rows, head_count, HD)
    arrived_heads = arrived.reshape(2, all_rows, head_count, HD)
    text_scores = jnp.einsum("thd,khd->htk", query_heads, text_heads[0], preferred_element_type=jnp.float32)
    rebuilt = stale_heads.astype(jnp.float32) + arrived_heads.astype(jnp.float32)
    image_scores = jnp.einsum(
        "thd,khd->htk", query_heads.astype(jnp.float32), rebuilt[0], precision=lax.Precision.HIGHEST
    )
    scores = jnp.concatenate([text_scores, image_scores], axis=2) * scale_factor
    row_peak = jnp.max(scores, axis=2, keepdims=True)
    weights = jnp.exp(scores - row_peak).astype(jnp.bfloat16)
    row_total = jnp.sum(weights.astype(jnp.float32), axis=2)
    text_part = jnp.einsum(
        "htk,khd->thd", weights[:, :, :text_count], text_heads[1], preferred_element_type=jnp.float32
    )
    image_part = jnp.einsum(
        "htk,khd->thd",
        weights[:, :, text_count:].astype(jnp.float32),
        rebuilt[1],
        precision=lax.Precision.HIGHEST,
    )
    attended = ((text_part + image_part) / row_total.T[:, :, None]).astype(jnp.bfloat16).reshape(tok_rows, row_width)
    partial_terms = jnp.dot(
        attended, lax.all_gather(out_weight, "patch", axis=1, tiled=True), preferred_element_type=jnp.float32
    )
    column_share = lax.psum_scatter(partial_terms, "head", scatter_dimension=1, tiled=True)
    return (out_gate * (column_share + out_bias)).astype(jnp.bfloat16)


def aligned(value, step):
    return pl.multiple_of(value * step, step)


def place():
    me = lax.axis_index("patch")
    return me // SPREAD, lax.rem(me, SPREAD)


def pack_kernel(queries_hbm, codes_hbm, exponents_hbm, *rest):
    outs, (codes, queries, exponents, held, sems) = rest[:-5], rest[-5:]
    groups, kinds, rows, width = held.shape
    group, _ = place()
    per = width // HD
    copies = [
        pltpu.make_async_copy(exponents_hbm, exponents, sems.at[0]),
        pltpu.make_async_copy(codes_hbm, codes, sems.at[1]),
        pltpu.make_async_copy(queries_hbm, queries, sems.at[2]),
    ]
    for copy in copies:
        copy.start()
    copies[0].wait()
    copies[1].wait()
    eye = lax.broadcasted_iota(jnp.int32, (rows, rows), 0) == lax.broadcasted_iota(jnp.int32, (rows, rows), 1)
    eye = eye.astype(jnp.float32).astype(jnp.bfloat16)
    for kind in range(kinds - 1):
        scales = jnp.left_shift(1, exponents[:, kind, :] + 16).astype(jnp.float32) * (2.0**-16)
        scales = lax.dot_general(eye, scales.astype(jnp.bfloat16), NT, preferred_element_type=jnp.float32)
        for head in range(groups * per):
            inside = slice((head % per) * HD, (head % per + 1) * HD)
            whole = slice(head * HD, (head + 1) * HD)
            decoded = codes[kind, :, whole].astype(jnp.float32) * scales[:, head : head + 1]
            held[head // per, kind, :, inside] = decoded.astype(jnp.bfloat16)
    copies[2].wait()
    for target in range(groups):
        held[target, kinds - 1] = queries[:, target * width : (target + 1) * width]
    for turn in range(groups):
        outs[turn][...] = held[jnp.bitwise_xor(group, turn)]
    outs[groups][...] = held[group, 0 : kinds - 1]


def pack(groups, queries, codes, exponents):
    rows, width = queries.shape
    kinds = codes.shape[0]
    share = width // groups
    bf16 = jnp.bfloat16
    exponents = exponents.transpose(2, 0, 1)
    shapes = [(kinds + 1, rows, share)] * groups + [(kinds, rows, share)]
    outs = pl.pallas_call(
        pack_kernel,
        out_shape=[jax.ShapeDtypeStruct(shape, bf16) for shape in shapes],
        in_specs=[HBM] * 3,
        out_specs=[VMEM] * len(shapes),
        scratch_shapes=[
            pltpu.VMEM(codes.shape, jnp.int32),
            pltpu.VMEM(queries.shape, bf16),
            pltpu.VMEM(exponents.shape, jnp.int32),
            pltpu.VMEM((groups, kinds + 1, rows, share), bf16),
            pltpu.SemaphoreType.DMA((3,)),
        ],
        compiler_params=pltpu.CompilerParams(vmem_limit_bytes=PACK_LIMIT),
        cost_estimate=pl.CostEstimate(flops=2 * codes.size, bytes_accessed=6 * codes.size, transcendentals=0),
    )(queries, codes, exponents)
    return outs


def pick_kernel(text_hbm, stale_hbm, text, stale, sems):
    group, spot = place()
    width = text.shape[2]
    groups = text_hbm.shape[2] // width
    rows = stale.shape[2] // groups
    columns = pl.ds(aligned(group, width), width)
    copies = [pltpu.make_async_copy(text_hbm.at[:, :, columns], text, sems.at[0])]
    for twist in range(SPREAD):
        for position in range(groups):
            origin = jnp.bitwise_xor(group, (groups - position) % groups)
            token = origin * SPREAD + jnp.bitwise_xor(spot, twist)
            copies.append(
                pltpu.make_async_copy(
                    stale_hbm.at[:, pl.ds(aligned(token, rows), rows), columns],
                    stale.at[twist, :, pl.ds(position * rows, rows), :],
                    sems.at[len(copies)],
                )
            )
    for copy in copies:
        copy.start()
    for copy in copies:
        copy.wait()


def pick(groups, text_kv, stale_kv):
    kinds, texts, heads_width = text_kv.shape
    width = heads_width // groups
    return pl.pallas_call(
        pick_kernel,
        out_shape=[
            jax.ShapeDtypeStruct((kinds, texts, width), jnp.bfloat16),
            jax.ShapeDtypeStruct((SPREAD, kinds, stale_kv.shape[1] // SPREAD, width), jnp.bfloat16),
        ],
        in_specs=[HBM] * 2,
        out_specs=[VMEM] * 2,
        scratch_shapes=[pltpu.SemaphoreType.DMA((1 + SPREAD * groups,))],
        compiler_params=pltpu.CompilerParams(vmem_limit_bytes=PICK_LIMIT),
        cost_estimate=pl.CostEstimate(flops=0, bytes_accessed=8 << 20, transcendentals=0),
    )(text_kv, stale_kv)


def merge_kernel(*refs):
    parts, (every, some, query) = refs[:-3], refs[-3:]
    groups, kinds, rows, _ = every.shape
    group, _ = place()
    for position, part in enumerate(parts):
        every[position] = part[0:kinds]
        if position:
            some[position - 1] = part[0:kinds]
        origin = jnp.bitwise_xor(group, (groups - position) % groups)
        query[pl.ds(aligned(origin, rows), rows), :] = part[kinds]


def merge(parts):
    kinds, rows, width = parts[0].shape
    shapes = [(len(parts), kinds - 1, rows, width), (len(parts) - 1, kinds - 1, rows, width), (len(parts) * rows, width)]
    return pl.pallas_call(
        merge_kernel,
        out_shape=[jax.ShapeDtypeStruct(shape, jnp.bfloat16) for shape in shapes],
        in_specs=[VMEM] * len(parts),
        out_specs=[VMEM] * 3,
        compiler_params=pltpu.CompilerParams(vmem_limit_bytes=SMALL),
        cost_estimate=pl.CostEstimate(flops=0, bytes_accessed=4 * len(parts) * parts[0].size, transcendentals=0),
    )(*parts)


def absorb(queries, segments, states):
    scores = [
        [
            sum(lax.dot_general(query, key, NT, preferred_element_type=jnp.float32) for key in keys) * HD**-0.5
            for keys, _ in parts
        ]
        for query, parts in zip(queries, segments)
    ]
    peaks = [[jnp.max(score, axis=1, keepdims=True) for score in row] for row in scores]
    if states is not None:
        peaks = [row + [state[0]] for row, state in zip(peaks, states)]
    peaks = [functools.reduce(jnp.maximum, row) for row in peaks]
    weights = [
        [jnp.exp(score - peak).astype(jnp.bfloat16) for score in row] for row, peak in zip(scores, peaks)
    ]
    totals = [sum(jnp.sum(w.astype(jnp.float32), axis=1, keepdims=True) for w in row) for row in weights]
    mixes = [
        sum(
            jnp.dot(w, value, preferred_element_type=jnp.float32)
            for w, (_, values) in zip(row, parts)
            for value in values
        )
        for row, parts in zip(weights, segments)
    ]
    if states is not None:
        fades = [jnp.exp(state[0] - peak) for state, peak in zip(states, peaks)]
        totals = [total + state[1] * fade for total, state, fade in zip(totals, states, fades)]
        mixes = [mix + state[2] * fade for mix, state, fade in zip(mixes, states, fades)]
    return list(zip(peaks, totals, mixes))


def columns_of(width):
    return [slice(start, start + HD) for start in range(0, width, HD)]


def image_segment(stale, twist, residual):
    def of(cols):
        both = [(stale[twist, kind, :, cols], residual(kind, cols)) for kind in range(2)]
        return both[0], both[1]

    return of


def whole_part(part):
    return lambda kind, cols: part[:, kind, :, cols].reshape(-1, HD)


def split_part(own, some):
    return lambda kind, cols: jnp.concatenate([own[kind, :, cols], some[:, kind, :, cols].reshape(-1, HD)], axis=0)


def near_kernel(query, every, text, stale, peak, total, mixed):
    heads = columns_of(query.shape[1])
    image = image_segment(stale, 0, whole_part(every))
    segments = [[((text[0, :, cols],), (text[1, :, cols],)), image(cols)] for cols in heads]
    states = absorb([query[:, cols] for cols in heads], segments, None)
    for head, state in enumerate(states):
        peak[head], total[head], mixed[head] = state


def middle_kernel(query, near, own_far, some_far, stale, peak_in, total_in, mixed_in, peak, total, mixed):
    heads = columns_of(query.shape[1])
    images = [
        image_segment(stale, 1, whole_part(near)),
        image_segment(stale, 2, split_part(own_far, some_far)),
    ]
    segments = [[image(cols) for image in images] for cols in heads]
    states = [(peak_in[head], total_in[head], mixed_in[head]) for head in range(len(heads))]
    states = absorb([query[:, cols] for cols in heads], segments, states)
    for head, state in enumerate(states):
        peak[head], total[head], mixed[head] = state


def last_kernel(query, own_corner, some_corner, stale, peak, total, mixed, full, most, last):
    heads = columns_of(query.shape[1])
    image = image_segment(stale, 3, split_part(own_corner, some_corner))
    states = [(peak[head], total[head], mixed[head]) for head in range(len(heads))]
    states = absorb([query[:, cols] for cols in heads], [[image(cols)] for cols in heads], states)
    for cols, (_, sums, mix) in zip(heads, states):
        value = (mix / sums).astype(jnp.bfloat16)
        full[:, cols] = value
        if cols is not heads[-1]:
            most[:, cols] = value
        else:
            last[...] = value


def attend_call(kernel, operands, shapes, keys):
    tokens, width = operands[0].shape
    return pl.pallas_call(
        kernel,
        out_shape=shapes,
        in_specs=[VMEM] * len(operands),
        out_specs=[VMEM] * len(shapes),
        compiler_params=pltpu.CompilerParams(vmem_limit_bytes=SMALL),
        cost_estimate=pl.CostEstimate(
            flops=8 * tokens * width * keys, bytes_accessed=8 * width * keys, transcendentals=tokens * keys * width // HD
        ),
    )(*operands)


def state_shapes(query):
    tokens, width = query.shape
    heads = width // HD
    return [jax.ShapeDtypeStruct((heads, tokens, size), jnp.float32) for size in (1, 1, HD)]


def result_shapes(query):
    tokens, width = query.shape
    return [jax.ShapeDtypeStruct((tokens, size), jnp.bfloat16) for size in (width, width - HD, HD)]


def order_kernel(*refs):
    pieces, out = refs[:-1], refs[-1]
    _, spot = place()
    span = out.shape[0] // SPREAD
    for twist, piece in enumerate(pieces):
        out[pl.ds(aligned(jnp.bitwise_xor(spot, twist), span), span), :] = piece[...]


def order(pieces):
    span, depth = pieces[0].shape
    shape = (SPREAD * span, depth)
    return pl.pallas_call(
        order_kernel,
        out_shape=jax.ShapeDtypeStruct(shape, jnp.bfloat16),
        in_specs=[VMEM] * len(pieces),
        out_specs=VMEM,
        compiler_params=pltpu.CompilerParams(vmem_limit_bytes=SMALL),
        cost_estimate=pl.CostEstimate(flops=0, bytes_accessed=4 * shape[0] * depth, transcendentals=0),
    )(*pieces)


def term_of(part, weight, turn, skip, width):
    group, _ = place()
    start = jnp.bitwise_xor(group, turn) * width + skip
    columns = pl.ds(pl.multiple_of(start, HD), part.shape[1])
    return lax.dot_general(part[...], weight[:, columns], NT, preferred_element_type=jnp.float32)


def begin_kernel(full, beside, across_most, across_last, weight, out):
    width = full.shape[1]
    total = term_of(full, weight, 0, 0, width) + term_of(beside, weight, 1, 0, width)
    total += term_of(across_most, weight, 2, 0, width)
    out[...] = total + term_of(across_last, weight, 2, width - HD, width)


def begin(parts, weight):
    tokens = parts[0].shape[0]
    columns, depth = weight.shape
    return pl.pallas_call(
        begin_kernel,
        out_shape=jax.ShapeDtypeStruct((tokens, columns), jnp.float32),
        in_specs=[VMEM] * (len(parts) + 1),
        out_specs=VMEM,
        compiler_params=pltpu.CompilerParams(vmem_limit_bytes=SMALL),
        cost_estimate=pl.CostEstimate(
            flops=2 * tokens * columns * depth, bytes_accessed=4 * tokens * columns, transcendentals=0
        ),
    )(*parts, weight)


def close_kernel(partial, most, last, weight, *rest):
    outs, total = rest[:-1], rest[-1]
    group, _ = place()
    rows = outs[0].shape[0]
    width = most.shape[1] + last.shape[1]
    added = partial[...] + term_of(most, weight, 3, 0, width) + term_of(last, weight, 3, width - HD, width)
    total[...] = added.astype(jnp.bfloat16)
    for turn, out in enumerate(outs):
        out[...] = total[pl.ds(aligned(jnp.bitwise_xor(group, turn), rows), rows), :]


def close(groups, partial, parts, weight):
    tokens, columns = partial.shape
    return pl.pallas_call(
        close_kernel,
        out_shape=[jax.ShapeDtypeStruct((tokens // groups, columns), jnp.bfloat16)] * groups,
        in_specs=[VMEM] * 4,
        out_specs=[VMEM] * groups,
        scratch_shapes=[pltpu.VMEM((tokens, columns), jnp.bfloat16)],
        compiler_params=pltpu.CompilerParams(vmem_limit_bytes=SMALL),
        cost_estimate=pl.CostEstimate(
            flops=tokens * weight.size, bytes_accessed=8 * tokens * columns, transcendentals=0
        ),
    )(partial, *parts, weight)


def divide_kernel(*refs):
    parts, (keep, send, held) = refs[:-3], refs[-3:]
    group, _ = place()
    half = lax.axis_index("head")
    blocks = keep.shape[0]
    for position, part in enumerate(parts):
        held[jnp.bitwise_xor(group, (len(parts) - position) % len(parts))] = part[...]
    for block in range(blocks):
        keep[block] = held[half * blocks + block]
        send[block] = held[(1 - half) * blocks + block]


def divide(parts):
    groups = len(parts)
    shape = jax.ShapeDtypeStruct((groups // 2, *parts[0].shape), jnp.bfloat16)
    return pl.pallas_call(
        divide_kernel,
        out_shape=[shape] * 2,
        in_specs=[VMEM] * groups,
        out_specs=[VMEM] * 2,
        scratch_shapes=[pltpu.VMEM((groups, *parts[0].shape), jnp.bfloat16)],
        compiler_params=pltpu.CompilerParams(vmem_limit_bytes=SMALL),
        cost_estimate=pl.CostEstimate(flops=0, bytes_accessed=4 * groups * parts[0].size, transcendentals=0),
    )(*parts)


def finish_kernel(kept, arrived, bias, gate, out):
    blocks, _, columns = kept.shape
    for block in range(blocks):
        cols = slice(block * columns, (block + 1) * columns)
        total = kept[block].astype(jnp.float32) + arrived[block].astype(jnp.float32)
        out[:, cols] = (gate[:, cols] * (total + bias[:, cols])).astype(jnp.bfloat16)


def finish(kept, arrived, bias, gate):
    blocks, rows, columns = kept.shape
    width = blocks * columns
    return pl.pallas_call(
        finish_kernel,
        out_shape=jax.ShapeDtypeStruct((rows, width), jnp.bfloat16),
        in_specs=[VMEM] * 4,
        out_specs=VMEM,
        compiler_params=pltpu.CompilerParams(vmem_limit_bytes=SMALL),
        cost_estimate=pl.CostEstimate(flops=3 * rows * width, bytes_accessed=4 * rows * width, transcendentals=0),
    )(kept, arrived, bias.reshape(1, width), gate.reshape(1, width))


def after(value, *others):
    return lax.optimization_barrier((value, *others))[0]


def grouped_body(queries, stale_kv, codes, exponents, text_kv, out_weight, out_bias, out_gate):
    groups = lax.axis_size("patch") // SPREAD
    size = groups * SPREAD

    def swap(value, twist):
        return lax.ppermute(value, "patch", [(p, p ^ twist) for p in range(size)])

    def along(values):
        return [swap(values[turn], turn * SPREAD) for turn in reversed(range(1, groups))]

    weight = out_weight.T
    weight_far = swap(weight, 2)
    *packed, own = pack(groups, queries, codes, exponents)
    text, stale = pick(groups, text_kv, stale_kv)

    every, some, query = merge([packed[0], *along(packed)])
    own_far = swap(own, 2)

    ready = (every, some, query, weight, weight_far, own_far, text, stale)
    every, some, query, weight, weight_far = lax.optimization_barrier(ready)[:5]
    near, some_far = swap(every, 1), swap(some, 2)
    share = stale.shape[2]
    state = attend_call(near_kernel, [query, every, text, stale], state_shapes(query), share + text.shape[1])

    near, some_far, own_far = lax.optimization_barrier((near, some_far, own_far, *state))[:3]
    own_corner, some_corner = swap(own_far, 1), swap(some_far, 1)
    state = attend_call(middle_kernel, [query, near, own_far, some_far, stale, *state], state_shapes(query), 2 * share)
    weight, weight_far = lax.optimization_barrier((weight, weight_far, own_corner, some_corner, *state))[:2]
    weight_near, weight_corner = swap(weight, 1), swap(weight_far, 1)
    operands = [query, own_corner, some_corner, stale, *state]
    full, most, last = attend_call(last_kernel, operands, result_shapes(query), share)

    across_most, across_last = swap(most, 2 * SPREAD), swap(last, 2 * SPREAD)
    beside = swap(full, SPREAD)
    final_most = swap(across_most, SPREAD)
    final_last = swap(after(across_last, beside, weight_near, weight_corner), SPREAD)
    weight = order([weight, weight_near, weight_far, weight_corner])
    partial = begin([full, beside, across_most, across_last], weight)
    terms = close(groups, partial, [final_most, final_last], weight)

    kept, sent = divide([terms[0], *along(terms)])
    received = lax.ppermute(sent, "head", [(0, 1), (1, 0)])
    return finish(kept, received, out_bias, out_gate)


def solution(mesh):
    patches, halves = mesh.shape["patch"], mesh.shape["head"]
    placed = (
        P("patch", "head"),
        P(None, None, "head"),
        P(None, "patch", "head"),
        P(None, "patch", "head"),
        P(None, None, "head"),
        P("head", "patch"),
        P("head"),
        P("head"),
    )

    def body(*args):
        heads = args[0].shape[1] // HD
        groups = patches // SPREAD
        if groups != 4 or patches % SPREAD or heads % groups or halves != 2:
            return plain_body(*args)
        return grouped_body(*args)

    return jax.shard_map(body, mesh=mesh, in_specs=placed, out_specs=P("patch", "head"), check_vma=False)
```

```python
import functools

import jax
import jax.numpy as jnp
from jax import lax
from jax.experimental import pallas as pl
from jax.experimental.pallas import tpu as pltpu
from jax.sharding import PartitionSpec as P

HD = 128
SPREAD = 4
PACK_LIMIT = 56 << 20
SMALL = 16 << 20
PICK_LIMIT = 50 << 20
VMEM = pl.BlockSpec(memory_space=pltpu.VMEM)
HBM = pl.BlockSpec(memory_space=pltpu.HBM)
NT = (((1,), (1,)), ((), ()))


def plain_body(queries, stale_kv, codes, exponents, text_kv, out_weight, out_bias, out_gate):
    tok_rows = queries.shape[0]
    row_width = queries.shape[1]
    head_count = row_width // HD
    text_count = text_kv.shape[1]
    scale_factor = HD ** (-0.5)
    blocks = jnp.exp2(exponents.astype(jnp.float32))
    decoded = codes.astype(jnp.float32).reshape(2, tok_rows, head_count, HD) * blocks[..., None]
    decoded = decoded.astype(jnp.bfloat16).reshape(2, tok_rows, row_width)
    arrived = lax.all_gather(decoded, "patch", axis=1, tiled=True)
    all_rows = arrived.shape[1]
    query_heads = queries.reshape(tok_rows, head_count, HD)
    text_heads = text_kv.reshape(2, text_count, head_count, HD)
    stale_heads = stale_kv.reshape(2, all_rows, head_count, HD)
    arrived_heads = arrived.reshape(2, all_rows, head_count, HD)
    text_scores = jnp.einsum("thd,khd->htk", query_heads, text_heads[0], preferred_element_type=jnp.float32)
    rebuilt = stale_heads.astype(jnp.float32) + arrived_heads.astype(jnp.float32)
    image_scores = jnp.einsum(
        "thd,khd->htk", query_heads.astype(jnp.float32), rebuilt[0], precision=lax.Precision.HIGHEST
    )
    scores = jnp.concatenate([text_scores, image_scores], axis=2) * scale_factor
    row_peak = jnp.max(scores, axis=2, keepdims=True)
    weights = jnp.exp(scores - row_peak).astype(jnp.bfloat16)
    row_total = jnp.sum(weights.astype(jnp.float32), axis=2)
    text_part = jnp.einsum(
        "htk,khd->thd", weights[:, :, :text_count], text_heads[1], preferred_element_type=jnp.float32
    )
    image_part = jnp.einsum(
        "htk,khd->thd",
        weights[:, :, text_count:].astype(jnp.float32),
        rebuilt[1],
        precision=lax.Precision.HIGHEST,
    )
    attended = ((text_part + image_part) / row_total.T[:, :, None]).astype(jnp.bfloat16).reshape(tok_rows, row_width)
    partial_terms = jnp.dot(
        attended, lax.all_gather(out_weight, "patch", axis=1, tiled=True), preferred_element_type=jnp.float32
    )
    column_share = lax.psum_scatter(partial_terms, "head", scatter_dimension=1, tiled=True)
    return (out_gate * (column_share + out_bias)).astype(jnp.bfloat16)


def aligned(value, step):
    return pl.multiple_of(value * step, step)


def place():
    me = lax.axis_index("patch")
    return me // SPREAD, lax.rem(me, SPREAD)


def pack_kernel(queries_hbm, codes_hbm, exponents_hbm, *rest):
    outs, (codes, queries, exponents, held, sems) = rest[:-5], rest[-5:]
    groups, kinds, rows, width = held.shape
    group, _ = place()
    per = width // HD
    copies = [
        pltpu.make_async_copy(exponents_hbm, exponents, sems.at[0]),
        pltpu.make_async_copy(codes_hbm, codes, sems.at[1]),
        pltpu.make_async_copy(queries_hbm, queries, sems.at[2]),
    ]
    for copy in copies:
        copy.start()
    copies[0].wait()
    copies[1].wait()
    eye = lax.broadcasted_iota(jnp.int32, (rows, rows), 0) == lax.broadcasted_iota(jnp.int32, (rows, rows), 1)
    eye = eye.astype(jnp.float32).astype(jnp.bfloat16)
    for kind in range(kinds - 1):
        scales = jnp.left_shift(1, exponents[:, kind, :] + 16).astype(jnp.float32) * (2.0**-16)
        scales = lax.dot_general(eye, scales.astype(jnp.bfloat16), NT, preferred_element_type=jnp.float32)
        for head in range(groups * per):
            inside = slice((head % per) * HD, (head % per + 1) * HD)
            whole = slice(head * HD, (head + 1) * HD)
            decoded = codes[kind, :, whole].astype(jnp.float32) * scales[:, head : head + 1]
            held[head // per, kind, :, inside] = decoded.astype(jnp.bfloat16)
    copies[2].wait()
    for target in range(groups):
        held[target, kinds - 1] = queries[:, target * width : (target + 1) * width]
    for turn in range(groups):
        outs[turn][...] = held[jnp.bitwise_xor(group, turn)]
    outs[groups][...] = held[group, 0 : kinds - 1]


def pack(groups, queries, codes, exponents):
    rows, width = queries.shape
    kinds = codes.shape[0]
    share = width // groups
    bf16 = jnp.bfloat16
    exponents = exponents.transpose(2, 0, 1)
    shapes = [(kinds + 1, rows, share)] * groups + [(kinds, rows, share)]
    outs = pl.pallas_call(
        pack_kernel,
        out_shape=[jax.ShapeDtypeStruct(shape, bf16) for shape in shapes],
        in_specs=[HBM] * 3,
        out_specs=[VMEM] * len(shapes),
        scratch_shapes=[
            pltpu.VMEM(codes.shape, jnp.int32),
            pltpu.VMEM(queries.shape, bf16),
            pltpu.VMEM(exponents.shape, jnp.int32),
            pltpu.VMEM((groups, kinds + 1, rows, share), bf16),
            pltpu.SemaphoreType.DMA((3,)),
        ],
        compiler_params=pltpu.CompilerParams(vmem_limit_bytes=PACK_LIMIT),
        cost_estimate=pl.CostEstimate(flops=2 * codes.size, bytes_accessed=6 * codes.size, transcendentals=0),
    )(queries, codes, exponents)
    return outs


def pick_kernel(text_hbm, stale_hbm, text, stale, sems):
    group, spot = place()
    width = text.shape[2]
    groups = text_hbm.shape[2] // width
    rows = stale.shape[2] // groups
    columns = pl.ds(aligned(group, width), width)
    copies = [pltpu.make_async_copy(text_hbm.at[:, :, columns], text, sems.at[0])]
    for twist in range(SPREAD):
        for position in range(groups):
            origin = jnp.bitwise_xor(group, (groups - position) % groups)
            token = origin * SPREAD + jnp.bitwise_xor(spot, twist)
            copies.append(
                pltpu.make_async_copy(
                    stale_hbm.at[:, pl.ds(aligned(token, rows), rows), columns],
                    stale.at[twist, :, pl.ds(position * rows, rows), :],
                    sems.at[len(copies)],
                )
            )
    for copy in copies:
        copy.start()
    for copy in copies:
        copy.wait()


def pick(groups, text_kv, stale_kv):
    kinds, texts, heads_width = text_kv.shape
    width = heads_width // groups
    return pl.pallas_call(
        pick_kernel,
        out_shape=[
            jax.ShapeDtypeStruct((kinds, texts, width), jnp.bfloat16),
            jax.ShapeDtypeStruct((SPREAD, kinds, stale_kv.shape[1] // SPREAD, width), jnp.bfloat16),
        ],
        in_specs=[HBM] * 2,
        out_specs=[VMEM] * 2,
        scratch_shapes=[pltpu.SemaphoreType.DMA((1 + SPREAD * groups,))],
        compiler_params=pltpu.CompilerParams(vmem_limit_bytes=PICK_LIMIT),
        cost_estimate=pl.CostEstimate(flops=0, bytes_accessed=8 << 20, transcendentals=0),
    )(text_kv, stale_kv)


def merge_kernel(*refs):
    parts, (every, some, query) = refs[:-3], refs[-3:]
    groups, kinds, rows, _ = every.shape
    group, _ = place()
    for position, part in enumerate(parts):
        every[position] = part[0:kinds]
        if position:
            some[position - 1] = part[0:kinds]
        origin = jnp.bitwise_xor(group, (groups - position) % groups)
        query[pl.ds(aligned(origin, rows), rows), :] = part[kinds]


def merge(parts):
    kinds, rows, width = parts[0].shape
    shapes = [(len(parts), kinds - 1, rows, width), (len(parts) - 1, kinds - 1, rows, width), (len(parts) * rows, width)]
    return pl.pallas_call(
        merge_kernel,
        out_shape=[jax.ShapeDtypeStruct(shape, jnp.bfloat16) for shape in shapes],
        in_specs=[VMEM] * len(parts),
        out_specs=[VMEM] * 3,
        compiler_params=pltpu.CompilerParams(vmem_limit_bytes=SMALL),
        cost_estimate=pl.CostEstimate(flops=0, bytes_accessed=4 * len(parts) * parts[0].size, transcendentals=0),
    )(*parts)


def absorb(queries, segments, states):
    scores = [
        [
            lax.dot_general(
                query if key.shape[1] == HD else jnp.concatenate([query, query], axis=1),
                key,
                NT,
                preferred_element_type=jnp.float32,
            )
            * HD**-0.5
            for key, _ in parts
        ]
        for query, parts in zip(queries, segments)
    ]
    peaks = [[jnp.max(score, axis=1, keepdims=True) for score in row] for row in scores]
    if states is not None:
        peaks = [row + [state[0]] for row, state in zip(peaks, states)]
    peaks = [functools.reduce(jnp.maximum, row) for row in peaks]
    weights = [
        [jnp.exp(score - peak).astype(jnp.bfloat16) for score in row] for row, peak in zip(scores, peaks)
    ]
    totals = [sum(jnp.sum(w.astype(jnp.float32), axis=1, keepdims=True) for w in row) for row in weights]
    mixes = [
        sum(jnp.dot(w, value, preferred_element_type=jnp.float32) for w, (_, value) in zip(row, parts))
        for row, parts in zip(weights, segments)
    ]
    if states is not None:
        fades = [jnp.exp(state[0] - peak) for state, peak in zip(states, peaks)]
        totals = [total + state[1] * fade for total, state, fade in zip(totals, states, fades)]
        mixes = [mix + state[2] * fade for mix, state, fade in zip(mixes, states, fades)]
    return list(zip(peaks, totals, mixes))


def columns_of(width):
    return [slice(start, start + HD) for start in range(0, width, HD)]


def image_segment(stale, twist, residual):
    def of(cols):
        key = jnp.concatenate([stale[twist, 0, :, cols], residual(0, cols)], axis=1)
        value = stale[twist, 1, :, cols].astype(jnp.float32) + residual(1, cols).astype(jnp.float32)
        return key, value.astype(jnp.bfloat16)

    return of


def whole_part(part):
    return lambda kind, cols: part[:, kind, :, cols].reshape(-1, HD)


def split_part(own, some):
    return lambda kind, cols: jnp.concatenate([own[kind, :, cols], some[:, kind, :, cols].reshape(-1, HD)], axis=0)


def near_kernel(query, every, text, stale, peak, total, mixed):
    heads = columns_of(query.shape[1])
    image = image_segment(stale, 0, whole_part(every))
    segments = [[(text[0, :, cols], text[1, :, cols]), image(cols)] for cols in heads]
    states = absorb([query[:, cols] for cols in heads], segments, None)
    for head, state in enumerate(states):
        peak[head], total[head], mixed[head] = state


def middle_kernel(query, near, own_far, some_far, stale, peak_in, total_in, mixed_in, peak, total, mixed):
    heads = columns_of(query.shape[1])
    images = [
        image_segment(stale, 1, whole_part(near)),
        image_segment(stale, 2, split_part(own_far, some_far)),
    ]
    segments = [[image(cols) for image in images] for cols in heads]
    states = [(peak_in[head], total_in[head], mixed_in[head]) for head in range(len(heads))]
    states = absorb([query[:, cols] for cols in heads], segments, states)
    for head, state in enumerate(states):
        peak[head], total[head], mixed[head] = state


def last_kernel(query, own_corner, some_corner, stale, peak, total, mixed, full, most, last):
    heads = columns_of(query.shape[1])
    image = image_segment(stale, 3, split_part(own_corner, some_corner))
    states = [(peak[head], total[head], mixed[head]) for head in range(len(heads))]
    states = absorb([query[:, cols] for cols in heads], [[image(cols)] for cols in heads], states)
    for cols, (_, sums, mix) in zip(heads, states):
        value = (mix / sums).astype(jnp.bfloat16)
        full[:, cols] = value
        if cols is not heads[-1]:
            most[:, cols] = value
        else:
            last[...] = value


def attend_call(kernel, operands, shapes, keys):
    tokens, width = operands[0].shape
    return pl.pallas_call(
        kernel,
        out_shape=shapes,
        in_specs=[VMEM] * len(operands),
        out_specs=[VMEM] * len(shapes),
        compiler_params=pltpu.CompilerParams(vmem_limit_bytes=SMALL),
        cost_estimate=pl.CostEstimate(
            flops=8 * tokens * width * keys, bytes_accessed=8 * width * keys, transcendentals=tokens * keys * width // HD
        ),
    )(*operands)


def state_shapes(query):
    tokens, width = query.shape
    heads = width // HD
    return [jax.ShapeDtypeStruct((heads, tokens, size), jnp.float32) for size in (1, 1, HD)]


def result_shapes(query):
    tokens, width = query.shape
    return [jax.ShapeDtypeStruct((tokens, size), jnp.bfloat16) for size in (width, width - HD, HD)]


def order_kernel(*refs):
    pieces, out = refs[:-1], refs[-1]
    _, spot = place()
    span = out.shape[0] // SPREAD
    for twist, piece in enumerate(pieces):
        out[pl.ds(aligned(jnp.bitwise_xor(spot, twist), span), span), :] = piece[...]


def order(pieces):
    span, depth = pieces[0].shape
    shape = (SPREAD * span, depth)
    return pl.pallas_call(
        order_kernel,
        out_shape=jax.ShapeDtypeStruct(shape, jnp.bfloat16),
        in_specs=[VMEM] * len(pieces),
        out_specs=VMEM,
        compiler_params=pltpu.CompilerParams(vmem_limit_bytes=SMALL),
        cost_estimate=pl.CostEstimate(flops=0, bytes_accessed=4 * shape[0] * depth, transcendentals=0),
    )(*pieces)


def term_of(part, weight, turn, skip, width):
    group, _ = place()
    start = jnp.bitwise_xor(group, turn) * width + skip
    columns = pl.ds(pl.multiple_of(start, HD), part.shape[1])
    return lax.dot_general(part[...], weight[:, columns], NT, preferred_element_type=jnp.float32)


def begin_kernel(full, across_most, beside_most, across_last, beside_last, weight, out):
    width = full.shape[1]
    total = term_of(full, weight, 0, 0, width) + term_of(across_most, weight, 2, 0, width)
    total += term_of(beside_most, weight, 1, 0, width)
    total += term_of(across_last, weight, 2, width - HD, width)
    out[...] = total + term_of(beside_last, weight, 1, width - HD, width)


def begin(parts, weight):
    tokens = parts[0].shape[0]
    columns, depth = weight.shape
    return pl.pallas_call(
        begin_kernel,
        out_shape=jax.ShapeDtypeStruct((tokens, columns), jnp.float32),
        in_specs=[VMEM] * (len(parts) + 1),
        out_specs=VMEM,
        compiler_params=pltpu.CompilerParams(vmem_limit_bytes=SMALL),
        cost_estimate=pl.CostEstimate(
            flops=2 * tokens * columns * depth, bytes_accessed=4 * tokens * columns, transcendentals=0
        ),
    )(*parts, weight)


def close_kernel(partial, most, last, weight, *rest):
    outs, total = rest[:-1], rest[-1]
    group, _ = place()
    rows = outs[0].shape[0]
    width = most.shape[1] + last.shape[1]
    added = partial[...] + term_of(most, weight, 3, 0, width) + term_of(last, weight, 3, width - HD, width)
    total[...] = added.astype(jnp.bfloat16)
    for turn, out in enumerate(outs):
        out[...] = total[pl.ds(aligned(jnp.bitwise_xor(group, turn), rows), rows), :]


def close(groups, partial, parts, weight):
    tokens, columns = partial.shape
    return pl.pallas_call(
        close_kernel,
        out_shape=[jax.ShapeDtypeStruct((tokens // groups, columns), jnp.bfloat16)] * groups,
        in_specs=[VMEM] * 4,
        out_specs=[VMEM] * groups,
        scratch_shapes=[pltpu.VMEM((tokens, columns), jnp.bfloat16)],
        compiler_params=pltpu.CompilerParams(vmem_limit_bytes=SMALL),
        cost_estimate=pl.CostEstimate(
            flops=tokens * weight.size, bytes_accessed=8 * tokens * columns, transcendentals=0
        ),
    )(partial, *parts, weight)


def divide_kernel(*refs):
    parts, (keep, send, held) = refs[:-3], refs[-3:]
    group, _ = place()
    half = lax.axis_index("head")
    blocks = keep.shape[0]
    for position, part in enumerate(parts):
        held[jnp.bitwise_xor(group, (len(parts) - position) % len(parts))] = part[...]
    for block in range(blocks):
        keep[block] = held[half * blocks + block]
        send[block] = held[(1 - half) * blocks + block]


def divide(parts):
    groups = len(parts)
    shape = jax.ShapeDtypeStruct((groups // 2, *parts[0].shape), jnp.bfloat16)
    return pl.pallas_call(
        divide_kernel,
        out_shape=[shape] * 2,
        in_specs=[VMEM] * groups,
        out_specs=[VMEM] * 2,
        scratch_shapes=[pltpu.VMEM((groups, *parts[0].shape), jnp.bfloat16)],
        compiler_params=pltpu.CompilerParams(vmem_limit_bytes=SMALL),
        cost_estimate=pl.CostEstimate(flops=0, bytes_accessed=4 * groups * parts[0].size, transcendentals=0),
    )(*parts)


def finish_kernel(kept, arrived, bias, gate, out):
    blocks, _, columns = kept.shape
    for block in range(blocks):
        cols = slice(block * columns, (block + 1) * columns)
        total = kept[block].astype(jnp.float32) + arrived[block].astype(jnp.float32)
        out[:, cols] = (gate[:, cols] * (total + bias[:, cols])).astype(jnp.bfloat16)


def finish(kept, arrived, bias, gate):
    blocks, rows, columns = kept.shape
    width = blocks * columns
    return pl.pallas_call(
        finish_kernel,
        out_shape=jax.ShapeDtypeStruct((rows, width), jnp.bfloat16),
        in_specs=[VMEM] * 4,
        out_specs=VMEM,
        compiler_params=pltpu.CompilerParams(vmem_limit_bytes=SMALL),
        cost_estimate=pl.CostEstimate(flops=3 * rows * width, bytes_accessed=4 * rows * width, transcendentals=0),
    )(kept, arrived, bias.reshape(1, width), gate.reshape(1, width))


def after(value, *others):
    return lax.optimization_barrier((value, *others))[0]


def grouped_body(queries, stale_kv, codes, exponents, text_kv, out_weight, out_bias, out_gate):
    groups = lax.axis_size("patch") // SPREAD
    size = groups * SPREAD

    def swap(value, twist):
        return lax.ppermute(value, "patch", [(p, p ^ twist) for p in range(size)])

    def along(values):
        return [swap(values[turn], turn * SPREAD) for turn in reversed(range(1, groups))]

    weight = out_weight.T
    weight_far = swap(weight, 2)
    *packed, own = pack(groups, queries, codes, exponents)
    text, stale = pick(groups, text_kv, stale_kv)

    every, some, query = merge([packed[0], *along(packed)])
    own_far = swap(own, 2)

    ready = (every, some, query, weight, weight_far, own_far, text, stale)
    every, some, query, weight, weight_far = lax.optimization_barrier(ready)[:5]
    near, some_far = swap(every, 1), swap(some, 2)
    share = stale.shape[2]
    state = attend_call(near_kernel, [query, every, text, stale], state_shapes(query), share + text.shape[1])

    near, some_far, own_far = lax.optimization_barrier((near, some_far, own_far, *state))[:3]
    own_corner, some_corner = swap(own_far, 1), swap(some_far, 1)
    state = attend_call(middle_kernel, [query, near, own_far, some_far, stale, *state], state_shapes(query), 2 * share)
    weight, weight_far = lax.optimization_barrier((weight, weight_far, own_corner, some_corner, *state))[:2]
    weight_near, weight_corner = swap(weight, 1), swap(weight_far, 1)
    operands = [query, own_corner, some_corner, stale, *state]
    full, most, last = attend_call(last_kernel, operands, result_shapes(query), share)

    across_most, across_last = swap(most, 2 * SPREAD), swap(last, 2 * SPREAD)
    beside_most, beside_last = swap(most, SPREAD), swap(last, SPREAD)
    final_most = swap(across_most, SPREAD)
    final_last = swap(across_last, SPREAD)
    weight = order([weight, weight_near, weight_far, weight_corner])
    partial = begin([full, across_most, beside_most, across_last, beside_last], weight)
    terms = close(groups, partial, [final_most, final_last], weight)

    kept, sent = divide([terms[0], *along(terms)])
    received = lax.ppermute(sent, "head", [(0, 1), (1, 0)])
    return finish(kept, received, out_bias, out_gate)


def solution(mesh):
    patches, halves = mesh.shape["patch"], mesh.shape["head"]
    placed = (
        P("patch", "head"),
        P(None, None, "head"),
        P(None, "patch", "head"),
        P(None, "patch", "head"),
        P(None, None, "head"),
        P("head", "patch"),
        P("head"),
        P("head"),
    )

    def body(*args):
        heads = args[0].shape[1] // HD
        groups = patches // SPREAD
        if groups != 4 or patches % SPREAD or heads % groups or halves != 2:
            return plain_body(*args)
        return grouped_body(*args)

    return jax.shard_map(body, mesh=mesh, in_specs=placed, out_specs=P("patch", "head"), check_vma=False)
```

```python
import functools

import jax
import jax.numpy as jnp
from jax import lax
from jax.experimental import pallas as pl
from jax.experimental.pallas import tpu as pltpu
from jax.sharding import PartitionSpec as P

HD = 128
SPREAD = 4
PACK_LIMIT = 56 << 20
SMALL = 16 << 20
PICK_LIMIT = 50 << 20
VMEM = pl.BlockSpec(memory_space=pltpu.VMEM)
HBM = pl.BlockSpec(memory_space=pltpu.HBM)
NT = (((1,), (1,)), ((), ()))


def plain_body(queries, stale_kv, codes, exponents, text_kv, out_weight, out_bias, out_gate):
    tok_rows = queries.shape[0]
    row_width = queries.shape[1]
    head_count = row_width // HD
    text_count = text_kv.shape[1]
    scale_factor = HD ** (-0.5)
    blocks = jnp.exp2(exponents.astype(jnp.float32))
    decoded = codes.astype(jnp.float32).reshape(2, tok_rows, head_count, HD) * blocks[..., None]
    decoded = decoded.astype(jnp.bfloat16).reshape(2, tok_rows, row_width)
    arrived = lax.all_gather(decoded, "patch", axis=1, tiled=True)
    all_rows = arrived.shape[1]
    query_heads = queries.reshape(tok_rows, head_count, HD)
    text_heads = text_kv.reshape(2, text_count, head_count, HD)
    stale_heads = stale_kv.reshape(2, all_rows, head_count, HD)
    arrived_heads = arrived.reshape(2, all_rows, head_count, HD)
    text_scores = jnp.einsum("thd,khd->htk", query_heads, text_heads[0], preferred_element_type=jnp.float32)
    rebuilt = stale_heads.astype(jnp.float32) + arrived_heads.astype(jnp.float32)
    image_scores = jnp.einsum(
        "thd,khd->htk", query_heads.astype(jnp.float32), rebuilt[0], precision=lax.Precision.HIGHEST
    )
    scores = jnp.concatenate([text_scores, image_scores], axis=2) * scale_factor
    row_peak = jnp.max(scores, axis=2, keepdims=True)
    weights = jnp.exp(scores - row_peak).astype(jnp.bfloat16)
    row_total = jnp.sum(weights.astype(jnp.float32), axis=2)
    text_part = jnp.einsum(
        "htk,khd->thd", weights[:, :, :text_count], text_heads[1], preferred_element_type=jnp.float32
    )
    image_part = jnp.einsum(
        "htk,khd->thd",
        weights[:, :, text_count:].astype(jnp.float32),
        rebuilt[1],
        precision=lax.Precision.HIGHEST,
    )
    attended = ((text_part + image_part) / row_total.T[:, :, None]).astype(jnp.bfloat16).reshape(tok_rows, row_width)
    partial_terms = jnp.dot(
        attended, lax.all_gather(out_weight, "patch", axis=1, tiled=True), preferred_element_type=jnp.float32
    )
    column_share = lax.psum_scatter(partial_terms, "head", scatter_dimension=1, tiled=True)
    return (out_gate * (column_share + out_bias)).astype(jnp.bfloat16)


def aligned(value, step):
    return pl.multiple_of(value * step, step)


def place():
    me = lax.axis_index("patch")
    return me // SPREAD, lax.rem(me, SPREAD)


def pieces_of(rows):
    first = rows // 48 * 32
    return [(0, first), (first, rows - first)]


def pack_kernel(queries_hbm, codes_hbm, exponents_hbm, *rest):
    outs, (codes, queries, exponents, held, sems) = rest[:-5], rest[-5:]
    groups, kinds, rows, width = held.shape
    group, _ = place()
    per = width // HD
    copies = [
        pltpu.make_async_copy(exponents_hbm, exponents, sems.at[0]),
        pltpu.make_async_copy(codes_hbm, codes, sems.at[1]),
        pltpu.make_async_copy(queries_hbm, queries, sems.at[2]),
    ]
    for copy in copies:
        copy.start()
    copies[0].wait()
    copies[1].wait()
    eye = lax.broadcasted_iota(jnp.int32, (rows, rows), 0) == lax.broadcasted_iota(jnp.int32, (rows, rows), 1)
    eye = eye.astype(jnp.float32).astype(jnp.bfloat16)
    for kind in range(kinds - 1):
        scales = jnp.left_shift(1, exponents[:, kind, :] + 16).astype(jnp.float32) * (2.0**-16)
        scales = lax.dot_general(eye, scales.astype(jnp.bfloat16), NT, preferred_element_type=jnp.float32)
        for head in range(groups * per):
            inside = slice((head % per) * HD, (head % per + 1) * HD)
            whole = slice(head * HD, (head + 1) * HD)
            decoded = codes[kind, :, whole].astype(jnp.float32) * scales[:, head : head + 1]
            held[head // per, kind, :, inside] = decoded.astype(jnp.bfloat16)
    copies[2].wait()
    for target in range(groups):
        held[target, kinds - 1] = queries[:, target * width : (target + 1) * width]
    for turn in range(groups):
        outs[turn][...] = held[jnp.bitwise_xor(group, turn)]
    outs[groups][...] = held[group, 0 : kinds - 1]


def pack(groups, queries, codes, exponents):
    rows, width = queries.shape
    kinds = codes.shape[0]
    share = width // groups
    bf16 = jnp.bfloat16
    exponents = exponents.transpose(2, 0, 1)
    shapes = [(kinds + 1, rows, share)] * groups + [(kinds, rows, share)]
    outs = pl.pallas_call(
        pack_kernel,
        out_shape=[jax.ShapeDtypeStruct(shape, bf16) for shape in shapes],
        in_specs=[HBM] * 3,
        out_specs=[VMEM] * len(shapes),
        scratch_shapes=[
            pltpu.VMEM(codes.shape, jnp.int32),
            pltpu.VMEM(queries.shape, bf16),
            pltpu.VMEM(exponents.shape, jnp.int32),
            pltpu.VMEM((groups, kinds + 1, rows, share), bf16),
            pltpu.SemaphoreType.DMA((3,)),
        ],
        compiler_params=pltpu.CompilerParams(vmem_limit_bytes=PACK_LIMIT),
        cost_estimate=pl.CostEstimate(flops=2 * codes.size, bytes_accessed=6 * codes.size, transcendentals=0),
    )(queries, codes, exponents)
    return outs


def pick_kernel(text_hbm, stale_hbm, text, stale, sems):
    group, spot = place()
    width = text.shape[2]
    groups = text_hbm.shape[2] // width
    rows = stale.shape[2] // groups
    columns = pl.ds(aligned(group, width), width)
    copies = [pltpu.make_async_copy(text_hbm.at[:, :, columns], text, sems.at[0])]
    for twist in range(SPREAD):
        for position in range(groups):
            origin = jnp.bitwise_xor(group, (groups - position) % groups)
            token = origin * SPREAD + jnp.bitwise_xor(spot, twist)
            copies.append(
                pltpu.make_async_copy(
                    stale_hbm.at[:, pl.ds(aligned(token, rows), rows), columns],
                    stale.at[twist, :, pl.ds(position * rows, rows), :],
                    sems.at[len(copies)],
                )
            )
    for copy in copies:
        copy.start()
    for copy in copies:
        copy.wait()


def pick(groups, text_kv, stale_kv):
    kinds, texts, heads_width = text_kv.shape
    width = heads_width // groups
    return pl.pallas_call(
        pick_kernel,
        out_shape=[
            jax.ShapeDtypeStruct((kinds, texts, width), jnp.bfloat16),
            jax.ShapeDtypeStruct((SPREAD, kinds, stale_kv.shape[1] // SPREAD, width), jnp.bfloat16),
        ],
        in_specs=[HBM] * 2,
        out_specs=[VMEM] * 2,
        scratch_shapes=[pltpu.SemaphoreType.DMA((1 + SPREAD * groups,))],
        compiler_params=pltpu.CompilerParams(vmem_limit_bytes=PICK_LIMIT),
        cost_estimate=pl.CostEstimate(flops=0, bytes_accessed=8 << 20, transcendentals=0),
    )(text_kv, stale_kv)


def merge_kernel(*refs):
    parts, (every, some, query) = refs[:-3], refs[-3:]
    groups, kinds, rows, _ = every.shape
    group, _ = place()
    for position, part in enumerate(parts):
        every[position] = part[0:kinds]
        if position:
            some[position - 1] = part[0:kinds]
        origin = jnp.bitwise_xor(group, (groups - position) % groups)
        for skip, height in pieces_of(rows):
            start = groups * skip + origin * height
            query[pl.ds(pl.multiple_of(start, 16), height), :] = part[kinds, skip : skip + height, :]


def merge(parts):
    kinds, rows, width = parts[0].shape
    shapes = [(len(parts), kinds - 1, rows, width), (len(parts) - 1, kinds - 1, rows, width), (len(parts) * rows, width)]
    return pl.pallas_call(
        merge_kernel,
        out_shape=[jax.ShapeDtypeStruct(shape, jnp.bfloat16) for shape in shapes],
        in_specs=[VMEM] * len(parts),
        out_specs=[VMEM] * 3,
        compiler_params=pltpu.CompilerParams(vmem_limit_bytes=SMALL),
        cost_estimate=pl.CostEstimate(flops=0, bytes_accessed=4 * len(parts) * parts[0].size, transcendentals=0),
    )(*parts)


def absorb(queries, segments, states):
    scores = [
        [
            lax.dot_general(
                query if key.shape[1] == HD else jnp.concatenate([query, query], axis=1),
                key,
                NT,
                preferred_element_type=jnp.float32,
            )
            * HD**-0.5
            for key, _ in parts
        ]
        for query, parts in zip(queries, segments)
    ]
    peaks = [[jnp.max(score, axis=1, keepdims=True) for score in row] for row in scores]
    if states is not None:
        peaks = [row + [state[0]] for row, state in zip(peaks, states)]
    peaks = [functools.reduce(jnp.maximum, row) for row in peaks]
    weights = [
        [jnp.exp(score - peak).astype(jnp.bfloat16) for score in row] for row, peak in zip(scores, peaks)
    ]
    totals = [sum(jnp.sum(w.astype(jnp.float32), axis=1, keepdims=True) for w in row) for row in weights]
    mixes = [
        sum(jnp.dot(w, value, preferred_element_type=jnp.float32) for w, (_, value) in zip(row, parts))
        for row, parts in zip(weights, segments)
    ]
    if states is not None:
        fades = [jnp.exp(state[0] - peak) for state, peak in zip(states, peaks)]
        totals = [total + state[1] * fade for total, state, fade in zip(totals, states, fades)]
        mixes = [mix + state[2] * fade for mix, state, fade in zip(mixes, states, fades)]
    return list(zip(peaks, totals, mixes))


def columns_of(width):
    return [slice(start, start + HD) for start in range(0, width, HD)]


def image_segment(stale, twist, residual):
    def of(cols):
        key = jnp.concatenate([stale[twist, 0, :, cols], residual(0, cols)], axis=1)
        value = stale[twist, 1, :, cols].astype(jnp.float32) + residual(1, cols).astype(jnp.float32)
        return key, value.astype(jnp.bfloat16)

    return of


def whole_part(part):
    return lambda kind, cols: part[:, kind, :, cols].reshape(-1, HD)


def split_part(own, some):
    return lambda kind, cols: jnp.concatenate([own[kind, :, cols], some[:, kind, :, cols].reshape(-1, HD)], axis=0)


def near_kernel(query, every, text, stale, peak, total, mixed):
    heads = columns_of(query.shape[1])
    image = image_segment(stale, 0, whole_part(every))
    segments = [[(text[0, :, cols], text[1, :, cols]), image(cols)] for cols in heads]
    states = absorb([query[:, cols] for cols in heads], segments, None)
    for head, state in enumerate(states):
        peak[head], total[head], mixed[head] = state


def middle_kernel(query, near, own_far, some_far, stale, peak_in, total_in, mixed_in, peak, total, mixed):
    heads = columns_of(query.shape[1])
    images = [
        image_segment(stale, 1, whole_part(near)),
        image_segment(stale, 2, split_part(own_far, some_far)),
    ]
    segments = [[image(cols) for image in images] for cols in heads]
    states = [(peak_in[head], total_in[head], mixed_in[head]) for head in range(len(heads))]
    states = absorb([query[:, cols] for cols in heads], segments, states)
    for head, state in enumerate(states):
        peak[head], total[head], mixed[head] = state


def last_kernel(query, own_corner, some_corner, stale, peak, total, mixed, most, last):
    heads = columns_of(query.shape[1])
    image = image_segment(stale, 3, split_part(own_corner, some_corner))
    states = [(peak[head], total[head], mixed[head]) for head in range(len(heads))]
    states = absorb([query[:, cols] for cols in heads], [[image(cols)] for cols in heads], states)
    for cols, (_, sums, mix) in zip(heads, states):
        value = (mix / sums).astype(jnp.bfloat16)
        most[:, cols] = value[0 : most.shape[0]]
        last[:, cols] = value[most.shape[0] :]


def attend_call(kernel, operands, shapes, keys):
    tokens, width = operands[0].shape
    return pl.pallas_call(
        kernel,
        out_shape=shapes,
        in_specs=[VMEM] * len(operands),
        out_specs=[VMEM] * len(shapes),
        compiler_params=pltpu.CompilerParams(vmem_limit_bytes=SMALL),
        cost_estimate=pl.CostEstimate(
            flops=8 * tokens * width * keys, bytes_accessed=8 * width * keys, transcendentals=tokens * keys * width // HD
        ),
    )(*operands)


def state_shapes(query):
    tokens, width = query.shape
    heads = width // HD
    return [jax.ShapeDtypeStruct((heads, tokens, size), jnp.float32) for size in (1, 1, HD)]


def result_shapes(query, rows):
    tokens, width = query.shape
    return [jax.ShapeDtypeStruct((tokens // rows * height, width), jnp.bfloat16) for _, height in pieces_of(rows)]


def order_kernel(*refs):
    pieces, out = refs[:-1], refs[-1]
    _, spot = place()
    span = out.shape[0] // SPREAD
    for twist, piece in enumerate(pieces):
        out[pl.ds(aligned(jnp.bitwise_xor(spot, twist), span), span), :] = piece[...]


def order(pieces):
    span, depth = pieces[0].shape
    shape = (SPREAD * span, depth)
    return pl.pallas_call(
        order_kernel,
        out_shape=jax.ShapeDtypeStruct(shape, jnp.bfloat16),
        in_specs=[VMEM] * len(pieces),
        out_specs=VMEM,
        compiler_params=pltpu.CompilerParams(vmem_limit_bytes=SMALL),
        cost_estimate=pl.CostEstimate(flops=0, bytes_accessed=4 * shape[0] * depth, transcendentals=0),
    )(*pieces)


def term_of(part, weight, turn):
    group, _ = place()
    width = part.shape[1]
    columns = pl.ds(aligned(jnp.bitwise_xor(group, turn), width), width)
    return lax.dot_general(part[...], weight[:, columns], NT, preferred_element_type=jnp.float32)


def begin_kernel(own, across, beside, weight, out):
    out[...] = term_of(own, weight, 0) + term_of(across, weight, 2) + term_of(beside, weight, 1)


def begin(parts, weight):
    tokens = parts[0].shape[0]
    columns, depth = weight.shape
    return pl.pallas_call(
        begin_kernel,
        out_shape=jax.ShapeDtypeStruct((tokens, columns), jnp.float32),
        in_specs=[VMEM] * (len(parts) + 1),
        out_specs=VMEM,
        compiler_params=pltpu.CompilerParams(vmem_limit_bytes=SMALL),
        cost_estimate=pl.CostEstimate(
            flops=2 * tokens * columns * depth, bytes_accessed=4 * tokens * columns, transcendentals=0
        ),
    )(*parts, weight)


def close_kernel(partial, final, weight, *rest):
    outs, total = rest[:-1], rest[-1]
    group, _ = place()
    rows = outs[0].shape[0]
    total[...] = (partial[...] + term_of(final, weight, 3)).astype(jnp.bfloat16)
    for turn, out in enumerate(outs):
        out[...] = total[pl.ds(aligned(jnp.bitwise_xor(group, turn), rows), rows), :]


def close(groups, partial, final, weight):
    tokens, columns = partial.shape
    return pl.pallas_call(
        close_kernel,
        out_shape=[jax.ShapeDtypeStruct((tokens // groups, columns), jnp.bfloat16)] * groups,
        in_specs=[VMEM] * 3,
        out_specs=[VMEM] * groups,
        scratch_shapes=[pltpu.VMEM((tokens, columns), jnp.bfloat16)],
        compiler_params=pltpu.CompilerParams(vmem_limit_bytes=SMALL),
        cost_estimate=pl.CostEstimate(
            flops=tokens * weight.size, bytes_accessed=8 * tokens * columns, transcendentals=0
        ),
    )(partial, final, weight)


def divide_kernel(*refs):
    parts, (keep, send, held) = refs[:-3], refs[-3:]
    group, _ = place()
    half = lax.axis_index("head")
    blocks = keep.shape[0]
    for position, part in enumerate(parts):
        held[jnp.bitwise_xor(group, (len(parts) - position) % len(parts))] = part[...]
    for block in range(blocks):
        keep[block] = held[half * blocks + block]
        send[block] = held[(1 - half) * blocks + block]


def divide(parts):
    groups = len(parts)
    shape = jax.ShapeDtypeStruct((groups // 2, *parts[0].shape), jnp.bfloat16)
    return pl.pallas_call(
        divide_kernel,
        out_shape=[shape] * 2,
        in_specs=[VMEM] * groups,
        out_specs=[VMEM] * 2,
        scratch_shapes=[pltpu.VMEM((groups, *parts[0].shape), jnp.bfloat16)],
        compiler_params=pltpu.CompilerParams(vmem_limit_bytes=SMALL),
        cost_estimate=pl.CostEstimate(flops=0, bytes_accessed=4 * groups * parts[0].size, transcendentals=0),
    )(*parts)


def finish_kernel(*refs):
    pairs, (bias, gate, out) = refs[:-3], refs[-3:]
    start = 0
    for kept, arrived in zip(pairs[0::2], pairs[1::2]):
        blocks, rows, columns = kept.shape
        for block in range(blocks):
            cols = slice(block * columns, (block + 1) * columns)
            total = kept[block].astype(jnp.float32) + arrived[block].astype(jnp.float32)
            out[start : start + rows, cols] = (gate[:, cols] * (total + bias[:, cols])).astype(jnp.bfloat16)
        start += rows


def finish(pairs, bias, gate):
    blocks, _, columns = pairs[0].shape
    width = blocks * columns
    rows = sum(kept.shape[1] for kept in pairs[0::2])
    return pl.pallas_call(
        finish_kernel,
        out_shape=jax.ShapeDtypeStruct((rows, width), jnp.bfloat16),
        in_specs=[VMEM] * (len(pairs) + 2),
        out_specs=VMEM,
        compiler_params=pltpu.CompilerParams(vmem_limit_bytes=SMALL),
        cost_estimate=pl.CostEstimate(flops=3 * rows * width, bytes_accessed=4 * rows * width, transcendentals=0),
    )(*pairs, bias.reshape(1, width), gate.reshape(1, width))


def after(value, *others):
    return lax.optimization_barrier((value, *others))[0]


def grouped_body(queries, stale_kv, codes, exponents, text_kv, out_weight, out_bias, out_gate):
    groups = lax.axis_size("patch") // SPREAD
    size = groups * SPREAD

    def swap(value, twist):
        return lax.ppermute(value, "patch", [(p, p ^ twist) for p in range(size)])

    def along(values):
        return [swap(values[turn], turn * SPREAD) for turn in reversed(range(1, groups))]

    weight = out_weight.T
    weight_far = swap(weight, 2)
    *packed, own = pack(groups, queries, codes, exponents)
    text, stale = pick(groups, text_kv, stale_kv)

    every, some, query = merge([packed[0], *along(packed)])
    own_far = swap(own, 2)

    ready = (every, some, query, weight, weight_far, own_far, text, stale)
    every, some, query, weight, weight_far = lax.optimization_barrier(ready)[:5]
    near, some_far = swap(every, 1), swap(some, 2)
    share = stale.shape[2]
    state = attend_call(near_kernel, [query, every, text, stale], state_shapes(query), share + text.shape[1])

    near, some_far, own_far = lax.optimization_barrier((near, some_far, own_far, *state))[:3]
    own_corner, some_corner = swap(own_far, 1), swap(some_far, 1)
    state = attend_call(middle_kernel, [query, near, own_far, some_far, stale, *state], state_shapes(query), 2 * share)
    weight, weight_far = lax.optimization_barrier((weight, weight_far, own_corner, some_corner, *state))[:2]
    weight_near, weight_corner = swap(weight, 1), swap(weight_far, 1)
    operands = [query, own_corner, some_corner, stale, *state]
    parts = attend_call(last_kernel, operands, result_shapes(query, every.shape[2]), share)

    weight = order([weight, weight_near, weight_far, weight_corner])
    pairs = []
    for part in parts:
        across, beside = swap(part, 2 * SPREAD), swap(part, SPREAD)
        final = swap(across, SPREAD)
        terms = close(groups, begin([part, across, beside], weight), final, weight)
        kept, sent = divide([terms[0], *along(terms)])
        pairs += [kept, lax.ppermute(sent, "head", [(0, 1), (1, 0)])]
    return finish(pairs, out_bias, out_gate)


def solution(mesh):
    patches, halves = mesh.shape["patch"], mesh.shape["head"]
    placed = (
        P("patch", "head"),
        P(None, None, "head"),
        P(None, "patch", "head"),
        P(None, "patch", "head"),
        P(None, None, "head"),
        P("head", "patch"),
        P("head"),
        P("head"),
    )

    def body(*args):
        heads = args[0].shape[1] // HD
        groups = patches // SPREAD
        if groups != 4 or patches % SPREAD or heads % groups or halves != 2:
            return plain_body(*args)
        return grouped_body(*args)

    return jax.shard_map(body, mesh=mesh, in_specs=placed, out_specs=P("patch", "head"), check_vma=False)
```

```python
import functools

import jax
import jax.numpy as jnp
from jax import lax
from jax.experimental import pallas as pl
from jax.experimental.pallas import tpu as pltpu
from jax.sharding import PartitionSpec as P

HD = 128
SPREAD = 4
PACK_LIMIT = 56 << 20
SMALL = 16 << 20
PICK_LIMIT = 50 << 20
VMEM = pl.BlockSpec(memory_space=pltpu.VMEM)
HBM = pl.BlockSpec(memory_space=pltpu.HBM)
NT = (((1,), (1,)), ((), ()))


def plain_body(queries, stale_kv, codes, exponents, text_kv, out_weight, out_bias, out_gate):
    tok_rows = queries.shape[0]
    row_width = queries.shape[1]
    head_count = row_width // HD
    text_count = text_kv.shape[1]
    scale_factor = HD ** (-0.5)
    blocks = jnp.exp2(exponents.astype(jnp.float32))
    decoded = codes.astype(jnp.float32).reshape(2, tok_rows, head_count, HD) * blocks[..., None]
    decoded = decoded.astype(jnp.bfloat16).reshape(2, tok_rows, row_width)
    arrived = lax.all_gather(decoded, "patch", axis=1, tiled=True)
    all_rows = arrived.shape[1]
    query_heads = queries.reshape(tok_rows, head_count, HD)
    text_heads = text_kv.reshape(2, text_count, head_count, HD)
    stale_heads = stale_kv.reshape(2, all_rows, head_count, HD)
    arrived_heads = arrived.reshape(2, all_rows, head_count, HD)
    text_scores = jnp.einsum("thd,khd->htk", query_heads, text_heads[0], preferred_element_type=jnp.float32)
    rebuilt = stale_heads.astype(jnp.float32) + arrived_heads.astype(jnp.float32)
    image_scores = jnp.einsum(
        "thd,khd->htk", query_heads.astype(jnp.float32), rebuilt[0], precision=lax.Precision.HIGHEST
    )
    scores = jnp.concatenate([text_scores, image_scores], axis=2) * scale_factor
    row_peak = jnp.max(scores, axis=2, keepdims=True)
    weights = jnp.exp(scores - row_peak).astype(jnp.bfloat16)
    row_total = jnp.sum(weights.astype(jnp.float32), axis=2)
    text_part = jnp.einsum(
        "htk,khd->thd", weights[:, :, :text_count], text_heads[1], preferred_element_type=jnp.float32
    )
    image_part = jnp.einsum(
        "htk,khd->thd",
        weights[:, :, text_count:].astype(jnp.float32),
        rebuilt[1],
        precision=lax.Precision.HIGHEST,
    )
    attended = ((text_part + image_part) / row_total.T[:, :, None]).astype(jnp.bfloat16).reshape(tok_rows, row_width)
    partial_terms = jnp.dot(
        attended, lax.all_gather(out_weight, "patch", axis=1, tiled=True), preferred_element_type=jnp.float32
    )
    column_share = lax.psum_scatter(partial_terms, "head", scatter_dimension=1, tiled=True)
    return (out_gate * (column_share + out_bias)).astype(jnp.bfloat16)


def aligned(value, step):
    return pl.multiple_of(value * step, step)


def place():
    me = lax.axis_index("patch")
    return me // SPREAD, lax.rem(me, SPREAD)


def pack_kernel(queries_hbm, codes_hbm, exponents_hbm, *rest):
    outs, (codes, queries, exponents, held, sems) = rest[:-5], rest[-5:]
    groups, kinds, rows, width = held.shape
    group, _ = place()
    per = width // HD
    copies = [
        pltpu.make_async_copy(exponents_hbm, exponents, sems.at[0]),
        pltpu.make_async_copy(codes_hbm, codes, sems.at[1]),
        pltpu.make_async_copy(queries_hbm, queries, sems.at[2]),
    ]
    for copy in copies:
        copy.start()
    copies[0].wait()
    copies[1].wait()
    eye = lax.broadcasted_iota(jnp.int32, (rows, rows), 0) == lax.broadcasted_iota(jnp.int32, (rows, rows), 1)
    eye = eye.astype(jnp.float32).astype(jnp.bfloat16)
    for kind in range(kinds - 1):
        scales = jnp.left_shift(1, exponents[:, kind, :] + 16).astype(jnp.float32) * (2.0**-16)
        scales = lax.dot_general(eye, scales.astype(jnp.bfloat16), NT, preferred_element_type=jnp.float32)
        for head in range(groups * per):
            inside = slice((head % per) * HD, (head % per + 1) * HD)
            whole = slice(head * HD, (head + 1) * HD)
            decoded = codes[kind, :, whole].astype(jnp.float32) * scales[:, head : head + 1]
            held[head // per, kind, :, inside] = decoded.astype(jnp.bfloat16)
    copies[2].wait()
    for target in range(groups):
        held[target, kinds - 1] = queries[:, target * width : (target + 1) * width]
    for turn in range(groups):
        outs[turn][...] = held[jnp.bitwise_xor(group, turn)]
    outs[groups][...] = held[group, 0 : kinds - 1]


def pack(groups, queries, codes, exponents):
    rows, width = queries.shape
    kinds = codes.shape[0]
    share = width // groups
    bf16 = jnp.bfloat16
    exponents = exponents.transpose(2, 0, 1)
    shapes = [(kinds + 1, rows, share)] * groups + [(kinds, rows, share)]
    outs = pl.pallas_call(
        pack_kernel,
        out_shape=[jax.ShapeDtypeStruct(shape, bf16) for shape in shapes],
        in_specs=[HBM] * 3,
        out_specs=[VMEM] * len(shapes),
        scratch_shapes=[
            pltpu.VMEM(codes.shape, jnp.int32),
            pltpu.VMEM(queries.shape, bf16),
            pltpu.VMEM(exponents.shape, jnp.int32),
            pltpu.VMEM((groups, kinds + 1, rows, share), bf16),
            pltpu.SemaphoreType.DMA((3,)),
        ],
        compiler_params=pltpu.CompilerParams(vmem_limit_bytes=PACK_LIMIT),
        cost_estimate=pl.CostEstimate(flops=2 * codes.size, bytes_accessed=6 * codes.size, transcendentals=0),
    )(queries, codes, exponents)
    return outs


def pick_kernel(text_hbm, stale_hbm, text, stale, sems):
    group, spot = place()
    width = text.shape[2]
    groups = text_hbm.shape[2] // width
    rows = stale.shape[2] // groups
    columns = pl.ds(aligned(group, width), width)
    copies = [pltpu.make_async_copy(text_hbm.at[:, :, columns], text, sems.at[0])]
    for twist in range(SPREAD):
        for position in range(groups):
            origin = jnp.bitwise_xor(group, (groups - position) % groups)
            token = origin * SPREAD + jnp.bitwise_xor(spot, twist)
            copies.append(
                pltpu.make_async_copy(
                    stale_hbm.at[:, pl.ds(aligned(token, rows), rows), columns],
                    stale.at[twist, :, pl.ds(position * rows, rows), :],
                    sems.at[len(copies)],
                )
            )
    for copy in copies:
        copy.start()
    for copy in copies:
        copy.wait()


def pick(groups, text_kv, stale_kv):
    kinds, texts, heads_width = text_kv.shape
    width = heads_width // groups
    return pl.pallas_call(
        pick_kernel,
        out_shape=[
            jax.ShapeDtypeStruct((kinds, texts, width), jnp.bfloat16),
            jax.ShapeDtypeStruct((SPREAD, kinds, stale_kv.shape[1] // SPREAD, width), jnp.bfloat16),
        ],
        in_specs=[HBM] * 2,
        out_specs=[VMEM] * 2,
        scratch_shapes=[pltpu.SemaphoreType.DMA((1 + SPREAD * groups,))],
        compiler_params=pltpu.CompilerParams(vmem_limit_bytes=PICK_LIMIT),
        cost_estimate=pl.CostEstimate(flops=0, bytes_accessed=8 << 20, transcendentals=0),
    )(text_kv, stale_kv)


def merge_kernel(*refs):
    parts, (every, some, query) = refs[:-3], refs[-3:]
    groups, kinds, rows, _ = every.shape
    group, _ = place()
    for position, part in enumerate(parts):
        every[position] = part[0:kinds]
        if position:
            some[position - 1] = part[0:kinds]
        origin = jnp.bitwise_xor(group, (groups - position) % groups)
        query[pl.ds(aligned(origin, rows), rows), :] = part[kinds]


def merge(parts):
    kinds, rows, width = parts[0].shape
    shapes = [(len(parts), kinds - 1, rows, width), (len(parts) - 1, kinds - 1, rows, width), (len(parts) * rows, width)]
    return pl.pallas_call(
        merge_kernel,
        out_shape=[jax.ShapeDtypeStruct(shape, jnp.bfloat16) for shape in shapes],
        in_specs=[VMEM] * len(parts),
        out_specs=[VMEM] * 3,
        compiler_params=pltpu.CompilerParams(vmem_limit_bytes=SMALL),
        cost_estimate=pl.CostEstimate(flops=0, bytes_accessed=4 * len(parts) * parts[0].size, transcendentals=0),
    )(*parts)


def absorb(queries, segments, states):
    scores = [
        [
            lax.dot_general(
                query if key.shape[1] == HD else jnp.concatenate([query, query], axis=1),
                key,
                NT,
                preferred_element_type=jnp.float32,
            )
            * HD**-0.5
            for key, _ in parts
        ]
        for query, parts in zip(queries, segments)
    ]
    peaks = [[jnp.max(score, axis=1, keepdims=True) for score in row] for row in scores]
    if states is not None:
        peaks = [row + [state[0]] for row, state in zip(peaks, states)]
    peaks = [functools.reduce(jnp.maximum, row) for row in peaks]
    weights = [
        [jnp.exp(score - peak).astype(jnp.bfloat16) for score in row] for row, peak in zip(scores, peaks)
    ]
    totals = [sum(jnp.sum(w.astype(jnp.float32), axis=1, keepdims=True) for w in row) for row in weights]
    mixes = [
        sum(jnp.dot(w, value, preferred_element_type=jnp.float32) for w, (_, value) in zip(row, parts))
        for row, parts in zip(weights, segments)
    ]
    if states is not None:
        fades = [jnp.exp(state[0] - peak) for state, peak in zip(states, peaks)]
        totals = [total + state[1] * fade for total, state, fade in zip(totals, states, fades)]
        mixes = [mix + state[2] * fade for mix, state, fade in zip(mixes, states, fades)]
    return list(zip(peaks, totals, mixes))


def columns_of(width):
    return [slice(start, start + HD) for start in range(0, width, HD)]


def image_segment(stale, twist, residual):
    def of(cols):
        key = jnp.concatenate([stale[twist, 0, :, cols], residual(0, cols)], axis=1)
        value = stale[twist, 1, :, cols].astype(jnp.float32) + residual(1, cols).astype(jnp.float32)
        return key, value.astype(jnp.bfloat16)

    return of


def whole_part(part):
    return lambda kind, cols: part[:, kind, :, cols].reshape(-1, HD)


def split_part(own, some):
    return lambda kind, cols: jnp.concatenate([own[kind, :, cols], some[:, kind, :, cols].reshape(-1, HD)], axis=0)


def near_kernel(query, every, near, text, stale, peak, total, mixed):
    heads = columns_of(query.shape[1])
    images = [image_segment(stale, 0, whole_part(every)), image_segment(stale, 1, whole_part(near))]
    segments = [[(text[0, :, cols], text[1, :, cols])] + [image(cols) for image in images] for cols in heads]
    states = absorb([query[:, cols] for cols in heads], segments, None)
    for head, state in enumerate(states):
        peak[head], total[head], mixed[head] = state


def middle_kernel(query, own_far, some_far, stale, peak_in, total_in, mixed_in, peak, total, mixed):
    heads = columns_of(query.shape[1])
    image = image_segment(stale, 2, split_part(own_far, some_far))
    segments = [[image(cols)] for cols in heads]
    states = [(peak_in[head], total_in[head], mixed_in[head]) for head in range(len(heads))]
    states = absorb([query[:, cols] for cols in heads], segments, states)
    for head, state in enumerate(states):
        peak[head], total[head], mixed[head] = state


def last_kernel(query, own_corner, some_corner, stale, peak, total, mixed, out):
    heads = columns_of(query.shape[1])
    image = image_segment(stale, 3, split_part(own_corner, some_corner))
    states = [(peak[head], total[head], mixed[head]) for head in range(len(heads))]
    states = absorb([query[:, cols] for cols in heads], [[image(cols)] for cols in heads], states)
    for cols, (_, sums, mix) in zip(heads, states):
        out[:, cols] = (mix / sums).astype(jnp.bfloat16)


def attend_call(kernel, operands, shapes, keys):
    tokens, width = operands[0].shape
    return pl.pallas_call(
        kernel,
        out_shape=shapes,
        in_specs=[VMEM] * len(operands),
        out_specs=[VMEM] * len(shapes),
        compiler_params=pltpu.CompilerParams(vmem_limit_bytes=SMALL),
        cost_estimate=pl.CostEstimate(
            flops=8 * tokens * width * keys, bytes_accessed=8 * width * keys, transcendentals=tokens * keys * width // HD
        ),
    )(*operands)


def state_shapes(query):
    tokens, width = query.shape
    heads = width // HD
    return [jax.ShapeDtypeStruct((heads, tokens, size), jnp.float32) for size in (1, 1, HD)]


def order_kernel(*refs):
    pieces, out = refs[:-1], refs[-1]
    _, spot = place()
    span = out.shape[0] // SPREAD
    for twist, piece in enumerate(pieces):
        out[pl.ds(aligned(jnp.bitwise_xor(spot, twist), span), span), :] = piece[...]


def order(pieces):
    span, depth = pieces[0].shape
    shape = (SPREAD * span, depth)
    return pl.pallas_call(
        order_kernel,
        out_shape=jax.ShapeDtypeStruct(shape, jnp.bfloat16),
        in_specs=[VMEM] * len(pieces),
        out_specs=VMEM,
        compiler_params=pltpu.CompilerParams(vmem_limit_bytes=SMALL),
        cost_estimate=pl.CostEstimate(flops=0, bytes_accessed=4 * shape[0] * depth, transcendentals=0),
    )(*pieces)


def term_of(part, weight, turn):
    group, _ = place()
    width = part.shape[1]
    columns = pl.ds(aligned(jnp.bitwise_xor(group, turn), width), width)
    return lax.dot_general(part[...], weight[:, columns], NT, preferred_element_type=jnp.float32)


def begin_kernel(own, third, weight, out):
    out[...] = term_of(own, weight, 0) + term_of(third, weight, 3)


def begin(parts, weight):
    tokens = parts[0].shape[0]
    columns, depth = weight.shape
    return pl.pallas_call(
        begin_kernel,
        out_shape=jax.ShapeDtypeStruct((tokens, columns), jnp.float32),
        in_specs=[VMEM] * (len(parts) + 1),
        out_specs=VMEM,
        compiler_params=pltpu.CompilerParams(vmem_limit_bytes=SMALL),
        cost_estimate=pl.CostEstimate(
            flops=2 * tokens * columns * depth, bytes_accessed=4 * tokens * columns, transcendentals=0
        ),
    )(*parts, weight)


def close_kernel(partial, second, first, weight, *rest):
    outs, total = rest[:-1], rest[-1]
    group, _ = place()
    rows = outs[0].shape[0]
    total[...] = (partial[...] + term_of(second, weight, 2) + term_of(first, weight, 1)).astype(jnp.bfloat16)
    for turn, out in enumerate(outs):
        out[...] = total[pl.ds(aligned(jnp.bitwise_xor(group, turn), rows), rows), :]


def close(groups, partial, second, first, weight):
    tokens, columns = partial.shape
    return pl.pallas_call(
        close_kernel,
        out_shape=[jax.ShapeDtypeStruct((tokens // groups, columns), jnp.bfloat16)] * groups,
        in_specs=[VMEM] * 4,
        out_specs=[VMEM] * groups,
        scratch_shapes=[pltpu.VMEM((tokens, columns), jnp.bfloat16)],
        compiler_params=pltpu.CompilerParams(vmem_limit_bytes=SMALL),
        cost_estimate=pl.CostEstimate(
            flops=tokens * weight.size, bytes_accessed=8 * tokens * columns, transcendentals=0
        ),
    )(partial, second, first, weight)


def divide_kernel(*refs):
    parts, (keep, send, held) = refs[:-3], refs[-3:]
    group, _ = place()
    half = lax.axis_index("head")
    blocks = keep.shape[0]
    for position, part in enumerate(parts):
        held[jnp.bitwise_xor(group, (len(parts) - position) % len(parts))] = part[...]
    for block in range(blocks):
        keep[block] = held[half * blocks + block]
        send[block] = held[(1 - half) * blocks + block]


def divide(parts):
    groups = len(parts)
    shape = jax.ShapeDtypeStruct((groups // 2, *parts[0].shape), jnp.bfloat16)
    return pl.pallas_call(
        divide_kernel,
        out_shape=[shape] * 2,
        in_specs=[VMEM] * groups,
        out_specs=[VMEM] * 2,
        scratch_shapes=[pltpu.VMEM((groups, *parts[0].shape), jnp.bfloat16)],
        compiler_params=pltpu.CompilerParams(vmem_limit_bytes=SMALL),
        cost_estimate=pl.CostEstimate(flops=0, bytes_accessed=4 * groups * parts[0].size, transcendentals=0),
    )(*parts)


def finish_kernel(kept, arrived, bias, gate, out):
    blocks, _, columns = kept.shape
    for block in range(blocks):
        cols = slice(block * columns, (block + 1) * columns)
        total = kept[block].astype(jnp.float32) + arrived[block].astype(jnp.float32)
        out[:, cols] = (gate[:, cols] * (total + bias[:, cols])).astype(jnp.bfloat16)


def finish(kept, arrived, bias, gate):
    blocks, rows, columns = kept.shape
    width = blocks * columns
    return pl.pallas_call(
        finish_kernel,
        out_shape=jax.ShapeDtypeStruct((rows, width), jnp.bfloat16),
        in_specs=[VMEM] * 4,
        out_specs=VMEM,
        compiler_params=pltpu.CompilerParams(vmem_limit_bytes=SMALL),
        cost_estimate=pl.CostEstimate(flops=3 * rows * width, bytes_accessed=4 * rows * width, transcendentals=0),
    )(kept, arrived, bias.reshape(1, width), gate.reshape(1, width))


def after(value, *others):
    return lax.optimization_barrier((value, *others))[0]


def grouped_body(queries, stale_kv, codes, exponents, text_kv, out_weight, out_bias, out_gate):
    groups = lax.axis_size("patch") // SPREAD
    size = groups * SPREAD

    def swap(value, twist):
        return lax.ppermute(value, "patch", [(p, p ^ twist) for p in range(size)])

    def along(values):
        return [swap(values[turn], turn * SPREAD) for turn in reversed(range(1, groups))]

    weight = out_weight.T
    weight_far = swap(weight, 2)
    *packed, own = pack(groups, queries, codes, exponents)
    text, stale = pick(groups, text_kv, stale_kv)

    every, some, query = merge([packed[0], *along(packed)])
    own_far = swap(own, 2)

    ready = (every, some, query, weight, weight_far, own_far, text, stale)
    every, some, query, weight, weight_far = lax.optimization_barrier(ready)[:5]
    near, some_far = swap(every, 1), swap(some, 2)
    share = stale.shape[2]
    operands = [query, every, near, text, stale]
    state = attend_call(near_kernel, operands, state_shapes(query), 2 * share + text.shape[1])

    some_far, own_far = lax.optimization_barrier((some_far, own_far, *state))[:2]
    own_corner, some_corner = swap(own_far, 1), swap(some_far, 1)
    state = attend_call(middle_kernel, [query, own_far, some_far, stale, *state], state_shapes(query), share)
    weight, weight_far = lax.optimization_barrier((weight, weight_far, own_corner, some_corner, *state))[:2]
    weight_near, weight_corner = swap(weight, 1), swap(weight_far, 1)
    operands = [query, own_corner, some_corner, stale, *state]
    shape = jax.ShapeDtypeStruct(query.shape, jnp.bfloat16)
    (attended,) = attend_call(last_kernel, operands, [shape], share)

    third, second, first = along([attended] * groups)
    weight = order([weight, weight_near, weight_far, weight_corner])
    terms = close(groups, begin([attended, third], weight), second, first, weight)
    kept, sent = divide([terms[0], *along(terms)])
    received = lax.ppermute(sent, "head", [(0, 1), (1, 0)])
    return finish(kept, received, out_bias, out_gate)


def solution(mesh):
    patches, halves = mesh.shape["patch"], mesh.shape["head"]
    placed = (
        P("patch", "head"),
        P(None, None, "head"),
        P(None, "patch", "head"),
        P(None, "patch", "head"),
        P(None, None, "head"),
        P("head", "patch"),
        P("head"),
        P("head"),
    )

    def body(*args):
        heads = args[0].shape[1] // HD
        groups = patches // SPREAD
        if groups != 4 or patches % SPREAD or heads % groups or halves != 2:
            return plain_body(*args)
        return grouped_body(*args)

    return jax.shard_map(body, mesh=mesh, in_specs=placed, out_specs=P("patch", "head"), check_vma=False)
```

```python
import functools

import jax
import jax.numpy as jnp
from jax import lax
from jax.experimental import pallas as pl
from jax.experimental.pallas import tpu as pltpu
from jax.sharding import PartitionSpec as P

HD = 128
SPREAD = 4
TURNS = (0, 2, 3, 1)
PACK_LIMIT = 56 << 20
SMALL = 16 << 20
PICK_LIMIT = 50 << 20
VMEM = pl.BlockSpec(memory_space=pltpu.VMEM)
HBM = pl.BlockSpec(memory_space=pltpu.HBM)
NT = (((1,), (1,)), ((), ()))


def plain_body(queries, stale_kv, codes, exponents, text_kv, out_weight, out_bias, out_gate):
    tok_rows = queries.shape[0]
    row_width = queries.shape[1]
    head_count = row_width // HD
    text_count = text_kv.shape[1]
    scale_factor = HD ** (-0.5)
    blocks = jnp.exp2(exponents.astype(jnp.float32))
    decoded = codes.astype(jnp.float32).reshape(2, tok_rows, head_count, HD) * blocks[..., None]
    decoded = decoded.astype(jnp.bfloat16).reshape(2, tok_rows, row_width)
    arrived = lax.all_gather(decoded, "patch", axis=1, tiled=True)
    all_rows = arrived.shape[1]
    query_heads = queries.reshape(tok_rows, head_count, HD)
    text_heads = text_kv.reshape(2, text_count, head_count, HD)
    stale_heads = stale_kv.reshape(2, all_rows, head_count, HD)
    arrived_heads = arrived.reshape(2, all_rows, head_count, HD)
    text_scores = jnp.einsum("thd,khd->htk", query_heads, text_heads[0], preferred_element_type=jnp.float32)
    rebuilt = stale_heads.astype(jnp.float32) + arrived_heads.astype(jnp.float32)
    image_scores = jnp.einsum(
        "thd,khd->htk", query_heads.astype(jnp.float32), rebuilt[0], precision=lax.Precision.HIGHEST
    )
    scores = jnp.concatenate([text_scores, image_scores], axis=2) * scale_factor
    row_peak = jnp.max(scores, axis=2, keepdims=True)
    weights = jnp.exp(scores - row_peak).astype(jnp.bfloat16)
    row_total = jnp.sum(weights.astype(jnp.float32), axis=2)
    text_part = jnp.einsum(
        "htk,khd->thd", weights[:, :, :text_count], text_heads[1], preferred_element_type=jnp.float32
    )
    image_part = jnp.einsum(
        "htk,khd->thd",
        weights[:, :, text_count:].astype(jnp.float32),
        rebuilt[1],
        precision=lax.Precision.HIGHEST,
    )
    attended = ((text_part + image_part) / row_total.T[:, :, None]).astype(jnp.bfloat16).reshape(tok_rows, row_width)
    partial_terms = jnp.dot(
        attended, lax.all_gather(out_weight, "patch", axis=1, tiled=True), preferred_element_type=jnp.float32
    )
    column_share = lax.psum_scatter(partial_terms, "head", scatter_dimension=1, tiled=True)
    return (out_gate * (column_share + out_bias)).astype(jnp.bfloat16)


def aligned(value, step):
    return pl.multiple_of(value * step, step)


def place():
    me = lax.axis_index("patch")
    return me // SPREAD, lax.rem(me, SPREAD)


def pack_kernel(queries_hbm, codes_hbm, exponents_hbm, *rest):
    outs, (codes, queries, exponents, held, sems) = rest[:-5], rest[-5:]
    groups, kinds, rows, width = held.shape
    group, _ = place()
    per = width // HD
    copies = [
        pltpu.make_async_copy(exponents_hbm, exponents, sems.at[0]),
        pltpu.make_async_copy(codes_hbm, codes, sems.at[1]),
        pltpu.make_async_copy(queries_hbm, queries, sems.at[2]),
    ]
    for copy in copies:
        copy.start()
    copies[0].wait()
    copies[1].wait()
    eye = lax.broadcasted_iota(jnp.int32, (rows, rows), 0) == lax.broadcasted_iota(jnp.int32, (rows, rows), 1)
    eye = eye.astype(jnp.float32).astype(jnp.bfloat16)
    for kind in range(kinds - 1):
        scales = jnp.left_shift(1, exponents[:, kind, :] + 16).astype(jnp.float32) * (2.0**-16)
        scales = lax.dot_general(eye, scales.astype(jnp.bfloat16), NT, preferred_element_type=jnp.float32)
        for head in range(groups * per):
            inside = slice((head % per) * HD, (head % per + 1) * HD)
            whole = slice(head * HD, (head + 1) * HD)
            decoded = codes[kind, :, whole].astype(jnp.float32) * scales[:, head : head + 1]
            held[head // per, kind, :, inside] = decoded.astype(jnp.bfloat16)
    copies[2].wait()
    for target in range(groups):
        held[target, kinds - 1] = queries[:, target * width : (target + 1) * width]
    for turn in range(groups):
        outs[turn][...] = held[jnp.bitwise_xor(group, turn)]
    outs[groups][...] = held[group, 0 : kinds - 1]


def pack(groups, queries, codes, exponents):
    rows, width = queries.shape
    kinds = codes.shape[0]
    share = width // groups
    bf16 = jnp.bfloat16
    exponents = exponents.transpose(2, 0, 1)
    shapes = [(kinds + 1, rows, share)] * groups + [(kinds, rows, share)]
    outs = pl.pallas_call(
        pack_kernel,
        out_shape=[jax.ShapeDtypeStruct(shape, bf16) for shape in shapes],
        in_specs=[HBM] * 3,
        out_specs=[VMEM] * len(shapes),
        scratch_shapes=[
            pltpu.VMEM(codes.shape, jnp.int32),
            pltpu.VMEM(queries.shape, bf16),
            pltpu.VMEM(exponents.shape, jnp.int32),
            pltpu.VMEM((groups, kinds + 1, rows, share), bf16),
            pltpu.SemaphoreType.DMA((3,)),
        ],
        compiler_params=pltpu.CompilerParams(vmem_limit_bytes=PACK_LIMIT),
        cost_estimate=pl.CostEstimate(flops=2 * codes.size, bytes_accessed=6 * codes.size, transcendentals=0),
    )(queries, codes, exponents)
    return outs


def pick_kernel(text_hbm, stale_hbm, text, stale, sems):
    group, spot = place()
    width = text.shape[2]
    groups = text_hbm.shape[2] // width
    rows = stale.shape[2] // groups
    columns = pl.ds(aligned(group, width), width)
    copies = [pltpu.make_async_copy(text_hbm.at[:, :, columns], text, sems.at[0])]
    for twist in range(SPREAD):
        for position in range(groups):
            origin = jnp.bitwise_xor(group, TURNS[position])
            token = origin * SPREAD + jnp.bitwise_xor(spot, twist)
            copies.append(
                pltpu.make_async_copy(
                    stale_hbm.at[:, pl.ds(aligned(token, rows), rows), columns],
                    stale.at[twist, :, pl.ds(position * rows, rows), :],
                    sems.at[len(copies)],
                )
            )
    for copy in copies:
        copy.start()
    for copy in copies:
        copy.wait()


def pick(groups, text_kv, stale_kv):
    kinds, texts, heads_width = text_kv.shape
    width = heads_width // groups
    return pl.pallas_call(
        pick_kernel,
        out_shape=[
            jax.ShapeDtypeStruct((kinds, texts, width), jnp.bfloat16),
            jax.ShapeDtypeStruct((SPREAD, kinds, stale_kv.shape[1] // SPREAD, width), jnp.bfloat16),
        ],
        in_specs=[HBM] * 2,
        out_specs=[VMEM] * 2,
        scratch_shapes=[pltpu.SemaphoreType.DMA((1 + SPREAD * groups,))],
        compiler_params=pltpu.CompilerParams(vmem_limit_bytes=PICK_LIMIT),
        cost_estimate=pl.CostEstimate(flops=0, bytes_accessed=8 << 20, transcendentals=0),
    )(text_kv, stale_kv)


def merge_kernel(*refs):
    parts, (every, some, query) = refs[:-3], refs[-3:]
    groups, kinds, rows, _ = every.shape
    group, _ = place()
    for position, part in enumerate(parts):
        every[position] = part[0:kinds]
        if position:
            some[position - 1] = part[0:kinds]
        origin = jnp.bitwise_xor(group, TURNS[position])
        query[pl.ds(aligned(origin, rows), rows), :] = part[kinds]


def merge(parts):
    kinds, rows, width = parts[0].shape
    shapes = [(len(parts), kinds - 1, rows, width), (len(parts) - 1, kinds - 1, rows, width), (len(parts) * rows, width)]
    return pl.pallas_call(
        merge_kernel,
        out_shape=[jax.ShapeDtypeStruct(shape, jnp.bfloat16) for shape in shapes],
        in_specs=[VMEM] * len(parts),
        out_specs=[VMEM] * 3,
        compiler_params=pltpu.CompilerParams(vmem_limit_bytes=SMALL),
        cost_estimate=pl.CostEstimate(flops=0, bytes_accessed=4 * len(parts) * parts[0].size, transcendentals=0),
    )(*parts)


def absorb(queries, segments, states):
    scores = [
        [
            lax.dot_general(
                query if key.shape[1] == HD else jnp.concatenate([query, query], axis=1),
                key,
                NT,
                preferred_element_type=jnp.float32,
            )
            * HD**-0.5
            for key, _ in parts
        ]
        for query, parts in zip(queries, segments)
    ]
    peaks = [[jnp.max(score, axis=1, keepdims=True) for score in row] for row in scores]
    if states is not None:
        peaks = [row + [state[0]] for row, state in zip(peaks, states)]
    peaks = [functools.reduce(jnp.maximum, row) for row in peaks]
    weights = [
        [jnp.exp(score - peak).astype(jnp.bfloat16) for score in row] for row, peak in zip(scores, peaks)
    ]
    totals = [sum(jnp.sum(w.astype(jnp.float32), axis=1, keepdims=True) for w in row) for row in weights]
    mixes = [
        sum(jnp.dot(w, value, preferred_element_type=jnp.float32) for w, (_, value) in zip(row, parts))
        for row, parts in zip(weights, segments)
    ]
    if states is not None:
        fades = [jnp.exp(state[0] - peak) for state, peak in zip(states, peaks)]
        totals = [total + state[1] * fade for total, state, fade in zip(totals, states, fades)]
        mixes = [mix + state[2] * fade for mix, state, fade in zip(mixes, states, fades)]
    return list(zip(peaks, totals, mixes))


def columns_of(width):
    return [slice(start, start + HD) for start in range(0, width, HD)]


def image_segment(stale, twist, residual):
    def of(cols):
        key = jnp.concatenate([stale[twist, 0, :, cols], residual(0, cols)], axis=1)
        value = stale[twist, 1, :, cols].astype(jnp.float32) + residual(1, cols).astype(jnp.float32)
        return key, value.astype(jnp.bfloat16)

    return of


def whole_part(part):
    return lambda kind, cols: part[:, kind, :, cols].reshape(-1, HD)


def split_part(own, some):
    return lambda kind, cols: jnp.concatenate([own[kind, :, cols], some[:, kind, :, cols].reshape(-1, HD)], axis=0)


def near_kernel(query, every, near, text, stale, peak, total, mixed):
    heads = columns_of(query.shape[1])
    images = [image_segment(stale, 0, whole_part(every)), image_segment(stale, 1, whole_part(near))]
    segments = [[(text[0, :, cols], text[1, :, cols])] + [image(cols) for image in images] for cols in heads]
    states = absorb([query[:, cols] for cols in heads], segments, None)
    for head, state in enumerate(states):
        peak[head], total[head], mixed[head] = state


def middle_kernel(query, own_far, some_far, stale, peak_in, total_in, mixed_in, peak, total, mixed):
    heads = columns_of(query.shape[1])
    image = image_segment(stale, 2, split_part(own_far, some_far))
    segments = [[image(cols)] for cols in heads]
    states = [(peak_in[head], total_in[head], mixed_in[head]) for head in range(len(heads))]
    states = absorb([query[:, cols] for cols in heads], segments, states)
    for head, state in enumerate(states):
        peak[head], total[head], mixed[head] = state


def last_kernel(query, own_corner, some_corner, stale, peak, total, mixed, out, most):
    heads = columns_of(query.shape[1])
    image = image_segment(stale, 3, split_part(own_corner, some_corner))
    states = [(peak[head], total[head], mixed[head]) for head in range(len(heads))]
    states = absorb([query[:, cols] for cols in heads], [[image(cols)] for cols in heads], states)
    for cols, (_, sums, mix) in zip(heads, states):
        value = (mix / sums).astype(jnp.bfloat16)
        out[:, cols] = value
        if cols is not heads[-1]:
            most[:, cols] = value


def attend_call(kernel, operands, shapes, keys):
    tokens, width = operands[0].shape
    return pl.pallas_call(
        kernel,
        out_shape=shapes,
        in_specs=[VMEM] * len(operands),
        out_specs=[VMEM] * len(shapes),
        compiler_params=pltpu.CompilerParams(vmem_limit_bytes=SMALL),
        cost_estimate=pl.CostEstimate(
            flops=8 * tokens * width * keys, bytes_accessed=8 * width * keys, transcendentals=tokens * keys * width // HD
        ),
    )(*operands)


def state_shapes(query):
    tokens, width = query.shape
    heads = width // HD
    return [jax.ShapeDtypeStruct((heads, tokens, size), jnp.float32) for size in (1, 1, HD)]


def order_kernel(*refs):
    pieces, out = refs[:-1], refs[-1]
    _, spot = place()
    span = out.shape[0] // SPREAD
    for twist, piece in enumerate(pieces):
        out[pl.ds(aligned(jnp.bitwise_xor(spot, twist), span), span), :] = piece[...]


def order(pieces):
    span, depth = pieces[0].shape
    shape = (SPREAD * span, depth)
    return pl.pallas_call(
        order_kernel,
        out_shape=jax.ShapeDtypeStruct(shape, jnp.bfloat16),
        in_specs=[VMEM] * len(pieces),
        out_specs=VMEM,
        compiler_params=pltpu.CompilerParams(vmem_limit_bytes=SMALL),
        cost_estimate=pl.CostEstimate(flops=0, bytes_accessed=4 * shape[0] * depth, transcendentals=0),
    )(*pieces)


def term_of(part, weight, turn, width, skip=0):
    group, _ = place()
    start = jnp.bitwise_xor(group, turn) * width + skip
    columns = pl.ds(pl.multiple_of(start, HD), part.shape[1])
    return lax.dot_general(part[...], weight[:, columns], NT, preferred_element_type=jnp.float32)


def begin_kernel(own, second, first, weight, out):
    width = own.shape[1]
    out[...] = term_of(own, weight, 0, width) + term_of(second, weight, 2, width) + term_of(first, weight, 1, width)


def begin(parts, weight):
    tokens = parts[0].shape[0]
    columns, depth = weight.shape
    return pl.pallas_call(
        begin_kernel,
        out_shape=jax.ShapeDtypeStruct((tokens, columns), jnp.float32),
        in_specs=[VMEM] * (len(parts) + 1),
        out_specs=VMEM,
        compiler_params=pltpu.CompilerParams(vmem_limit_bytes=SMALL),
        cost_estimate=pl.CostEstimate(
            flops=2 * tokens * columns * depth, bytes_accessed=4 * tokens * columns, transcendentals=0
        ),
    )(*parts, weight)


def close_kernel(partial, most, last, weight, *rest):
    outs, total = rest[:-1], rest[-1]
    group, _ = place()
    rows = outs[0].shape[0]
    width = most.shape[1] + last.shape[1]
    added = partial[...] + term_of(most, weight, 3, width) + term_of(last, weight, 3, width, width - HD)
    total[...] = added.astype(jnp.bfloat16)
    for turn, out in enumerate(outs):
        out[...] = total[pl.ds(aligned(jnp.bitwise_xor(group, turn), rows), rows), :]


def close(groups, partial, most, last, weight):
    tokens, columns = partial.shape
    return pl.pallas_call(
        close_kernel,
        out_shape=[jax.ShapeDtypeStruct((tokens // groups, columns), jnp.bfloat16)] * groups,
        in_specs=[VMEM] * 4,
        out_specs=[VMEM] * groups,
        scratch_shapes=[pltpu.VMEM((tokens, columns), jnp.bfloat16)],
        compiler_params=pltpu.CompilerParams(vmem_limit_bytes=SMALL),
        cost_estimate=pl.CostEstimate(
            flops=tokens * weight.size, bytes_accessed=8 * tokens * columns, transcendentals=0
        ),
    )(partial, most, last, weight)


def divide_kernel(*refs):
    parts, (keep, send, held) = refs[:-3], refs[-3:]
    group, _ = place()
    half = lax.axis_index("head")
    blocks = keep.shape[0]
    for position, part in enumerate(parts):
        held[jnp.bitwise_xor(group, TURNS[position])] = part[...]
    for block in range(blocks):
        keep[block] = held[half * blocks + block]
        send[block] = held[(1 - half) * blocks + block]


def divide(parts):
    groups = len(parts)
    shape = jax.ShapeDtypeStruct((groups // 2, *parts[0].shape), jnp.bfloat16)
    return pl.pallas_call(
        divide_kernel,
        out_shape=[shape] * 2,
        in_specs=[VMEM] * groups,
        out_specs=[VMEM] * 2,
        scratch_shapes=[pltpu.VMEM((groups, *parts[0].shape), jnp.bfloat16)],
        compiler_params=pltpu.CompilerParams(vmem_limit_bytes=SMALL),
        cost_estimate=pl.CostEstimate(flops=0, bytes_accessed=4 * groups * parts[0].size, transcendentals=0),
    )(*parts)


def finish_kernel(kept, arrived, bias, gate, out):
    blocks, _, columns = kept.shape
    for block in range(blocks):
        cols = slice(block * columns, (block + 1) * columns)
        total = kept[block].astype(jnp.float32) + arrived[block].astype(jnp.float32)
        out[:, cols] = (gate[:, cols] * (total + bias[:, cols])).astype(jnp.bfloat16)


def finish(kept, arrived, bias, gate):
    blocks, rows, columns = kept.shape
    width = blocks * columns
    return pl.pallas_call(
        finish_kernel,
        out_shape=jax.ShapeDtypeStruct((rows, width), jnp.bfloat16),
        in_specs=[VMEM] * 4,
        out_specs=VMEM,
        compiler_params=pltpu.CompilerParams(vmem_limit_bytes=SMALL),
        cost_estimate=pl.CostEstimate(flops=3 * rows * width, bytes_accessed=4 * rows * width, transcendentals=0),
    )(kept, arrived, bias.reshape(1, width), gate.reshape(1, width))


def after(value, *others):
    return lax.optimization_barrier((value, *others))[0]


def grouped_body(queries, stale_kv, codes, exponents, text_kv, out_weight, out_bias, out_gate):
    groups = lax.axis_size("patch") // SPREAD
    size = groups * SPREAD

    def swap(value, twist):
        return lax.ppermute(value, "patch", [(p, p ^ twist) for p in range(size)])

    def along(values):
        return [swap(values[turn], turn * SPREAD) for turn in TURNS[1:]]

    weight = out_weight.T
    weight_far = swap(weight, 2)
    *packed, own = pack(groups, queries, codes, exponents)
    text, stale = pick(groups, text_kv, stale_kv)

    every, some, query = merge([packed[0], *along(packed)])
    own_far = swap(own, 2)

    ready = (every, some, query, weight, weight_far, own_far, text, stale)
    every, some, query, weight, weight_far = lax.optimization_barrier(ready)[:5]
    near, some_far = swap(every, 1), swap(some, 2)
    share = stale.shape[2]
    operands = [query, every, near, text, stale]
    state = attend_call(near_kernel, operands, state_shapes(query), 2 * share + text.shape[1])

    some_far, own_far = lax.optimization_barrier((some_far, own_far, *state))[:2]
    own_corner, some_corner = swap(own_far, 1), swap(some_far, 1)
    state = attend_call(middle_kernel, [query, own_far, some_far, stale, *state], state_shapes(query), share)
    weight, weight_far = lax.optimization_barrier((weight, weight_far, own_corner, some_corner, *state))[:2]
    weight_near, weight_corner = swap(weight, 1), swap(weight_far, 1)
    operands = [query, own_corner, some_corner, stale, *state]
    tokens, width = query.shape
    shapes = [jax.ShapeDtypeStruct((tokens, size), jnp.bfloat16) for size in (width, width - HD)]
    attended, most = attend_call(last_kernel, operands, shapes, share)

    second, first, third = (swap(value, turn * SPREAD) for turn, value in ((2, attended), (1, attended), (3, most)))
    passed = swap(second[:, width - HD :], SPREAD)
    weight = order([weight, weight_near, weight_far, weight_corner])
    terms = close(groups, begin([attended, second, first], weight), third, passed, weight)
    kept, sent = divide([terms[0], *along(terms)])
    received = lax.ppermute(sent, "head", [(0, 1), (1, 0)])
    return finish(kept, received, out_bias, out_gate)


def solution(mesh):
    patches, halves = mesh.shape["patch"], mesh.shape["head"]
    placed = (
        P("patch", "head"),
        P(None, None, "head"),
        P(None, "patch", "head"),
        P(None, "patch", "head"),
        P(None, None, "head"),
        P("head", "patch"),
        P("head"),
        P("head"),
    )

    def body(*args):
        heads = args[0].shape[1] // HD
        groups = patches // SPREAD
        if groups != 4 or patches % SPREAD or heads % groups or halves != 2:
            return plain_body(*args)
        return grouped_body(*args)

    return jax.shard_map(body, mesh=mesh, in_specs=placed, out_specs=P("patch", "head"), check_vma=False)
```

```python
import functools

import jax
import jax.numpy as jnp
from jax import lax
from jax.experimental import pallas as pl
from jax.experimental.pallas import tpu as pltpu
from jax.sharding import PartitionSpec as P

HD = 128
SPREAD = 4
TURNS = (0, 2, 3, 1)
PACK_LIMIT = 56 << 20
SMALL = 16 << 20
PICK_LIMIT = 50 << 20
VMEM = pl.BlockSpec(memory_space=pltpu.VMEM)
HBM = pl.BlockSpec(memory_space=pltpu.HBM)
NT = (((1,), (1,)), ((), ()))


def plain_body(queries, stale_kv, codes, exponents, text_kv, out_weight, out_bias, out_gate):
    tok_rows = queries.shape[0]
    row_width = queries.shape[1]
    head_count = row_width // HD
    text_count = text_kv.shape[1]
    scale_factor = HD ** (-0.5)
    blocks = jnp.exp2(exponents.astype(jnp.float32))
    decoded = codes.astype(jnp.float32).reshape(2, tok_rows, head_count, HD) * blocks[..., None]
    decoded = decoded.astype(jnp.bfloat16).reshape(2, tok_rows, row_width)
    arrived = lax.all_gather(decoded, "patch", axis=1, tiled=True)
    all_rows = arrived.shape[1]
    query_heads = queries.reshape(tok_rows, head_count, HD)
    text_heads = text_kv.reshape(2, text_count, head_count, HD)
    stale_heads = stale_kv.reshape(2, all_rows, head_count, HD)
    arrived_heads = arrived.reshape(2, all_rows, head_count, HD)
    text_scores = jnp.einsum("thd,khd->htk", query_heads, text_heads[0], preferred_element_type=jnp.float32)
    rebuilt = stale_heads.astype(jnp.float32) + arrived_heads.astype(jnp.float32)
    image_scores = jnp.einsum(
        "thd,khd->htk", query_heads.astype(jnp.float32), rebuilt[0], precision=lax.Precision.HIGHEST
    )
    scores = jnp.concatenate([text_scores, image_scores], axis=2) * scale_factor
    row_peak = jnp.max(scores, axis=2, keepdims=True)
    weights = jnp.exp(scores - row_peak).astype(jnp.bfloat16)
    row_total = jnp.sum(weights.astype(jnp.float32), axis=2)
    text_part = jnp.einsum(
        "htk,khd->thd", weights[:, :, :text_count], text_heads[1], preferred_element_type=jnp.float32
    )
    image_part = jnp.einsum(
        "htk,khd->thd",
        weights[:, :, text_count:].astype(jnp.float32),
        rebuilt[1],
        precision=lax.Precision.HIGHEST,
    )
    attended = ((text_part + image_part) / row_total.T[:, :, None]).astype(jnp.bfloat16).reshape(tok_rows, row_width)
    partial_terms = jnp.dot(
        attended, lax.all_gather(out_weight, "patch", axis=1, tiled=True), preferred_element_type=jnp.float32
    )
    column_share = lax.psum_scatter(partial_terms, "head", scatter_dimension=1, tiled=True)
    return (out_gate * (column_share + out_bias)).astype(jnp.bfloat16)


def aligned(value, step):
    return pl.multiple_of(value * step, step)


def place():
    me = lax.axis_index("patch")
    return me // SPREAD, lax.rem(me, SPREAD)


def pack_kernel(queries_hbm, codes_hbm, exponents_hbm, *rest):
    outs, (codes, queries, exponents, held, sems) = rest[:-5], rest[-5:]
    groups, kinds, rows, width = held.shape
    group, _ = place()
    per = width // HD
    copies = [
        pltpu.make_async_copy(exponents_hbm, exponents, sems.at[0]),
        pltpu.make_async_copy(codes_hbm, codes, sems.at[1]),
        pltpu.make_async_copy(queries_hbm, queries, sems.at[2]),
    ]
    for copy in copies:
        copy.start()
    copies[0].wait()
    copies[1].wait()
    eye = lax.broadcasted_iota(jnp.int32, (rows, rows), 0) == lax.broadcasted_iota(jnp.int32, (rows, rows), 1)
    eye = eye.astype(jnp.float32).astype(jnp.bfloat16)
    for kind in range(kinds - 1):
        scales = jnp.left_shift(1, exponents[:, kind, :] + 16).astype(jnp.float32) * (2.0**-16)
        scales = lax.dot_general(eye, scales.astype(jnp.bfloat16), NT, preferred_element_type=jnp.float32)
        for head in range(groups * per):
            inside = slice((head % per) * HD, (head % per + 1) * HD)
            whole = slice(head * HD, (head + 1) * HD)
            decoded = codes[kind, :, whole].astype(jnp.float32) * scales[:, head : head + 1]
            held[head // per, kind, :, inside] = decoded.astype(jnp.bfloat16)
    copies[2].wait()
    for target in range(groups):
        held[target, kinds - 1] = queries[:, target * width : (target + 1) * width]
    for turn in range(groups):
        outs[turn][...] = held[jnp.bitwise_xor(group, turn)]
    outs[groups][...] = held[group, 0 : kinds - 1]


def pack(groups, queries, codes, exponents):
    rows, width = queries.shape
    kinds = codes.shape[0]
    share = width // groups
    bf16 = jnp.bfloat16
    exponents = exponents.transpose(2, 0, 1)
    shapes = [(kinds + 1, rows, share)] * groups + [(kinds, rows, share)]
    outs = pl.pallas_call(
        pack_kernel,
        out_shape=[jax.ShapeDtypeStruct(shape, bf16) for shape in shapes],
        in_specs=[HBM] * 3,
        out_specs=[VMEM] * len(shapes),
        scratch_shapes=[
            pltpu.VMEM(codes.shape, jnp.int32),
            pltpu.VMEM(queries.shape, bf16),
            pltpu.VMEM(exponents.shape, jnp.int32),
            pltpu.VMEM((groups, kinds + 1, rows, share), bf16),
            pltpu.SemaphoreType.DMA((3,)),
        ],
        compiler_params=pltpu.CompilerParams(vmem_limit_bytes=PACK_LIMIT),
        cost_estimate=pl.CostEstimate(flops=2 * codes.size, bytes_accessed=6 * codes.size, transcendentals=0),
    )(queries, codes, exponents)
    return outs


def pick_kernel(text_hbm, stale_hbm, text, stale, sems):
    group, spot = place()
    width = text.shape[2]
    groups = text_hbm.shape[2] // width
    rows = stale.shape[2] // groups
    columns = pl.ds(aligned(group, width), width)
    copies = [pltpu.make_async_copy(text_hbm.at[:, :, columns], text, sems.at[0])]
    for twist in range(SPREAD):
        for position in range(groups):
            origin = jnp.bitwise_xor(group, TURNS[position])
            token = origin * SPREAD + jnp.bitwise_xor(spot, twist)
            copies.append(
                pltpu.make_async_copy(
                    stale_hbm.at[:, pl.ds(aligned(token, rows), rows), columns],
                    stale.at[twist, :, pl.ds(position * rows, rows), :],
                    sems.at[len(copies)],
                )
            )
    for copy in copies:
        copy.start()
    for copy in copies:
        copy.wait()


def pick(groups, text_kv, stale_kv):
    kinds, texts, heads_width = text_kv.shape
    width = heads_width // groups
    return pl.pallas_call(
        pick_kernel,
        out_shape=[
            jax.ShapeDtypeStruct((kinds, texts, width), jnp.bfloat16),
            jax.ShapeDtypeStruct((SPREAD, kinds, stale_kv.shape[1] // SPREAD, width), jnp.bfloat16),
        ],
        in_specs=[HBM] * 2,
        out_specs=[VMEM] * 2,
        scratch_shapes=[pltpu.SemaphoreType.DMA((1 + SPREAD * groups,))],
        compiler_params=pltpu.CompilerParams(vmem_limit_bytes=PICK_LIMIT),
        cost_estimate=pl.CostEstimate(flops=0, bytes_accessed=8 << 20, transcendentals=0),
    )(text_kv, stale_kv)


def merge_kernel(*refs):
    parts, (every, some, query) = refs[:-3], refs[-3:]
    groups, kinds, rows, _ = every.shape
    group, _ = place()
    for position, part in enumerate(parts):
        every[position] = part[0:kinds]
        if position:
            some[position - 1] = part[0:kinds]
        origin = jnp.bitwise_xor(group, TURNS[position])
        query[pl.ds(aligned(origin, rows), rows), :] = part[kinds]


def merge(parts):
    kinds, rows, width = parts[0].shape
    shapes = [(len(parts), kinds - 1, rows, width), (len(parts) - 1, kinds - 1, rows, width), (len(parts) * rows, width)]
    return pl.pallas_call(
        merge_kernel,
        out_shape=[jax.ShapeDtypeStruct(shape, jnp.bfloat16) for shape in shapes],
        in_specs=[VMEM] * len(parts),
        out_specs=[VMEM] * 3,
        compiler_params=pltpu.CompilerParams(vmem_limit_bytes=SMALL),
        cost_estimate=pl.CostEstimate(flops=0, bytes_accessed=4 * len(parts) * parts[0].size, transcendentals=0),
    )(*parts)


def absorb(queries, segments, states):
    scores = [
        [
            lax.dot_general(
                query if key.shape[1] == HD else jnp.concatenate([query, query], axis=1),
                key,
                NT,
                preferred_element_type=jnp.float32,
            )
            * HD**-0.5
            for key, _ in parts
        ]
        for query, parts in zip(queries, segments)
    ]
    peaks = [[jnp.max(score, axis=1, keepdims=True) for score in row] for row in scores]
    if states is not None:
        peaks = [row + [state[0]] for row, state in zip(peaks, states)]
    peaks = [functools.reduce(jnp.maximum, row) for row in peaks]
    weights = [
        [jnp.exp(score - peak).astype(jnp.bfloat16) for score in row] for row, peak in zip(scores, peaks)
    ]
    totals = [sum(jnp.sum(w.astype(jnp.float32), axis=1, keepdims=True) for w in row) for row in weights]
    mixes = [
        sum(jnp.dot(w, value, preferred_element_type=jnp.float32) for w, (_, value) in zip(row, parts))
        for row, parts in zip(weights, segments)
    ]
    if states is not None:
        fades = [jnp.exp(state[0] - peak) for state, peak in zip(states, peaks)]
        totals = [total + state[1] * fade for total, state, fade in zip(totals, states, fades)]
        mixes = [mix + state[2] * fade for mix, state, fade in zip(mixes, states, fades)]
    return list(zip(peaks, totals, mixes))


def columns_of(width):
    return [slice(start, start + HD) for start in range(0, width, HD)]


def image_segment(stale, twist, residual):
    def of(cols):
        key = jnp.concatenate([stale[twist, 0, :, cols], residual(0, cols)], axis=1)
        value = stale[twist, 1, :, cols].astype(jnp.float32) + residual(1, cols).astype(jnp.float32)
        return key, value.astype(jnp.bfloat16)

    return of


def whole_part(part):
    return lambda kind, cols: part[:, kind, :, cols].reshape(-1, HD)


def split_part(own, some):
    return lambda kind, cols: jnp.concatenate([own[kind, :, cols], some[:, kind, :, cols].reshape(-1, HD)], axis=0)


def near_kernel(query, every, near, text, stale, peak, total, mixed):
    heads = columns_of(query.shape[1])
    images = [image_segment(stale, 0, whole_part(every)), image_segment(stale, 1, whole_part(near))]
    segments = [[(text[0, :, cols], text[1, :, cols])] + [image(cols) for image in images] for cols in heads]
    states = absorb([query[:, cols] for cols in heads], segments, None)
    for head, state in enumerate(states):
        peak[head], total[head], mixed[head] = state


def middle_kernel(query, own_far, some_far, stale, peak_in, total_in, mixed_in, peak, total, mixed):
    heads = columns_of(query.shape[1])
    image = image_segment(stale, 2, split_part(own_far, some_far))
    segments = [[image(cols)] for cols in heads]
    states = [(peak_in[head], total_in[head], mixed_in[head]) for head in range(len(heads))]
    states = absorb([query[:, cols] for cols in heads], segments, states)
    for head, state in enumerate(states):
        peak[head], total[head], mixed[head] = state


def last_kernel(query, own_corner, some_corner, stale, peak, total, mixed, out, most):
    heads = columns_of(query.shape[1])
    image = image_segment(stale, 3, split_part(own_corner, some_corner))
    states = [(peak[head], total[head], mixed[head]) for head in range(len(heads))]
    states = absorb([query[:, cols] for cols in heads], [[image(cols)] for cols in heads], states)
    for cols, (_, sums, mix) in zip(heads, states):
        value = (mix / sums).astype(jnp.bfloat16)
        out[:, cols] = value
        if cols is not heads[-1]:
            most[:, cols] = value


def attend_call(kernel, operands, shapes, keys):
    tokens, width = operands[0].shape
    return pl.pallas_call(
        kernel,
        out_shape=shapes,
        in_specs=[VMEM] * len(operands),
        out_specs=[VMEM] * len(shapes),
        compiler_params=pltpu.CompilerParams(vmem_limit_bytes=SMALL),
        cost_estimate=pl.CostEstimate(
            flops=8 * tokens * width * keys, bytes_accessed=8 * width * keys, transcendentals=tokens * keys * width // HD
        ),
    )(*operands)


def state_shapes(query):
    tokens, width = query.shape
    heads = width // HD
    return [jax.ShapeDtypeStruct((heads, tokens, size), jnp.float32) for size in (1, 1, HD)]


def order_kernel(*refs):
    pieces, out = refs[:-1], refs[-1]
    _, spot = place()
    span = out.shape[0] // SPREAD
    for twist, piece in enumerate(pieces):
        out[pl.ds(aligned(jnp.bitwise_xor(spot, twist), span), span), :] = piece[...]


def order(pieces):
    span, depth = pieces[0].shape
    shape = (SPREAD * span, depth)
    return pl.pallas_call(
        order_kernel,
        out_shape=jax.ShapeDtypeStruct(shape, jnp.bfloat16),
        in_specs=[VMEM] * len(pieces),
        out_specs=VMEM,
        compiler_params=pltpu.CompilerParams(vmem_limit_bytes=SMALL),
        cost_estimate=pl.CostEstimate(flops=0, bytes_accessed=4 * shape[0] * depth, transcendentals=0),
    )(*pieces)


def term_of(part, weight, turn, width, skip=0):
    group, _ = place()
    start = jnp.bitwise_xor(group, turn) * width + skip
    columns = pl.ds(pl.multiple_of(start, HD), part.shape[1])
    return lax.dot_general(part[...], weight[:, columns], NT, preferred_element_type=jnp.float32)


def begin_kernel(own, second, first, weight, out):
    width = own.shape[1]
    out[...] = term_of(own, weight, 0, width) + term_of(second, weight, 2, width) + term_of(first, weight, 1, width)


def begin(parts, weight):
    tokens = parts[0].shape[0]
    columns, depth = weight.shape
    return pl.pallas_call(
        begin_kernel,
        out_shape=jax.ShapeDtypeStruct((tokens, columns), jnp.float32),
        in_specs=[VMEM] * (len(parts) + 1),
        out_specs=VMEM,
        compiler_params=pltpu.CompilerParams(vmem_limit_bytes=SMALL),
        cost_estimate=pl.CostEstimate(
            flops=2 * tokens * columns * depth, bytes_accessed=4 * tokens * columns, transcendentals=0
        ),
    )(*parts, weight)


def close_kernel(partial, most, last, weight, *rest):
    outs, total = rest[:-1], rest[-1]
    group, _ = place()
    rows = outs[0].shape[0]
    width = most.shape[1] + last.shape[1]
    added = partial[...] + term_of(most, weight, 3, width) + term_of(last, weight, 3, width, width - HD)
    total[...] = added.astype(jnp.bfloat16)
    for turn, out in enumerate(outs):
        out[...] = total[pl.ds(aligned(jnp.bitwise_xor(group, turn), rows), rows), :]


def close(groups, partial, most, last, weight):
    tokens, columns = partial.shape
    return pl.pallas_call(
        close_kernel,
        out_shape=[jax.ShapeDtypeStruct((tokens // groups, columns), jnp.bfloat16)] * groups,
        in_specs=[VMEM] * 4,
        out_specs=[VMEM] * groups,
        scratch_shapes=[pltpu.VMEM((tokens, columns), jnp.bfloat16)],
        compiler_params=pltpu.CompilerParams(vmem_limit_bytes=SMALL),
        cost_estimate=pl.CostEstimate(
            flops=tokens * weight.size, bytes_accessed=8 * tokens * columns, transcendentals=0
        ),
    )(partial, most, last, weight)


def at_home(group):
    return group // TURNS[1] == lax.axis_index("head")


def divide_kernel(far, near, keep, send):
    group, _ = place()

    @pl.when(at_home(group))
    def _():
        keep[...] = near[...]
        send[...] = far[...]

    @pl.when(jnp.logical_not(at_home(group)))
    def _():
        keep[...] = far[...]
        send[...] = near[...]


def divide(far, near):
    return pl.pallas_call(
        divide_kernel,
        out_shape=[jax.ShapeDtypeStruct(near.shape, near.dtype)] * 2,
        in_specs=[VMEM] * 2,
        out_specs=[VMEM] * 2,
        compiler_params=pltpu.CompilerParams(vmem_limit_bytes=SMALL),
        cost_estimate=pl.CostEstimate(flops=0, bytes_accessed=8 * near.size, transcendentals=0),
    )(far, near)


def finish_kernel(kept_even, arrived_even, kept_odd, arrived_odd, bias, gate, out, held):
    group, _ = place()
    columns = kept_even.shape[1]
    side = lax.rem(group, 2)
    held[side] = kept_even[...].astype(jnp.float32) + arrived_even[...].astype(jnp.float32)
    held[1 - side] = kept_odd[...].astype(jnp.float32) + arrived_odd[...].astype(jnp.float32)
    for block in range(2):
        cols = slice(block * columns, (block + 1) * columns)
        out[:, cols] = (gate[:, cols] * (held[block] + bias[:, cols])).astype(jnp.bfloat16)


def finish(pieces, bias, gate):
    rows, columns = pieces[0].shape
    width = 2 * columns
    return pl.pallas_call(
        finish_kernel,
        out_shape=jax.ShapeDtypeStruct((rows, width), jnp.bfloat16),
        in_specs=[VMEM] * (len(pieces) + 2),
        out_specs=VMEM,
        scratch_shapes=[pltpu.VMEM((2, rows, columns), jnp.float32)],
        compiler_params=pltpu.CompilerParams(vmem_limit_bytes=SMALL),
        cost_estimate=pl.CostEstimate(flops=3 * rows * width, bytes_accessed=4 * rows * width, transcendentals=0),
    )(*pieces, bias.reshape(1, width), gate.reshape(1, width))


def after(value, *others):
    return lax.optimization_barrier((value, *others))[0]


def grouped_body(queries, stale_kv, codes, exponents, text_kv, out_weight, out_bias, out_gate):
    groups = lax.axis_size("patch") // SPREAD
    size = groups * SPREAD

    def swap(value, twist):
        return lax.ppermute(value, "patch", [(p, p ^ twist) for p in range(size)])

    def along(values):
        return [swap(values[turn], turn * SPREAD) for turn in TURNS[1:]]

    weight = out_weight.T
    weight_far = swap(weight, 2)
    *packed, own = pack(groups, queries, codes, exponents)
    text, stale = pick(groups, text_kv, stale_kv)

    every, some, query = merge([packed[0], *along(packed)])
    own_far = swap(own, 2)

    ready = (every, some, query, weight, weight_far, own_far, text, stale)
    every, some, query, weight, weight_far = lax.optimization_barrier(ready)[:5]
    near, some_far = swap(every, 1), swap(some, 2)
    share = stale.shape[2]
    operands = [query, every, near, text, stale]
    state = attend_call(near_kernel, operands, state_shapes(query), 2 * share + text.shape[1])

    some_far, own_far = lax.optimization_barrier((some_far, own_far, *state))[:2]
    own_corner, some_corner = swap(own_far, 1), swap(some_far, 1)
    state = attend_call(middle_kernel, [query, own_far, some_far, stale, *state], state_shapes(query), share)
    weight, weight_far = lax.optimization_barrier((weight, weight_far, own_corner, some_corner, *state))[:2]
    weight_near, weight_corner = swap(weight, 1), swap(weight_far, 1)
    operands = [query, own_corner, some_corner, stale, *state]
    tokens, width = query.shape
    shapes = [jax.ShapeDtypeStruct((tokens, size), jnp.bfloat16) for size in (width, width - HD)]
    attended, most = attend_call(last_kernel, operands, shapes, share)

    second, first, third = (swap(value, turn * SPREAD) for turn, value in ((2, attended), (1, attended), (3, most)))
    passed = swap(second[:, width - HD :], SPREAD)
    weight = order([weight, weight_near, weight_far, weight_corner])
    terms = close(groups, begin([attended, second, first], weight), third, passed, weight)
    second, third, first = along(terms)
    pieces = []
    for near, far in ((terms[0], second), (first, third)):
        kept, sent = divide(far, near)
        pieces += [kept, lax.ppermute(sent, "head", [(0, 1), (1, 0)])]
    return finish(pieces, out_bias, out_gate)


def solution(mesh):
    patches, halves = mesh.shape["patch"], mesh.shape["head"]
    placed = (
        P("patch", "head"),
        P(None, None, "head"),
        P(None, "patch", "head"),
        P(None, "patch", "head"),
        P(None, None, "head"),
        P("head", "patch"),
        P("head"),
        P("head"),
    )

    def body(*args):
        heads = args[0].shape[1] // HD
        groups = patches // SPREAD
        if groups != 4 or patches % SPREAD or heads % groups or halves != 2:
            return plain_body(*args)
        return grouped_body(*args)

    return jax.shard_map(body, mesh=mesh, in_specs=placed, out_specs=P("patch", "head"), check_vma=False)
```

```python
import functools

import jax
import jax.numpy as jnp
from jax import lax
from jax.experimental import pallas as pl
from jax.experimental.pallas import tpu as pltpu
from jax.sharding import PartitionSpec as P

HD = 128
SPREAD = 4
TURNS = (0, 2, 3, 1)
PACK_LIMIT = 56 << 20
SMALL = 16 << 20
PICK_LIMIT = 50 << 20
VMEM = pl.BlockSpec(memory_space=pltpu.VMEM)
HBM = pl.BlockSpec(memory_space=pltpu.HBM)
NT = (((1,), (1,)), ((), ()))


def plain_body(queries, stale_kv, codes, exponents, text_kv, out_weight, out_bias, out_gate):
    tok_rows = queries.shape[0]
    row_width = queries.shape[1]
    head_count = row_width // HD
    text_count = text_kv.shape[1]
    scale_factor = HD ** (-0.5)
    blocks = jnp.exp2(exponents.astype(jnp.float32))
    decoded = codes.astype(jnp.float32).reshape(2, tok_rows, head_count, HD) * blocks[..., None]
    decoded = decoded.astype(jnp.bfloat16).reshape(2, tok_rows, row_width)
    arrived = lax.all_gather(decoded, "patch", axis=1, tiled=True)
    all_rows = arrived.shape[1]
    query_heads = queries.reshape(tok_rows, head_count, HD)
    text_heads = text_kv.reshape(2, text_count, head_count, HD)
    stale_heads = stale_kv.reshape(2, all_rows, head_count, HD)
    arrived_heads = arrived.reshape(2, all_rows, head_count, HD)
    text_scores = jnp.einsum("thd,khd->htk", query_heads, text_heads[0], preferred_element_type=jnp.float32)
    rebuilt = stale_heads.astype(jnp.float32) + arrived_heads.astype(jnp.float32)
    image_scores = jnp.einsum(
        "thd,khd->htk", query_heads.astype(jnp.float32), rebuilt[0], precision=lax.Precision.HIGHEST
    )
    scores = jnp.concatenate([text_scores, image_scores], axis=2) * scale_factor
    row_peak = jnp.max(scores, axis=2, keepdims=True)
    weights = jnp.exp(scores - row_peak).astype(jnp.bfloat16)
    row_total = jnp.sum(weights.astype(jnp.float32), axis=2)
    text_part = jnp.einsum(
        "htk,khd->thd", weights[:, :, :text_count], text_heads[1], preferred_element_type=jnp.float32
    )
    image_part = jnp.einsum(
        "htk,khd->thd",
        weights[:, :, text_count:].astype(jnp.float32),
        rebuilt[1],
        precision=lax.Precision.HIGHEST,
    )
    attended = ((text_part + image_part) / row_total.T[:, :, None]).astype(jnp.bfloat16).reshape(tok_rows, row_width)
    partial_terms = jnp.dot(
        attended, lax.all_gather(out_weight, "patch", axis=1, tiled=True), preferred_element_type=jnp.float32
    )
    column_share = lax.psum_scatter(partial_terms, "head", scatter_dimension=1, tiled=True)
    return (out_gate * (column_share + out_bias)).astype(jnp.bfloat16)


def aligned(value, step):
    return pl.multiple_of(value * step, step)


def place():
    me = lax.axis_index("patch")
    return me // SPREAD, lax.rem(me, SPREAD)


def pack_kernel(queries_hbm, codes_hbm, exponents_hbm, *rest):
    outs, (codes, queries, exponents, held, sems) = rest[:-5], rest[-5:]
    groups, kinds, rows, width = held.shape
    group, _ = place()
    per = width // HD
    copies = [
        pltpu.make_async_copy(exponents_hbm, exponents, sems.at[0]),
        pltpu.make_async_copy(codes_hbm, codes, sems.at[1]),
        pltpu.make_async_copy(queries_hbm, queries, sems.at[2]),
    ]
    for copy in copies:
        copy.start()
    copies[0].wait()
    copies[1].wait()
    eye = lax.broadcasted_iota(jnp.int32, (rows, rows), 0) == lax.broadcasted_iota(jnp.int32, (rows, rows), 1)
    eye = eye.astype(jnp.float32).astype(jnp.bfloat16)
    for kind in range(kinds - 1):
        scales = jnp.left_shift(1, exponents[:, kind, :] + 16).astype(jnp.float32) * (2.0**-16)
        scales = lax.dot_general(eye, scales.astype(jnp.bfloat16), NT, preferred_element_type=jnp.float32)
        for head in range(groups * per):
            inside = slice((head % per) * HD, (head % per + 1) * HD)
            whole = slice(head * HD, (head + 1) * HD)
            decoded = codes[kind, :, whole].astype(jnp.float32) * scales[:, head : head + 1]
            held[head // per, kind, :, inside] = decoded.astype(jnp.bfloat16)
    copies[2].wait()
    for target in range(groups):
        held[target, kinds - 1] = queries[:, target * width : (target + 1) * width]
    writes = [
        pltpu.make_async_copy(held.at[jnp.bitwise_xor(group, turn)], outs[turn], sems.at[3 + turn])
        for turn in range(groups)
    ]
    for write in writes:
        write.start()
    for write in writes:
        write.wait()


def pack(groups, queries, codes, exponents):
    rows, width = queries.shape
    kinds = codes.shape[0]
    share = width // groups
    bf16 = jnp.bfloat16
    exponents = exponents.transpose(2, 0, 1)
    shapes = [(kinds + 1, rows, share)] * groups
    outs = pl.pallas_call(
        pack_kernel,
        out_shape=[jax.ShapeDtypeStruct(shape, bf16) for shape in shapes],
        in_specs=[HBM] * 3,
        out_specs=[HBM] * len(shapes),
        scratch_shapes=[
            pltpu.VMEM(codes.shape, jnp.int32),
            pltpu.VMEM(queries.shape, bf16),
            pltpu.VMEM(exponents.shape, jnp.int32),
            pltpu.VMEM((groups, kinds + 1, rows, share), bf16),
            pltpu.SemaphoreType.DMA((3 + groups,)),
        ],
        compiler_params=pltpu.CompilerParams(vmem_limit_bytes=PACK_LIMIT),
        cost_estimate=pl.CostEstimate(flops=2 * codes.size, bytes_accessed=6 * codes.size, transcendentals=0),
    )(queries, codes, exponents)
    return outs


def pick_kernel(text_hbm, stale_hbm, text, stale, sems):
    group, spot = place()
    width = text.shape[2]
    groups = text_hbm.shape[2] // width
    rows = stale.shape[2] // groups
    columns = pl.ds(aligned(group, width), width)
    copies = [pltpu.make_async_copy(text_hbm.at[:, :, columns], text, sems.at[0])]
    for twist in range(SPREAD):
        for position in range(groups):
            origin = jnp.bitwise_xor(group, TURNS[position])
            token = origin * SPREAD + jnp.bitwise_xor(spot, twist)
            copies.append(
                pltpu.make_async_copy(
                    stale_hbm.at[:, pl.ds(aligned(token, rows), rows), columns],
                    stale.at[twist, :, pl.ds(position * rows, rows), :],
                    sems.at[len(copies)],
                )
            )
    for copy in copies:
        copy.start()
    for copy in copies:
        copy.wait()


def pick(groups, text_kv, stale_kv):
    kinds, texts, heads_width = text_kv.shape
    width = heads_width // groups
    return pl.pallas_call(
        pick_kernel,
        out_shape=[
            jax.ShapeDtypeStruct((kinds, texts, width), jnp.bfloat16),
            jax.ShapeDtypeStruct((SPREAD, kinds, stale_kv.shape[1] // SPREAD, width), jnp.bfloat16),
        ],
        in_specs=[HBM] * 2,
        out_specs=[VMEM] * 2,
        scratch_shapes=[pltpu.SemaphoreType.DMA((1 + SPREAD * groups,))],
        compiler_params=pltpu.CompilerParams(vmem_limit_bytes=PICK_LIMIT),
        cost_estimate=pl.CostEstimate(flops=0, bytes_accessed=8 << 20, transcendentals=0),
    )(text_kv, stale_kv)


def merge_kernel(*refs):
    parts, (every, query) = refs[:-2], refs[-2:]
    groups, kinds, rows, _ = every.shape
    group, _ = place()
    for position, part in enumerate(parts):
        every[position] = part[0:kinds]
        origin = jnp.bitwise_xor(group, TURNS[position])
        query[pl.ds(aligned(origin, rows), rows), :] = part[kinds]


def merge(parts):
    kinds, rows, width = parts[0].shape
    shapes = [(len(parts), kinds - 1, rows, width), (len(parts) * rows, width)]
    return pl.pallas_call(
        merge_kernel,
        out_shape=[jax.ShapeDtypeStruct(shape, jnp.bfloat16) for shape in shapes],
        in_specs=[VMEM] * len(parts),
        out_specs=[VMEM] * 2,
        compiler_params=pltpu.CompilerParams(vmem_limit_bytes=SMALL),
        cost_estimate=pl.CostEstimate(flops=0, bytes_accessed=4 * len(parts) * parts[0].size, transcendentals=0),
    )(*parts)


def absorb(queries, segments, states):
    scores = [
        [
            lax.dot_general(
                query if key.shape[1] == HD else jnp.concatenate([query, query], axis=1),
                key,
                NT,
                preferred_element_type=jnp.float32,
            )
            * HD**-0.5
            for key, _ in parts
        ]
        for query, parts in zip(queries, segments)
    ]
    peaks = [[jnp.max(score, axis=1, keepdims=True) for score in row] for row in scores]
    if states is not None:
        peaks = [row + [state[0]] for row, state in zip(peaks, states)]
    peaks = [functools.reduce(jnp.maximum, row) for row in peaks]
    weights = [
        [jnp.exp(score - peak).astype(jnp.bfloat16) for score in row] for row, peak in zip(scores, peaks)
    ]
    totals = [sum(jnp.sum(w.astype(jnp.float32), axis=1, keepdims=True) for w in row) for row in weights]
    mixes = [
        sum(jnp.dot(w, value, preferred_element_type=jnp.float32) for w, (_, value) in zip(row, parts))
        for row, parts in zip(weights, segments)
    ]
    if states is not None:
        fades = [jnp.exp(state[0] - peak) for state, peak in zip(states, peaks)]
        totals = [total + state[1] * fade for total, state, fade in zip(totals, states, fades)]
        mixes = [mix + state[2] * fade for mix, state, fade in zip(mixes, states, fades)]
    return list(zip(peaks, totals, mixes))


def columns_of(width):
    return [slice(start, start + HD) for start in range(0, width, HD)]


def image_segment(stale, twist, residual):
    def of(cols):
        key = jnp.concatenate([stale[twist, 0, :, cols], residual(0, cols)], axis=1)
        value = stale[twist, 1, :, cols].astype(jnp.float32) + residual(1, cols).astype(jnp.float32)
        return key, value.astype(jnp.bfloat16)

    return of


def whole_part(part):
    return lambda kind, cols: part[:, kind, :, cols].reshape(-1, HD)


def near_kernel(query, every, near, text, stale, peak, total, mixed):
    heads = columns_of(query.shape[1])
    images = [image_segment(stale, 0, whole_part(every)), image_segment(stale, 1, whole_part(near))]
    segments = [[(text[0, :, cols], text[1, :, cols])] + [image(cols) for image in images] for cols in heads]
    states = absorb([query[:, cols] for cols in heads], segments, None)
    for head, state in enumerate(states):
        peak[head], total[head], mixed[head] = state


def middle_kernel(query, far, stale, peak_in, total_in, mixed_in, peak, total, mixed):
    heads = columns_of(query.shape[1])
    image = image_segment(stale, 2, whole_part(far))
    segments = [[image(cols)] for cols in heads]
    states = [(peak_in[head], total_in[head], mixed_in[head]) for head in range(len(heads))]
    states = absorb([query[:, cols] for cols in heads], segments, states)
    for head, state in enumerate(states):
        peak[head], total[head], mixed[head] = state


def last_kernel(query, corner, stale, peak, total, mixed, out, most):
    heads = columns_of(query.shape[1])
    image = image_segment(stale, 3, whole_part(corner))
    states = [(peak[head], total[head], mixed[head]) for head in range(len(heads))]
    states = absorb([query[:, cols] for cols in heads], [[image(cols)] for cols in heads], states)
    for cols, (_, sums, mix) in zip(heads, states):
        value = (mix / sums).astype(jnp.bfloat16)
        out[:, cols] = value
        if cols is not heads[-1]:
            most[:, cols] = value


def attend_call(kernel, operands, shapes, keys):
    tokens, width = operands[0].shape
    return pl.pallas_call(
        kernel,
        out_shape=shapes,
        in_specs=[VMEM] * len(operands),
        out_specs=[VMEM] * len(shapes),
        compiler_params=pltpu.CompilerParams(vmem_limit_bytes=SMALL),
        cost_estimate=pl.CostEstimate(
            flops=8 * tokens * width * keys, bytes_accessed=8 * width * keys, transcendentals=tokens * keys * width // HD
        ),
    )(*operands)


def state_shapes(query):
    tokens, width = query.shape
    heads = width // HD
    return [jax.ShapeDtypeStruct((heads, tokens, size), jnp.float32) for size in (1, 1, HD)]


def stack_kernel(first, second, out):
    out[0] = first[...]
    out[1] = second[...]


def stack(first, second):
    return pl.pallas_call(
        stack_kernel,
        out_shape=jax.ShapeDtypeStruct((2, *first.shape), first.dtype),
        in_specs=[VMEM] * 2,
        out_specs=VMEM,
        compiler_params=pltpu.CompilerParams(vmem_limit_bytes=SMALL),
        cost_estimate=pl.CostEstimate(flops=0, bytes_accessed=8 * first.size, transcendentals=0),
    )(first, second)


def order_kernel(own, across, out):
    _, spot = place()
    span = own.shape[1]
    for twist in range(SPREAD):
        piece = (own, across)[twist % 2][twist // 2]
        out[pl.ds(aligned(jnp.bitwise_xor(spot, twist), span), span), :] = piece


def order(own, across):
    count, span, depth = own.shape
    shape = (2 * count * span, depth)
    return pl.pallas_call(
        order_kernel,
        out_shape=jax.ShapeDtypeStruct(shape, jnp.bfloat16),
        in_specs=[VMEM] * 2,
        out_specs=VMEM,
        compiler_params=pltpu.CompilerParams(vmem_limit_bytes=SMALL),
        cost_estimate=pl.CostEstimate(flops=0, bytes_accessed=4 * shape[0] * depth, transcendentals=0),
    )(own, across)


def term_of(part, weight, turn, width, skip=0):
    group, _ = place()
    start = jnp.bitwise_xor(group, turn) * width + skip
    columns = pl.ds(pl.multiple_of(start, HD), part.shape[1])
    return lax.dot_general(part[...], weight[:, columns], NT, preferred_element_type=jnp.float32)


def begin_kernel(own, second, first, weight, out):
    width = own.shape[1]
    out[...] = term_of(own, weight, 0, width) + term_of(second, weight, 2, width) + term_of(first, weight, 1, width)


def begin(parts, weight):
    tokens = parts[0].shape[0]
    columns, depth = weight.shape
    return pl.pallas_call(
        begin_kernel,
        out_shape=jax.ShapeDtypeStruct((tokens, columns), jnp.float32),
        in_specs=[VMEM] * (len(parts) + 1),
        out_specs=VMEM,
        compiler_params=pltpu.CompilerParams(vmem_limit_bytes=SMALL),
        cost_estimate=pl.CostEstimate(
            flops=2 * tokens * columns * depth, bytes_accessed=4 * tokens * columns, transcendentals=0
        ),
    )(*parts, weight)


def close_kernel(partial, most, last, weight, *rest):
    outs, total = rest[:-1], rest[-1]
    group, _ = place()
    rows = outs[0].shape[0]
    width = most.shape[1] + last.shape[1]
    added = partial[...] + term_of(most, weight, 3, width) + term_of(last, weight, 3, width, width - HD)
    total[...] = added.astype(jnp.bfloat16)
    for turn, out in enumerate(outs):
        out[...] = total[pl.ds(aligned(jnp.bitwise_xor(group, turn), rows), rows), :]


def close(groups, partial, most, last, weight):
    tokens, columns = partial.shape
    return pl.pallas_call(
        close_kernel,
        out_shape=[jax.ShapeDtypeStruct((tokens // groups, columns), jnp.bfloat16)] * groups,
        in_specs=[VMEM] * 4,
        out_specs=[VMEM] * groups,
        scratch_shapes=[pltpu.VMEM((tokens, columns), jnp.bfloat16)],
        compiler_params=pltpu.CompilerParams(vmem_limit_bytes=SMALL),
        cost_estimate=pl.CostEstimate(
            flops=tokens * weight.size, bytes_accessed=8 * tokens * columns, transcendentals=0
        ),
    )(partial, most, last, weight)


def at_home(group):
    return group // TURNS[1] == lax.axis_index("head")


def divide_kernel(far, near, keep, send):
    group, _ = place()

    @pl.when(at_home(group))
    def _():
        keep[...] = near[...]
        send[...] = far[...]

    @pl.when(jnp.logical_not(at_home(group)))
    def _():
        keep[...] = far[...]
        send[...] = near[...]


def divide(far, near):
    return pl.pallas_call(
        divide_kernel,
        out_shape=[jax.ShapeDtypeStruct(near.shape, near.dtype)] * 2,
        in_specs=[VMEM] * 2,
        out_specs=[VMEM] * 2,
        compiler_params=pltpu.CompilerParams(vmem_limit_bytes=SMALL),
        cost_estimate=pl.CostEstimate(flops=0, bytes_accessed=8 * near.size, transcendentals=0),
    )(far, near)


def finish_kernel(kept_even, arrived_even, kept_odd, arrived_odd, bias, gate, out, held):
    group, _ = place()
    columns = kept_even.shape[1]
    side = lax.rem(group, 2)
    held[side] = kept_even[...].astype(jnp.float32) + arrived_even[...].astype(jnp.float32)
    held[1 - side] = kept_odd[...].astype(jnp.float32) + arrived_odd[...].astype(jnp.float32)
    for block in range(2):
        cols = slice(block * columns, (block + 1) * columns)
        out[:, cols] = (gate[:, cols] * (held[block] + bias[:, cols])).astype(jnp.bfloat16)


def finish(pieces, bias, gate):
    rows, columns = pieces[0].shape
    width = 2 * columns
    return pl.pallas_call(
        finish_kernel,
        out_shape=jax.ShapeDtypeStruct((rows, width), jnp.bfloat16),
        in_specs=[VMEM] * (len(pieces) + 2),
        out_specs=VMEM,
        scratch_shapes=[pltpu.VMEM((2, rows, columns), jnp.float32)],
        compiler_params=pltpu.CompilerParams(vmem_limit_bytes=SMALL),
        cost_estimate=pl.CostEstimate(flops=3 * rows * width, bytes_accessed=4 * rows * width, transcendentals=0),
    )(*pieces, bias.reshape(1, width), gate.reshape(1, width))


def after(value, *others):
    return lax.optimization_barrier((value, *others))[0]


def grouped_body(queries, stale_kv, codes, exponents, text_kv, out_weight, out_bias, out_gate):
    groups = lax.axis_size("patch") // SPREAD
    size = groups * SPREAD

    def swap(value, twist):
        return lax.ppermute(value, "patch", [(p, p ^ twist) for p in range(size)])

    def along(values):
        return [swap(values[turn], turn * SPREAD) for turn in TURNS[1:]]

    weight = out_weight.T
    weight_far = swap(weight, 2)
    packed = pack(groups, queries, codes, exponents)
    text, stale = pick(groups, text_kv, stale_kv)

    every, query = merge([packed[0], *along(packed)])

    ready = (every, query, weight, weight_far, text, stale)
    every, query, weight, weight_far = lax.optimization_barrier(ready)[:4]
    far, near = swap(every, 2), swap(every, 1)
    share = stale.shape[2]
    operands = [query, every, near, text, stale]
    state = attend_call(near_kernel, operands, state_shapes(query), 2 * share + text.shape[1])

    far, weight = lax.optimization_barrier((far, stack(weight, weight_far), *state))[:2]
    corner = swap(far, 1)
    state = attend_call(middle_kernel, [query, far, stale, *state], state_shapes(query), share)
    weight = after(weight, corner, *state)
    weight_across = swap(weight, 1)
    operands = [query, corner, stale, *state]
    tokens, width = query.shape
    shapes = [jax.ShapeDtypeStruct((tokens, size), jnp.bfloat16) for size in (width, width - HD)]
    attended, most = attend_call(last_kernel, operands, shapes, share)

    second, first, third = (swap(value, turn * SPREAD) for turn, value in ((2, attended), (1, attended), (3, most)))
    passed = swap(second[:, width - HD :], SPREAD)
    weight = order(weight, weight_across)
    terms = close(groups, begin([attended, second, first], weight), third, passed, weight)
    second, third, first = along(terms)
    pieces = []
    for near, far in ((terms[0], second), (first, third)):
        kept, sent = divide(far, near)
        pieces += [kept, lax.ppermute(sent, "head", [(0, 1), (1, 0)])]
    return finish(pieces, out_bias, out_gate)


def solution(mesh):
    patches, halves = mesh.shape["patch"], mesh.shape["head"]
    placed = (
        P("patch", "head"),
        P(None, None, "head"),
        P(None, "patch", "head"),
        P(None, "patch", "head"),
        P(None, None, "head"),
        P("head", "patch"),
        P("head"),
        P("head"),
    )

    def body(*args):
        heads = args[0].shape[1] // HD
        groups = patches // SPREAD
        if groups != 4 or patches % SPREAD or heads % groups or halves != 2:
            return plain_body(*args)
        return grouped_body(*args)

    return jax.shard_map(body, mesh=mesh, in_specs=placed, out_specs=P("patch", "head"), check_vma=False)
```

```python
import functools

import jax
import jax.numpy as jnp
from jax import lax
from jax.experimental import pallas as pl
from jax.experimental.pallas import tpu as pltpu
from jax.sharding import PartitionSpec as P

HD = 128
SPREAD = 4
TURNS = (0, 2, 3, 1)
PACK_LIMIT = 56 << 20
SMALL = 16 << 20
PICK_LIMIT = 50 << 20
VMEM = pl.BlockSpec(memory_space=pltpu.VMEM)
HBM = pl.BlockSpec(memory_space=pltpu.HBM)
NT = (((1,), (1,)), ((), ()))


def plain_body(queries, stale_kv, codes, exponents, text_kv, out_weight, out_bias, out_gate):
    tok_rows = queries.shape[0]
    row_width = queries.shape[1]
    head_count = row_width // HD
    text_count = text_kv.shape[1]
    scale_factor = HD ** (-0.5)
    blocks = jnp.exp2(exponents.astype(jnp.float32))
    decoded = codes.astype(jnp.float32).reshape(2, tok_rows, head_count, HD) * blocks[..., None]
    decoded = decoded.astype(jnp.bfloat16).reshape(2, tok_rows, row_width)
    arrived = lax.all_gather(decoded, "patch", axis=1, tiled=True)
    all_rows = arrived.shape[1]
    query_heads = queries.reshape(tok_rows, head_count, HD)
    text_heads = text_kv.reshape(2, text_count, head_count, HD)
    stale_heads = stale_kv.reshape(2, all_rows, head_count, HD)
    arrived_heads = arrived.reshape(2, all_rows, head_count, HD)
    text_scores = jnp.einsum("thd,khd->htk", query_heads, text_heads[0], preferred_element_type=jnp.float32)
    rebuilt = stale_heads.astype(jnp.float32) + arrived_heads.astype(jnp.float32)
    image_scores = jnp.einsum(
        "thd,khd->htk", query_heads.astype(jnp.float32), rebuilt[0], precision=lax.Precision.HIGHEST
    )
    scores = jnp.concatenate([text_scores, image_scores], axis=2) * scale_factor
    row_peak = jnp.max(scores, axis=2, keepdims=True)
    weights = jnp.exp(scores - row_peak).astype(jnp.bfloat16)
    row_total = jnp.sum(weights.astype(jnp.float32), axis=2)
    text_part = jnp.einsum(
        "htk,khd->thd", weights[:, :, :text_count], text_heads[1], preferred_element_type=jnp.float32
    )
    image_part = jnp.einsum(
        "htk,khd->thd",
        weights[:, :, text_count:].astype(jnp.float32),
        rebuilt[1],
        precision=lax.Precision.HIGHEST,
    )
    attended = ((text_part + image_part) / row_total.T[:, :, None]).astype(jnp.bfloat16).reshape(tok_rows, row_width)
    partial_terms = jnp.dot(
        attended, lax.all_gather(out_weight, "patch", axis=1, tiled=True), preferred_element_type=jnp.float32
    )
    column_share = lax.psum_scatter(partial_terms, "head", scatter_dimension=1, tiled=True)
    return (out_gate * (column_share + out_bias)).astype(jnp.bfloat16)


def aligned(value, step):
    return pl.multiple_of(value * step, step)


def place():
    me = lax.axis_index("patch")
    return me // SPREAD, lax.rem(me, SPREAD)


def pack_kernel(queries_hbm, codes_hbm, exponents_hbm, weight_hbm, *rest):
    outs, early, (codes, queries, exponents, held, sems) = rest[:-6], rest[-6], rest[-5:]
    groups, kinds, rows, width = held.shape
    group, _ = place()
    per = width // HD
    copies = [
        pltpu.make_async_copy(exponents_hbm, exponents, sems.at[0]),
        pltpu.make_async_copy(codes_hbm, codes, sems.at[1]),
        pltpu.make_async_copy(queries_hbm, queries, sems.at[2]),
        pltpu.make_async_copy(weight_hbm.at[0 : early.shape[0]], early, sems.at[3]),
    ]
    for copy in copies:
        copy.start()
    copies[0].wait()
    copies[1].wait()
    eye = lax.broadcasted_iota(jnp.int32, (rows, rows), 0) == lax.broadcasted_iota(jnp.int32, (rows, rows), 1)
    eye = eye.astype(jnp.float32).astype(jnp.bfloat16)
    for kind in range(kinds - 1):
        scales = jnp.left_shift(1, exponents[:, kind, :] + 16).astype(jnp.float32) * (2.0**-16)
        scales = lax.dot_general(eye, scales.astype(jnp.bfloat16), NT, preferred_element_type=jnp.float32)
        for head in range(groups * per):
            inside = slice((head % per) * HD, (head % per + 1) * HD)
            whole = slice(head * HD, (head + 1) * HD)
            decoded = codes[kind, :, whole].astype(jnp.float32) * scales[:, head : head + 1]
            held[head // per, kind, :, inside] = decoded.astype(jnp.bfloat16)
    copies[2].wait()
    for target in range(groups):
        held[target, kinds - 1] = queries[:, target * width : (target + 1) * width]
    for turn in range(groups):
        outs[turn][...] = held[jnp.bitwise_xor(group, turn)]
    outs[groups][...] = held[group, 0 : kinds - 1]
    copies[3].wait()


def pack(groups, queries, codes, exponents, weight, cut):
    rows, width = queries.shape
    kinds = codes.shape[0]
    share = width // groups
    bf16 = jnp.bfloat16
    exponents = exponents.transpose(2, 0, 1)
    shapes = [(kinds + 1, rows, share)] * groups + [(kinds, rows, share), (cut, weight.shape[1])]
    outs = pl.pallas_call(
        pack_kernel,
        out_shape=[jax.ShapeDtypeStruct(shape, bf16) for shape in shapes],
        in_specs=[HBM] * 4,
        out_specs=[VMEM] * len(shapes),
        scratch_shapes=[
            pltpu.VMEM(codes.shape, jnp.int32),
            pltpu.VMEM(queries.shape, bf16),
            pltpu.VMEM(exponents.shape, jnp.int32),
            pltpu.VMEM((groups, kinds + 1, rows, share), bf16),
            pltpu.SemaphoreType.DMA((4,)),
        ],
        compiler_params=pltpu.CompilerParams(vmem_limit_bytes=PACK_LIMIT),
        cost_estimate=pl.CostEstimate(flops=2 * codes.size, bytes_accessed=6 * codes.size, transcendentals=0),
    )(queries, codes, exponents, weight)
    return outs


def pick_kernel(text_hbm, stale_hbm, text, stale, sems):
    group, spot = place()
    width = text.shape[2]
    groups = text_hbm.shape[2] // width
    rows = stale.shape[2] // groups
    columns = pl.ds(aligned(group, width), width)
    copies = [pltpu.make_async_copy(text_hbm.at[:, :, columns], text, sems.at[0])]
    for twist in range(SPREAD):
        for position in range(groups):
            origin = jnp.bitwise_xor(group, TURNS[position])
            token = origin * SPREAD + jnp.bitwise_xor(spot, twist)
            copies.append(
                pltpu.make_async_copy(
                    stale_hbm.at[:, pl.ds(aligned(token, rows), rows), columns],
                    stale.at[twist, :, pl.ds(position * rows, rows), :],
                    sems.at[len(copies)],
                )
            )
    for copy in copies:
        copy.start()
    for copy in copies:
        copy.wait()


def pick(groups, text_kv, stale_kv):
    kinds, texts, heads_width = text_kv.shape
    width = heads_width // groups
    return pl.pallas_call(
        pick_kernel,
        out_shape=[
            jax.ShapeDtypeStruct((kinds, texts, width), jnp.bfloat16),
            jax.ShapeDtypeStruct((SPREAD, kinds, stale_kv.shape[1] // SPREAD, width), jnp.bfloat16),
        ],
        in_specs=[HBM] * 2,
        out_specs=[VMEM] * 2,
        scratch_shapes=[pltpu.SemaphoreType.DMA((1 + SPREAD * groups,))],
        compiler_params=pltpu.CompilerParams(vmem_limit_bytes=PICK_LIMIT),
        cost_estimate=pl.CostEstimate(flops=0, bytes_accessed=8 << 20, transcendentals=0),
    )(text_kv, stale_kv)


def merge_kernel(*refs):
    parts, (every, some, query) = refs[:-3], refs[-3:]
    groups, kinds, rows, _ = every.shape
    group, _ = place()
    for position, part in enumerate(parts):
        every[position] = part[0:kinds]
        if position:
            some[position - 1] = part[0:kinds]
        origin = jnp.bitwise_xor(group, TURNS[position])
        query[pl.ds(aligned(origin, rows), rows), :] = part[kinds]


def merge(parts):
    kinds, rows, width = parts[0].shape
    shapes = [(len(parts), kinds - 1, rows, width), (len(parts) - 1, kinds - 1, rows, width), (len(parts) * rows, width)]
    return pl.pallas_call(
        merge_kernel,
        out_shape=[jax.ShapeDtypeStruct(shape, jnp.bfloat16) for shape in shapes],
        in_specs=[VMEM] * len(parts),
        out_specs=[VMEM] * 3,
        compiler_params=pltpu.CompilerParams(vmem_limit_bytes=SMALL),
        cost_estimate=pl.CostEstimate(flops=0, bytes_accessed=4 * len(parts) * parts[0].size, transcendentals=0),
    )(*parts)


def absorb(queries, segments, states):
    scores = [
        [
            lax.dot_general(
                query if key.shape[1] == HD else jnp.concatenate([query, query], axis=1),
                key,
                NT,
                preferred_element_type=jnp.float32,
            )
            * HD**-0.5
            for key, _ in parts
        ]
        for query, parts in zip(queries, segments)
    ]
    peaks = [[jnp.max(score, axis=1, keepdims=True) for score in row] for row in scores]
    if states is not None:
        peaks = [row + [state[0]] for row, state in zip(peaks, states)]
    peaks = [functools.reduce(jnp.maximum, row) for row in peaks]
    weights = [
        [jnp.exp(score - peak).astype(jnp.bfloat16) for score in row] for row, peak in zip(scores, peaks)
    ]
    totals = [sum(jnp.sum(w.astype(jnp.float32), axis=1, keepdims=True) for w in row) for row in weights]
    mixes = [
        sum(jnp.dot(w, value, preferred_element_type=jnp.float32) for w, (_, value) in zip(row, parts))
        for row, parts in zip(weights, segments)
    ]
    if states is not None:
        fades = [jnp.exp(state[0] - peak) for state, peak in zip(states, peaks)]
        totals = [total + state[1] * fade for total, state, fade in zip(totals, states, fades)]
        mixes = [mix + state[2] * fade for mix, state, fade in zip(mixes, states, fades)]
    return list(zip(peaks, totals, mixes))


def columns_of(width):
    return [slice(start, start + HD) for start in range(0, width, HD)]


def image_segment(stale, twist, residual):
    def of(cols):
        key = jnp.concatenate([stale[twist, 0, :, cols], residual(0, cols)], axis=1)
        value = stale[twist, 1, :, cols].astype(jnp.float32) + residual(1, cols).astype(jnp.float32)
        return key, value.astype(jnp.bfloat16)

    return of


def whole_part(part):
    return lambda kind, cols: part[:, kind, :, cols].reshape(-1, HD)


def split_part(own, some):
    return lambda kind, cols: jnp.concatenate([own[kind, :, cols], some[:, kind, :, cols].reshape(-1, HD)], axis=0)


def near_kernel(query, every, near, text, stale, peak, total, mixed):
    heads = columns_of(query.shape[1])
    images = [image_segment(stale, 0, whole_part(every)), image_segment(stale, 1, whole_part(near))]
    segments = [[(text[0, :, cols], text[1, :, cols])] + [image(cols) for image in images] for cols in heads]
    states = absorb([query[:, cols] for cols in heads], segments, None)
    for head, state in enumerate(states):
        peak[head], total[head], mixed[head] = state


def middle_kernel(query, own_far, some_far, stale, peak_in, total_in, mixed_in, peak, total, mixed):
    heads = columns_of(query.shape[1])
    image = image_segment(stale, 2, split_part(own_far, some_far))
    segments = [[image(cols)] for cols in heads]
    states = [(peak_in[head], total_in[head], mixed_in[head]) for head in range(len(heads))]
    states = absorb([query[:, cols] for cols in heads], segments, states)
    for head, state in enumerate(states):
        peak[head], total[head], mixed[head] = state


def last_kernel(query, own_corner, some_corner, stale, peak, total, mixed, out, most):
    heads = columns_of(query.shape[1])
    image = image_segment(stale, 3, split_part(own_corner, some_corner))
    states = [(peak[head], total[head], mixed[head]) for head in range(len(heads))]
    states = absorb([query[:, cols] for cols in heads], [[image(cols)] for cols in heads], states)
    for cols, (_, sums, mix) in zip(heads, states):
        value = (mix / sums).astype(jnp.bfloat16)
        out[:, cols] = value
        if cols is not heads[-1]:
            most[:, cols] = value


def attend_call(kernel, operands, shapes, keys):
    tokens, width = operands[0].shape
    return pl.pallas_call(
        kernel,
        out_shape=shapes,
        in_specs=[VMEM] * len(operands),
        out_specs=[VMEM] * len(shapes),
        compiler_params=pltpu.CompilerParams(vmem_limit_bytes=SMALL),
        cost_estimate=pl.CostEstimate(
            flops=8 * tokens * width * keys, bytes_accessed=8 * width * keys, transcendentals=tokens * keys * width // HD
        ),
    )(*operands)


def state_shapes(query):
    tokens, width = query.shape
    heads = width // HD
    return [jax.ShapeDtypeStruct((heads, tokens, size), jnp.float32) for size in (1, 1, HD)]


def order_kernel(weight, near, early, late, early_corner, late_corner, out):
    _, spot = place()
    span, cut = weight.shape[0], early.shape[0]
    pieces = [(0, 0, weight), (1, 0, near), (2, 0, early), (2, cut, late), (3, 0, early_corner), (3, cut, late_corner)]
    for twist, skip, piece in pieces:
        start = jnp.bitwise_xor(spot, twist) * span + skip
        out[pl.ds(pl.multiple_of(start, 16), piece.shape[0]), :] = piece[...]


def order(*pieces):
    span, depth = pieces[0].shape
    shape = (SPREAD * span, depth)
    return pl.pallas_call(
        order_kernel,
        out_shape=jax.ShapeDtypeStruct(shape, jnp.bfloat16),
        in_specs=[VMEM] * len(pieces),
        out_specs=VMEM,
        compiler_params=pltpu.CompilerParams(vmem_limit_bytes=SMALL),
        cost_estimate=pl.CostEstimate(flops=0, bytes_accessed=4 * shape[0] * depth, transcendentals=0),
    )(*pieces)


def term_of(part, weight, turn, width, skip=0):
    group, _ = place()
    start = jnp.bitwise_xor(group, turn) * width + skip
    columns = pl.ds(pl.multiple_of(start, HD), part.shape[1])
    return lax.dot_general(part[...], weight[:, columns], NT, preferred_element_type=jnp.float32)


def begin_kernel(own, second, first, weight, out):
    width = own.shape[1]
    out[...] = term_of(own, weight, 0, width) + term_of(second, weight, 2, width) + term_of(first, weight, 1, width)


def begin(parts, weight):
    tokens = parts[0].shape[0]
    columns, depth = weight.shape
    return pl.pallas_call(
        begin_kernel,
        out_shape=jax.ShapeDtypeStruct((tokens, columns), jnp.float32),
        in_specs=[VMEM] * (len(parts) + 1),
        out_specs=VMEM,
        compiler_params=pltpu.CompilerParams(vmem_limit_bytes=SMALL),
        cost_estimate=pl.CostEstimate(
            flops=2 * tokens * columns * depth, bytes_accessed=4 * tokens * columns, transcendentals=0
        ),
    )(*parts, weight)


def close_kernel(partial, most, last, weight, *rest):
    outs, total = rest[:-1], rest[-1]
    group, _ = place()
    rows = outs[0].shape[0]
    width = most.shape[1] + last.shape[1]
    added = partial[...] + term_of(most, weight, 3, width) + term_of(last, weight, 3, width, width - HD)
    total[...] = added.astype(jnp.bfloat16)
    for turn, out in enumerate(outs):
        out[...] = total[pl.ds(aligned(jnp.bitwise_xor(group, turn), rows), rows), :]


def close(groups, partial, most, last, weight):
    tokens, columns = partial.shape
    return pl.pallas_call(
        close_kernel,
        out_shape=[jax.ShapeDtypeStruct((tokens // groups, columns), jnp.bfloat16)] * groups,
        in_specs=[VMEM] * 4,
        out_specs=[VMEM] * groups,
        scratch_shapes=[pltpu.VMEM((tokens, columns), jnp.bfloat16)],
        compiler_params=pltpu.CompilerParams(vmem_limit_bytes=SMALL),
        cost_estimate=pl.CostEstimate(
            flops=tokens * weight.size, bytes_accessed=8 * tokens * columns, transcendentals=0
        ),
    )(partial, most, last, weight)


def at_home(group):
    return group // TURNS[1] == lax.axis_index("head")


def divide_kernel(far, near, keep, send):
    group, _ = place()

    @pl.when(at_home(group))
    def _():
        keep[...] = near[...]
        send[...] = far[...]

    @pl.when(jnp.logical_not(at_home(group)))
    def _():
        keep[...] = far[...]
        send[...] = near[...]


def divide(far, near):
    return pl.pallas_call(
        divide_kernel,
        out_shape=[jax.ShapeDtypeStruct(near.shape, near.dtype)] * 2,
        in_specs=[VMEM] * 2,
        out_specs=[VMEM] * 2,
        compiler_params=pltpu.CompilerParams(vmem_limit_bytes=SMALL),
        cost_estimate=pl.CostEstimate(flops=0, bytes_accessed=8 * near.size, transcendentals=0),
    )(far, near)


def finish_kernel(kept_even, arrived_even, kept_odd, arrived_odd, bias, gate, out, held):
    group, _ = place()
    columns = kept_even.shape[1]
    side = lax.rem(group, 2)
    held[side] = kept_even[...].astype(jnp.float32) + arrived_even[...].astype(jnp.float32)
    held[1 - side] = kept_odd[...].astype(jnp.float32) + arrived_odd[...].astype(jnp.float32)
    for block in range(2):
        cols = slice(block * columns, (block + 1) * columns)
        out[:, cols] = (gate[:, cols] * (held[block] + bias[:, cols])).astype(jnp.bfloat16)


def finish(pieces, bias, gate):
    rows, columns = pieces[0].shape
    width = 2 * columns
    return pl.pallas_call(
        finish_kernel,
        out_shape=jax.ShapeDtypeStruct((rows, width), jnp.bfloat16),
        in_specs=[VMEM] * (len(pieces) + 2),
        out_specs=VMEM,
        scratch_shapes=[pltpu.VMEM((2, rows, columns), jnp.float32)],
        compiler_params=pltpu.CompilerParams(vmem_limit_bytes=SMALL),
        cost_estimate=pl.CostEstimate(flops=3 * rows * width, bytes_accessed=4 * rows * width, transcendentals=0),
    )(*pieces, bias.reshape(1, width), gate.reshape(1, width))


def after(value, *others):
    return lax.optimization_barrier((value, *others))[0]


def grouped_body(queries, stale_kv, codes, exponents, text_kv, out_weight, out_bias, out_gate):
    groups = lax.axis_size("patch") // SPREAD
    size = groups * SPREAD

    def swap(value, twist):
        return lax.ppermute(value, "patch", [(p, p ^ twist) for p in range(size)])

    def along(values):
        return [swap(values[turn], turn * SPREAD) for turn in TURNS[1:]]

    weight = out_weight.T
    cut = weight.shape[0] - 16
    *packed, own, early = pack(groups, queries, codes, exponents, weight, cut)
    text, stale = pick(groups, text_kv, stale_kv)

    every, some, query = merge([packed[0], *along(packed)])
    own_far, early = swap(own, 2), swap(early, 2)

    ready = (every, some, query, weight, early, own_far, text, stale)
    every, some, query, weight, early = lax.optimization_barrier(ready)[:5]
    near, some_far = swap(every, 1), swap(some, 2)
    share = stale.shape[2]
    operands = [query, every, near, text, stale]
    state = attend_call(near_kernel, operands, state_shapes(query), 2 * share + text.shape[1])

    some_far, own_far, weight = lax.optimization_barrier((some_far, own_far, weight, *state))[:3]
    late, late_corner = swap(weight[cut:], 2), swap(weight[cut:], 3)
    own_corner, some_corner = swap(own_far, 1), swap(some_far, 1)
    state = attend_call(middle_kernel, [query, own_far, some_far, stale, *state], state_shapes(query), share)
    weight, early = lax.optimization_barrier((weight, early, own_corner, some_corner, *state))[:2]
    weight_near, early_corner = swap(weight, 1), swap(early, 1)
    operands = [query, own_corner, some_corner, stale, *state]
    tokens, width = query.shape
    shapes = [jax.ShapeDtypeStruct((tokens, size), jnp.bfloat16) for size in (width, width - HD)]
    attended, most = attend_call(last_kernel, operands, shapes, share)

    second, third = swap(attended, 2 * SPREAD), swap(most, 3 * SPREAD)
    attended, late, late_corner = lax.optimization_barrier((attended, late, late_corner))
    first = swap(attended, SPREAD)
    passed = swap(second[:, width - HD :], SPREAD)
    weight = order(weight, weight_near, early, late, early_corner, late_corner)
    terms = close(groups, begin([attended, second, first], weight), third, passed, weight)
    second, third, first = along(terms)
    pieces = []
    for near, far in ((terms[0], second), (first, third)):
        kept, sent = divide(far, near)
        pieces += [kept, lax.ppermute(sent, "head", [(0, 1), (1, 0)])]
    return finish(pieces, out_bias, out_gate)


def solution(mesh):
    patches, halves = mesh.shape["patch"], mesh.shape["head"]
    placed = (
        P("patch", "head"),
        P(None, None, "head"),
        P(None, "patch", "head"),
        P(None, "patch", "head"),
        P(None, None, "head"),
        P("head", "patch"),
        P("head"),
        P("head"),
    )

    def body(*args):
        heads = args[0].shape[1] // HD
        groups = patches // SPREAD
        if groups != 4 or patches % SPREAD or heads % groups or halves != 2:
            return plain_body(*args)
        return grouped_body(*args)

    return jax.shard_map(body, mesh=mesh, in_specs=placed, out_specs=P("patch", "head"), check_vma=False)
```

```python
import functools

import jax
import jax.numpy as jnp
from jax import lax
from jax.experimental import pallas as pl
from jax.experimental.pallas import tpu as pltpu
from jax.sharding import PartitionSpec as P

HD = 128
SPREAD = 4
TURNS = (0, 2, 3, 1)
PACK_LIMIT = 56 << 20
SMALL = 16 << 20
PICK_LIMIT = 50 << 20
VMEM = pl.BlockSpec(memory_space=pltpu.VMEM)
HBM = pl.BlockSpec(memory_space=pltpu.HBM)
NT = (((1,), (1,)), ((), ()))


def plain_body(queries, stale_kv, codes, exponents, text_kv, out_weight, out_bias, out_gate):
    tok_rows = queries.shape[0]
    row_width = queries.shape[1]
    head_count = row_width // HD
    text_count = text_kv.shape[1]
    scale_factor = HD ** (-0.5)
    blocks = jnp.exp2(exponents.astype(jnp.float32))
    decoded = codes.astype(jnp.float32).reshape(2, tok_rows, head_count, HD) * blocks[..., None]
    decoded = decoded.astype(jnp.bfloat16).reshape(2, tok_rows, row_width)
    arrived = lax.all_gather(decoded, "patch", axis=1, tiled=True)
    all_rows = arrived.shape[1]
    query_heads = queries.reshape(tok_rows, head_count, HD)
    text_heads = text_kv.reshape(2, text_count, head_count, HD)
    stale_heads = stale_kv.reshape(2, all_rows, head_count, HD)
    arrived_heads = arrived.reshape(2, all_rows, head_count, HD)
    text_scores = jnp.einsum("thd,khd->htk", query_heads, text_heads[0], preferred_element_type=jnp.float32)
    rebuilt = stale_heads.astype(jnp.float32) + arrived_heads.astype(jnp.float32)
    image_scores = jnp.einsum(
        "thd,khd->htk", query_heads.astype(jnp.float32), rebuilt[0], precision=lax.Precision.HIGHEST
    )
    scores = jnp.concatenate([text_scores, image_scores], axis=2) * scale_factor
    row_peak = jnp.max(scores, axis=2, keepdims=True)
    weights = jnp.exp(scores - row_peak).astype(jnp.bfloat16)
    row_total = jnp.sum(weights.astype(jnp.float32), axis=2)
    text_part = jnp.einsum(
        "htk,khd->thd", weights[:, :, :text_count], text_heads[1], preferred_element_type=jnp.float32
    )
    image_part = jnp.einsum(
        "htk,khd->thd",
        weights[:, :, text_count:].astype(jnp.float32),
        rebuilt[1],
        precision=lax.Precision.HIGHEST,
    )
    attended = ((text_part + image_part) / row_total.T[:, :, None]).astype(jnp.bfloat16).reshape(tok_rows, row_width)
    partial_terms = jnp.dot(
        attended, lax.all_gather(out_weight, "patch", axis=1, tiled=True), preferred_element_type=jnp.float32
    )
    column_share = lax.psum_scatter(partial_terms, "head", scatter_dimension=1, tiled=True)
    return (out_gate * (column_share + out_bias)).astype(jnp.bfloat16)


def aligned(value, step):
    return pl.multiple_of(value * step, step)


def place():
    me = lax.axis_index("patch")
    return me // SPREAD, lax.rem(me, SPREAD)


def pack_kernel(queries_hbm, codes_hbm, exponents_hbm, *rest):
    outs, (codes, queries, exponents, held, sems) = rest[:-5], rest[-5:]
    groups, kinds, rows, width = held.shape
    group, _ = place()
    per = width // HD
    copies = [
        pltpu.make_async_copy(exponents_hbm, exponents, sems.at[0]),
        pltpu.make_async_copy(codes_hbm, codes, sems.at[1]),
        pltpu.make_async_copy(queries_hbm, queries, sems.at[2]),
    ]
    for copy in copies:
        copy.start()
    copies[0].wait()
    copies[1].wait()
    eye = lax.broadcasted_iota(jnp.int32, (rows, rows), 0) == lax.broadcasted_iota(jnp.int32, (rows, rows), 1)
    eye = eye.astype(jnp.float32).astype(jnp.bfloat16)
    for kind in range(kinds - 1):
        scales = jnp.left_shift(1, exponents[:, kind, :] + 16).astype(jnp.float32) * (2.0**-16)
        scales = lax.dot_general(eye, scales.astype(jnp.bfloat16), NT, preferred_element_type=jnp.float32)
        for head in range(groups * per):
            inside = slice((head % per) * HD, (head % per + 1) * HD)
            whole = slice(head * HD, (head + 1) * HD)
            decoded = codes[kind, :, whole].astype(jnp.float32) * scales[:, head : head + 1]
            held[head // per, kind, :, inside] = decoded.astype(jnp.bfloat16)
    copies[2].wait()
    for target in range(groups):
        held[target, kinds - 1] = queries[:, target * width : (target + 1) * width]
    for turn in range(groups):
        outs[turn][...] = held[jnp.bitwise_xor(group, turn)]
    outs[groups][...] = held[group, 0 : kinds - 1]


def pack(groups, queries, codes, exponents):
    rows, width = queries.shape
    kinds = codes.shape[0]
    share = width // groups
    bf16 = jnp.bfloat16
    exponents = exponents.transpose(2, 0, 1)
    shapes = [(kinds + 1, rows, share)] * groups + [(kinds, rows, share)]
    outs = pl.pallas_call(
        pack_kernel,
        out_shape=[jax.ShapeDtypeStruct(shape, bf16) for shape in shapes],
        in_specs=[HBM] * 3,
        out_specs=[VMEM] * len(shapes),
        scratch_shapes=[
            pltpu.VMEM(codes.shape, jnp.int32),
            pltpu.VMEM(queries.shape, bf16),
            pltpu.VMEM(exponents.shape, jnp.int32),
            pltpu.VMEM((groups, kinds + 1, rows, share), bf16),
            pltpu.SemaphoreType.DMA((3,)),
        ],
        compiler_params=pltpu.CompilerParams(vmem_limit_bytes=PACK_LIMIT),
        cost_estimate=pl.CostEstimate(flops=2 * codes.size, bytes_accessed=6 * codes.size, transcendentals=0),
    )(queries, codes, exponents)
    return outs


def pick_kernel(text_hbm, stale_hbm, text, stale, sems):
    group, spot = place()
    width = text.shape[2]
    groups = text_hbm.shape[2] // width
    rows = stale.shape[2] // groups
    columns = pl.ds(aligned(group, width), width)
    copies = [pltpu.make_async_copy(text_hbm.at[:, :, columns], text, sems.at[0])]
    for twist in range(SPREAD):
        for position in range(groups):
            origin = jnp.bitwise_xor(group, TURNS[position])
            token = origin * SPREAD + jnp.bitwise_xor(spot, twist)
            copies.append(
                pltpu.make_async_copy(
                    stale_hbm.at[:, pl.ds(aligned(token, rows), rows), columns],
                    stale.at[twist, :, pl.ds(position * rows, rows), :],
                    sems.at[len(copies)],
                )
            )
    for copy in copies:
        copy.start()
    for copy in copies:
        copy.wait()


def pick(groups, text_kv, stale_kv):
    kinds, texts, heads_width = text_kv.shape
    width = heads_width // groups
    return pl.pallas_call(
        pick_kernel,
        out_shape=[
            jax.ShapeDtypeStruct((kinds, texts, width), jnp.bfloat16),
            jax.ShapeDtypeStruct((SPREAD, kinds, stale_kv.shape[1] // SPREAD, width), jnp.bfloat16),
        ],
        in_specs=[HBM] * 2,
        out_specs=[VMEM] * 2,
        scratch_shapes=[pltpu.SemaphoreType.DMA((1 + SPREAD * groups,))],
        compiler_params=pltpu.CompilerParams(vmem_limit_bytes=PICK_LIMIT),
        cost_estimate=pl.CostEstimate(flops=0, bytes_accessed=8 << 20, transcendentals=0),
    )(text_kv, stale_kv)


def merge_kernel(*refs):
    parts, (every, some, query) = refs[:-3], refs[-3:]
    groups, kinds, rows, _ = every.shape
    group, _ = place()
    for position, part in enumerate(parts):
        every[position] = part[0:kinds]
        if position:
            some[position - 1] = part[0:kinds]
        origin = jnp.bitwise_xor(group, TURNS[position])
        query[pl.ds(aligned(origin, rows), rows), :] = part[kinds]


def merge(parts):
    kinds, rows, width = parts[0].shape
    shapes = [(len(parts), kinds - 1, rows, width), (len(parts) - 1, kinds - 1, rows, width), (len(parts) * rows, width)]
    return pl.pallas_call(
        merge_kernel,
        out_shape=[jax.ShapeDtypeStruct(shape, jnp.bfloat16) for shape in shapes],
        in_specs=[VMEM] * len(parts),
        out_specs=[VMEM] * 3,
        compiler_params=pltpu.CompilerParams(vmem_limit_bytes=SMALL),
        cost_estimate=pl.CostEstimate(flops=0, bytes_accessed=4 * len(parts) * parts[0].size, transcendentals=0),
    )(*parts)


def absorb(queries, segments, states):
    scores = [
        [
            lax.dot_general(
                query if key.shape[1] == HD else jnp.concatenate([query, query], axis=1),
                key,
                NT,
                preferred_element_type=jnp.float32,
            )
            * HD**-0.5
            for key, _ in parts
        ]
        for query, parts in zip(queries, segments)
    ]
    peaks = [[jnp.max(score, axis=1, keepdims=True) for score in row] for row in scores]
    if states is not None:
        peaks = [row + [state[0]] for row, state in zip(peaks, states)]
    peaks = [functools.reduce(jnp.maximum, row) for row in peaks]
    weights = [
        [jnp.exp(score - peak).astype(jnp.bfloat16) for score in row] for row, peak in zip(scores, peaks)
    ]
    totals = [sum(jnp.sum(w.astype(jnp.float32), axis=1, keepdims=True) for w in row) for row in weights]
    mixes = [
        sum(jnp.dot(w, value, preferred_element_type=jnp.float32) for w, (_, value) in zip(row, parts))
        for row, parts in zip(weights, segments)
    ]
    if states is not None:
        fades = [jnp.exp(state[0] - peak) for state, peak in zip(states, peaks)]
        totals = [total + state[1] * fade for total, state, fade in zip(totals, states, fades)]
        mixes = [mix + state[2] * fade for mix, state, fade in zip(mixes, states, fades)]
    return list(zip(peaks, totals, mixes))


def columns_of(width):
    return [slice(start, start + HD) for start in range(0, width, HD)]


def image_segment(stale, twist, residual):
    def of(cols):
        key = jnp.concatenate([stale[twist, 0, :, cols], residual(0, cols)], axis=1)
        value = stale[twist, 1, :, cols].astype(jnp.float32) + residual(1, cols).astype(jnp.float32)
        return key, value.astype(jnp.bfloat16)

    return of


def whole_part(part):
    return lambda kind, cols: part[:, kind, :, cols].reshape(-1, HD)


def split_part(own, some):
    return lambda kind, cols: jnp.concatenate([own[kind, :, cols], some[:, kind, :, cols].reshape(-1, HD)], axis=0)


def near_kernel(query, every, near, text, stale, peak, total, mixed):
    heads = columns_of(query.shape[1])
    images = [image_segment(stale, 0, whole_part(every)), image_segment(stale, 1, whole_part(near))]
    segments = [[(text[0, :, cols], text[1, :, cols])] + [image(cols) for image in images] for cols in heads]
    states = absorb([query[:, cols] for cols in heads], segments, None)
    for head, state in enumerate(states):
        peak[head], total[head], mixed[head] = state


def middle_kernel(query, own_far, some_far, stale, peak_in, total_in, mixed_in, peak, total, mixed):
    heads = columns_of(query.shape[1])
    image = image_segment(stale, 2, split_part(own_far, some_far))
    segments = [[image(cols)] for cols in heads]
    states = [(peak_in[head], total_in[head], mixed_in[head]) for head in range(len(heads))]
    states = absorb([query[:, cols] for cols in heads], segments, states)
    for head, state in enumerate(states):
        peak[head], total[head], mixed[head] = state


def last_kernel(query, own_corner, some_corner, stale, peak, total, mixed, out):
    heads = columns_of(query.shape[1])
    image = image_segment(stale, 3, split_part(own_corner, some_corner))
    states = [(peak[head], total[head], mixed[head]) for head in range(len(heads))]
    states = absorb([query[:, cols] for cols in heads], [[image(cols)] for cols in heads], states)
    for cols, (_, sums, mix) in zip(heads, states):
        out[:, cols] = (mix / sums).astype(jnp.bfloat16)


def attend_call(kernel, operands, shapes, keys):
    tokens, width = operands[0].shape
    return pl.pallas_call(
        kernel,
        out_shape=shapes,
        in_specs=[VMEM] * len(operands),
        out_specs=[VMEM] * len(shapes),
        compiler_params=pltpu.CompilerParams(vmem_limit_bytes=SMALL),
        cost_estimate=pl.CostEstimate(
            flops=8 * tokens * width * keys, bytes_accessed=8 * width * keys, transcendentals=tokens * keys * width // HD
        ),
    )(*operands)


def state_shapes(query):
    tokens, width = query.shape
    heads = width // HD
    return [jax.ShapeDtypeStruct((heads, tokens, size), jnp.float32) for size in (1, 1, HD)]


def stack_kernel(first, second, out):
    out[0] = first[...]
    out[1] = second[...]


def stack(first, second):
    return pl.pallas_call(
        stack_kernel,
        out_shape=jax.ShapeDtypeStruct((2, *first.shape), first.dtype),
        in_specs=[VMEM] * 2,
        out_specs=VMEM,
        compiler_params=pltpu.CompilerParams(vmem_limit_bytes=SMALL),
        cost_estimate=pl.CostEstimate(flops=0, bytes_accessed=8 * first.size, transcendentals=0),
    )(first, second)


def order_kernel(own, across, out):
    _, spot = place()
    span = own.shape[1]
    for twist in range(SPREAD):
        piece = (own, across)[twist % 2][twist // 2]
        out[pl.ds(aligned(jnp.bitwise_xor(spot, twist), span), span), :] = piece


def order(own, across):
    count, span, depth = own.shape
    shape = (2 * count * span, depth)
    return pl.pallas_call(
        order_kernel,
        out_shape=jax.ShapeDtypeStruct(shape, jnp.bfloat16),
        in_specs=[VMEM] * 2,
        out_specs=VMEM,
        compiler_params=pltpu.CompilerParams(vmem_limit_bytes=SMALL),
        cost_estimate=pl.CostEstimate(flops=0, bytes_accessed=4 * shape[0] * depth, transcendentals=0),
    )(own, across)


def term_of(part, weight, turn, width, skip=0):
    group, _ = place()
    start = jnp.bitwise_xor(group, turn) * width + skip
    columns = pl.ds(pl.multiple_of(start, HD), part.shape[1])
    return lax.dot_general(part[...], weight[:, columns], NT, preferred_element_type=jnp.float32)


def begin_kernel(own, second, first, weight, out):
    width = own.shape[1]
    out[...] = term_of(own, weight, 0, width) + term_of(second, weight, 2, width) + term_of(first, weight, 1, width)


def begin(parts, weight):
    tokens = parts[0].shape[0]
    columns, depth = weight.shape
    return pl.pallas_call(
        begin_kernel,
        out_shape=jax.ShapeDtypeStruct((tokens, columns), jnp.float32),
        in_specs=[VMEM] * (len(parts) + 1),
        out_specs=VMEM,
        compiler_params=pltpu.CompilerParams(vmem_limit_bytes=SMALL),
        cost_estimate=pl.CostEstimate(
            flops=2 * tokens * columns * depth, bytes_accessed=4 * tokens * columns, transcendentals=0
        ),
    )(*parts, weight)


def close_kernel(partial, third, weight, *rest):
    outs, total = rest[:-1], rest[-1]
    group, _ = place()
    rows = outs[0].shape[0]
    total[...] = (partial[...] + term_of(third, weight, 3, third.shape[1])).astype(jnp.bfloat16)
    for turn, out in enumerate(outs):
        out[...] = total[pl.ds(aligned(jnp.bitwise_xor(group, turn), rows), rows), :]


def close(groups, partial, third, weight):
    tokens, columns = partial.shape
    return pl.pallas_call(
        close_kernel,
        out_shape=[jax.ShapeDtypeStruct((tokens // groups, columns), jnp.bfloat16)] * groups,
        in_specs=[VMEM] * 3,
        out_specs=[VMEM] * groups,
        scratch_shapes=[pltpu.VMEM((tokens, columns), jnp.bfloat16)],
        compiler_params=pltpu.CompilerParams(vmem_limit_bytes=SMALL),
        cost_estimate=pl.CostEstimate(
            flops=tokens * weight.size, bytes_accessed=8 * tokens * columns, transcendentals=0
        ),
    )(partial, third, weight)


def at_home(group):
    return group // TURNS[1] == lax.axis_index("head")


def divide_kernel(far, near, keep, send):
    group, _ = place()

    @pl.when(at_home(group))
    def _():
        keep[...] = near[...]
        send[...] = far[...]

    @pl.when(jnp.logical_not(at_home(group)))
    def _():
        keep[...] = far[...]
        send[...] = near[...]


def divide(far, near):
    return pl.pallas_call(
        divide_kernel,
        out_shape=[jax.ShapeDtypeStruct(near.shape, near.dtype)] * 2,
        in_specs=[VMEM] * 2,
        out_specs=[VMEM] * 2,
        compiler_params=pltpu.CompilerParams(vmem_limit_bytes=SMALL),
        cost_estimate=pl.CostEstimate(flops=0, bytes_accessed=8 * near.size, transcendentals=0),
    )(far, near)


def finish_kernel(kept_even, arrived_even, kept_odd, arrived_odd, bias, gate, out, held):
    group, _ = place()
    columns = kept_even.shape[1]
    side = lax.rem(group, 2)
    held[side] = kept_even[...].astype(jnp.float32) + arrived_even[...].astype(jnp.float32)
    held[1 - side] = kept_odd[...].astype(jnp.float32) + arrived_odd[...].astype(jnp.float32)
    for block in range(2):
        cols = slice(block * columns, (block + 1) * columns)
        out[:, cols] = (gate[:, cols] * (held[block] + bias[:, cols])).astype(jnp.bfloat16)


def finish(pieces, bias, gate):
    rows, columns = pieces[0].shape
    width = 2 * columns
    return pl.pallas_call(
        finish_kernel,
        out_shape=jax.ShapeDtypeStruct((rows, width), jnp.bfloat16),
        in_specs=[VMEM] * (len(pieces) + 2),
        out_specs=VMEM,
        scratch_shapes=[pltpu.VMEM((2, rows, columns), jnp.float32)],
        compiler_params=pltpu.CompilerParams(vmem_limit_bytes=SMALL),
        cost_estimate=pl.CostEstimate(flops=3 * rows * width, bytes_accessed=4 * rows * width, transcendentals=0),
    )(*pieces, bias.reshape(1, width), gate.reshape(1, width))


def after(value, *others):
    return lax.optimization_barrier((value, *others))[0]


def grouped_body(queries, stale_kv, codes, exponents, text_kv, out_weight, out_bias, out_gate):
    groups = lax.axis_size("patch") // SPREAD
    size = groups * SPREAD

    def swap(value, twist):
        return lax.ppermute(value, "patch", [(p, p ^ twist) for p in range(size)])

    def along(values):
        return [swap(values[turn], turn * SPREAD) for turn in TURNS[1:]]

    weight = out_weight.T
    weight_far = swap(weight, 2)
    *packed, own = pack(groups, queries, codes, exponents)
    text, stale = pick(groups, text_kv, stale_kv)

    every, some, query = merge([packed[0], *along(packed)])
    own_far = swap(own, 2)

    ready = (every, some, query, weight, weight_far, own_far, text, stale)
    every, some, query, weight, weight_far = lax.optimization_barrier(ready)[:5]
    near, some_far = swap(every, 1), swap(some, 2)
    share = stale.shape[2]
    operands = [query, every, near, text, stale]
    state = attend_call(near_kernel, operands, state_shapes(query), 2 * share + text.shape[1])

    ready = (some_far, own_far, stack(weight, weight_far), *state)
    some_far, own_far, weight = lax.optimization_barrier(ready)[:3]
    own_corner, some_corner = swap(own_far, 1), swap(some_far, 1)
    state = attend_call(middle_kernel, [query, own_far, some_far, stale, *state], state_shapes(query), share)
    weight = after(weight, own_corner, some_corner, *state)
    weight_across = swap(weight, 1)
    operands = [query, own_corner, some_corner, stale, *state]
    shape = jax.ShapeDtypeStruct(query.shape, jnp.bfloat16)
    (attended,) = attend_call(last_kernel, operands, [shape], share)

    second, first = swap(attended, 2 * SPREAD), swap(attended, SPREAD)
    third = swap(second, SPREAD)
    weight = order(weight, weight_across)
    terms = close(groups, begin([attended, second, first], weight), third, weight)
    second, third, first = along(terms)
    pieces = []
    for near, far in ((terms[0], second), (first, third)):
        kept, sent = divide(far, near)
        pieces += [kept, lax.ppermute(sent, "head", [(0, 1), (1, 0)])]
    return finish(pieces, out_bias, out_gate)


def solution(mesh):
    patches, halves = mesh.shape["patch"], mesh.shape["head"]
    placed = (
        P("patch", "head"),
        P(None, None, "head"),
        P(None, "patch", "head"),
        P(None, "patch", "head"),
        P(None, None, "head"),
        P("head", "patch"),
        P("head"),
        P("head"),
    )

    def body(*args):
        heads = args[0].shape[1] // HD
        groups = patches // SPREAD
        if groups != 4 or patches % SPREAD or heads % groups or halves != 2:
            return plain_body(*args)
        return grouped_body(*args)

    return jax.shard_map(body, mesh=mesh, in_specs=placed, out_specs=P("patch", "head"), check_vma=False)
```

```python
import functools

import jax
import jax.numpy as jnp
from jax import lax
from jax.experimental import pallas as pl
from jax.experimental.pallas import tpu as pltpu
from jax.sharding import PartitionSpec as P

HD = 128
SPREAD = 4
TURNS = (0, 2, 3, 1)
PACK_LIMIT = 56 << 20
SMALL = 16 << 20
PICK_LIMIT = 50 << 20
VMEM = pl.BlockSpec(memory_space=pltpu.VMEM)
HBM = pl.BlockSpec(memory_space=pltpu.HBM)
NT = (((1,), (1,)), ((), ()))


def plain_body(queries, stale_kv, codes, exponents, text_kv, out_weight, out_bias, out_gate):
    tok_rows = queries.shape[0]
    row_width = queries.shape[1]
    head_count = row_width // HD
    text_count = text_kv.shape[1]
    scale_factor = HD ** (-0.5)
    blocks = jnp.exp2(exponents.astype(jnp.float32))
    decoded = codes.astype(jnp.float32).reshape(2, tok_rows, head_count, HD) * blocks[..., None]
    decoded = decoded.astype(jnp.bfloat16).reshape(2, tok_rows, row_width)
    arrived = lax.all_gather(decoded, "patch", axis=1, tiled=True)
    all_rows = arrived.shape[1]
    query_heads = queries.reshape(tok_rows, head_count, HD)
    text_heads = text_kv.reshape(2, text_count, head_count, HD)
    stale_heads = stale_kv.reshape(2, all_rows, head_count, HD)
    arrived_heads = arrived.reshape(2, all_rows, head_count, HD)
    text_scores = jnp.einsum("thd,khd->htk", query_heads, text_heads[0], preferred_element_type=jnp.float32)
    rebuilt = stale_heads.astype(jnp.float32) + arrived_heads.astype(jnp.float32)
    image_scores = jnp.einsum(
        "thd,khd->htk", query_heads.astype(jnp.float32), rebuilt[0], precision=lax.Precision.HIGHEST
    )
    scores = jnp.concatenate([text_scores, image_scores], axis=2) * scale_factor
    row_peak = jnp.max(scores, axis=2, keepdims=True)
    weights = jnp.exp(scores - row_peak).astype(jnp.bfloat16)
    row_total = jnp.sum(weights.astype(jnp.float32), axis=2)
    text_part = jnp.einsum(
        "htk,khd->thd", weights[:, :, :text_count], text_heads[1], preferred_element_type=jnp.float32
    )
    image_part = jnp.einsum(
        "htk,khd->thd",
        weights[:, :, text_count:].astype(jnp.float32),
        rebuilt[1],
        precision=lax.Precision.HIGHEST,
    )
    attended = ((text_part + image_part) / row_total.T[:, :, None]).astype(jnp.bfloat16).reshape(tok_rows, row_width)
    partial_terms = jnp.dot(
        attended, lax.all_gather(out_weight, "patch", axis=1, tiled=True), preferred_element_type=jnp.float32
    )
    column_share = lax.psum_scatter(partial_terms, "head", scatter_dimension=1, tiled=True)
    return (out_gate * (column_share + out_bias)).astype(jnp.bfloat16)


def aligned(value, step):
    return pl.multiple_of(value * step, step)


def place():
    me = lax.axis_index("patch")
    return me // SPREAD, lax.rem(me, SPREAD)


def pack_kernel(queries_hbm, codes_hbm, exponents_hbm, *rest):
    outs, (codes, queries, exponents, held, sems) = rest[:-5], rest[-5:]
    groups, kinds, rows, width = held.shape
    group, _ = place()
    per = width // HD
    copies = [
        pltpu.make_async_copy(exponents_hbm, exponents, sems.at[0]),
        pltpu.make_async_copy(codes_hbm, codes, sems.at[1]),
        pltpu.make_async_copy(queries_hbm, queries, sems.at[2]),
    ]
    for copy in copies:
        copy.start()
    copies[0].wait()
    copies[1].wait()
    eye = lax.broadcasted_iota(jnp.int32, (rows, rows), 0) == lax.broadcasted_iota(jnp.int32, (rows, rows), 1)
    eye = eye.astype(jnp.float32).astype(jnp.bfloat16)
    for kind in range(kinds - 1):
        scales = jnp.left_shift(1, exponents[:, kind, :] + 16).astype(jnp.float32) * (2.0**-16)
        scales = lax.dot_general(eye, scales.astype(jnp.bfloat16), NT, preferred_element_type=jnp.float32)
        for head in range(groups * per):
            inside = slice((head % per) * HD, (head % per + 1) * HD)
            whole = slice(head * HD, (head + 1) * HD)
            decoded = codes[kind, :, whole].astype(jnp.float32) * scales[:, head : head + 1]
            held[head // per, kind, :, inside] = decoded.astype(jnp.bfloat16)
    copies[2].wait()
    for target in range(groups):
        held[target, kinds - 1] = queries[:, target * width : (target + 1) * width]
    for turn in range(groups):
        outs[turn][...] = held[jnp.bitwise_xor(group, turn)]
    outs[groups][...] = held[group, 0 : kinds - 1]


def pack(groups, queries, codes, exponents):
    rows, width = queries.shape
    kinds = codes.shape[0]
    share = width // groups
    bf16 = jnp.bfloat16
    exponents = exponents.transpose(2, 0, 1)
    shapes = [(kinds + 1, rows, share)] * groups + [(kinds, rows, share)]
    outs = pl.pallas_call(
        pack_kernel,
        out_shape=[jax.ShapeDtypeStruct(shape, bf16) for shape in shapes],
        in_specs=[HBM] * 3,
        out_specs=[VMEM] * len(shapes),
        scratch_shapes=[
            pltpu.VMEM(codes.shape, jnp.int32),
            pltpu.VMEM(queries.shape, bf16),
            pltpu.VMEM(exponents.shape, jnp.int32),
            pltpu.VMEM((groups, kinds + 1, rows, share), bf16),
            pltpu.SemaphoreType.DMA((3,)),
        ],
        compiler_params=pltpu.CompilerParams(vmem_limit_bytes=PACK_LIMIT),
        cost_estimate=pl.CostEstimate(flops=2 * codes.size, bytes_accessed=6 * codes.size, transcendentals=0),
    )(queries, codes, exponents)
    return outs


def pick_kernel(text_hbm, stale_hbm, text, stale, sems):
    group, spot = place()
    width = text.shape[2]
    groups = text_hbm.shape[2] // width
    rows = stale.shape[2] // groups
    columns = pl.ds(aligned(group, width), width)
    copies = [pltpu.make_async_copy(text_hbm.at[:, :, columns], text, sems.at[0])]
    for twist in range(SPREAD):
        for position in range(groups):
            origin = jnp.bitwise_xor(group, TURNS[position])
            token = origin * SPREAD + jnp.bitwise_xor(spot, twist)
            copies.append(
                pltpu.make_async_copy(
                    stale_hbm.at[:, pl.ds(aligned(token, rows), rows), columns],
                    stale.at[twist, :, pl.ds(position * rows, rows), :],
                    sems.at[len(copies)],
                )
            )
    for copy in copies:
        copy.start()
    for copy in copies:
        copy.wait()


def pick(groups, text_kv, stale_kv):
    kinds, texts, heads_width = text_kv.shape
    width = heads_width // groups
    return pl.pallas_call(
        pick_kernel,
        out_shape=[
            jax.ShapeDtypeStruct((kinds, texts, width), jnp.bfloat16),
            jax.ShapeDtypeStruct((SPREAD, kinds, stale_kv.shape[1] // SPREAD, width), jnp.bfloat16),
        ],
        in_specs=[HBM] * 2,
        out_specs=[VMEM] * 2,
        scratch_shapes=[pltpu.SemaphoreType.DMA((1 + SPREAD * groups,))],
        compiler_params=pltpu.CompilerParams(vmem_limit_bytes=PICK_LIMIT),
        cost_estimate=pl.CostEstimate(flops=0, bytes_accessed=8 << 20, transcendentals=0),
    )(text_kv, stale_kv)


def merge_kernel(*refs):
    parts, (every, some, left, right, query) = refs[:-5], refs[-5:]
    groups, kinds, rows, _ = every.shape
    group, _ = place()
    for position, part in enumerate(parts):
        every[position] = part[0:kinds]
        if position:
            some[position - 1] = part[0:kinds]
        (left, right)[position // 2][position % 2] = part[0:kinds]
        origin = jnp.bitwise_xor(group, TURNS[position])
        query[pl.ds(aligned(origin, rows), rows), :] = part[kinds]


def merge(parts):
    kinds, rows, width = parts[0].shape
    counts = (len(parts), len(parts) - 1, len(parts) // 2, len(parts) // 2)
    shapes = [(count, kinds - 1, rows, width) for count in counts] + [(len(parts) * rows, width)]
    return pl.pallas_call(
        merge_kernel,
        out_shape=[jax.ShapeDtypeStruct(shape, jnp.bfloat16) for shape in shapes],
        in_specs=[VMEM] * len(parts),
        out_specs=[VMEM] * 5,
        compiler_params=pltpu.CompilerParams(vmem_limit_bytes=SMALL),
        cost_estimate=pl.CostEstimate(flops=0, bytes_accessed=4 * len(parts) * parts[0].size, transcendentals=0),
    )(*parts)


def absorb(queries, segments, states):
    scores = [
        [
            lax.dot_general(
                query if key.shape[1] == HD else jnp.concatenate([query, query], axis=1),
                key,
                NT,
                preferred_element_type=jnp.float32,
            )
            * HD**-0.5
            for key, _ in parts
        ]
        for query, parts in zip(queries, segments)
    ]
    peaks = [[jnp.max(score, axis=1, keepdims=True) for score in row] for row in scores]
    if states is not None:
        peaks = [row + [state[0]] for row, state in zip(peaks, states)]
    peaks = [functools.reduce(jnp.maximum, row) for row in peaks]
    weights = [
        [jnp.exp(score - peak).astype(jnp.bfloat16) for score in row] for row, peak in zip(scores, peaks)
    ]
    totals = [sum(jnp.sum(w.astype(jnp.float32), axis=1, keepdims=True) for w in row) for row in weights]
    mixes = [
        sum(jnp.dot(w, value, preferred_element_type=jnp.float32) for w, (_, value) in zip(row, parts))
        for row, parts in zip(weights, segments)
    ]
    if states is not None:
        fades = [jnp.exp(state[0] - peak) for state, peak in zip(states, peaks)]
        totals = [total + state[1] * fade for total, state, fade in zip(totals, states, fades)]
        mixes = [mix + state[2] * fade for mix, state, fade in zip(mixes, states, fades)]
    return list(zip(peaks, totals, mixes))


def columns_of(width):
    return [slice(start, start + HD) for start in range(0, width, HD)]


def image_segment(stale, twist, residual):
    def of(cols):
        key = jnp.concatenate([stale[twist, 0, :, cols], residual(0, cols)], axis=1)
        value = stale[twist, 1, :, cols].astype(jnp.float32) + residual(1, cols).astype(jnp.float32)
        return key, value.astype(jnp.bfloat16)

    return of


def whole_part(part):
    return lambda kind, cols: part[:, kind, :, cols].reshape(-1, HD)


def halves_part(*parts):
    wholes = [whole_part(part) for part in parts]
    return lambda kind, cols: jnp.concatenate([whole(kind, cols) for whole in wholes], axis=0)


def split_part(own, some):
    return lambda kind, cols: jnp.concatenate([own[kind, :, cols], some[:, kind, :, cols].reshape(-1, HD)], axis=0)


def near_kernel(query, every, left, right, text, stale, peak, total, mixed):
    heads = columns_of(query.shape[1])
    images = [image_segment(stale, 0, whole_part(every)), image_segment(stale, 1, halves_part(left, right))]
    segments = [[(text[0, :, cols], text[1, :, cols])] + [image(cols) for image in images] for cols in heads]
    states = absorb([query[:, cols] for cols in heads], segments, None)
    for head, state in enumerate(states):
        peak[head], total[head], mixed[head] = state


def middle_kernel(query, own_far, some_far, stale, peak_in, total_in, mixed_in, peak, total, mixed):
    heads = columns_of(query.shape[1])
    image = image_segment(stale, 2, split_part(own_far, some_far))
    segments = [[image(cols)] for cols in heads]
    states = [(peak_in[head], total_in[head], mixed_in[head]) for head in range(len(heads))]
    states = absorb([query[:, cols] for cols in heads], segments, states)
    for head, state in enumerate(states):
        peak[head], total[head], mixed[head] = state


def last_kernel(query, own_corner, some_corner, stale, peak, total, mixed, out):
    heads = columns_of(query.shape[1])
    image = image_segment(stale, 3, split_part(own_corner, some_corner))
    states = [(peak[head], total[head], mixed[head]) for head in range(len(heads))]
    states = absorb([query[:, cols] for cols in heads], [[image(cols)] for cols in heads], states)
    for cols, (_, sums, mix) in zip(heads, states):
        out[:, cols] = (mix / sums).astype(jnp.bfloat16)


def attend_call(kernel, operands, shapes, keys):
    tokens, width = operands[0].shape
    return pl.pallas_call(
        kernel,
        out_shape=shapes,
        in_specs=[VMEM] * len(operands),
        out_specs=[VMEM] * len(shapes),
        compiler_params=pltpu.CompilerParams(vmem_limit_bytes=SMALL),
        cost_estimate=pl.CostEstimate(
            flops=8 * tokens * width * keys, bytes_accessed=8 * width * keys, transcendentals=tokens * keys * width // HD
        ),
    )(*operands)


def state_shapes(query):
    tokens, width = query.shape
    heads = width // HD
    return [jax.ShapeDtypeStruct((heads, tokens, size), jnp.float32) for size in (1, 1, HD)]


def stack_kernel(first, second, out):
    out[0] = first[...]
    out[1] = second[...]


def stack(first, second):
    return pl.pallas_call(
        stack_kernel,
        out_shape=jax.ShapeDtypeStruct((2, *first.shape), first.dtype),
        in_specs=[VMEM] * 2,
        out_specs=VMEM,
        compiler_params=pltpu.CompilerParams(vmem_limit_bytes=SMALL),
        cost_estimate=pl.CostEstimate(flops=0, bytes_accessed=8 * first.size, transcendentals=0),
    )(first, second)


def order_kernel(own, across, out):
    _, spot = place()
    span = own.shape[1]
    for twist in range(SPREAD):
        piece = (own, across)[twist % 2][twist // 2]
        out[pl.ds(aligned(jnp.bitwise_xor(spot, twist), span), span), :] = piece


def order(own, across):
    count, span, depth = own.shape
    shape = (2 * count * span, depth)
    return pl.pallas_call(
        order_kernel,
        out_shape=jax.ShapeDtypeStruct(shape, jnp.bfloat16),
        in_specs=[VMEM] * 2,
        out_specs=VMEM,
        compiler_params=pltpu.CompilerParams(vmem_limit_bytes=SMALL),
        cost_estimate=pl.CostEstimate(flops=0, bytes_accessed=4 * shape[0] * depth, transcendentals=0),
    )(own, across)


def term_of(part, weight, turn, width, skip=0):
    group, _ = place()
    start = jnp.bitwise_xor(group, turn) * width + skip
    columns = pl.ds(pl.multiple_of(start, HD), part.shape[1])
    return lax.dot_general(part[...], weight[:, columns], NT, preferred_element_type=jnp.float32)


def begin_kernel(own, second, first, weight, out):
    width = own.shape[1]
    out[...] = term_of(own, weight, 0, width) + term_of(second, weight, 2, width) + term_of(first, weight, 1, width)


def begin(parts, weight):
    tokens = parts[0].shape[0]
    columns, depth = weight.shape
    return pl.pallas_call(
        begin_kernel,
        out_shape=jax.ShapeDtypeStruct((tokens, columns), jnp.float32),
        in_specs=[VMEM] * (len(parts) + 1),
        out_specs=VMEM,
        compiler_params=pltpu.CompilerParams(vmem_limit_bytes=SMALL),
        cost_estimate=pl.CostEstimate(
            flops=2 * tokens * columns * depth, bytes_accessed=4 * tokens * columns, transcendentals=0
        ),
    )(*parts, weight)


def close_kernel(partial, third, weight, *rest):
    outs, total = rest[:-1], rest[-1]
    group, _ = place()
    rows = outs[0].shape[0]
    total[...] = (partial[...] + term_of(third, weight, 3, third.shape[1])).astype(jnp.bfloat16)
    for turn, out in enumerate(outs):
        out[...] = total[pl.ds(aligned(jnp.bitwise_xor(group, turn), rows), rows), :]


def close(groups, partial, third, weight):
    tokens, columns = partial.shape
    return pl.pallas_call(
        close_kernel,
        out_shape=[jax.ShapeDtypeStruct((tokens // groups, columns), jnp.bfloat16)] * groups,
        in_specs=[VMEM] * 3,
        out_specs=[VMEM] * groups,
        scratch_shapes=[pltpu.VMEM((tokens, columns), jnp.bfloat16)],
        compiler_params=pltpu.CompilerParams(vmem_limit_bytes=SMALL),
        cost_estimate=pl.CostEstimate(
            flops=tokens * weight.size, bytes_accessed=8 * tokens * columns, transcendentals=0
        ),
    )(partial, third, weight)


def at_home(group):
    return group // TURNS[1] == lax.axis_index("head")


def divide_kernel(far, near, keep, send):
    group, _ = place()

    @pl.when(at_home(group))
    def _():
        keep[...] = near[...]
        send[...] = far[...]

    @pl.when(jnp.logical_not(at_home(group)))
    def _():
        keep[...] = far[...]
        send[...] = near[...]


def divide(far, near):
    return pl.pallas_call(
        divide_kernel,
        out_shape=[jax.ShapeDtypeStruct(near.shape, near.dtype)] * 2,
        in_specs=[VMEM] * 2,
        out_specs=[VMEM] * 2,
        compiler_params=pltpu.CompilerParams(vmem_limit_bytes=SMALL),
        cost_estimate=pl.CostEstimate(flops=0, bytes_accessed=8 * near.size, transcendentals=0),
    )(far, near)


def finish_kernel(kept_even, arrived_even, kept_odd, arrived_odd, bias, gate, out, held):
    group, _ = place()
    columns = kept_even.shape[1]
    side = lax.rem(group, 2)
    held[side] = kept_even[...].astype(jnp.float32) + arrived_even[...].astype(jnp.float32)
    held[1 - side] = kept_odd[...].astype(jnp.float32) + arrived_odd[...].astype(jnp.float32)
    for block in range(2):
        cols = slice(block * columns, (block + 1) * columns)
        out[:, cols] = (gate[:, cols] * (held[block] + bias[:, cols])).astype(jnp.bfloat16)


def finish(pieces, bias, gate):
    rows, columns = pieces[0].shape
    width = 2 * columns
    return pl.pallas_call(
        finish_kernel,
        out_shape=jax.ShapeDtypeStruct((rows, width), jnp.bfloat16),
        in_specs=[VMEM] * (len(pieces) + 2),
        out_specs=VMEM,
        scratch_shapes=[pltpu.VMEM((2, rows, columns), jnp.float32)],
        compiler_params=pltpu.CompilerParams(vmem_limit_bytes=SMALL),
        cost_estimate=pl.CostEstimate(flops=3 * rows * width, bytes_accessed=4 * rows * width, transcendentals=0),
    )(*pieces, bias.reshape(1, width), gate.reshape(1, width))


def after(value, *others):
    return lax.optimization_barrier((value, *others))[0]


def grouped_body(queries, stale_kv, codes, exponents, text_kv, out_weight, out_bias, out_gate):
    groups = lax.axis_size("patch") // SPREAD
    size = groups * SPREAD

    def swap(value, twist):
        return lax.ppermute(value, "patch", [(p, p ^ twist) for p in range(size)])

    def along(values):
        return [swap(values[turn], turn * SPREAD) for turn in TURNS[1:]]

    weight = out_weight.T
    weight_far = swap(weight, 2)
    *packed, own = pack(groups, queries, codes, exponents)
    text, stale = pick(groups, text_kv, stale_kv)

    every, some, left, right, query = merge([packed[0], *along(packed)])
    own_far = swap(own, 2)

    ready = (every, some, left, right, query, weight, weight_far, own_far, text, stale)
    every, some, left, right, query, weight, weight_far = lax.optimization_barrier(ready)[:7]
    left, right, some_far = swap(left, 1), swap(right, 1), swap(some, 2)
    share = stale.shape[2]
    operands = [query, every, left, right, text, stale]
    state = attend_call(near_kernel, operands, state_shapes(query), 2 * share + text.shape[1])

    ready = (some_far, own_far, stack(weight, weight_far), *state)
    some_far, own_far, weight = lax.optimization_barrier(ready)[:3]
    own_corner, some_corner = swap(own_far, 1), swap(some_far, 1)
    state = attend_call(middle_kernel, [query, own_far, some_far, stale, *state], state_shapes(query), share)
    weight = after(weight, own_corner, some_corner, *state)
    weight_across = swap(weight, 1)
    operands = [query, own_corner, some_corner, stale, *state]
    shape = jax.ShapeDtypeStruct(query.shape, jnp.bfloat16)
    (attended,) = attend_call(last_kernel, operands, [shape], share)

    second, first = swap(attended, 2 * SPREAD), swap(attended, SPREAD)
    third = swap(second, SPREAD)
    weight = order(weight, weight_across)
    terms = close(groups, begin([attended, second, first], weight), third, weight)
    second, third, first = along(terms)
    pieces = []
    for near, far in ((terms[0], second), (first, third)):
        kept, sent = divide(far, near)
        pieces += [kept, lax.ppermute(sent, "head", [(0, 1), (1, 0)])]
    return finish(pieces, out_bias, out_gate)


def solution(mesh):
    patches, halves = mesh.shape["patch"], mesh.shape["head"]
    placed = (
        P("patch", "head"),
        P(None, None, "head"),
        P(None, "patch", "head"),
        P(None, "patch", "head"),
        P(None, None, "head"),
        P("head", "patch"),
        P("head"),
        P("head"),
    )

    def body(*args):
        heads = args[0].shape[1] // HD
        groups = patches // SPREAD
        if groups != 4 or patches % SPREAD or heads % groups or halves != 2:
            return plain_body(*args)
        return grouped_body(*args)

    return jax.shard_map(body, mesh=mesh, in_specs=placed, out_specs=P("patch", "head"), check_vma=False)
```

```python
import functools

import jax
import jax.numpy as jnp
from jax import lax
from jax.experimental import pallas as pl
from jax.experimental.pallas import tpu as pltpu
from jax.sharding import PartitionSpec as P

HD = 128
SPREAD = 4
TURNS = (0, 2, 3, 1)
PACK_LIMIT = 56 << 20
SMALL = 16 << 20
PICK_LIMIT = 50 << 20
VMEM = pl.BlockSpec(memory_space=pltpu.VMEM)
HBM = pl.BlockSpec(memory_space=pltpu.HBM)
NT = (((1,), (1,)), ((), ()))


def plain_body(queries, stale_kv, codes, exponents, text_kv, out_weight, out_bias, out_gate):
    tok_rows = queries.shape[0]
    row_width = queries.shape[1]
    head_count = row_width // HD
    text_count = text_kv.shape[1]
    scale_factor = HD ** (-0.5)
    blocks = jnp.exp2(exponents.astype(jnp.float32))
    decoded = codes.astype(jnp.float32).reshape(2, tok_rows, head_count, HD) * blocks[..., None]
    decoded = decoded.astype(jnp.bfloat16).reshape(2, tok_rows, row_width)
    arrived = lax.all_gather(decoded, "patch", axis=1, tiled=True)
    all_rows = arrived.shape[1]
    query_heads = queries.reshape(tok_rows, head_count, HD)
    text_heads = text_kv.reshape(2, text_count, head_count, HD)
    stale_heads = stale_kv.reshape(2, all_rows, head_count, HD)
    arrived_heads = arrived.reshape(2, all_rows, head_count, HD)
    text_scores = jnp.einsum("thd,khd->htk", query_heads, text_heads[0], preferred_element_type=jnp.float32)
    rebuilt = stale_heads.astype(jnp.float32) + arrived_heads.astype(jnp.float32)
    image_scores = jnp.einsum(
        "thd,khd->htk", query_heads.astype(jnp.float32), rebuilt[0], precision=lax.Precision.HIGHEST
    )
    scores = jnp.concatenate([text_scores, image_scores], axis=2) * scale_factor
    row_peak = jnp.max(scores, axis=2, keepdims=True)
    weights = jnp.exp(scores - row_peak).astype(jnp.bfloat16)
    row_total = jnp.sum(weights.astype(jnp.float32), axis=2)
    text_part = jnp.einsum(
        "htk,khd->thd", weights[:, :, :text_count], text_heads[1], preferred_element_type=jnp.float32
    )
    image_part = jnp.einsum(
        "htk,khd->thd",
        weights[:, :, text_count:].astype(jnp.float32),
        rebuilt[1],
        precision=lax.Precision.HIGHEST,
    )
    attended = ((text_part + image_part) / row_total.T[:, :, None]).astype(jnp.bfloat16).reshape(tok_rows, row_width)
    partial_terms = jnp.dot(
        attended, lax.all_gather(out_weight, "patch", axis=1, tiled=True), preferred_element_type=jnp.float32
    )
    column_share = lax.psum_scatter(partial_terms, "head", scatter_dimension=1, tiled=True)
    return (out_gate * (column_share + out_bias)).astype(jnp.bfloat16)


def aligned(value, step):
    return pl.multiple_of(value * step, step)


def place():
    me = lax.axis_index("patch")
    return me // SPREAD, lax.rem(me, SPREAD)


def pack_kernel(queries_hbm, codes_hbm, exponents_hbm, *rest):
    outs, (codes, queries, exponents, held, sems) = rest[:-5], rest[-5:]
    groups, kinds, rows, width = held.shape
    group, _ = place()
    per = width // HD
    copies = [
        pltpu.make_async_copy(exponents_hbm, exponents, sems.at[0]),
        pltpu.make_async_copy(codes_hbm, codes, sems.at[1]),
        pltpu.make_async_copy(queries_hbm, queries, sems.at[2]),
    ]
    for copy in copies:
        copy.start()
    copies[0].wait()
    copies[1].wait()
    eye = lax.broadcasted_iota(jnp.int32, (rows, rows), 0) == lax.broadcasted_iota(jnp.int32, (rows, rows), 1)
    eye = eye.astype(jnp.float32).astype(jnp.bfloat16)
    for kind in range(kinds - 1):
        scales = jnp.left_shift(1, exponents[:, kind, :] + 16).astype(jnp.float32) * (2.0**-16)
        scales = lax.dot_general(eye, scales.astype(jnp.bfloat16), NT, preferred_element_type=jnp.float32)
        for head in range(groups * per):
            inside = slice((head % per) * HD, (head % per + 1) * HD)
            whole = slice(head * HD, (head + 1) * HD)
            decoded = codes[kind, :, whole].astype(jnp.float32) * scales[:, head : head + 1]
            held[head // per, kind, :, inside] = decoded.astype(jnp.bfloat16)
    copies[2].wait()
    for target in range(groups):
        held[target, kinds - 1] = queries[:, target * width : (target + 1) * width]
    for turn in range(groups):
        outs[turn][...] = held[jnp.bitwise_xor(group, turn)]
    outs[groups][...] = held[group, 0 : kinds - 1]


def pack(groups, queries, codes, exponents):
    rows, width = queries.shape
    kinds = codes.shape[0]
    share = width // groups
    bf16 = jnp.bfloat16
    exponents = exponents.transpose(2, 0, 1)
    shapes = [(kinds + 1, rows, share)] * groups + [(kinds, rows, share)]
    outs = pl.pallas_call(
        pack_kernel,
        out_shape=[jax.ShapeDtypeStruct(shape, bf16) for shape in shapes],
        in_specs=[HBM] * 3,
        out_specs=[VMEM] * len(shapes),
        scratch_shapes=[
            pltpu.VMEM(codes.shape, jnp.int32),
            pltpu.VMEM(queries.shape, bf16),
            pltpu.VMEM(exponents.shape, jnp.int32),
            pltpu.VMEM((groups, kinds + 1, rows, share), bf16),
            pltpu.SemaphoreType.DMA((3,)),
        ],
        compiler_params=pltpu.CompilerParams(vmem_limit_bytes=PACK_LIMIT),
        cost_estimate=pl.CostEstimate(flops=2 * codes.size, bytes_accessed=6 * codes.size, transcendentals=0),
    )(queries, codes, exponents)
    return outs


def pick_kernel(text_hbm, stale_hbm, text, stale, sems):
    group, spot = place()
    width = text.shape[2]
    groups = text_hbm.shape[2] // width
    rows = stale.shape[2] // groups
    columns = pl.ds(aligned(group, width), width)
    copies = [pltpu.make_async_copy(text_hbm.at[:, :, columns], text, sems.at[0])]
    for twist in range(SPREAD):
        for position in range(groups):
            origin = jnp.bitwise_xor(group, TURNS[position])
            token = origin * SPREAD + jnp.bitwise_xor(spot, twist)
            copies.append(
                pltpu.make_async_copy(
                    stale_hbm.at[:, pl.ds(aligned(token, rows), rows), columns],
                    stale.at[twist, :, pl.ds(position * rows, rows), :],
                    sems.at[len(copies)],
                )
            )
    for copy in copies:
        copy.start()
    for copy in copies:
        copy.wait()


def pick(groups, text_kv, stale_kv):
    kinds, texts, heads_width = text_kv.shape
    width = heads_width // groups
    return pl.pallas_call(
        pick_kernel,
        out_shape=[
            jax.ShapeDtypeStruct((kinds, texts, width), jnp.bfloat16),
            jax.ShapeDtypeStruct((SPREAD, kinds, stale_kv.shape[1] // SPREAD, width), jnp.bfloat16),
        ],
        in_specs=[HBM] * 2,
        out_specs=[VMEM] * 2,
        scratch_shapes=[pltpu.SemaphoreType.DMA((1 + SPREAD * groups,))],
        compiler_params=pltpu.CompilerParams(vmem_limit_bytes=PICK_LIMIT),
        cost_estimate=pl.CostEstimate(flops=0, bytes_accessed=8 << 20, transcendentals=0),
    )(text_kv, stale_kv)


def merge_kernel(*refs):
    parts, (every, some, left, right, query) = refs[:-5], refs[-5:]
    groups, kinds, rows, _ = every.shape
    group, _ = place()
    for position, part in enumerate(parts):
        every[position] = part[0:kinds]
        if position:
            some[position - 1] = part[0:kinds]
        (left, right)[position // 2][position % 2] = part[0:kinds]
        origin = jnp.bitwise_xor(group, TURNS[position])
        query[pl.ds(aligned(origin, rows), rows), :] = part[kinds]


def merge(parts):
    kinds, rows, width = parts[0].shape
    counts = (len(parts), len(parts) - 1, len(parts) // 2, len(parts) // 2)
    shapes = [(count, kinds - 1, rows, width) for count in counts] + [(len(parts) * rows, width)]
    return pl.pallas_call(
        merge_kernel,
        out_shape=[jax.ShapeDtypeStruct(shape, jnp.bfloat16) for shape in shapes],
        in_specs=[VMEM] * len(parts),
        out_specs=[VMEM] * 5,
        compiler_params=pltpu.CompilerParams(vmem_limit_bytes=SMALL),
        cost_estimate=pl.CostEstimate(flops=0, bytes_accessed=4 * len(parts) * parts[0].size, transcendentals=0),
    )(*parts)


def absorb(queries, segments, states):
    scores = [
        [
            lax.dot_general(
                query if key.shape[1] == HD else jnp.concatenate([query, query], axis=1),
                key,
                NT,
                preferred_element_type=jnp.float32,
            )
            * HD**-0.5
            for key, _ in parts
        ]
        for query, parts in zip(queries, segments)
    ]
    peaks = [[jnp.max(score, axis=1, keepdims=True) for score in row] for row in scores]
    if states is not None:
        peaks = [row + [state[0]] for row, state in zip(peaks, states)]
    peaks = [functools.reduce(jnp.maximum, row) for row in peaks]
    weights = [
        [jnp.exp(score - peak).astype(jnp.bfloat16) for score in row] for row, peak in zip(scores, peaks)
    ]
    totals = [sum(jnp.sum(w.astype(jnp.float32), axis=1, keepdims=True) for w in row) for row in weights]
    mixes = [
        sum(jnp.dot(w, value, preferred_element_type=jnp.float32) for w, (_, value) in zip(row, parts))
        for row, parts in zip(weights, segments)
    ]
    if states is not None:
        fades = [jnp.exp(state[0] - peak) for state, peak in zip(states, peaks)]
        totals = [total + state[1] * fade for total, state, fade in zip(totals, states, fades)]
        mixes = [mix + state[2] * fade for mix, state, fade in zip(mixes, states, fades)]
    return list(zip(peaks, totals, mixes))


def columns_of(width):
    return [slice(start, start + HD) for start in range(0, width, HD)]


def image_segment(stale, twist, residual):
    def of(cols):
        key = jnp.concatenate([stale[twist, 0, :, cols], residual(0, cols)], axis=1)
        value = stale[twist, 1, :, cols].astype(jnp.float32) + residual(1, cols).astype(jnp.float32)
        return key, value.astype(jnp.bfloat16)

    return of


def whole_part(part):
    return lambda kind, cols: part[:, kind, :, cols].reshape(-1, HD)


def halves_part(*parts):
    wholes = [whole_part(part) for part in parts]
    return lambda kind, cols: jnp.concatenate([whole(kind, cols) for whole in wholes], axis=0)


def split_part(own, some):
    return lambda kind, cols: jnp.concatenate([own[kind, :, cols], some[:, kind, :, cols].reshape(-1, HD)], axis=0)


def near_kernel(query, every, left, right, text, stale, peak, total, mixed):
    heads = columns_of(query.shape[1])
    images = [image_segment(stale, 0, whole_part(every)), image_segment(stale, 1, halves_part(left, right))]
    segments = [[(text[0, :, cols], text[1, :, cols])] + [image(cols) for image in images] for cols in heads]
    states = absorb([query[:, cols] for cols in heads], segments, None)
    for head, state in enumerate(states):
        peak[head], total[head], mixed[head] = state


def middle_kernel(query, own_far, some_far, stale, peak_in, total_in, mixed_in, peak, total, mixed):
    heads = columns_of(query.shape[1])
    image = image_segment(stale, 2, split_part(own_far, some_far))
    segments = [[image(cols)] for cols in heads]
    states = [(peak_in[head], total_in[head], mixed_in[head]) for head in range(len(heads))]
    states = absorb([query[:, cols] for cols in heads], segments, states)
    for head, state in enumerate(states):
        peak[head], total[head], mixed[head] = state


def last_kernel(query, own_corner, some_corner, stale, peak, total, mixed, out):
    heads = columns_of(query.shape[1])
    image = image_segment(stale, 3, split_part(own_corner, some_corner))
    states = [(peak[head], total[head], mixed[head]) for head in range(len(heads))]
    states = absorb([query[:, cols] for cols in heads], [[image(cols)] for cols in heads], states)
    for cols, (_, sums, mix) in zip(heads, states):
        out[:, cols] = (mix / sums).astype(jnp.bfloat16)


def attend_call(kernel, operands, shapes, keys):
    tokens, width = operands[0].shape
    return pl.pallas_call(
        kernel,
        out_shape=shapes,
        in_specs=[VMEM] * len(operands),
        out_specs=[VMEM] * len(shapes),
        compiler_params=pltpu.CompilerParams(vmem_limit_bytes=SMALL),
        cost_estimate=pl.CostEstimate(
            flops=8 * tokens * width * keys, bytes_accessed=8 * width * keys, transcendentals=tokens * keys * width // HD
        ),
    )(*operands)


def state_shapes(query):
    tokens, width = query.shape
    heads = width // HD
    return [jax.ShapeDtypeStruct((heads, tokens, size), jnp.float32) for size in (1, 1, HD)]


def stack_kernel(first, second, out):
    out[0] = first[...]
    out[1] = second[...]


def stack(first, second):
    return pl.pallas_call(
        stack_kernel,
        out_shape=jax.ShapeDtypeStruct((2, *first.shape), first.dtype),
        in_specs=[VMEM] * 2,
        out_specs=VMEM,
        compiler_params=pltpu.CompilerParams(vmem_limit_bytes=SMALL),
        cost_estimate=pl.CostEstimate(flops=0, bytes_accessed=8 * first.size, transcendentals=0),
    )(first, second)


def order_kernel(own, across, out):
    _, spot = place()
    span = own.shape[1]
    for twist in range(SPREAD):
        piece = (own, across)[twist % 2][twist // 2]
        out[pl.ds(aligned(jnp.bitwise_xor(spot, twist), span), span), :] = piece


def order(own, across):
    count, span, depth = own.shape
    shape = (2 * count * span, depth)
    return pl.pallas_call(
        order_kernel,
        out_shape=jax.ShapeDtypeStruct(shape, jnp.bfloat16),
        in_specs=[VMEM] * 2,
        out_specs=VMEM,
        compiler_params=pltpu.CompilerParams(vmem_limit_bytes=SMALL),
        cost_estimate=pl.CostEstimate(flops=0, bytes_accessed=4 * shape[0] * depth, transcendentals=0),
    )(own, across)


def term_of(part, weight, turn, width, skip=0):
    group, _ = place()
    start = jnp.bitwise_xor(group, turn) * width + skip
    columns = pl.ds(pl.multiple_of(start, HD), part.shape[1])
    return lax.dot_general(part[...], weight[:, columns], NT, preferred_element_type=jnp.float32)


def begin_kernel(own, second, first, weight, out):
    width = own.shape[1]
    out[...] = term_of(own, weight, 0, width) + term_of(second, weight, 2, width) + term_of(first, weight, 1, width)


def begin(parts, weight):
    tokens = parts[0].shape[0]
    columns, depth = weight.shape
    return pl.pallas_call(
        begin_kernel,
        out_shape=jax.ShapeDtypeStruct((tokens, columns), jnp.float32),
        in_specs=[VMEM] * (len(parts) + 1),
        out_specs=VMEM,
        compiler_params=pltpu.CompilerParams(vmem_limit_bytes=SMALL),
        cost_estimate=pl.CostEstimate(
            flops=2 * tokens * columns * depth, bytes_accessed=4 * tokens * columns, transcendentals=0
        ),
    )(*parts, weight)


def close_kernel(partial, third, weight, *rest):
    outs, total = rest[:-1], rest[-1]
    group, _ = place()
    rows = outs[0].shape[0]
    total[...] = (partial[...] + term_of(third, weight, 3, third.shape[1])).astype(jnp.bfloat16)
    for turn, out in enumerate(outs):
        out[...] = total[pl.ds(aligned(jnp.bitwise_xor(group, turn), rows), rows), :]


def close(groups, partial, third, weight):
    tokens, columns = partial.shape
    return pl.pallas_call(
        close_kernel,
        out_shape=[jax.ShapeDtypeStruct((tokens // groups, columns), jnp.bfloat16)] * groups,
        in_specs=[VMEM] * 3,
        out_specs=[VMEM] * groups,
        scratch_shapes=[pltpu.VMEM((tokens, columns), jnp.bfloat16)],
        compiler_params=pltpu.CompilerParams(vmem_limit_bytes=SMALL),
        cost_estimate=pl.CostEstimate(
            flops=tokens * weight.size, bytes_accessed=8 * tokens * columns, transcendentals=0
        ),
    )(partial, third, weight)


def divide_kernel(*refs):
    parts, (keep, send, held) = refs[:-3], refs[-3:]
    group, _ = place()
    half = lax.axis_index("head")
    blocks = keep.shape[0]
    for position, part in enumerate(parts):
        held[jnp.bitwise_xor(group, TURNS[position])] = part[...]
    for block in range(blocks):
        keep[block] = held[half * blocks + block]
        send[block] = held[(1 - half) * blocks + block]


def divide(parts):
    groups = len(parts)
    shape = jax.ShapeDtypeStruct((groups // 2, *parts[0].shape), jnp.bfloat16)
    return pl.pallas_call(
        divide_kernel,
        out_shape=[shape] * 2,
        in_specs=[VMEM] * groups,
        out_specs=[VMEM] * 2,
        scratch_shapes=[pltpu.VMEM((groups, *parts[0].shape), jnp.bfloat16)],
        compiler_params=pltpu.CompilerParams(vmem_limit_bytes=SMALL),
        cost_estimate=pl.CostEstimate(flops=0, bytes_accessed=4 * groups * parts[0].size, transcendentals=0),
    )(*parts)


def finish_kernel(kept, arrived, bias, gate, out):
    blocks, _, columns = kept.shape
    for block in range(blocks):
        cols = slice(block * columns, (block + 1) * columns)
        total = kept[block].astype(jnp.float32) + arrived[block].astype(jnp.float32)
        out[:, cols] = (gate[:, cols] * (total + bias[:, cols])).astype(jnp.bfloat16)


def finish(kept, arrived, bias, gate):
    blocks, rows, columns = kept.shape
    width = blocks * columns
    return pl.pallas_call(
        finish_kernel,
        out_shape=jax.ShapeDtypeStruct((rows, width), jnp.bfloat16),
        in_specs=[VMEM] * 4,
        out_specs=VMEM,
        compiler_params=pltpu.CompilerParams(vmem_limit_bytes=SMALL),
        cost_estimate=pl.CostEstimate(flops=3 * rows * width, bytes_accessed=4 * rows * width, transcendentals=0),
    )(kept, arrived, bias.reshape(1, width), gate.reshape(1, width))


def after(value, *others):
    return lax.optimization_barrier((value, *others))[0]


def grouped_body(queries, stale_kv, codes, exponents, text_kv, out_weight, out_bias, out_gate):
    groups = lax.axis_size("patch") // SPREAD
    size = groups * SPREAD

    def swap(value, twist):
        return lax.ppermute(value, "patch", [(p, p ^ twist) for p in range(size)])

    def along(values):
        return [swap(values[turn], turn * SPREAD) for turn in TURNS[1:]]

    weight = out_weight.T
    weight_far = swap(weight, 2)
    *packed, own = pack(groups, queries, codes, exponents)
    text, stale = pick(groups, text_kv, stale_kv)

    every, some, left, right, query = merge([packed[0], *along(packed)])
    own_far = swap(own, 2)

    ready = (every, some, left, right, query, weight, weight_far, own_far, text, stale)
    every, some, left, right, query, weight, weight_far = lax.optimization_barrier(ready)[:7]
    left, right, some_far = swap(left, 1), swap(right, 1), swap(some, 2)
    share = stale.shape[2]
    operands = [query, every, left, right, text, stale]
    state = attend_call(near_kernel, operands, state_shapes(query), 2 * share + text.shape[1])

    ready = (some_far, own_far, stack(weight, weight_far), *state)
    some_far, own_far, weight = lax.optimization_barrier(ready)[:3]
    own_corner, some_corner = swap(own_far, 1), swap(some_far, 1)
    state = attend_call(middle_kernel, [query, own_far, some_far, stale, *state], state_shapes(query), share)
    weight = after(weight, own_corner, some_corner, *state)
    weight_across = swap(weight, 1)
    operands = [query, own_corner, some_corner, stale, *state]
    shape = jax.ShapeDtypeStruct(query.shape, jnp.bfloat16)
    (attended,) = attend_call(last_kernel, operands, [shape], share)

    second, first = swap(attended, 2 * SPREAD), swap(attended, SPREAD)
    third = swap(second, SPREAD)
    weight = order(weight, weight_across)
    terms = close(groups, begin([attended, second, first], weight), third, weight)
    kept, sent = divide([terms[0], *along(terms)])
    received = lax.ppermute(sent, "head", [(0, 1), (1, 0)])
    return finish(kept, received, out_bias, out_gate)


def solution(mesh):
    patches, halves = mesh.shape["patch"], mesh.shape["head"]
    placed = (
        P("patch", "head"),
        P(None, None, "head"),
        P(None, "patch", "head"),
        P(None, "patch", "head"),
        P(None, None, "head"),
        P("head", "patch"),
        P("head"),
        P("head"),
    )

    def body(*args):
        heads = args[0].shape[1] // HD
        groups = patches // SPREAD
        if groups != 4 or patches % SPREAD or heads % groups or halves != 2:
            return plain_body(*args)
        return grouped_body(*args)

    return jax.shard_map(body, mesh=mesh, in_specs=placed, out_specs=P("patch", "head"), check_vma=False)
```

```python
import functools

import jax
import jax.numpy as jnp
from jax import lax
from jax.experimental import pallas as pl
from jax.experimental.pallas import tpu as pltpu
from jax.sharding import PartitionSpec as P

HD = 128
SPREAD = 4
TURNS = (0, 2, 3, 1)
PACK_LIMIT = 56 << 20
SMALL = 16 << 20
PICK_LIMIT = 50 << 20
VMEM = pl.BlockSpec(memory_space=pltpu.VMEM)
HBM = pl.BlockSpec(memory_space=pltpu.HBM)
NT = (((1,), (1,)), ((), ()))


def plain_body(queries, stale_kv, codes, exponents, text_kv, out_weight, out_bias, out_gate):
    tok_rows = queries.shape[0]
    row_width = queries.shape[1]
    head_count = row_width // HD
    text_count = text_kv.shape[1]
    scale_factor = HD ** (-0.5)
    blocks = jnp.exp2(exponents.astype(jnp.float32))
    decoded = codes.astype(jnp.float32).reshape(2, tok_rows, head_count, HD) * blocks[..., None]
    decoded = decoded.astype(jnp.bfloat16).reshape(2, tok_rows, row_width)
    arrived = lax.all_gather(decoded, "patch", axis=1, tiled=True)
    all_rows = arrived.shape[1]
    query_heads = queries.reshape(tok_rows, head_count, HD)
    text_heads = text_kv.reshape(2, text_count, head_count, HD)
    stale_heads = stale_kv.reshape(2, all_rows, head_count, HD)
    arrived_heads = arrived.reshape(2, all_rows, head_count, HD)
    text_scores = jnp.einsum("thd,khd->htk", query_heads, text_heads[0], preferred_element_type=jnp.float32)
    rebuilt = stale_heads.astype(jnp.float32) + arrived_heads.astype(jnp.float32)
    image_scores = jnp.einsum(
        "thd,khd->htk", query_heads.astype(jnp.float32), rebuilt[0], precision=lax.Precision.HIGHEST
    )
    scores = jnp.concatenate([text_scores, image_scores], axis=2) * scale_factor
    row_peak = jnp.max(scores, axis=2, keepdims=True)
    weights = jnp.exp(scores - row_peak).astype(jnp.bfloat16)
    row_total = jnp.sum(weights.astype(jnp.float32), axis=2)
    text_part = jnp.einsum(
        "htk,khd->thd", weights[:, :, :text_count], text_heads[1], preferred_element_type=jnp.float32
    )
    image_part = jnp.einsum(
        "htk,khd->thd",
        weights[:, :, text_count:].astype(jnp.float32),
        rebuilt[1],
        precision=lax.Precision.HIGHEST,
    )
    attended = ((text_part + image_part) / row_total.T[:, :, None]).astype(jnp.bfloat16).reshape(tok_rows, row_width)
    partial_terms = jnp.dot(
        attended, lax.all_gather(out_weight, "patch", axis=1, tiled=True), preferred_element_type=jnp.float32
    )
    column_share = lax.psum_scatter(partial_terms, "head", scatter_dimension=1, tiled=True)
    return (out_gate * (column_share + out_bias)).astype(jnp.bfloat16)


def aligned(value, step):
    return pl.multiple_of(value * step, step)


def place():
    me = lax.axis_index("patch")
    return me // SPREAD, lax.rem(me, SPREAD)


def pack_kernel(queries_hbm, codes_hbm, exponents_hbm, *rest):
    outs, (codes, queries, exponents, held, sems) = rest[:-5], rest[-5:]
    groups, kinds, rows, width = held.shape
    group, _ = place()
    per = width // HD
    copies = [
        pltpu.make_async_copy(exponents_hbm, exponents, sems.at[0]),
        pltpu.make_async_copy(codes_hbm, codes, sems.at[1]),
        pltpu.make_async_copy(queries_hbm, queries, sems.at[2]),
    ]
    for copy in copies:
        copy.start()
    copies[0].wait()
    copies[1].wait()
    eye = lax.broadcasted_iota(jnp.int32, (rows, rows), 0) == lax.broadcasted_iota(jnp.int32, (rows, rows), 1)
    eye = eye.astype(jnp.float32).astype(jnp.bfloat16)
    for kind in range(kinds - 1):
        scales = jnp.left_shift(1, exponents[:, kind, :] + 16).astype(jnp.float32) * (2.0**-16)
        scales = lax.dot_general(eye, scales.astype(jnp.bfloat16), NT, preferred_element_type=jnp.float32)
        for head in range(groups * per):
            inside = slice((head % per) * HD, (head % per + 1) * HD)
            whole = slice(head * HD, (head + 1) * HD)
            decoded = codes[kind, :, whole].astype(jnp.float32) * scales[:, head : head + 1]
            held[head // per, kind, :, inside] = decoded.astype(jnp.bfloat16)
    copies[2].wait()
    for target in range(groups):
        held[target, kinds - 1] = queries[:, target * width : (target + 1) * width]
    for turn in range(groups):
        outs[turn][...] = held[jnp.bitwise_xor(group, turn)]
    outs[groups][...] = held[group, 0 : kinds - 1]


def pack(groups, queries, codes, exponents):
    rows, width = queries.shape
    kinds = codes.shape[0]
    share = width // groups
    bf16 = jnp.bfloat16
    exponents = exponents.transpose(2, 0, 1)
    shapes = [(kinds + 1, rows, share)] * groups + [(kinds, rows, share)]
    outs = pl.pallas_call(
        pack_kernel,
        out_shape=[jax.ShapeDtypeStruct(shape, bf16) for shape in shapes],
        in_specs=[HBM] * 3,
        out_specs=[VMEM] * len(shapes),
        scratch_shapes=[
            pltpu.VMEM(codes.shape, jnp.int32),
            pltpu.VMEM(queries.shape, bf16),
            pltpu.VMEM(exponents.shape, jnp.int32),
            pltpu.VMEM((groups, kinds + 1, rows, share), bf16),
            pltpu.SemaphoreType.DMA((3,)),
        ],
        compiler_params=pltpu.CompilerParams(vmem_limit_bytes=PACK_LIMIT),
        cost_estimate=pl.CostEstimate(flops=2 * codes.size, bytes_accessed=6 * codes.size, transcendentals=0),
    )(queries, codes, exponents)
    return outs


def pick_kernel(text_hbm, stale_hbm, text, stale, sems):
    group, spot = place()
    width = text.shape[2]
    groups = text_hbm.shape[2] // width
    rows = stale.shape[2] // groups
    columns = pl.ds(aligned(group, width), width)
    copies = [pltpu.make_async_copy(text_hbm.at[:, :, columns], text, sems.at[0])]
    for twist in range(SPREAD):
        for position in range(groups):
            origin = jnp.bitwise_xor(group, TURNS[position])
            token = origin * SPREAD + jnp.bitwise_xor(spot, twist)
            copies.append(
                pltpu.make_async_copy(
                    stale_hbm.at[:, pl.ds(aligned(token, rows), rows), columns],
                    stale.at[twist, :, pl.ds(position * rows, rows), :],
                    sems.at[len(copies)],
                )
            )
    for copy in copies:
        copy.start()
    for copy in copies:
        copy.wait()


def pick(groups, text_kv, stale_kv):
    kinds, texts, heads_width = text_kv.shape
    width = heads_width // groups
    return pl.pallas_call(
        pick_kernel,
        out_shape=[
            jax.ShapeDtypeStruct((kinds, texts, width), jnp.bfloat16),
            jax.ShapeDtypeStruct((SPREAD, kinds, stale_kv.shape[1] // SPREAD, width), jnp.bfloat16),
        ],
        in_specs=[HBM] * 2,
        out_specs=[VMEM] * 2,
        scratch_shapes=[pltpu.SemaphoreType.DMA((1 + SPREAD * groups,))],
        compiler_params=pltpu.CompilerParams(vmem_limit_bytes=PICK_LIMIT),
        cost_estimate=pl.CostEstimate(flops=0, bytes_accessed=8 << 20, transcendentals=0),
    )(text_kv, stale_kv)


def merge_kernel(*refs):
    parts, (every, some, left, right, query) = refs[:-5], refs[-5:]
    groups, kinds, rows, _ = every.shape
    group, _ = place()
    for position, part in enumerate(parts):
        every[position] = part[0:kinds]
        if position:
            some[position - 1] = part[0:kinds]
        (left, right)[position // 2][position % 2] = part[0:kinds]
        origin = jnp.bitwise_xor(group, TURNS[position])
        query[pl.ds(aligned(origin, rows), rows), :] = part[kinds]


def merge(parts):
    kinds, rows, width = parts[0].shape
    counts = (len(parts), len(parts) - 1, len(parts) // 2, len(parts) // 2)
    shapes = [(count, kinds - 1, rows, width) for count in counts] + [(len(parts) * rows, width)]
    return pl.pallas_call(
        merge_kernel,
        out_shape=[jax.ShapeDtypeStruct(shape, jnp.bfloat16) for shape in shapes],
        in_specs=[VMEM] * len(parts),
        out_specs=[VMEM] * 5,
        compiler_params=pltpu.CompilerParams(vmem_limit_bytes=SMALL),
        cost_estimate=pl.CostEstimate(flops=0, bytes_accessed=4 * len(parts) * parts[0].size, transcendentals=0),
    )(*parts)


def absorb(queries, segments, states):
    scores = [
        [
            lax.dot_general(
                query if key.shape[1] == HD else jnp.concatenate([query, query], axis=1),
                key,
                NT,
                preferred_element_type=jnp.float32,
            )
            * HD**-0.5
            for key, _ in parts
        ]
        for query, parts in zip(queries, segments)
    ]
    peaks = [[jnp.max(score, axis=1, keepdims=True) for score in row] for row in scores]
    if states is not None:
        peaks = [row + [state[0]] for row, state in zip(peaks, states)]
    peaks = [functools.reduce(jnp.maximum, row) for row in peaks]
    weights = [
        [jnp.exp(score - peak).astype(jnp.bfloat16) for score in row] for row, peak in zip(scores, peaks)
    ]
    totals = [sum(jnp.sum(w.astype(jnp.float32), axis=1, keepdims=True) for w in row) for row in weights]
    mixes = [
        sum(jnp.dot(w, value, preferred_element_type=jnp.float32) for w, (_, value) in zip(row, parts))
        for row, parts in zip(weights, segments)
    ]
    if states is not None:
        fades = [jnp.exp(state[0] - peak) for state, peak in zip(states, peaks)]
        totals = [total + state[1] * fade for total, state, fade in zip(totals, states, fades)]
        mixes = [mix + state[2] * fade for mix, state, fade in zip(mixes, states, fades)]
    return list(zip(peaks, totals, mixes))


def columns_of(width):
    return [slice(start, start + HD) for start in range(0, width, HD)]


def image_segment(stale, twist, residual):
    def of(cols):
        key = jnp.concatenate([stale[twist, 0, :, cols], residual(0, cols)], axis=1)
        value = stale[twist, 1, :, cols].astype(jnp.float32) + residual(1, cols).astype(jnp.float32)
        return key, value.astype(jnp.bfloat16)

    return of


def whole_part(part):
    return lambda kind, cols: part[:, kind, :, cols].reshape(-1, HD)


def halves_part(*parts):
    wholes = [whole_part(part) for part in parts]
    return lambda kind, cols: jnp.concatenate([whole(kind, cols) for whole in wholes], axis=0)


def split_part(own, some):
    return lambda kind, cols: jnp.concatenate([own[kind, :, cols], some[:, kind, :, cols].reshape(-1, HD)], axis=0)


def near_kernel(query, every, left, right, text, stale, peak, total, mixed):
    heads = columns_of(query.shape[1])
    images = [image_segment(stale, 0, whole_part(every)), image_segment(stale, 1, halves_part(left, right))]
    segments = [[(text[0, :, cols], text[1, :, cols])] + [image(cols) for image in images] for cols in heads]
    states = absorb([query[:, cols] for cols in heads], segments, None)
    for head, state in enumerate(states):
        peak[head], total[head], mixed[head] = state


def middle_kernel(query, own_far, some_far, stale, peak_in, total_in, mixed_in, peak, total, mixed):
    heads = columns_of(query.shape[1])
    image = image_segment(stale, 2, split_part(own_far, some_far))
    segments = [[image(cols)] for cols in heads]
    states = [(peak_in[head], total_in[head], mixed_in[head]) for head in range(len(heads))]
    states = absorb([query[:, cols] for cols in heads], segments, states)
    for head, state in enumerate(states):
        peak[head], total[head], mixed[head] = state


def last_kernel(query, own_corner, some_corner, stale, peak, total, mixed, out):
    heads = columns_of(query.shape[1])
    image = image_segment(stale, 3, split_part(own_corner, some_corner))
    states = [(peak[head], total[head], mixed[head]) for head in range(len(heads))]
    states = absorb([query[:, cols] for cols in heads], [[image(cols)] for cols in heads], states)
    for cols, (_, sums, mix) in zip(heads, states):
        out[:, cols] = (mix / sums).astype(jnp.bfloat16)


def attend_call(kernel, operands, shapes, keys):
    tokens, width = operands[0].shape
    return pl.pallas_call(
        kernel,
        out_shape=shapes,
        in_specs=[VMEM] * len(operands),
        out_specs=[VMEM] * len(shapes),
        compiler_params=pltpu.CompilerParams(vmem_limit_bytes=SMALL),
        cost_estimate=pl.CostEstimate(
            flops=8 * tokens * width * keys, bytes_accessed=8 * width * keys, transcendentals=tokens * keys * width // HD
        ),
    )(*operands)


def state_shapes(query):
    tokens, width = query.shape
    heads = width // HD
    return [jax.ShapeDtypeStruct((heads, tokens, size), jnp.float32) for size in (1, 1, HD)]


def stack_kernel(first, second, out):
    out[0] = first[...]
    out[1] = second[...]


def stack(first, second):
    return pl.pallas_call(
        stack_kernel,
        out_shape=jax.ShapeDtypeStruct((2, *first.shape), first.dtype),
        in_specs=[VMEM] * 2,
        out_specs=VMEM,
        compiler_params=pltpu.CompilerParams(vmem_limit_bytes=SMALL),
        cost_estimate=pl.CostEstimate(flops=0, bytes_accessed=8 * first.size, transcendentals=0),
    )(first, second)


def order_kernel(own, across, out):
    _, spot = place()
    span = own.shape[1]
    for twist in range(SPREAD):
        piece = (own, across)[twist % 2][twist // 2]
        out[pl.ds(aligned(jnp.bitwise_xor(spot, twist), span), span), :] = piece


def order(own, across):
    count, span, depth = own.shape
    shape = (2 * count * span, depth)
    return pl.pallas_call(
        order_kernel,
        out_shape=jax.ShapeDtypeStruct(shape, jnp.bfloat16),
        in_specs=[VMEM] * 2,
        out_specs=VMEM,
        compiler_params=pltpu.CompilerParams(vmem_limit_bytes=SMALL),
        cost_estimate=pl.CostEstimate(flops=0, bytes_accessed=4 * shape[0] * depth, transcendentals=0),
    )(own, across)


def term_of(part, weight, turn, width, skip=0):
    group, _ = place()
    start = jnp.bitwise_xor(group, turn) * width + skip
    columns = pl.ds(pl.multiple_of(start, HD), part.shape[1])
    return lax.dot_general(part[...], weight[:, columns], NT, preferred_element_type=jnp.float32)


def begin_kernel(own, second, first, weight, out):
    width = own.shape[1]
    out[...] = term_of(own, weight, 0, width) + term_of(second, weight, 2, width) + term_of(first, weight, 1, width)


def begin(parts, weight):
    tokens = parts[0].shape[0]
    columns, depth = weight.shape
    return pl.pallas_call(
        begin_kernel,
        out_shape=jax.ShapeDtypeStruct((tokens, columns), jnp.float32),
        in_specs=[VMEM] * (len(parts) + 1),
        out_specs=VMEM,
        compiler_params=pltpu.CompilerParams(vmem_limit_bytes=SMALL),
        cost_estimate=pl.CostEstimate(
            flops=2 * tokens * columns * depth, bytes_accessed=4 * tokens * columns, transcendentals=0
        ),
    )(*parts, weight)


def close_kernel(partial, third, weight, *rest):
    outs, total = rest[:-1], rest[-1]
    group, _ = place()
    rows = outs[0].shape[0]
    total[...] = (partial[...] + term_of(third, weight, 3, third.shape[1])).astype(jnp.bfloat16)
    for turn, out in enumerate(outs):
        out[...] = total[pl.ds(aligned(jnp.bitwise_xor(group, turn), rows), rows), :]


def close(groups, partial, third, weight):
    tokens, columns = partial.shape
    return pl.pallas_call(
        close_kernel,
        out_shape=[jax.ShapeDtypeStruct((tokens // groups, columns), jnp.bfloat16)] * groups,
        in_specs=[VMEM] * 3,
        out_specs=[VMEM] * groups,
        scratch_shapes=[pltpu.VMEM((tokens, columns), jnp.bfloat16)],
        compiler_params=pltpu.CompilerParams(vmem_limit_bytes=SMALL),
        cost_estimate=pl.CostEstimate(
            flops=tokens * weight.size, bytes_accessed=8 * tokens * columns, transcendentals=0
        ),
    )(partial, third, weight)


def divide_kernel(*refs):
    parts, (keep, send, held) = refs[:-3], refs[-3:]
    group, _ = place()
    half = lax.axis_index("head")
    blocks = keep.shape[0]
    for position, part in enumerate(parts):
        held[jnp.bitwise_xor(group, TURNS[position])] = part[...]
    for block in range(blocks):
        keep[block] = held[half * blocks + block]
        send[block] = held[(1 - half) * blocks + block]


def divide(parts):
    groups = len(parts)
    shape = jax.ShapeDtypeStruct((groups // 2, *parts[0].shape), jnp.bfloat16)
    return pl.pallas_call(
        divide_kernel,
        out_shape=[shape] * 2,
        in_specs=[VMEM] * groups,
        out_specs=[VMEM] * 2,
        scratch_shapes=[pltpu.VMEM((groups, *parts[0].shape), jnp.bfloat16)],
        compiler_params=pltpu.CompilerParams(vmem_limit_bytes=SMALL),
        cost_estimate=pl.CostEstimate(flops=0, bytes_accessed=4 * groups * parts[0].size, transcendentals=0),
    )(*parts)


def finish_kernel(kept, arrived, bias, gate, out):
    blocks, _, columns = kept.shape
    for block in range(blocks):
        cols = slice(block * columns, (block + 1) * columns)
        total = kept[block].astype(jnp.float32) + arrived[block].astype(jnp.float32)
        out[:, cols] = (gate[:, cols] * (total + bias[:, cols])).astype(jnp.bfloat16)


def finish(kept, arrived, bias, gate):
    blocks, rows, columns = kept.shape
    width = blocks * columns
    return pl.pallas_call(
        finish_kernel,
        out_shape=jax.ShapeDtypeStruct((rows, width), jnp.bfloat16),
        in_specs=[VMEM] * 4,
        out_specs=VMEM,
        compiler_params=pltpu.CompilerParams(vmem_limit_bytes=SMALL),
        cost_estimate=pl.CostEstimate(flops=3 * rows * width, bytes_accessed=4 * rows * width, transcendentals=0),
    )(kept, arrived, bias.reshape(1, width), gate.reshape(1, width))


def after(value, *others):
    return lax.optimization_barrier((value, *others))[0]


def grouped_body(queries, stale_kv, codes, exponents, text_kv, out_weight, out_bias, out_gate):
    groups = lax.axis_size("patch") // SPREAD
    size = groups * SPREAD

    def swap(value, twist):
        return lax.ppermute(value, "patch", [(p, p ^ twist) for p in range(size)])

    def along(values):
        return [swap(values[turn], turn * SPREAD) for turn in TURNS[1:]]

    weight = out_weight.T
    weight_far = swap(weight, 2)
    *packed, own = pack(groups, queries, codes, exponents)
    text, stale = pick(groups, text_kv, stale_kv)

    every, some, left, right, query = merge([packed[0], *along(packed)])
    own_far = swap(own, 2)

    ready = (every, some, left, right, query, own_far, text, stale)
    every, some, left, right, query = lax.optimization_barrier(ready)[:5]
    left, right, some_far = swap(left, 1), swap(right, 1), swap(some, 2)
    share = stale.shape[2]
    operands = [query, every, left, right, text, stale]
    state = attend_call(near_kernel, operands, state_shapes(query), 2 * share + text.shape[1])

    ready = (some_far, own_far, stack(weight, weight_far), *state)
    some_far, own_far, weight = lax.optimization_barrier(ready)[:3]
    own_corner, some_corner = swap(own_far, 1), swap(some_far, 1)
    state = attend_call(middle_kernel, [query, own_far, some_far, stale, *state], state_shapes(query), share)
    weight = after(weight, own_corner, some_corner, *state)
    weight_across = swap(weight, 1)
    operands = [query, own_corner, some_corner, stale, *state]
    shape = jax.ShapeDtypeStruct(query.shape, jnp.bfloat16)
    (attended,) = attend_call(last_kernel, operands, [shape], share)

    second, first = swap(attended, 2 * SPREAD), swap(attended, SPREAD)
    third = swap(second, SPREAD)
    weight = order(weight, weight_across)
    terms = close(groups, begin([attended, second, first], weight), third, weight)
    kept, sent = divide([terms[0], *along(terms)])
    received = lax.ppermute(sent, "head", [(0, 1), (1, 0)])
    return finish(kept, received, out_bias, out_gate)


def solution(mesh):
    patches, halves = mesh.shape["patch"], mesh.shape["head"]
    placed = (
        P("patch", "head"),
        P(None, None, "head"),
        P(None, "patch", "head"),
        P(None, "patch", "head"),
        P(None, None, "head"),
        P("head", "patch"),
        P("head"),
        P("head"),
    )

    def body(*args):
        heads = args[0].shape[1] // HD
        groups = patches // SPREAD
        if groups != 4 or patches % SPREAD or heads % groups or halves != 2:
            return plain_body(*args)
        return grouped_body(*args)

    return jax.shard_map(body, mesh=mesh, in_specs=placed, out_specs=P("patch", "head"), check_vma=False)
```

```python
import functools

import jax
import jax.numpy as jnp
from jax import lax
from jax.experimental import pallas as pl
from jax.experimental.pallas import tpu as pltpu
from jax.sharding import PartitionSpec as P

HD = 128
SPREAD = 4
TURNS = (0, 2, 3, 1)
PACK_LIMIT = 56 << 20
SMALL = 16 << 20
PICK_LIMIT = 50 << 20
VMEM = pl.BlockSpec(memory_space=pltpu.VMEM)
HBM = pl.BlockSpec(memory_space=pltpu.HBM)
NT = (((1,), (1,)), ((), ()))


def plain_body(queries, stale_kv, codes, exponents, text_kv, out_weight, out_bias, out_gate):
    tok_rows = queries.shape[0]
    row_width = queries.shape[1]
    head_count = row_width // HD
    text_count = text_kv.shape[1]
    scale_factor = HD ** (-0.5)
    blocks = jnp.exp2(exponents.astype(jnp.float32))
    decoded = codes.astype(jnp.float32).reshape(2, tok_rows, head_count, HD) * blocks[..., None]
    decoded = decoded.astype(jnp.bfloat16).reshape(2, tok_rows, row_width)
    arrived = lax.all_gather(decoded, "patch", axis=1, tiled=True)
    all_rows = arrived.shape[1]
    query_heads = queries.reshape(tok_rows, head_count, HD)
    text_heads = text_kv.reshape(2, text_count, head_count, HD)
    stale_heads = stale_kv.reshape(2, all_rows, head_count, HD)
    arrived_heads = arrived.reshape(2, all_rows, head_count, HD)
    text_scores = jnp.einsum("thd,khd->htk", query_heads, text_heads[0], preferred_element_type=jnp.float32)
    rebuilt = stale_heads.astype(jnp.float32) + arrived_heads.astype(jnp.float32)
    image_scores = jnp.einsum(
        "thd,khd->htk", query_heads.astype(jnp.float32), rebuilt[0], precision=lax.Precision.HIGHEST
    )
    scores = jnp.concatenate([text_scores, image_scores], axis=2) * scale_factor
    row_peak = jnp.max(scores, axis=2, keepdims=True)
    weights = jnp.exp(scores - row_peak).astype(jnp.bfloat16)
    row_total = jnp.sum(weights.astype(jnp.float32), axis=2)
    text_part = jnp.einsum(
        "htk,khd->thd", weights[:, :, :text_count], text_heads[1], preferred_element_type=jnp.float32
    )
    image_part = jnp.einsum(
        "htk,khd->thd",
        weights[:, :, text_count:].astype(jnp.float32),
        rebuilt[1],
        precision=lax.Precision.HIGHEST,
    )
    attended = ((text_part + image_part) / row_total.T[:, :, None]).astype(jnp.bfloat16).reshape(tok_rows, row_width)
    partial_terms = jnp.dot(
        attended, lax.all_gather(out_weight, "patch", axis=1, tiled=True), preferred_element_type=jnp.float32
    )
    column_share = lax.psum_scatter(partial_terms, "head", scatter_dimension=1, tiled=True)
    return (out_gate * (column_share + out_bias)).astype(jnp.bfloat16)


def aligned(value, step):
    return pl.multiple_of(value * step, step)


def place():
    me = lax.axis_index("patch")
    return me // SPREAD, lax.rem(me, SPREAD)


def pack_kernel(queries_hbm, codes_hbm, exponents_hbm, *rest):
    outs, (codes, queries, exponents, held, sems) = rest[:-5], rest[-5:]
    groups, kinds, rows, width = held.shape
    group, _ = place()
    per = width // HD
    copies = [
        pltpu.make_async_copy(exponents_hbm, exponents, sems.at[0]),
        pltpu.make_async_copy(codes_hbm, codes, sems.at[1]),
        pltpu.make_async_copy(queries_hbm, queries, sems.at[2]),
    ]
    for copy in copies:
        copy.start()
    copies[0].wait()
    copies[1].wait()
    eye = lax.broadcasted_iota(jnp.int32, (rows, rows), 0) == lax.broadcasted_iota(jnp.int32, (rows, rows), 1)
    eye = eye.astype(jnp.float32).astype(jnp.bfloat16)
    for kind in range(kinds - 1):
        scales = jnp.left_shift(1, exponents[:, kind, :] + 16).astype(jnp.float32) * (2.0**-16)
        scales = lax.dot_general(eye, scales.astype(jnp.bfloat16), NT, preferred_element_type=jnp.float32)
        for head in range(groups * per):
            inside = slice((head % per) * HD, (head % per + 1) * HD)
            whole = slice(head * HD, (head + 1) * HD)
            decoded = codes[kind, :, whole].astype(jnp.float32) * scales[:, head : head + 1]
            held[head // per, kind, :, inside] = decoded.astype(jnp.bfloat16)
    copies[2].wait()
    for target in range(groups):
        held[target, kinds - 1] = queries[:, target * width : (target + 1) * width]
    for turn in range(groups):
        outs[turn][...] = held[jnp.bitwise_xor(group, turn)]
    outs[groups][...] = held[group, 0 : kinds - 1]


def pack(groups, queries, codes, exponents):
    rows, width = queries.shape
    kinds = codes.shape[0]
    share = width // groups
    bf16 = jnp.bfloat16
    exponents = exponents.transpose(2, 0, 1)
    shapes = [(kinds + 1, rows, share)] * groups + [(kinds, rows, share)]
    outs = pl.pallas_call(
        pack_kernel,
        out_shape=[jax.ShapeDtypeStruct(shape, bf16) for shape in shapes],
        in_specs=[HBM] * 3,
        out_specs=[VMEM] * len(shapes),
        scratch_shapes=[
            pltpu.VMEM(codes.shape, jnp.int32),
            pltpu.VMEM(queries.shape, bf16),
            pltpu.VMEM(exponents.shape, jnp.int32),
            pltpu.VMEM((groups, kinds + 1, rows, share), bf16),
            pltpu.SemaphoreType.DMA((3,)),
        ],
        compiler_params=pltpu.CompilerParams(vmem_limit_bytes=PACK_LIMIT),
        cost_estimate=pl.CostEstimate(flops=2 * codes.size, bytes_accessed=6 * codes.size, transcendentals=0),
    )(queries, codes, exponents)
    return outs


def pick_kernel(text_hbm, stale_hbm, text, stale, sems):
    group, spot = place()
    width = text.shape[2]
    groups = text_hbm.shape[2] // width
    rows = stale.shape[2] // groups
    columns = pl.ds(aligned(group, width), width)
    copies = [pltpu.make_async_copy(text_hbm.at[:, :, columns], text, sems.at[0])]
    for twist in range(SPREAD):
        for position in range(groups):
            origin = jnp.bitwise_xor(group, TURNS[position])
            token = origin * SPREAD + jnp.bitwise_xor(spot, twist)
            copies.append(
                pltpu.make_async_copy(
                    stale_hbm.at[:, pl.ds(aligned(token, rows), rows), columns],
                    stale.at[twist, :, pl.ds(position * rows, rows), :],
                    sems.at[len(copies)],
                )
            )
    for copy in copies:
        copy.start()
    for copy in copies:
        copy.wait()


def pick(groups, text_kv, stale_kv):
    kinds, texts, heads_width = text_kv.shape
    width = heads_width // groups
    return pl.pallas_call(
        pick_kernel,
        out_shape=[
            jax.ShapeDtypeStruct((kinds, texts, width), jnp.bfloat16),
            jax.ShapeDtypeStruct((SPREAD, kinds, stale_kv.shape[1] // SPREAD, width), jnp.bfloat16),
        ],
        in_specs=[HBM] * 2,
        out_specs=[VMEM] * 2,
        scratch_shapes=[pltpu.SemaphoreType.DMA((1 + SPREAD * groups,))],
        compiler_params=pltpu.CompilerParams(vmem_limit_bytes=PICK_LIMIT),
        cost_estimate=pl.CostEstimate(flops=0, bytes_accessed=8 << 20, transcendentals=0),
    )(text_kv, stale_kv)


def merge_kernel(*refs):
    parts, (every, some, left, right, query) = refs[:-5], refs[-5:]
    groups, kinds, rows, _ = every.shape
    group, _ = place()
    for position, part in enumerate(parts):
        every[position] = part[0:kinds]
        if position:
            some[position - 1] = part[0:kinds]
        (left, right)[position // 2][position % 2] = part[0:kinds]
        origin = jnp.bitwise_xor(group, TURNS[position])
        query[pl.ds(aligned(origin, rows), rows), :] = part[kinds]


def merge(parts):
    kinds, rows, width = parts[0].shape
    counts = (len(parts), len(parts) - 1, len(parts) // 2, len(parts) // 2)
    shapes = [(count, kinds - 1, rows, width) for count in counts] + [(len(parts) * rows, width)]
    return pl.pallas_call(
        merge_kernel,
        out_shape=[jax.ShapeDtypeStruct(shape, jnp.bfloat16) for shape in shapes],
        in_specs=[VMEM] * len(parts),
        out_specs=[VMEM] * 5,
        compiler_params=pltpu.CompilerParams(vmem_limit_bytes=SMALL),
        cost_estimate=pl.CostEstimate(flops=0, bytes_accessed=4 * len(parts) * parts[0].size, transcendentals=0),
    )(*parts)


def absorb(queries, segments, states):
    scores = [
        [
            lax.dot_general(
                query if key.shape[1] == HD else jnp.concatenate([query, query], axis=1),
                key,
                NT,
                preferred_element_type=jnp.float32,
            )
            * HD**-0.5
            for key, _ in parts
        ]
        for query, parts in zip(queries, segments)
    ]
    peaks = [[jnp.max(score, axis=1, keepdims=True) for score in row] for row in scores]
    if states is not None:
        peaks = [row + [state[0]] for row, state in zip(peaks, states)]
    peaks = [functools.reduce(jnp.maximum, row) for row in peaks]
    weights = [
        [jnp.exp(score - peak).astype(jnp.bfloat16) for score in row] for row, peak in zip(scores, peaks)
    ]
    totals = [sum(jnp.sum(w.astype(jnp.float32), axis=1, keepdims=True) for w in row) for row in weights]
    mixes = [
        sum(jnp.dot(w, value, preferred_element_type=jnp.float32) for w, (_, value) in zip(row, parts))
        for row, parts in zip(weights, segments)
    ]
    if states is not None:
        fades = [jnp.exp(state[0] - peak) for state, peak in zip(states, peaks)]
        totals = [total + state[1] * fade for total, state, fade in zip(totals, states, fades)]
        mixes = [mix + state[2] * fade for mix, state, fade in zip(mixes, states, fades)]
    return list(zip(peaks, totals, mixes))


def columns_of(width):
    return [slice(start, start + HD) for start in range(0, width, HD)]


def image_segment(stale, twist, residual):
    def of(cols):
        key = jnp.concatenate([stale[twist, 0, :, cols], residual(0, cols)], axis=1)
        value = stale[twist, 1, :, cols].astype(jnp.float32) + residual(1, cols).astype(jnp.float32)
        return key, value.astype(jnp.bfloat16)

    return of


def whole_part(part):
    return lambda kind, cols: part[:, kind, :, cols].reshape(-1, HD)


def halves_part(*parts):
    wholes = [whole_part(part) for part in parts]
    return lambda kind, cols: jnp.concatenate([whole(kind, cols) for whole in wholes], axis=0)


def split_part(own, some):
    return lambda kind, cols: jnp.concatenate([own[kind, :, cols], some[:, kind, :, cols].reshape(-1, HD)], axis=0)


def near_kernel(query, every, left, right, text, stale, peak, total, mixed):
    heads = columns_of(query.shape[1])
    images = [image_segment(stale, 0, whole_part(every)), image_segment(stale, 1, halves_part(left, right))]
    segments = [[(text[0, :, cols], text[1, :, cols])] + [image(cols) for image in images] for cols in heads]
    states = absorb([query[:, cols] for cols in heads], segments, None)
    for head, state in enumerate(states):
        peak[head], total[head], mixed[head] = state


def middle_kernel(query, own_far, some_far, stale, peak_in, total_in, mixed_in, peak, total, mixed):
    heads = columns_of(query.shape[1])
    image = image_segment(stale, 2, split_part(own_far, some_far))
    segments = [[image(cols)] for cols in heads]
    states = [(peak_in[head], total_in[head], mixed_in[head]) for head in range(len(heads))]
    states = absorb([query[:, cols] for cols in heads], segments, states)
    for head, state in enumerate(states):
        peak[head], total[head], mixed[head] = state


def last_kernel(query, own_corner, some_corner, stale, peak, total, mixed, out):
    heads = columns_of(query.shape[1])
    image = image_segment(stale, 3, split_part(own_corner, some_corner))
    states = [(peak[head], total[head], mixed[head]) for head in range(len(heads))]
    states = absorb([query[:, cols] for cols in heads], [[image(cols)] for cols in heads], states)
    for cols, (_, sums, mix) in zip(heads, states):
        out[:, cols] = (mix / sums).astype(jnp.bfloat16)


def attend_call(kernel, operands, shapes, keys):
    tokens, width = operands[0].shape
    return pl.pallas_call(
        kernel,
        out_shape=shapes,
        in_specs=[VMEM] * len(operands),
        out_specs=[VMEM] * len(shapes),
        compiler_params=pltpu.CompilerParams(vmem_limit_bytes=SMALL),
        cost_estimate=pl.CostEstimate(
            flops=8 * tokens * width * keys, bytes_accessed=8 * width * keys, transcendentals=tokens * keys * width // HD
        ),
    )(*operands)


def state_shapes(query):
    tokens, width = query.shape
    heads = width // HD
    return [jax.ShapeDtypeStruct((heads, tokens, size), jnp.float32) for size in (1, 1, HD)]


def stack_kernel(first, second, out):
    out[0] = first[...]
    out[1] = second[...]


def stack(first, second):
    return pl.pallas_call(
        stack_kernel,
        out_shape=jax.ShapeDtypeStruct((2, *first.shape), first.dtype),
        in_specs=[VMEM] * 2,
        out_specs=VMEM,
        compiler_params=pltpu.CompilerParams(vmem_limit_bytes=SMALL),
        cost_estimate=pl.CostEstimate(flops=0, bytes_accessed=8 * first.size, transcendentals=0),
    )(first, second)


def order_kernel(own, across, out):
    _, spot = place()
    span = own.shape[1]
    for twist in range(SPREAD):
        piece = (own, across)[twist % 2][twist // 2]
        out[pl.ds(aligned(jnp.bitwise_xor(spot, twist), span), span), :] = piece


def order(own, across):
    count, span, depth = own.shape
    shape = (2 * count * span, depth)
    return pl.pallas_call(
        order_kernel,
        out_shape=jax.ShapeDtypeStruct(shape, jnp.bfloat16),
        in_specs=[VMEM] * 2,
        out_specs=VMEM,
        compiler_params=pltpu.CompilerParams(vmem_limit_bytes=SMALL),
        cost_estimate=pl.CostEstimate(flops=0, bytes_accessed=4 * shape[0] * depth, transcendentals=0),
    )(own, across)


def term_of(part, weight, turn, width, skip=0):
    group, _ = place()
    start = jnp.bitwise_xor(group, turn) * width + skip
    columns = pl.ds(pl.multiple_of(start, HD), part.shape[1])
    return lax.dot_general(part[...], weight[:, columns], NT, preferred_element_type=jnp.float32)


def begin_kernel(own, second, first, weight, out):
    width = own.shape[1]
    out[...] = term_of(own, weight, 0, width) + term_of(second, weight, 2, width) + term_of(first, weight, 1, width)


def begin(parts, weight):
    tokens = parts[0].shape[0]
    columns, depth = weight.shape
    return pl.pallas_call(
        begin_kernel,
        out_shape=jax.ShapeDtypeStruct((tokens, columns), jnp.float32),
        in_specs=[VMEM] * (len(parts) + 1),
        out_specs=VMEM,
        compiler_params=pltpu.CompilerParams(vmem_limit_bytes=SMALL),
        cost_estimate=pl.CostEstimate(
            flops=2 * tokens * columns * depth, bytes_accessed=4 * tokens * columns, transcendentals=0
        ),
    )(*parts, weight)


def close_kernel(partial, third, weight, *rest):
    outs, total = rest[:-1], rest[-1]
    group, _ = place()
    rows = outs[0].shape[0]
    total[...] = (partial[...] + term_of(third, weight, 3, third.shape[1])).astype(jnp.bfloat16)
    for turn, out in enumerate(outs):
        out[...] = total[pl.ds(aligned(jnp.bitwise_xor(group, turn), rows), rows), :]


def close(groups, partial, third, weight):
    tokens, columns = partial.shape
    return pl.pallas_call(
        close_kernel,
        out_shape=[jax.ShapeDtypeStruct((tokens // groups, columns), jnp.bfloat16)] * groups,
        in_specs=[VMEM] * 3,
        out_specs=[VMEM] * groups,
        scratch_shapes=[pltpu.VMEM((tokens, columns), jnp.bfloat16)],
        compiler_params=pltpu.CompilerParams(vmem_limit_bytes=SMALL),
        cost_estimate=pl.CostEstimate(
            flops=tokens * weight.size, bytes_accessed=8 * tokens * columns, transcendentals=0
        ),
    )(partial, third, weight)


def divide_kernel(*refs):
    parts, (keep, send, held) = refs[:-3], refs[-3:]
    group, _ = place()
    half = lax.axis_index("head")
    blocks = keep.shape[0]
    for position, part in enumerate(parts):
        held[jnp.bitwise_xor(group, TURNS[position])] = part[...]
    for block in range(blocks):
        keep[block] = held[half * blocks + block]
        send[block] = held[(1 - half) * blocks + block]


def divide(parts):
    groups = len(parts)
    shape = jax.ShapeDtypeStruct((groups // 2, *parts[0].shape), jnp.bfloat16)
    return pl.pallas_call(
        divide_kernel,
        out_shape=[shape] * 2,
        in_specs=[VMEM] * groups,
        out_specs=[VMEM] * 2,
        scratch_shapes=[pltpu.VMEM((groups, *parts[0].shape), jnp.bfloat16)],
        compiler_params=pltpu.CompilerParams(vmem_limit_bytes=SMALL),
        cost_estimate=pl.CostEstimate(flops=0, bytes_accessed=4 * groups * parts[0].size, transcendentals=0),
    )(*parts)


def finish_kernel(kept, arrived, bias, gate, out):
    blocks, _, columns = kept.shape
    for block in range(blocks):
        cols = slice(block * columns, (block + 1) * columns)
        total = kept[block].astype(jnp.float32) + arrived[block].astype(jnp.float32)
        out[:, cols] = (gate[:, cols] * (total + bias[:, cols])).astype(jnp.bfloat16)


def finish(kept, arrived, bias, gate):
    blocks, rows, columns = kept.shape
    width = blocks * columns
    return pl.pallas_call(
        finish_kernel,
        out_shape=jax.ShapeDtypeStruct((rows, width), jnp.bfloat16),
        in_specs=[VMEM] * 4,
        out_specs=VMEM,
        compiler_params=pltpu.CompilerParams(vmem_limit_bytes=SMALL),
        cost_estimate=pl.CostEstimate(flops=3 * rows * width, bytes_accessed=4 * rows * width, transcendentals=0),
    )(kept, arrived, bias.reshape(1, width), gate.reshape(1, width))


def after(value, *others):
    return lax.optimization_barrier((value, *others))[0]


def grouped_body(queries, stale_kv, codes, exponents, text_kv, out_weight, out_bias, out_gate):
    groups = lax.axis_size("patch") // SPREAD
    size = groups * SPREAD

    def swap(value, twist):
        return lax.ppermute(value, "patch", [(p, p ^ twist) for p in range(size)])

    def along(values):
        return [swap(values[turn], turn * SPREAD) for turn in TURNS[1:]]

    weight = out_weight.T
    weight_far = swap(weight, 2)
    *packed, own = pack(groups, queries, codes, exponents)
    text, stale = pick(groups, text_kv, stale_kv)

    every, some, left, right, query = merge([packed[0], *along(packed)])
    own_far = swap(own, 2)

    ready = (every, some, left, right, query, text, stale)
    every, some, left, right, query = lax.optimization_barrier(ready)[:5]
    left, right, some_far = swap(left, 1), swap(right, 1), swap(some, 2)
    share = stale.shape[2]
    operands = [query, every, left, right, text, stale]
    state = attend_call(near_kernel, operands, state_shapes(query), 2 * share + text.shape[1])

    ready = (some_far, own_far, stack(weight, weight_far), *state)
    some_far, own_far, weight = lax.optimization_barrier(ready)[:3]
    own_corner, some_corner = swap(own_far, 1), swap(some_far, 1)
    state = attend_call(middle_kernel, [query, own_far, some_far, stale, *state], state_shapes(query), share)
    weight = after(weight, own_corner, some_corner, *state)
    weight_across = swap(weight, 1)
    operands = [query, own_corner, some_corner, stale, *state]
    shape = jax.ShapeDtypeStruct(query.shape, jnp.bfloat16)
    (attended,) = attend_call(last_kernel, operands, [shape], share)

    second, first = swap(attended, 2 * SPREAD), swap(attended, SPREAD)
    third = swap(second, SPREAD)
    weight = order(weight, weight_across)
    terms = close(groups, begin([attended, second, first], weight), third, weight)
    kept, sent = divide([terms[0], *along(terms)])
    received = lax.ppermute(sent, "head", [(0, 1), (1, 0)])
    return finish(kept, received, out_bias, out_gate)


def solution(mesh):
    patches, halves = mesh.shape["patch"], mesh.shape["head"]
    placed = (
        P("patch", "head"),
        P(None, None, "head"),
        P(None, "patch", "head"),
        P(None, "patch", "head"),
        P(None, None, "head"),
        P("head", "patch"),
        P("head"),
        P("head"),
    )

    def body(*args):
        heads = args[0].shape[1] // HD
        groups = patches // SPREAD
        if groups != 4 or patches % SPREAD or heads % groups or halves != 2:
            return plain_body(*args)
        return grouped_body(*args)

    return jax.shard_map(body, mesh=mesh, in_specs=placed, out_specs=P("patch", "head"), check_vma=False)
```
